256 devices in a mesh: gx: 64 (over y, z, core), gy: 4 (over x).
Axes of the slice: x: 4, y: 4, z: 8, core: 2. Of those that a mesh axis runs over, the one named last changes fastest.
Arguments:
- features: bfloat16 [49152, 256], P(('gx', 'gy')), may hold values from -6 to 6
- pre_act: bfloat16 [49152, 256], P(('gx', 'gy')), may hold values from -6 to 6
- grad_out: bfloat16 [49152, 256], P(('gx', 'gy')), may hold values from -24 to 24
- weight_one: bfloat16 [256, 6912], replicated, may hold values from -0.078125 to 0.078125
- weight_two: bfloat16 [256, 6912], replicated, may hold values from -0.078125 to 0.078125
- neighbours: int32 [49152, 27], P(('gx', 'gy')), may hold values from -1 to 383, as said below
- halo_list: int32 [256, 8, 24], P(('gx', 'gy')), may hold values from -1 to 191, as said below
- send_list: int32 [256, 64, 3], P(('gx', 'gy')), may hold values from -1 to 191, as said below
Outputs:
- grad_features: bfloat16 [49152, 256], P(('gx', 'gy'))
- grad_weight_one: float32 [256, 6912], P('gx', 'gy')
- grad_weight_two: float32 [256, 6912], P('gx', 'gy')
The draws below stay inside these ranges and needn't reach their ends.
Inputs may be any that keep to these rules, and one draw needn't show every extreme that they name: `neighbours`: A tile's live slots are its first ones: a quarter, a half, three quarters or all of its 192 slots, and tile 0 has all live. For a live slot, offset 13 names the slot itself and the others name a live slot of the same tile, a halo row (192 to 383), or -1; rows of dead slots are all -1. `halo_list`: entries are live slots of the sending tile, repeats allowed, or -1. `send_list`: every live slot of a tile appears exactly once in its list and dead slots never; -1 marks an unused place; a tile with all slots live fills all 3 places for every peer.
All inputs are finite; a program needn't handle non-finite values.
Results may differ from the reference program's by a relative error of at most 0.006.
Values may be sent and summed in bfloat16 or wider, within the bound.
No kernel may reach another device: no remote copies, remote signals or barrier semaphores. Data moves between devices by JAX's collectives and lax.ppermute only.
A program may use at most 128 MiB of HBM per device.

```python
import math
import jax
import jax.numpy as jnp
import numpy as np
from jax import lax

CHANNELS = 256
KERNEL = 27
SLOTS = 192
HALO = 24
CAP = 3
TILES = 256
SITES = 49152
N_GX = 64
N_GY = 4


def live_counts(key):
    levels = jax.random.randint(key, (TILES,), 0, 4)
    counts = SLOTS // 4 * jnp.array([1, 2, 3, 4], jnp.int32)[levels]
    return jnp.where(jnp.arange(TILES) == 0, SLOTS, counts)


def draw_neighbours(key, part):
    counts = live_counts(key)
    key = jax.random.fold_in(key, 1)
    subkeys = jax.random.split(key, 4)
    per_site = jnp.repeat(counts, SLOTS)
    slot_ids = jnp.tile(jnp.arange(SLOTS), TILES)
    present = jax.random.randint(subkeys[0], (SITES, KERNEL), 0, 10) < 7
    outside = jax.random.randint(subkeys[1], (SITES, KERNEL), 0, 10) < 3
    nearby = jax.random.randint(subkeys[2], (SITES, KERNEL), 0, 1 << 20) % per_site[:, None]
    remote = SLOTS + jax.random.randint(subkeys[3], (SITES, KERNEL), 0, 8 * HALO)
    neighbour_ids = jnp.where(outside, remote, nearby)
    neighbour_ids = jnp.where(present, neighbour_ids, -1)
    centre = jnp.arange(KERNEL) == KERNEL // 2
    neighbour_ids = jnp.where(centre[None, :], slot_ids[:, None], neighbour_ids)
    is_live = slot_ids < per_site
    return jnp.where(is_live[:, None], neighbour_ids, -1).astype(jnp.int32)


def draw_halo_list(key, part):
    counts = live_counts(key)
    key = jax.random.fold_in(key, 2)
    subkeys = jax.random.split(key, 2)
    chosen_slots = jax.random.randint(subkeys[0], (TILES, 8, HALO), 0, 1 << 20) % counts[:, None, None]
    unused = jax.random.randint(subkeys[1], (TILES, 8, HALO), 0, 8) == 0
    return jnp.where(unused, -1, chosen_slots).astype(jnp.int32)


def draw_send_list(key, part):
    counts = live_counts(key)
    key = jax.random.fold_in(key, 3)
    subkeys = jax.random.split(key, 2)
    slot_ids = jnp.arange(SLOTS)
    scores = jax.random.randint(subkeys[0], (TILES, SLOTS), 0, 1 << 16) * SLOTS + slot_ids[None, :]
    scores = jnp.where(slot_ids[None, :] < counts[:, None], scores, scores + (1 << 29))
    ranked = jnp.argsort(scores, axis=1)
    offset = jax.random.randint(subkeys[1], (TILES, 1, 1), 0, N_GX)
    peer_ids = jnp.arange(N_GX)[None, :, None]
    place_ids = jnp.arange(CAP)[None, None, :]
    rank_ids = place_ids * N_GX + (peer_ids - offset) % N_GX
    chosen = jnp.take_along_axis(ranked, rank_ids.reshape(TILES, -1), axis=1).reshape(TILES, N_GX, CAP)
    return jnp.where(rank_ids < counts[:, None, None], chosen, -1).astype(jnp.int32)


def raised(values, own_key, source, target, blocks, factor):
    def block_of(axis_at):
        return (jnp.arange(values.shape[axis_at]) // (values.shape[axis_at] // blocks)).reshape((-1,) + (1,) * (values.ndim - 1 - axis_at))

    first = jax.random.permutation(own_key, blocks)[block_of(target)]
    far = (block_of(target) + blocks // 2) % blocks
    return jnp.where((block_of(source) == first) | (block_of(source) == far), factor * values, values)


def steps_of(rng, dims, cuts, smallest, largest):
    factor_of, own = 1.0, jax.random.fold_in(rng, 6)
    for dim, shards_of in cuts:
        heights = jnp.exp(jax.random.uniform(jax.random.fold_in(own, dim), (shards_of,), jnp.float32, smallest / len(cuts), largest / len(cuts)))
        factor_of = factor_of * jnp.repeat(heights, dims[dim] // shards_of).reshape([-1 if axis == dim else 1 for axis in range(len(dims))])
    return factor_of


def gaussian(own_key, dims, deviation, bound, cuts=(), kind=jnp.bfloat16):
    values = deviation * jax.random.normal(own_key, dims, jnp.float32)
    if cuts:
        values = values * steps_of(own_key, dims, cuts, -0.22, 0.18)
    return jnp.clip(values, -bound, bound).astype(kind)


def gaussian_with(key, dims, width, bound, pieces, heavy, kind=jnp.bfloat16):
    values = width * jax.random.normal(key, dims, jnp.float32)
    if pieces:
        values = values * steps_of(key, dims, pieces, -0.22, 0.18)
    return jnp.clip(raised(values, jax.random.fold_in(key, 3), *heavy), -bound, bound).astype(kind)


def setup_inputs(seed: int = 0) -> dict:
    seeds = jax.random.split(jax.random.key(seed), 9)
    return {
        "features": gaussian(seeds[0], (SITES, CHANNELS), 1.0, 6.0, ((0, 256),)),
        "pre_act": gaussian(seeds[1], (SITES, CHANNELS), 1.0, 6.0, ((0, 256),)),
        "grad_out": gaussian_with(seeds[2], (SITES, CHANNELS), 1.0, 24.0, ((0, 256),), (0, 1, 256, 6.0)),
        "weight_one": gaussian(seeds[3], (CHANNELS, KERNEL * CHANNELS), (KERNEL * CHANNELS) ** -0.5, 0.078125),
        "weight_two": gaussian(seeds[4], (CHANNELS, KERNEL * CHANNELS), (KERNEL * CHANNELS) ** -0.5, 0.078125),
        "neighbours": draw_neighbours(jax.random.fold_in(seeds[8], 71), 0),
        "halo_list": draw_halo_list(jax.random.fold_in(seeds[8], 71), 0),
        "send_list": draw_send_list(jax.random.fold_in(seeds[8], 71), 0),
    }


DIRECTIONS = ((-1, -1), (-1, 0), (-1, 1), (0, -1), (0, 1), (1, -1), (1, 0), (1, 1))

def source_table():
    tile_ids = np.arange(N_GX * N_GY)
    line_ids = tile_ids // N_GY
    column_ids = tile_ids % N_GY
    source = np.zeros((tile_ids.size, 8), np.int32)
    present = np.zeros((tile_ids.size, 8), bool)
    for heading in range(8):
        step_x, step_y = DIRECTIONS[heading]
        from_x = line_ids - step_x
        from_y = column_ids - step_y
        inside = (from_x >= 0) & (from_x < N_GX) & (from_y >= 0) & (from_y < N_GY)
        source[:, heading] = np.where(inside, from_x * N_GY + from_y, 0)
        present[:, heading] = inside
    return (source, present)

def outside_rows(values, halo_list, source, present):
    chosen_slots = halo_list[source, np.arange(8)[None, :], :]
    usable = (chosen_slots >= 0) & present[:, :, None]
    flat_ids = jnp.where(usable, source[:, :, None] * SLOTS + chosen_slots, 0).astype(jnp.int32)
    gathered = values[flat_ids]
    gathered = jnp.where(usable[..., None], gathered, jnp.zeros((), values.dtype))
    return gathered.reshape(TILES, 8 * HALO, CHANNELS)

def returned(outgoing, halo_list, source, present):
    chosen_slots = halo_list[source, np.arange(8)[None, :], :]
    usable = (chosen_slots >= 0) & present[:, :, None]
    flat_ids = jnp.where(usable, source[:, :, None] * SLOTS + chosen_slots, SITES).astype(jnp.int32)
    summed = jax.ops.segment_sum(outgoing.reshape(-1, CHANNELS), flat_ids.reshape(-1), num_segments=SITES + 1)
    return summed[:SITES]

def device_pass(extended_all, neighbour_table, gradients, weight):
    extent = SLOTS + 8 * HALO

    def visit_tile(summed, carried):
        extended, table_rows, gradient = carried
        padded = jnp.concatenate([extended, jnp.zeros((1, CHANNELS), extended.dtype)], 0)
        where_to = jnp.where(table_rows < 0, extent, table_rows).astype(jnp.int32)
        columns = padded[where_to].reshape(SLOTS, KERNEL * CHANNELS)
        summed = summed + lax.dot_general(gradient, columns, (((0,), (0,)), ((), ())), preferred_element_type=jnp.float32)
        spread = jnp.dot(gradient, weight, preferred_element_type=jnp.float32)
        scattered = jax.ops.segment_sum(spread.reshape(SLOTS * KERNEL, CHANNELS), where_to.reshape(-1), num_segments=extent + 1)
        return (summed, scattered[:extent])
    initial = jnp.zeros((CHANNELS, KERNEL * CHANNELS), jnp.float32)
    return lax.scan(visit_tile, initial, (extended_all, neighbour_table, gradients))

def reference(features, pre_act, grad_out, weight_one, weight_two, neighbours, halo_list, send_list):
    source, present = source_table()
    pre_value = pre_act.astype(jnp.float32)
    hidden = jax.nn.silu(pre_value).astype(jnp.bfloat16)

    def extend_field(values):
        own_rows = values.reshape(TILES, SLOTS, CHANNELS)
        return jnp.concatenate([own_rows, outside_rows(values, halo_list, source, present)], 1)
    neighbour_table = neighbours.reshape(TILES, SLOTS, KERNEL)
    norm_scale = 1.0 / math.sqrt(SITES)
    total_two, scatter_two = device_pass(extend_field(hidden), neighbour_table, grad_out.reshape(TILES, SLOTS, CHANNELS), weight_two)
    grad_hidden = scatter_two[:, :SLOTS].reshape(SITES, CHANNELS) + returned(scatter_two[:, SLOTS:], halo_list, source, present)
    sigmoid_z = jax.nn.sigmoid(pre_value)
    grad_pre = (grad_hidden * sigmoid_z * (1.0 + pre_value * (1.0 - sigmoid_z))).astype(jnp.bfloat16)
    total_one, scatter_one = device_pass(extend_field(features), neighbour_table, grad_pre.reshape(TILES, SLOTS, CHANNELS), weight_one)
    grad_input = grad_out.astype(jnp.float32) + scatter_one[:, :SLOTS].reshape(SITES, CHANNELS)
    grad_input = (grad_input + returned(scatter_one[:, SLOTS:], halo_list, source, present)).astype(jnp.bfloat16)
    tile_ids = np.arange(TILES)
    line_ids = tile_ids // N_GY
    column_ids = tile_ids % N_GY
    sender = np.arange(N_GX)[None, :] * N_GY + column_ids[:, None]
    chosen = send_list[sender, line_ids[:, None], :]
    flat_ids = jnp.where(chosen >= 0, sender[:, :, None] * SLOTS + chosen, 0).astype(jnp.int32)
    balanced = jnp.where((chosen >= 0)[..., None], grad_input[flat_ids], jnp.zeros((), jnp.bfloat16))
    return (balanced.reshape(SITES, CHANNELS), total_one * norm_scale, total_two * norm_scale)
```

```python
import math

import jax
import jax.numpy as jnp
from jax import lax
from jax.experimental import pallas as pl
from jax.experimental.pallas import tpu as pltpu
from jax.sharding import PartitionSpec as P

C = 256
K = 27
S = 192
HB = 32
EXT = S + 8 * HB
QW = 1728
BF = jnp.bfloat16
F32 = jnp.float32
KSTEP = 3


def iota(shape, dim):
    return lax.broadcasted_iota(jnp.int32, shape, dim)


def onehot(mask):
    return jnp.where(mask, 1.0, 0.0).astype(BF)


def mm(a, b):
    return lax.dot_general(a, b, (((1,), (0,)), ((), ())), preferred_element_type=F32)


def mm_t(a, b):
    return lax.dot_general(a, b, (((0,), (0,)), ((), ())), preferred_element_type=F32)


def direction(a, b):
    grid = 3 * (a + 1) + (b + 1)
    return grid - jnp.where(grid > 4, 1, 0)


def channel_order():
    out = iota((C, C), 1)
    parity, rest = out // 128, out % 128
    source = 8 * (rest // 4) + 4 * parity + rest % 4
    return onehot(iota((C, C), 0) == source)


def halo_matrix(halo_row):
    return onehot(iota((S, 8 * HB), 0) == halo_row)


def pack_kernel(feat, pre, grad, nbr, halo, pay, nbt, hrow, wide):
    wide[...] = jnp.full(wide.shape, -1.0, F32)
    wide[0:S, 0:K] = nbr[...].astype(F32)
    table = jnp.transpose(wide[...])[0:32, :]
    halo_id = table - S
    heading = jnp.floor((halo_id + 0.5) * (1.0 / 24.0))
    table = jnp.where(table >= S, table + 8.0 * heading, table)
    nbt[...] = table
    shifted_up = table[:, 0:S] + 1.0
    high = jnp.floor(shifted_up * (1.0 / 16.0))
    z = pre[...].astype(F32)
    pay[0:S, 0:C] = feat[...]
    pay[0:S, C : 2 * C] = (z * (1.0 / (1.0 + jnp.exp(-z)))).astype(BF)
    pay[0:S, 2 * C : 3 * C] = mm(grad[...], channel_order()).astype(BF)
    halo_up = (halo[0] + 1).astype(F32).astype(BF)
    spread = mm(halo_up, onehot(iota((24, 8 * HB), 1) % HB == iota((24, 8 * HB), 0)))
    row = jnp.sum(
        jnp.where(iota((8, 8 * HB), 1) // HB == iota((8, 8 * HB), 0), spread, 0.0),
        axis=0,
        keepdims=True,
    )
    hrow[...] = jnp.broadcast_to(row.astype(jnp.int32) - 1, hrow.shape)
    pay[S : S + 32, :] = jnp.zeros((32, 3 * C), BF)
    pay[S : S + 32, 0:S] = high.astype(BF)
    pay[S : S + 32, C : C + S] = (shifted_up - 16.0 * high).astype(BF)
    pay[S : S + 32, 2 * C : 3 * C] = jnp.broadcast_to(row, (32, C)).astype(BF)


def spread_kernel(place, nbt, grad, weight, own, m1, m2, loc, acc):
    step = pl.program_id(0)

    @pl.when(step == 0)
    def _():
        acc[...] = jnp.zeros(acc.shape, F32)

    total = acc[...]
    terms = mm(grad[...], weight[...]).astype(BF)
    rows = iota((EXT, S), 0)
    for part in range(KSTEP):
        ids = nbt[pl.ds(step * KSTEP + part, 1), 0:S].astype(jnp.int32)
        total = total + mm(onehot(rows == ids), terms[:, part * C : (part + 1) * C])
    acc[...] = total

    @pl.when(step == K // KSTEP - 1)
    def _():
        even = place[0] % 2 == 0
        own[...] = acc[0:S, :]
        first, last = jnp.where(even, S, S + 160), jnp.where(even, S + 160, S)
        m1[...] = acc[pl.ds(pl.multiple_of(first, 32), 96), :].astype(BF)
        m2[...] = acc[pl.ds(pl.multiple_of(last, 32), 96), :].astype(BF)
        loc[...] = acc[S + 96 : S + 160, :].astype(BF)


def pass_kernel(place, loc, m1, m2, n1, n2):
    even = place[1] % 2 == 0
    first = jnp.where(even, 0, 1)
    for out, side in ((n1, first), (n2, 1 - first)):
        out[0:32, :] = loc[pl.ds(pl.multiple_of(side * 32, 32), 32), :]
        out[32:64, :] = m1[pl.ds(pl.multiple_of(side * 64, 32), 32), :]
        out[64:96, :] = m2[pl.ds(pl.multiple_of(side * 64, 32), 32), :]


def settled(place, own, m1, m2, n1, n2, hrow, back):
    da = jnp.where(place[0] % 2 == 0, 1, -1)
    db = jnp.where(place[1] % 2 == 0, 1, -1)
    back[direction(da, 0)] = m1[32:64, :]
    back[direction(-da, 0)] = m2[32:64, :]
    for ref, side in ((n1, db), (n2, -db)):
        back[direction(0, side)] = ref[0:32, :]
        back[direction(da, side)] = ref[32:64, :]
        back[direction(-da, side)] = ref[64:96, :]
    rows = back[...].reshape(8 * HB, C)
    return own[...] + mm(halo_matrix(hrow[0:1, :]), rows)


def gate_kernel(place, own, m1, m2, n1, n2, hrow, pre, out, ordered, back):
    hidden_grad = settled(place, own, m1, m2, n1, n2, hrow, back)
    z = pre[...].astype(F32)
    g = 1.0 / (1.0 + jnp.exp(-z))
    value = (hidden_grad * g * (1.0 + z * (1.0 - g))).astype(BF)
    out[...] = value
    ordered[...] = mm(value, channel_order()).astype(BF)


def rows_kernel(place, own, m1, m2, n1, n2, hrow, grad, send, out, back):
    total = settled(place, own, m1, m2, n1, n2, hrow, back)
    value = (grad[...].astype(F32) + total).astype(BF)
    chosen = onehot(iota((S, S), 0) == send[...])
    out[...] = mm_t(chosen, value).astype(BF)


def pick_kernel(place, p0, p1, p2, p3, o1, o2, loc, picked):
    column = place[1]
    for turn, pay in enumerate((p0, p1, p2, p3)):
        halo_row = pay[S : S + 16, 2 * C : 3 * C].astype(F32)[0:1, :].astype(jnp.int32) - 1
        rows = mm_t(halo_matrix(halo_row), pay[0:S, 0 : 2 * C])
        picked[column ^ turn] = rows.astype(BF)
    even = place[0] % 2 == 0
    up = pl.multiple_of(jnp.where(even, 160, 0), 32)
    down = pl.multiple_of(jnp.where(even, 0, 160), 32)
    none = jnp.zeros((HB, 2 * C), BF)
    for tile in range(4):
        for b in (-1, 0, 1):
            source = tile - b
            at = HB * (b + 1)
            inside = 0 <= source < 4
            o1[tile, at : at + HB, :] = picked[source, pl.ds(up + at, HB), :] if inside else none
            o2[tile, at : at + HB, :] = picked[source, pl.ds(down + at, HB), :] if inside else none
            if b:
                to = 0 if b < 0 else HB
                loc[tile, to : to + HB, :] = (
                    picked[source, 96 + to : 96 + to + HB, :] if inside else none
                )


def columns_kernel(
    place, p0, p1, p2, p3, r1, r2, loc, keep, send, cols_one, cols_two, ext, gt, ids, sel
):
    column = place[1]
    start = column * QW
    first_k = start // C
    offset = start % C
    even = place[0] % 2 == 0
    shift = onehot(iota((C, C), 0) == (iota((C, C), 1) + offset) % C)
    lane = iota((S, 2 * C), 1) % C
    early = lane < C - offset
    for turn, pay in enumerate((p0, p1, p2, p3)):
        tile = column ^ turn
        above, below = r1[tile], r2[tile]
        pieces = (
            (0, pay[0:S, 0 : 2 * C]),
            (S, jnp.where(even, above, below)),
            (S + 96, loc[tile]),
            (S + 160, jnp.where(even, below, above)),
        )
        for at, piece in pieces:
            size = piece.shape[0]
            ext[at : at + size, 0:C] = mm(piece[:, 0:C], shift).astype(BF)
            ext[at : at + size, C : 2 * C] = mm(piece[:, C : 2 * C], shift).astype(BF)
        gt[:, turn * S : (turn + 1) * S] = jnp.transpose(
            pay[0:S, 2 * C : 3 * C].astype(F32)
        ).astype(BF)
        high = pay[S : S + 32, 0:C].astype(F32)
        low = pay[S : S + 32, C : 2 * C].astype(F32)
        ids[0:32, :] = 16.0 * high + low - 1.0
        for part in range(8):
            sel[part : part + 1, :] = ids[pl.ds(first_k + part, 1), :]
        table = jnp.transpose(sel[...])[:, 0:8].astype(jnp.int32)
        extended = ext[...]
        previous = None
        for part in range(8):
            match = onehot(iota((S, EXT), 1) == table[0:S, part : part + 1])
            block = mm(match, extended).astype(BF)
            if part:
                merged = jnp.where(early, previous, block)
                at = (part - 1) * C
                cols_one[turn * S : (turn + 1) * S, at : at + C] = merged[:, 0:C]
                cols_two[turn * S : (turn + 1) * S, at : at + C] = merged[:, C : 2 * C]
            previous = block
    weight_blocks(place, gt, cols_two, keep, send)


def weight_blocks(place, gt, cols, keep, send):
    mine = pl.multiple_of((place[0] % 2) * 128, 128)
    other = pl.multiple_of(128 - mine, 128)
    for out, at in ((keep, mine), (send, other)):
        left = gt[pl.ds(at, 128), :]
        for part in range(7):
            out[:, part * C : (part + 1) * C] = mm(
                left, cols[:, part * C : (part + 1) * C]
            ).astype(BF)


def weight_kernel(place, g0, g1, g2, g3, cols, keep, send, gt):
    for turn, grad in enumerate((g0, g1, g2, g3)):
        gt[:, turn * S : (turn + 1) * S] = jnp.transpose(grad[...].astype(F32)).astype(BF)
    weight_blocks(place, gt, cols, keep, send)


def merge_kernel(k1, s1, k2, s2, out):
    row, col = iota((C, 128), 0), iota((C, 128), 1)
    for part in range(7):
        at = slice(part * C, (part + 1) * C)
        total = jnp.zeros((C, C), F32)
        for which, refs in enumerate(((k1, s1), (k2, s2))):
            place_of = onehot((row // 8 == col // 4) & (row % 8 == 4 * which + col % 4))
            for ref in refs:
                total = total + mm(place_of, ref[:, at])
        out[:, at] = total.astype(BF)


def final_kernel(scale, arrived, one, two):
    total = jnp.sum(arrived[...].astype(F32), axis=0) * scale
    one[...] = total[0:4, 0:QW]
    two[...] = total[4:8, 0:QW]


def sds(shape, dtype):
    return jax.ShapeDtypeStruct(shape, dtype)


SMEM = pl.BlockSpec(memory_space=pltpu.SMEM)
VM = pl.BlockSpec(memory_space=pltpu.VMEM)


def call(kernel, outs, *args, scratch=(), scalars=0, flops=10**8):
    return pl.pallas_call(
        kernel,
        out_shape=outs,
        in_specs=[SMEM] * scalars + [VM] * (len(args) - scalars),
        out_specs=jax.tree.map(lambda _: VM, outs),
        scratch_shapes=list(scratch),
        compiler_params=pltpu.CompilerParams(vmem_limit_bytes=40 * 2**20),
        cost_estimate=pl.CostEstimate(flops=flops, bytes_accessed=10**6, transcendentals=0),
    )(*args)


def spread(place, nbt, grad, weight):
    whole = lambda shape: pl.BlockSpec(shape, lambda n: (0,) * len(shape))
    return pl.pallas_call(
        spread_kernel,
        grid=(K // KSTEP,),
        out_shape=(sds((S, C), F32), sds((96, C), BF), sds((96, C), BF), sds((64, C), BF)),
        in_specs=[
            SMEM,
            whole((32, C)),
            whole((S, C)),
            pl.BlockSpec((C, KSTEP * C), lambda n: (0, n)),
        ],
        out_specs=(whole((S, C)), whole((96, C)), whole((96, C)), whole((64, C))),
        scratch_shapes=[pltpu.VMEM((EXT, C), F32)],
        compiler_params=pltpu.CompilerParams(vmem_limit_bytes=40 * 2**20),
        cost_estimate=pl.CostEstimate(
            flops=4 * 10**9, bytes_accessed=4 * 10**6, transcendentals=0
        ),
    )(place, nbt, grad, weight)


def partners(count, turn):
    if turn == 0:
        return list(range(count))
    if turn == 1:
        return [n ^ 1 for n in range(count)]
    pairs = [n - 1 if n % 2 == 0 else n + 1 for n in range(count)]
    return [n if 0 <= n < count else None for n in pairs]


def swap(value, axis, turn):
    pairs = [(n, q) for n, q in enumerate(partners(lax.axis_size(axis), turn)) if q is not None]
    return lax.ppermute(value, axis, pairs)


def cross(value, axis, mask):
    return lax.ppermute(value, axis, [(n, n ^ mask) for n in range(lax.axis_size(axis))])


def give_back(place, loc, m1, m2):
    m1, m2 = swap(m1, "gx", 1), swap(m2, "gx", 2)
    n1, n2 = call(
        pass_kernel, (sds((96, C), BF), sds((96, C), BF)), place, loc, m1, m2, scalars=1
    )
    return m1, m2, swap(n1, "gy", 1), swap(n2, "gy", 2)


def body(features, pre_act, grad_out, weight_one, weight_two, neighbours, halo_list, send_list):
    gx = lax.axis_size("gx")
    scale = 1.0 / math.sqrt(S * gx * lax.axis_size("gy"))
    place = jnp.stack([lax.axis_index("gx"), lax.axis_index("gy")]).astype(jnp.int32)
    pay, nbt, hrow = call(
        pack_kernel,
        (sds((S + 32, 3 * C), BF), sds((32, C), F32), sds((8, C), jnp.int32)),
        features,
        pre_act,
        grad_out,
        neighbours,
        halo_list,
        scratch=[pltpu.VMEM((C, 128), F32)],
    )
    pays = [pay] + [cross(pay, "gy", d) for d in (1, 2, 3)]
    own, m1, m2, loc = spread(place, nbt, grad_out, weight_two)
    m1, m2, n1, n2 = give_back(place, loc, m1, m2)
    back = pltpu.VMEM((8, HB, C), BF)
    grad_pre, ordered = call(
        gate_kernel,
        (sds((S, C), BF), sds((S, C), BF)),
        place,
        own,
        m1,
        m2,
        n1,
        n2,
        hrow,
        pre_act,
        scratch=[back],
        scalars=1,
    )
    grads = [ordered] + [cross(ordered, "gy", d) for d in (1, 2, 3)]
    own, m1, m2, loc = spread(place, nbt, grad_pre, weight_one)
    m1, m2, n1, n2 = give_back(place, loc, m1, m2)
    send = send_list.reshape(1, S)
    rows = call(
        rows_kernel,
        sds((S, C), BF),
        place,
        own,
        m1,
        m2,
        n1,
        n2,
        hrow,
        grad_out,
        send,
        scratch=[back],
        scalars=1,
    )
    balanced = lax.all_to_all(
        rows.reshape(gx, S // gx, C), "gx", split_axis=0, concat_axis=0, tiled=True
    ).reshape(S, C)

    picks = sds((4, 96, 2 * C), BF)
    o1, o2, near = call(
        pick_kernel,
        (picks, picks, sds((4, 64, 2 * C), BF)),
        place,
        *pays,
        scratch=[pltpu.VMEM((4, 8 * HB, 2 * C), BF)],
        scalars=1,
    )
    r1, r2 = swap(o1, "gx", 1), swap(o2, "gx", 2)
    wide = 7 * C
    half = sds((128, wide), BF)
    keep_two, send_two, cols_one = call(
        columns_kernel,
        (half, half, sds((4 * S, wide), BF)),
        place,
        *pays,
        r1,
        r2,
        near,
        scratch=[
            pltpu.VMEM((4 * S, wide), BF),
            pltpu.VMEM((EXT, 2 * C), BF),
            pltpu.VMEM((C, 4 * S), BF),
            pltpu.VMEM((32, C), F32),
            pltpu.VMEM((128, C), F32),
        ],
        scalars=1,
        flops=4 * 10**9,
    )
    come_two = cross(send_two, "gx", 1)
    keep_one, send_one = call(
        weight_kernel,
        (half, half),
        place,
        *grads,
        cols_one,
        scratch=[pltpu.VMEM((C, 4 * S), BF)],
        scalars=1,
        flops=10**9,
    )
    come_one = cross(send_one, "gx", 1)
    merged = call(merge_kernel, sds((C, wide), BF), keep_one, come_one, keep_two, come_two)
    groups = [[2 * c + e for c in range(gx // 2)] for e in range(2)]
    arrived = lax.all_to_all(
        merged.reshape(gx // 2, 8, wide),
        "gx",
        split_axis=0,
        concat_axis=0,
        tiled=True,
        axis_index_groups=groups,
    )
    out = sds((4, QW), F32)
    grad_one, grad_two = call(lambda *refs: final_kernel(scale, *refs), (out, out), arrived)
    return balanced, grad_one, grad_two


def solution(mesh):
    in_specs = (
        P(("gx", "gy"), None),
        P(("gx", "gy"), None),
        P(("gx", "gy"), None),
        P(),
        P(),
        P(("gx", "gy"), None),
        P(("gx", "gy"), None, None),
        P(("gx", "gy"), None, None),
    )
    out_specs = (P(("gx", "gy"), None), P("gx", "gy"), P("gx", "gy"))
    return jax.shard_map(body, mesh=mesh, in_specs=in_specs, out_specs=out_specs, check_vma=False)
```

```python
import math

import jax
import jax.numpy as jnp
from jax import lax
from jax.experimental import pallas as pl
from jax.experimental.pallas import tpu as pltpu
from jax.sharding import PartitionSpec as P

C = 256
K = 27
S = 192
HB = 32
EXT = S + 8 * HB
QW = 1728
BF = jnp.bfloat16
F32 = jnp.float32


def iota(shape, dim):
    return lax.broadcasted_iota(jnp.int32, shape, dim)


def onehot(mask):
    return jnp.where(mask, 1.0, 0.0).astype(BF)


def mm(a, b):
    return lax.dot_general(a, b, (((1,), (0,)), ((), ())), preferred_element_type=F32)


def mm_t(a, b):
    return lax.dot_general(a, b, (((0,), (0,)), ((), ())), preferred_element_type=F32)


def direction(a, b):
    grid = 3 * (a + 1) + (b + 1)
    return grid - jnp.where(grid > 4, 1, 0)


def channel_order():
    out = iota((C, C), 1)
    parity, rest = out // 128, out % 128
    source = 8 * (rest // 4) + 4 * parity + rest % 4
    return onehot(iota((C, C), 0) == source)


def halo_matrix(halo_row):
    return onehot(iota((S, 8 * HB), 0) == halo_row)


def pack_kernel(
    place, feat, pre, grad, nbr, halo, send, pay, nbt, hrow, srow, pre_out, grad_out,
    ids, halo_ids, send_ids, sems
):
    copies = [
        pltpu.make_async_copy(source, target, sems.at[n])
        for n, (source, target) in enumerate(
            (
                (nbr, ids),
                (halo, halo_ids),
                (send, send_ids),
                (feat, pay.at[0:S, 0:C]),
                (grad, grad_out),
                (pre, pre_out),
            )
        )
    ]
    for copy in copies:
        copy.start()
    for copy in copies:
        copy.wait()
    table = ids[...].astype(F32)
    heading = jnp.floor((table - S + 0.5) * (1.0 / 24.0))
    table = jnp.where(table >= S, table + 8.0 * heading, table)
    nbt[...] = jnp.full(nbt.shape, -1.0, F32)
    nbt[0:K, 0:S] = table
    shifted_up = table + 1.0
    high = jnp.floor(shifted_up * (1.0 / 16.0))
    pay[S : S + 32, :] = jnp.zeros((32, 3 * C), BF)
    pay[S : S + K, 0:S] = high.astype(BF)
    pay[S : S + K, C : C + S] = (shifted_up - 16.0 * high).astype(BF)
    z = pre_out[...].astype(F32)
    pay[0:S, C : 2 * C] = (z * (1.0 / (1.0 + jnp.exp(-z)))).astype(BF)
    pay[0:S, 2 * C : 3 * C] = mm(grad_out[...], channel_order()).astype(BF)
    halo_up = (halo_ids[0] + 1).astype(F32).astype(BF)
    spread = mm(halo_up, onehot(iota((24, 8 * HB), 1) % HB == iota((24, 8 * HB), 0)))
    row = jnp.sum(
        jnp.where(iota((8, 8 * HB), 1) // HB == iota((8, 8 * HB), 0), spread, 0.0),
        axis=0,
        keepdims=True,
    )
    hrow[...] = jnp.broadcast_to(row.astype(jnp.int32) - 1, hrow.shape)
    pay[S : S + 32, 2 * C : 3 * C] = jnp.broadcast_to(row, (32, C)).astype(BF)
    lane, peer = iota((64, C), 1), iota((64, C), 0)
    parity = jnp.where(lane < 128, place[0] % 2, 1 - place[0] % 2)
    pick = onehot(peer == 2 * (lane % 32) + parity)
    spot = (iota((1, C), 1) % 128) // 32
    total = jnp.zeros((1, C), F32)
    for c in range(3):
        up = jnp.broadcast_to((send_ids[c] + 1).astype(F32), (8, 64)).astype(BF)
        total = jnp.where(spot == c, mm(up, pick)[0:1, :], total)
    srow[...] = jnp.broadcast_to(total.astype(jnp.int32) - 1, srow.shape)


def spread_kernel(place, nbt, grad, weight, own, m1, m2, loc, held, acc, sems):
    copies = [
        pltpu.make_async_copy(
            weight.at[:, n * 9 * C : (n + 1) * 9 * C], held.at[n], sems.at[n]
        )
        for n in range(3)
    ]
    for copy in copies:
        copy.start()
    rows = iota((EXT, C), 0)
    table = nbt[...].astype(jnp.int32)
    gradient = grad[...]
    none = jnp.zeros((C - S, C), BF)
    for n in range(3):
        masks, terms = [], []
        for part in range(9):
            k = 9 * n + part
            masks.append(onehot(rows == table[k : k + 1, :]))
        copies[n].wait()
        for part in range(9):
            terms += [mm(gradient, held[n, :, part * C : (part + 1) * C]).astype(BF), none]
        total = mm(jnp.concatenate(masks, axis=1), jnp.concatenate(terms, axis=0))
        if n:
            acc[...] += total
        else:
            acc[...] = total
    even = place[0] % 2 == 0
    own[...] = acc[0:S, :]
    first, last = jnp.where(even, S, S + 160), jnp.where(even, S + 160, S)
    m1[...] = acc[pl.ds(pl.multiple_of(first, 32), 96), :].astype(BF)
    m2[...] = acc[pl.ds(pl.multiple_of(last, 32), 96), :].astype(BF)
    loc[...] = acc[S + 96 : S + 160, :].astype(BF)


def pass_kernel(place, loc, m1, m2, n1, n2):
    even = place[1] % 2 == 0
    first = jnp.where(even, 0, 1)
    for out, side in ((n1, first), (n2, 1 - first)):
        out[0:32, :] = loc[pl.ds(pl.multiple_of(side * 32, 32), 32), :]
        out[32:64, :] = m1[pl.ds(pl.multiple_of(side * 64, 32), 32), :]
        out[64:96, :] = m2[pl.ds(pl.multiple_of(side * 64, 32), 32), :]


def settled(place, own, m1, m2, n1, n2, hrow, back):
    da = jnp.where(place[0] % 2 == 0, 1, -1)
    db = jnp.where(place[1] % 2 == 0, 1, -1)
    back[direction(da, 0)] = m1[32:64, :]
    back[direction(-da, 0)] = m2[32:64, :]
    for ref, side in ((n1, db), (n2, -db)):
        back[direction(0, side)] = ref[0:32, :]
        back[direction(da, side)] = ref[32:64, :]
        back[direction(-da, side)] = ref[64:96, :]
    rows = back[...].reshape(8 * HB, C)
    return own[...] + mm(halo_matrix(hrow[0:1, :]), rows)


def gate_kernel(place, own, m1, m2, n1, n2, hrow, pre, out, ordered, back):
    hidden_grad = settled(place, own, m1, m2, n1, n2, hrow, back)
    z = pre[...].astype(F32)
    g = 1.0 / (1.0 + jnp.exp(-z))
    value = (hidden_grad * g * (1.0 + z * (1.0 - g))).astype(BF)
    out[...] = value
    ordered[...] = mm(value, channel_order()).astype(BF)


def rows_kernel(place, own, m1, m2, n1, n2, hrow, grad, srow, keep, send, back):
    total = settled(place, own, m1, m2, n1, n2, hrow, back)
    value = (grad[...].astype(F32) + total).astype(BF)
    chosen = mm_t(onehot(iota((S, C), 0) == srow[0:1, :]), value).astype(BF)
    keep[...] = chosen[0:128, :]
    send[...] = chosen[128:256, :]


def pick_kernel(place, p0, p1, p2, p3, late, o1, o2, loc, picked):
    column = place[1]
    for turn, pay in enumerate((p0, p1, p2, p3)):
        halo_row = pay[S : S + 16, 2 * C : 3 * C].astype(F32)[0:1, :].astype(jnp.int32) - 1
        rows = mm_t(halo_matrix(halo_row), pay[0:S, 0 : 2 * C])
        picked[column ^ turn] = rows.astype(BF)
    even = place[0] % 2 == 0
    up = pl.multiple_of(jnp.where(even, 160, 0), 32)
    down = pl.multiple_of(jnp.where(even, 0, 160), 32)
    none = jnp.zeros((HB, 2 * C), BF)
    for tile in range(4):
        for b in (-1, 0, 1):
            source = tile - b
            at = HB * (b + 1)
            inside = 0 <= source < 4
            o1[tile, at : at + HB, :] = picked[source, pl.ds(up + at, HB), :] if inside else none
            o2[tile, at : at + HB, :] = picked[source, pl.ds(down + at, HB), :] if inside else none
            if b:
                to = 0 if b < 0 else HB
                loc[tile, to : to + HB, :] = (
                    picked[source, 96 + to : 96 + to + HB, :] if inside else none
                )


def columns_kernel(
    place, p0, p1, p2, p3, r1, r2, loc, late, keep, send, cols_one, cols_two, ext, gt, ids, sel
):
    column = place[1]
    start = column * QW
    first_k = start // C
    offset = start % C
    even = place[0] % 2 == 0
    shift = onehot(iota((C, C), 0) == (iota((C, C), 1) + offset) % C)
    lane = iota((S, 2 * C), 1) % C
    early = lane < C - offset
    for turn, pay in enumerate((p0, p1, p2, p3)):
        tile = column ^ turn
        above, below = r1[tile], r2[tile]
        pieces = (
            (0, pay[0:S, 0 : 2 * C]),
            (S, jnp.where(even, above, below)),
            (S + 96, loc[tile]),
            (S + 160, jnp.where(even, below, above)),
        )
        for at, piece in pieces:
            size = piece.shape[0]
            ext[at : at + size, 0:C] = mm(piece[:, 0:C], shift).astype(BF)
            ext[at : at + size, C : 2 * C] = mm(piece[:, C : 2 * C], shift).astype(BF)
        gt[:, turn * S : (turn + 1) * S] = jnp.transpose(
            pay[0:S, 2 * C : 3 * C].astype(F32)
        ).astype(BF)
        high = pay[S : S + 32, 0:C].astype(F32)
        low = pay[S : S + 32, C : 2 * C].astype(F32)
        ids[0:32, :] = 16.0 * high + low - 1.0
        for part in range(8):
            sel[part : part + 1, :] = ids[pl.ds(first_k + part, 1), :]
        table = jnp.transpose(sel[...])[:, 0:8].astype(jnp.int32)
        extended = ext[...]
        previous = None
        for part in range(8):
            match = onehot(iota((S, EXT), 1) == table[0:S, part : part + 1])
            block = mm(match, extended).astype(BF)
            if part:
                merged = jnp.where(early, previous, block)
                at = (part - 1) * C
                cols_one[turn * S : (turn + 1) * S, at : at + C] = merged[:, 0:C]
                cols_two[turn * S : (turn + 1) * S, at : at + C] = merged[:, C : 2 * C]
            previous = block
    weight_blocks(place, gt, cols_two, keep, send)


def weight_blocks(place, gt, cols, keep, send):
    mine = pl.multiple_of((place[0] % 2) * 128, 128)
    other = pl.multiple_of(128 - mine, 128)
    for out, at in ((keep, mine), (send, other)):
        left = gt[pl.ds(at, 128), :]
        for part in range(7):
            out[:, part * C : (part + 1) * C] = mm(
                left, cols[:, part * C : (part + 1) * C]
            ).astype(BF)


def weight_kernel(place, g0, g1, g2, g3, cols, late, keep, send, gt):
    for turn, grad in enumerate((g0, g1, g2, g3)):
        gt[:, turn * S : (turn + 1) * S] = jnp.transpose(grad[...].astype(F32)).astype(BF)
    weight_blocks(place, gt, cols, keep, send)


def merge_kernel(place, k1, s1, k2, s2, rk, rs, out):
    row, col = iota((C, 128), 0), iota((C, 128), 1)
    for part in range(7):
        at = slice(part * C, (part + 1) * C)
        total = jnp.zeros((C, C), F32)
        for which, refs in enumerate(((k1, s1), (k2, s2))):
            place_of = onehot((row // 8 == col // 4) & (row % 8 == 4 * which + col % 4))
            for ref in refs:
                total = total + mm(place_of, ref[:, at])
        out[:, at] = total.astype(BF)
    mine = place[0] % 2
    total = jnp.zeros((C, C), F32)
    for ref, core in ((rk, mine), (rs, 1 - mine)):
        spot = (row // 8 == col % 32) & (row % 8 == 3 * core + col // 32) & (col < 96)
        total = total + mm(onehot(spot), ref[...])
    out[:, 7 * C : 8 * C] = total.astype(BF)


def final_kernel(scale, arrived, rows, one, two):
    total = jnp.sum(arrived[:, :, 0 : 7 * C].astype(F32), axis=0) * scale
    one[...] = total[0:4, 0:QW]
    two[...] = total[4:8, 0:QW]
    to, at = iota((S, C), 0), iota((S, C), 1)
    spot = (at // 8 == to // 6) & (at % 8 == to % 6)
    rows[...] = mm(onehot(spot), arrived[:, :, 7 * C : 8 * C].reshape(C, C)).astype(BF)


def sds(shape, dtype):
    return jax.ShapeDtypeStruct(shape, dtype)


SMEM = pl.BlockSpec(memory_space=pltpu.SMEM)
VM = pl.BlockSpec(memory_space=pltpu.VMEM)
HBM = pl.BlockSpec(memory_space=pltpu.HBM)
ANY = pl.BlockSpec(memory_space=pl.ANY)


def call(kernel, outs, *args, scratch=(), specs=None, late=0, flops=10**8):
    if specs is None:
        specs = [SMEM] + [VM] * (len(args) - 1 - late) + [ANY] * late
    return pl.pallas_call(
        kernel,
        out_shape=outs,
        in_specs=specs,
        out_specs=jax.tree.map(lambda _: VM, outs),
        scratch_shapes=list(scratch),
        compiler_params=pltpu.CompilerParams(vmem_limit_bytes=40 * 2**20),
        cost_estimate=pl.CostEstimate(flops=flops, bytes_accessed=10**6, transcendentals=0),
    )(*args)


def spread(place, nbt, grad, weight):
    edge = sds((96, C), BF)
    return call(
        spread_kernel,
        (sds((S, C), F32), edge, edge, sds((64, C), BF)),
        place,
        nbt,
        grad,
        weight,
        specs=[SMEM, VM, VM, HBM],
        scratch=[
            pltpu.VMEM((3, C, 9 * C), BF),
            pltpu.VMEM((EXT, C), F32),
            pltpu.SemaphoreType.DMA((3,)),
        ],
        flops=4 * 10**9,
    )


def partners(count, turn):
    if turn == 0:
        return list(range(count))
    if turn == 1:
        return [n ^ 1 for n in range(count)]
    pairs = [n - 1 if n % 2 == 0 else n + 1 for n in range(count)]
    return [n if 0 <= n < count else None for n in pairs]


def swap(value, axis, turn):
    pairs = [(n, q) for n, q in enumerate(partners(lax.axis_size(axis), turn)) if q is not None]
    return lax.ppermute(value, axis, pairs)


def cross(value, axis, mask):
    return lax.ppermute(value, axis, [(n, n ^ mask) for n in range(lax.axis_size(axis))])


def give_back(place, loc, m1, m2):
    m1, m2 = swap(m1, "gx", 1), swap(m2, "gx", 2)
    n1, n2 = call(pass_kernel, (sds((96, C), BF), sds((96, C), BF)), place, loc, m1, m2)
    return (m1, m2, swap(n1, "gy", 1), swap(n2, "gy", 2)), n1


def body(features, pre_act, grad_out, weight_one, weight_two, neighbours, halo_list, send_list):
    gx = lax.axis_size("gx")
    scale = 1.0 / math.sqrt(S * gx * lax.axis_size("gy"))
    place = jnp.stack([lax.axis_index("gx"), lax.axis_index("gy")]).astype(jnp.int32)
    tile = sds((S, C), BF)
    pay, nbt, hrow, srow, pre, grad = call(
        pack_kernel,
        (
            sds((S + 32, 3 * C), BF),
            sds((32, C), F32),
            sds((8, C), jnp.int32),
            sds((8, C), jnp.int32),
            tile,
            tile,
        ),
        place,
        features,
        pre_act,
        grad_out,
        neighbours.T,
        halo_list,
        jnp.transpose(send_list, (2, 0, 1)),
        specs=[SMEM] + [HBM] * 6,
        scratch=[
            pltpu.VMEM((K, S), jnp.int32),
            pltpu.VMEM((1, 8, 24), jnp.int32),
            pltpu.VMEM((3, 1, 64), jnp.int32),
            pltpu.SemaphoreType.DMA((6,)),
        ],
    )
    pays = [pay] + [cross(pay, "gy", d) for d in (1, 2, 3)]
    own, m1, m2, loc = spread(place, nbt, grad, weight_two)
    back = pltpu.VMEM((8, HB, C), BF)
    arrived, passed = give_back(place, loc, m1, m2)
    picks = sds((4, 96, 2 * C), BF)
    o1, o2, near = call(
        pick_kernel,
        (picks, picks, sds((4, 64, 2 * C), BF)),
        place,
        *pays,
        passed,
        scratch=[pltpu.VMEM((4, 8 * HB, 2 * C), BF)],
        late=1,
    )
    r1, r2 = swap(o1, "gx", 1), swap(o2, "gx", 2)
    grad_pre, ordered = call(
        gate_kernel, (tile, tile), place, own, *arrived, hrow, pre, scratch=[back]
    )
    grads = [ordered] + [cross(ordered, "gy", d) for d in (1, 2, 3)]
    own, m1, m2, loc = spread(place, nbt, grad_pre, weight_one)
    wide = 7 * C
    half = sds((128, wide), BF)
    keep_two, send_two, cols_one = call(
        columns_kernel,
        (half, half, sds((4 * S, wide), BF)),
        place,
        *pays,
        r1,
        r2,
        near,
        own,
        scratch=[
            pltpu.VMEM((4 * S, wide), BF),
            pltpu.VMEM((EXT, 2 * C), BF),
            pltpu.VMEM((C, 4 * S), BF),
            pltpu.VMEM((32, C), F32),
            pltpu.VMEM((128, C), F32),
        ],
        late=1,
        flops=4 * 10**9,
    )
    come_two = cross(send_two, "gx", 1)
    arrived, passed = give_back(place, loc, m1, m2)
    keep_one, send_one = call(
        weight_kernel,
        (half, half),
        place,
        *grads,
        cols_one,
        passed,
        scratch=[pltpu.VMEM((C, 4 * S), BF)],
        late=1,
        flops=10**9,
    )
    come_one = cross(send_one, "gx", 1)
    some = sds((128, C), BF)
    rows_keep, rows_send = call(
        rows_kernel, (some, some), place, own, *arrived, hrow, grad, srow, scratch=[back]
    )
    rows_come = cross(rows_send, "gx", 1)
    merged = call(
        merge_kernel,
        sds((C, 8 * C), BF),
        place,
        keep_one,
        come_one,
        keep_two,
        come_two,
        rows_keep,
        rows_come,
    )
    groups = [[2 * c + e for c in range(gx // 2)] for e in range(2)]
    collected = lax.all_to_all(
        merged.reshape(gx // 2, 8, 8 * C),
        "gx",
        split_axis=0,
        concat_axis=0,
        tiled=True,
        axis_index_groups=groups,
    )
    out = sds((4, QW), F32)
    return call(
        lambda *refs: final_kernel(scale, *refs), (tile, out, out), collected, specs=[VM]
    )


def solution(mesh):
    in_specs = (
        P(("gx", "gy"), None),
        P(("gx", "gy"), None),
        P(("gx", "gy"), None),
        P(),
        P(),
        P(("gx", "gy"), None),
        P(("gx", "gy"), None, None),
        P(("gx", "gy"), None, None),
    )
    out_specs = (P(("gx", "gy"), None), P("gx", "gy"), P("gx", "gy"))
    return jax.shard_map(body, mesh=mesh, in_specs=in_specs, out_specs=out_specs, check_vma=False)
```

```python
import math

import jax
import jax.numpy as jnp
from jax import lax
from jax.experimental import pallas as pl
from jax.experimental.pallas import tpu as pltpu
from jax.sharding import PartitionSpec as P

C = 256
K = 27
S = 192
HB = 32
EXT = S + 8 * HB
QW = 1728
BF = jnp.bfloat16
F32 = jnp.float32


def iota(shape, dim):
    return lax.broadcasted_iota(jnp.int32, shape, dim)


def onehot(mask):
    return jnp.where(mask, 1.0, 0.0).astype(BF)


def mm(a, b):
    return lax.dot_general(a, b, (((1,), (0,)), ((), ())), preferred_element_type=F32)


def mm_t(a, b):
    return lax.dot_general(a, b, (((0,), (0,)), ((), ())), preferred_element_type=F32)


def direction(a, b):
    grid = 3 * (a + 1) + (b + 1)
    return grid - jnp.where(grid > 4, 1, 0)


def channel_order():
    out = iota((C, C), 1)
    parity, rest = out // 128, out % 128
    source = 8 * (rest // 4) + 4 * parity + rest % 4
    return onehot(iota((C, C), 0) == source)


def halo_matrix(halo_row):
    return onehot(iota((S, 8 * HB), 0) == halo_row)


def pack_kernel(
    place, feat, pre, grad, nbr, halo, send, pay, nbt, hrow, srow, pre_out, grad_out,
    ids, halo_ids, send_ids, sems
):
    copies = [
        pltpu.make_async_copy(source, target, sems.at[n])
        for n, (source, target) in enumerate(
            (
                (nbr, ids),
                (halo, halo_ids),
                (send, send_ids),
                (feat, pay.at[0:S, 0:C]),
                (grad, grad_out),
                (pre, pre_out),
            )
        )
    ]
    for copy in copies:
        copy.start()
    for copy in copies:
        copy.wait()
    table = ids[...].astype(F32)
    heading = jnp.floor((table - S + 0.5) * (1.0 / 24.0))
    table = jnp.where(table >= S, table + 8.0 * heading, table)
    nbt[...] = jnp.full(nbt.shape, -1.0, F32)
    nbt[0:K, 0:S] = table
    shifted_up = table + 1.0
    high = jnp.floor(shifted_up * (1.0 / 16.0))
    pay[S : S + 32, :] = jnp.zeros((32, 3 * C), BF)
    pay[S : S + K, 0:S] = high.astype(BF)
    pay[S : S + K, C : C + S] = (shifted_up - 16.0 * high).astype(BF)
    z = pre_out[...].astype(F32)
    pay[0:S, C : 2 * C] = (z * (1.0 / (1.0 + jnp.exp(-z)))).astype(BF)
    pay[0:S, 2 * C : 3 * C] = mm(grad_out[...], channel_order()).astype(BF)
    halo_up = (halo_ids[0] + 1).astype(F32).astype(BF)
    spread = mm(halo_up, onehot(iota((24, 8 * HB), 1) % HB == iota((24, 8 * HB), 0)))
    row = jnp.sum(
        jnp.where(iota((8, 8 * HB), 1) // HB == iota((8, 8 * HB), 0), spread, 0.0),
        axis=0,
        keepdims=True,
    )
    hrow[...] = jnp.broadcast_to(row.astype(jnp.int32) - 1, hrow.shape)
    pay[S : S + 32, 2 * C : 3 * C] = jnp.broadcast_to(row, (32, C)).astype(BF)
    lane, peer = iota((64, C), 1), iota((64, C), 0)
    parity = jnp.where(lane < 128, place[0] % 2, 1 - place[0] % 2)
    pick = onehot(peer == 2 * (lane % 32) + parity)
    spot = (iota((1, C), 1) % 128) // 32
    total = jnp.zeros((1, C), F32)
    for c in range(3):
        up = jnp.broadcast_to((send_ids[c] + 1).astype(F32), (8, 64)).astype(BF)
        total = jnp.where(spot == c, mm(up, pick)[0:1, :], total)
    srow[...] = jnp.broadcast_to(total.astype(jnp.int32) - 1, srow.shape)


def spread_terms(place, nbt, grad, weight, own, m1, m2, loc, acc):
    rows = iota((EXT, C), 0)
    table = nbt[...].astype(jnp.int32)
    gradient = grad[...]
    none = jnp.zeros((C - S, C), BF)
    masks, terms = [], []
    for k in range(K):
        masks.append(onehot(rows == table[k : k + 1, :]))
        terms += [mm(gradient, weight[:, k * C : (k + 1) * C]).astype(BF), none]
    acc[...] = mm(jnp.concatenate(masks, axis=1), jnp.concatenate(terms, axis=0))
    even = place[0] % 2 == 0
    own[...] = acc[0:S, :]
    first, last = jnp.where(even, S, S + 160), jnp.where(even, S + 160, S)
    m1[0:96, :] = acc[pl.ds(pl.multiple_of(first, 32), 96), :].astype(BF)
    m2[0:96, :] = acc[pl.ds(pl.multiple_of(last, 32), 96), :].astype(BF)
    loc[...] = acc[S + 96 : S + 160, :].astype(BF)


def spread_kernel(place, nbt, grad, weight, own, m1, m2, loc, acc):
    spread_terms(place, nbt, grad, weight, own, m1, m2, loc, acc)


def spread_with_kernel(place, nbt, grad, weight, o1, o2, own, m1, m2, loc, acc):
    m1[96:, :] = o1[...]
    m2[96:, :] = o2[...]
    spread_terms(place, nbt, grad, weight, own, m1, m2, loc, acc)


def pass_kernel(place, loc, m1, m2, n1, n2):
    even = place[1] % 2 == 0
    first = jnp.where(even, 0, 1)
    for out, side in ((n1, first), (n2, 1 - first)):
        out[0:32, :] = loc[pl.ds(pl.multiple_of(side * 32, 32), 32), :]
        out[32:64, :] = m1[pl.ds(pl.multiple_of(side * 64, 32), 32), :]
        out[64:96, :] = m2[pl.ds(pl.multiple_of(side * 64, 32), 32), :]


def settled(place, own, m1, m2, n1, n2, hrow, back):
    da = jnp.where(place[0] % 2 == 0, 1, -1)
    db = jnp.where(place[1] % 2 == 0, 1, -1)
    back[direction(da, 0)] = m1[32:64, :]
    back[direction(-da, 0)] = m2[32:64, :]
    for ref, side in ((n1, db), (n2, -db)):
        back[direction(0, side)] = ref[0:32, :]
        back[direction(da, side)] = ref[32:64, :]
        back[direction(-da, side)] = ref[64:96, :]
    rows = back[...].reshape(8 * HB, C)
    return own[...] + mm(halo_matrix(hrow[0:1, :]), rows)


def gate_kernel(place, own, m1, m2, n1, n2, hrow, pre, late, out, ordered, back):
    hidden_grad = settled(place, own, m1, m2, n1, n2, hrow, back)
    z = pre[...].astype(F32)
    g = 1.0 / (1.0 + jnp.exp(-z))
    value = (hidden_grad * g * (1.0 + z * (1.0 - g))).astype(BF)
    out[...] = value
    ordered[...] = mm(value, channel_order()).astype(BF)


def rows_kernel(place, own, m1, m2, n1, n2, hrow, grad, srow, late, keep, send, back):
    total = settled(place, own, m1, m2, n1, n2, hrow, back)
    value = (grad[...].astype(F32) + total).astype(BF)
    chosen = mm_t(onehot(iota((S, C), 0) == srow[0:1, :]), value).astype(BF)
    keep[...] = chosen[0:128, :]
    send[...] = chosen[128:256, :]


def pick_kernel(place, p0, p1, p2, p3, late, o1, o2, loc, picked):
    column = place[1]
    for turn, pay in enumerate((p0, p1, p2, p3)):
        halo_row = pay[S : S + 16, 2 * C : 3 * C].astype(F32)[0:1, :].astype(jnp.int32) - 1
        rows = mm_t(halo_matrix(halo_row), pay[0:S, 0 : 2 * C])
        picked[column ^ turn] = rows.astype(BF)
    even = place[0] % 2 == 0
    up = pl.multiple_of(jnp.where(even, 160, 0), 32)
    down = pl.multiple_of(jnp.where(even, 0, 160), 32)
    none = jnp.zeros((HB, 2 * C), BF)
    for tile in range(4):
        for b in (-1, 0, 1):
            source = tile - b
            at = HB * (b + 1)
            for out, side in ((o1, up), (o2, down)):
                rows = picked[source, pl.ds(side + at, HB), :] if 0 <= source < 4 else none
                to = 96 * tile + at
                out[to : to + HB, :] = rows[:, 0:C]
                out[to + 384 : to + 384 + HB, :] = rows[:, C : 2 * C]
            if b:
                to = 0 if b < 0 else HB
                rows = picked[source, 96 + to : 96 + to + HB, :] if 0 <= source < 4 else none
                loc[tile, to : to + HB, :] = rows


def columns_kernel(
    place, p0, p1, p2, p3, r1, r2, loc, late, gt, cols_one, cols_two, ext, ids, sel
):
    column = place[1]
    start = column * QW
    first_k = start // C
    offset = start % C
    even = place[0] % 2 == 0
    shift = onehot(iota((C, C), 0) == (iota((C, C), 1) + offset) % C)
    lane = iota((S, 2 * C), 1) % C
    early = lane < C - offset
    for turn, pay in enumerate((p0, p1, p2, p3)):
        tile = column ^ turn
        for half in range(2):
            lanes = slice(half * C, (half + 1) * C)
            at = pl.multiple_of(96 + 384 * half + 96 * tile, 32)
            above, below = r1[pl.ds(at, 96), :], r2[pl.ds(at, 96), :]
            for to, piece in (
                (0, pay[0:S, lanes]),
                (S, jnp.where(even, above, below)),
                (S + 96, loc[tile, :, lanes]),
                (S + 160, jnp.where(even, below, above)),
            ):
                ext[to : to + piece.shape[0], lanes] = mm(piece, shift).astype(BF)
        gt[:, turn * S : (turn + 1) * S] = jnp.transpose(
            pay[0:S, 2 * C : 3 * C].astype(F32)
        ).astype(BF)
        high = pay[S : S + 32, 0:C].astype(F32)
        low = pay[S : S + 32, C : 2 * C].astype(F32)
        ids[0:32, :] = 16.0 * high + low - 1.0
        for part in range(8):
            sel[part : part + 1, :] = ids[pl.ds(first_k + part, 1), :]
        table = jnp.transpose(sel[...])[:, 0:8].astype(jnp.int32)
        extended = ext[...]
        previous = None
        for part in range(8):
            match = onehot(iota((S, EXT), 1) == table[0:S, part : part + 1])
            block = mm(match, extended).astype(BF)
            if part:
                merged = jnp.where(early, previous, block)
                at = (part - 1) * C
                cols_one[turn * S : (turn + 1) * S, at : at + C] = merged[:, 0:C]
                cols_two[turn * S : (turn + 1) * S, at : at + C] = merged[:, C : 2 * C]
            previous = block


def weight_blocks(place, gt, cols, keep, send):
    mine = pl.multiple_of((place[0] % 2) * 128, 128)
    other = pl.multiple_of(128 - mine, 128)
    for out, at in ((keep, mine), (send, other)):
        left = gt[pl.ds(at, 128), :]
        for part in range(7):
            out[:, part * C : (part + 1) * C] = mm(
                left, cols[:, part * C : (part + 1) * C]
            ).astype(BF)


def weight_two_kernel(place, gt, cols, late, keep, send):
    weight_blocks(place, gt, cols, keep, send)


def weight_one_kernel(place, g0, g1, g2, g3, cols, late, keep, send, gt):
    for turn, grad in enumerate((g0, g1, g2, g3)):
        gt[:, turn * S : (turn + 1) * S] = jnp.transpose(grad[...].astype(F32)).astype(BF)
    weight_blocks(place, gt, cols, keep, send)


def merge_kernel(place, k1, s1, k2, s2, rk, rs, *outs):
    row, col = iota((64, 128), 0), iota((64, 128), 1)
    mine = place[0] % 2
    line = place[0] // 16
    for turn, out in enumerate(outs):
        chip = 8 * (line ^ turn) + row // 8
        for part in range(7):
            at = slice(part * C, (part + 1) * C)
            total = jnp.zeros((64, C), F32)
            for which, refs in enumerate(((k1, s1), (k2, s2))):
                spot = onehot((chip == col // 4) & (row % 8 == 4 * which + col % 4))
                for ref in refs:
                    total = total + mm(spot, ref[:, at])
            out[:, at] = total.astype(BF)
        total = jnp.zeros((64, C), F32)
        for ref, core in ((rk, mine), (rs, 1 - mine)):
            spot = (chip == col % 32) & (row % 8 == 3 * core + col // 32) & (col < 96)
            total = total + mm(onehot(spot), ref[...])
        out[:, 7 * C : 8 * C] = total.astype(BF)


def line_kernel(place, a0, a1, a2, a3, out):
    line = place[0] // 16
    total = jnp.zeros((64, 7 * C), F32)
    for turn, part in enumerate((a0, a1, a2, a3)):
        total = total + part[:, 0 : 7 * C].astype(F32)
        at = pl.multiple_of(7 * C + (line ^ turn) * C, C)
        out[:, pl.ds(at, C)] = part[:, 7 * C : 8 * C]
    out[:, 0 : 7 * C] = total.astype(BF)


def final_kernel(scale, arrived, rows, one, two):
    total = jnp.sum(arrived[:, :, 0 : 7 * C].astype(F32), axis=0) * scale
    one[...] = total[0:4, 0:QW]
    two[...] = total[4:8, 0:QW]
    to, at = iota((48, 64), 0), iota((48, 64), 1)
    spot = onehot((at // 8 == to // 6) & (at % 8 == to % 6))
    for line in range(4):
        piece = arrived[:, :, (7 + line) * C : (8 + line) * C].reshape(64, C)
        rows[48 * line : 48 * line + 48, :] = mm(spot, piece).astype(BF)


def sds(shape, dtype):
    return jax.ShapeDtypeStruct(shape, dtype)


SMEM = pl.BlockSpec(memory_space=pltpu.SMEM)
VM = pl.BlockSpec(memory_space=pltpu.VMEM)
HBM = pl.BlockSpec(memory_space=pltpu.HBM)
ANY = pl.BlockSpec(memory_space=pl.ANY)


def call(kernel, outs, *args, scratch=(), specs=None, late=0, flops=10**5):
    if specs is None:
        specs = [SMEM] + [VM] * (len(args) - 1 - late) + [ANY] * late
    return pl.pallas_call(
        kernel,
        out_shape=outs,
        in_specs=specs,
        out_specs=jax.tree.map(lambda _: VM, outs),
        scratch_shapes=list(scratch),
        compiler_params=pltpu.CompilerParams(vmem_limit_bytes=40 * 2**20),
        cost_estimate=pl.CostEstimate(flops=flops, bytes_accessed=10**4, transcendentals=0),
    )(*args)


def spread(place, nbt, grad, weight, *picks):
    edge = sds((96 + (picks[0].shape[0] if picks else 0), C), BF)
    return call(
        spread_with_kernel if picks else spread_kernel,
        (sds((S, C), F32), edge, edge, sds((64, C), BF)),
        place,
        nbt,
        grad,
        weight,
        *picks,
        scratch=[pltpu.VMEM((EXT, C), F32)],
    )


def partners(count, turn):
    if turn == 0:
        return list(range(count))
    if turn == 1:
        return [n ^ 1 for n in range(count)]
    pairs = [n - 1 if n % 2 == 0 else n + 1 for n in range(count)]
    return [n if 0 <= n < count else None for n in pairs]


def swap(value, axis, turn):
    pairs = [(n, q) for n, q in enumerate(partners(lax.axis_size(axis), turn)) if q is not None]
    return lax.ppermute(value, axis, pairs)


def cross(value, axis, mask):
    return lax.ppermute(value, axis, [(n, n ^ mask) for n in range(lax.axis_size(axis))])


def give_back(place, loc, m1, m2):
    m1, m2 = swap(m1, "gx", 1), swap(m2, "gx", 2)
    n1, n2 = call(pass_kernel, (sds((96, C), BF), sds((96, C), BF)), place, loc, m1, m2)
    return (m1, m2, swap(n1, "gy", 1), swap(n2, "gy", 2)), n1


def body(features, pre_act, grad_out, weight_one, weight_two, neighbours, halo_list, send_list):
    gx = lax.axis_size("gx")
    scale = 1.0 / math.sqrt(S * gx * lax.axis_size("gy"))
    place = jnp.stack([lax.axis_index("gx"), lax.axis_index("gy")]).astype(jnp.int32)
    tile = sds((S, C), BF)
    pay, nbt, hrow, srow, pre, grad = call(
        pack_kernel,
        (
            sds((S + 32, 3 * C), BF),
            sds((32, C), F32),
            sds((8, C), jnp.int32),
            sds((8, C), jnp.int32),
            tile,
            tile,
        ),
        place,
        *[
            pltpu.with_memory_space_constraint(value, pltpu.HBM)
            for value in (
                features,
                pre_act,
                grad_out,
                neighbours.T,
                halo_list,
                jnp.transpose(send_list, (2, 0, 1)),
            )
        ],
        specs=[SMEM] + [HBM] * 6,
        flops=4 * 10**9,
        scratch=[
            pltpu.VMEM((K, S), jnp.int32),
            pltpu.VMEM((1, 8, 24), jnp.int32),
            pltpu.VMEM((3, 1, 64), jnp.int32),
            pltpu.SemaphoreType.DMA((6,)),
        ],
    )
    pays = [pay] + [cross(pay, "gy", d) for d in (1, 2, 3)]
    own, m1, m2, loc = spread(place, nbt, grad, weight_two)
    back = pltpu.VMEM((8, HB, C), BF)
    arrived, passed = give_back(place, loc, m1, m2)
    picks = sds((768, C), BF)
    o1, o2, near = call(
        pick_kernel,
        (picks, picks, sds((4, 64, 2 * C), BF)),
        place,
        *pays,
        passed,
        scratch=[pltpu.VMEM((4, 8 * HB, 2 * C), BF)],
        late=1,
    )
    grad_pre, ordered = call(
        gate_kernel,
        (tile, tile),
        place,
        own,
        *arrived,
        hrow,
        pre,
        near,
        scratch=[back],
        late=1,
    )
    grads = [ordered] + [cross(ordered, "gy", d) for d in (1, 2, 3)]
    own, m1, m2, loc = spread(place, nbt, grad_pre, weight_one, o1, o2)
    arrived, passed = give_back(place, loc, m1, m2)
    wide = 7 * C
    half = sds((128, wide), BF)
    stack = sds((4 * S, wide), BF)
    turned, cols_one, cols_two = call(
        columns_kernel,
        (sds((C, 4 * S), BF), stack, stack),
        place,
        *pays,
        arrived[0],
        arrived[1],
        near,
        passed,
        scratch=[
            pltpu.VMEM((EXT, 2 * C), BF),
            pltpu.VMEM((32, C), F32),
            pltpu.VMEM((128, C), F32),
        ],
        late=1,
    )
    some = sds((128, C), BF)
    rows_keep, rows_send = call(
        rows_kernel,
        (some, some),
        place,
        own,
        *arrived,
        hrow,
        grad,
        srow,
        turned,
        scratch=[back],
        late=1,
    )
    rows_come = cross(rows_send, "gx", 1)
    keep_two, send_two = call(
        weight_two_kernel, (half, half), place, turned, cols_two, rows_keep, late=1
    )
    come_two = cross(send_two, "gx", 1)
    keep_one, send_one = call(
        weight_one_kernel,
        (half, half),
        place,
        *grads,
        cols_one,
        keep_two,
        scratch=[pltpu.VMEM((C, 4 * S), BF)],
        late=1,
    )
    come_one = cross(send_one, "gx", 1)
    chunk = sds((64, 8 * C), BF)
    chunks = call(
        merge_kernel,
        (chunk,) * 4,
        place,
        keep_one,
        come_one,
        keep_two,
        come_two,
        rows_keep,
        rows_come,
    )
    chunks = [chunks[0]] + [cross(chunks[d], "gx", 16 * d) for d in (1, 2, 3)]
    summed = call(line_kernel, sds((64, 11 * C), BF), place, *chunks)
    groups = [[16 * y + 2 * z + e for z in range(8)] for y in range(4) for e in range(2)]
    collected = lax.all_to_all(
        summed.reshape(8, 8, 11 * C),
        "gx",
        split_axis=0,
        concat_axis=0,
        tiled=True,
        axis_index_groups=groups,
    )
    out = sds((4, QW), F32)
    return call(
        lambda *refs: final_kernel(scale, *refs), (tile, out, out), collected, specs=[VM]
    )


def solution(mesh):
    in_specs = (
        P(("gx", "gy"), None),
        P(("gx", "gy"), None),
        P(("gx", "gy"), None),
        P(),
        P(),
        P(("gx", "gy"), None),
        P(("gx", "gy"), None, None),
        P(("gx", "gy"), None, None),
    )
    out_specs = (P(("gx", "gy"), None), P("gx", "gy"), P("gx", "gy"))
    return jax.shard_map(body, mesh=mesh, in_specs=in_specs, out_specs=out_specs, check_vma=False)
```

```python
import math

import jax
import jax.numpy as jnp
from jax import lax
from jax.experimental import pallas as pl
from jax.experimental.pallas import tpu as pltpu
from jax.sharding import PartitionSpec as P

C = 256
K = 27
S = 192
HB = 32
EXT = S + 8 * HB
QW = 1728
BF = jnp.bfloat16
F32 = jnp.float32


def iota(shape, dim):
    return lax.broadcasted_iota(jnp.int32, shape, dim)


def onehot(mask):
    return jnp.where(mask, 1.0, 0.0).astype(BF)


def mm(a, b):
    return lax.dot_general(a, b, (((1,), (0,)), ((), ())), preferred_element_type=F32)


def mm_t(a, b):
    return lax.dot_general(a, b, (((0,), (0,)), ((), ())), preferred_element_type=F32)


def direction(a, b):
    grid = 3 * (a + 1) + (b + 1)
    return grid - jnp.where(grid > 4, 1, 0)


def channel_order():
    out = iota((C, C), 1)
    parity, rest = out // 128, out % 128
    source = 8 * (rest // 4) + 4 * parity + rest % 4
    return onehot(iota((C, C), 0) == source)


def halo_matrix(halo_row):
    return onehot(iota((S, 8 * HB), 0) == halo_row)


def pack_kernel(
    place, feat, pre, grad, nbr, halo, send, pay, nbt, hrow, srow, pre_out, grad_out,
    ids, halo_ids, send_ids, sems
):
    copies = [
        pltpu.make_async_copy(source, target, sems.at[n])
        for n, (source, target) in enumerate(
            (
                (nbr, ids),
                (halo, halo_ids),
                (send, send_ids),
                (feat, pay.at[0:S, 0:C]),
                (grad, grad_out),
                (pre, pre_out),
            )
        )
    ]
    for copy in copies:
        copy.start()
    for copy in copies:
        copy.wait()
    table = ids[...].astype(F32)
    heading = jnp.floor((table - S + 0.5) * (1.0 / 24.0))
    table = jnp.where(table >= S, table + 8.0 * heading, table)
    nbt[...] = jnp.full(nbt.shape, -1.0, F32)
    nbt[0:K, 0:S] = table
    shifted_up = table + 1.0
    high = jnp.floor(shifted_up * (1.0 / 16.0))
    pay[S : S + 32, :] = jnp.zeros((32, 3 * C), BF)
    pay[S : S + K, 0:S] = high.astype(BF)
    pay[S : S + K, C : C + S] = (shifted_up - 16.0 * high).astype(BF)
    z = pre_out[...].astype(F32)
    pay[0:S, C : 2 * C] = (z * (1.0 / (1.0 + jnp.exp(-z)))).astype(BF)
    pay[0:S, 2 * C : 3 * C] = mm(grad_out[...], channel_order()).astype(BF)
    halo_up = (halo_ids[0] + 1).astype(F32).astype(BF)
    spread = mm(halo_up, onehot(iota((24, 8 * HB), 1) % HB == iota((24, 8 * HB), 0)))
    row = jnp.sum(
        jnp.where(iota((8, 8 * HB), 1) // HB == iota((8, 8 * HB), 0), spread, 0.0),
        axis=0,
        keepdims=True,
    )
    hrow[...] = jnp.broadcast_to(row.astype(jnp.int32) - 1, hrow.shape)
    pay[S : S + 32, 2 * C : 3 * C] = jnp.broadcast_to(row, (32, C)).astype(BF)
    lane, peer = iota((64, C), 1), iota((64, C), 0)
    parity = jnp.where(lane < 128, place[0] % 2, 1 - place[0] % 2)
    pick = onehot(peer == 2 * ((lane % 128) // 4) + parity)
    spot = iota((1, C), 1) % 4
    total = jnp.zeros((1, C), F32)
    for c in range(3):
        up = jnp.broadcast_to((send_ids[c] + 1).astype(F32), (8, 64)).astype(BF)
        total = jnp.where(spot == c, mm(up, pick)[0:1, :], total)
    srow[...] = jnp.broadcast_to(total.astype(jnp.int32) - 1, srow.shape)


def spread_terms(place, nbt, grad, weight, own, m1, m2, loc, acc):
    rows = iota((EXT, C), 0)
    table = nbt[...].astype(jnp.int32)
    gradient = grad[...]
    none = jnp.zeros((C - S, C), BF)
    masks, terms = [], []
    for k in range(K):
        masks.append(onehot(rows == table[k : k + 1, :]))
        terms += [mm(gradient, weight[:, k * C : (k + 1) * C]).astype(BF), none]
    acc[...] = mm(jnp.concatenate(masks, axis=1), jnp.concatenate(terms, axis=0))
    even = place[0] % 2 == 0
    own[...] = acc[0:S, :]
    first, last = jnp.where(even, S, S + 160), jnp.where(even, S + 160, S)
    m1[0:96, :] = acc[pl.ds(pl.multiple_of(first, 32), 96), :].astype(BF)
    m2[0:96, :] = acc[pl.ds(pl.multiple_of(last, 32), 96), :].astype(BF)
    loc[...] = acc[S + 96 : S + 160, :].astype(BF)


def spread_kernel(place, nbt, grad, weight, own, m1, m2, loc, acc):
    spread_terms(place, nbt, grad, weight, own, m1, m2, loc, acc)


def spread_with_kernel(place, nbt, grad, weight, o1, o2, own, m1, m2, loc, acc):
    m1[96:, :] = o1[...]
    m2[96:, :] = o2[...]
    spread_terms(place, nbt, grad, weight, own, m1, m2, loc, acc)


def inner(position, count):
    return (position > 0) & (position < count - 1)


def masked(keep, rows):
    return jnp.where(keep, rows, jnp.zeros_like(rows))


def pass_kernel(place, loc, m1, m2, n1, n2):
    even = place[1] % 2 == 0
    first = jnp.where(even, 0, 1)
    far = inner(place[0], 64)
    for out, side in ((n1, first), (n2, 1 - first)):
        out[0:32, :] = loc[pl.ds(pl.multiple_of(side * 32, 32), 32), :]
        out[32:64, :] = m1[pl.ds(pl.multiple_of(side * 64, 32), 32), :]
        out[64:96, :] = masked(far, m2[pl.ds(pl.multiple_of(side * 64, 32), 32), :])


def settled(place, own, m1, m2, n1, n2, hrow, back):
    da = jnp.where(place[0] % 2 == 0, 1, -1)
    db = jnp.where(place[1] % 2 == 0, 1, -1)
    back[direction(da, 0)] = m1[32:64, :]
    back[direction(-da, 0)] = masked(inner(place[0], 64), m2[32:64, :])
    beside = inner(place[1], 4)
    for ref, side, keep in ((n1, db, True), (n2, -db, beside)):
        rows = ref[...] if keep is True else masked(keep, ref[...])
        back[direction(0, side)] = rows[0:32, :]
        back[direction(da, side)] = rows[32:64, :]
        back[direction(-da, side)] = rows[64:96, :]
    rows = back[...].reshape(8 * HB, C)
    return own[...] + mm(halo_matrix(hrow[0:1, :]), rows)


def gate_kernel(place, own, m1, m2, n1, n2, hrow, pre, late, out, ordered, back):
    hidden_grad = settled(place, own, m1, m2, n1, n2, hrow, back)
    z = pre[...].astype(F32)
    g = 1.0 / (1.0 + jnp.exp(-z))
    value = (hidden_grad * g * (1.0 + z * (1.0 - g))).astype(BF)
    out[...] = value
    ordered[...] = mm(value, channel_order()).astype(BF)


def rows_kernel(place, own, m1, m2, n1, n2, hrow, grad, srow, t, g1, g2, g3, keep, send, back):
    total = settled(place, own, m1, m2, n1, n2, hrow, back)
    value = (grad[...].astype(F32) + total).astype(BF)
    chosen = mm_t(onehot(iota((S, C), 0) == srow[0:1, :]), value).astype(BF)
    keep[...] = chosen[0:128, :]
    send[...] = chosen[128:256, :]


def pick_kernel(place, p0, p1, p2, p3, late, o1, o2, loc, picked):
    column = place[1]
    for turn, pay in enumerate((p0, p1, p2, p3)):
        halo_row = pay[S : S + 16, 2 * C : 3 * C].astype(F32)[0:1, :].astype(jnp.int32) - 1
        rows = mm_t(halo_matrix(halo_row), pay[0:S, 0 : 2 * C])
        picked[column ^ turn] = rows.astype(BF)
    even = place[0] % 2 == 0
    up = pl.multiple_of(jnp.where(even, 160, 0), 32)
    down = pl.multiple_of(jnp.where(even, 0, 160), 32)
    none = jnp.zeros((HB, 2 * C), BF)
    for tile in range(4):
        for b in (-1, 0, 1):
            source = tile - b
            at = HB * (b + 1)
            for out, side in ((o1, up), (o2, down)):
                rows = picked[source, pl.ds(side + at, HB), :] if 0 <= source < 4 else none
                to = 96 * tile + at
                out[to : to + HB, :] = rows[:, 0:C]
                out[to + 384 : to + 384 + HB, :] = rows[:, C : 2 * C]
            if b:
                to = 0 if b < 0 else HB
                rows = picked[source, 96 + to : 96 + to + HB, :] if 0 <= source < 4 else none
                loc[tile, to : to + HB, :] = rows


def columns_kernel(
    place, p0, p1, p2, p3, r1, r2, loc, late, gt, cols_one, cols_two, ext, ids, sel
):
    column = place[1]
    start = column * QW
    first_k = start // C
    offset = start % C
    even = place[0] % 2 == 0
    far = inner(place[0], 64)
    shift = onehot(iota((C, C), 0) == (iota((C, C), 1) + offset) % C)
    lane = iota((S, 2 * C), 1) % C
    early = lane < C - offset
    for turn, pay in enumerate((p0, p1, p2, p3)):
        tile = column ^ turn
        for half in range(2):
            lanes = slice(half * C, (half + 1) * C)
            at = pl.multiple_of(96 + 384 * half + 96 * tile, 32)
            above, below = r1[pl.ds(at, 96), :], masked(far, r2[pl.ds(at, 96), :])
            for to, piece in (
                (0, pay[0:S, lanes]),
                (S, jnp.where(even, above, below)),
                (S + 96, loc[tile, :, lanes]),
                (S + 160, jnp.where(even, below, above)),
            ):
                ext[to : to + piece.shape[0], lanes] = mm(piece, shift).astype(BF)
        gt[:, turn * S : (turn + 1) * S] = jnp.transpose(
            pay[0:S, 2 * C : 3 * C].astype(F32)
        ).astype(BF)
        high = pay[S : S + 32, 0:C].astype(F32)
        low = pay[S : S + 32, C : 2 * C].astype(F32)
        ids[0:32, :] = 16.0 * high + low - 1.0
        for part in range(8):
            sel[part : part + 1, :] = ids[pl.ds(first_k + part, 1), :]
        table = jnp.transpose(sel[...])[:, 0:8].astype(jnp.int32)
        extended = ext[...]
        previous = None
        for part in range(8):
            match = onehot(iota((S, EXT), 1) == table[0:S, part : part + 1])
            block = mm(match, extended).astype(BF)
            if part:
                merged = jnp.where(early, previous, block)
                at = (part - 1) * C
                cols_one[turn * S : (turn + 1) * S, at : at + C] = merged[:, 0:C]
                cols_two[turn * S : (turn + 1) * S, at : at + C] = merged[:, C : 2 * C]
            previous = block


def weight_blocks(place, gt, cols, keep, send):
    mine = pl.multiple_of((place[0] % 2) * 128, 128)
    other = pl.multiple_of(128 - mine, 128)
    for out, at in ((keep, mine), (send, other)):
        left = gt[pl.ds(at, 128), :]
        for part in range(7):
            out[:, part * C : (part + 1) * C] = mm(
                left, cols[:, part * C : (part + 1) * C]
            ).astype(out.dtype)


def weight_two_kernel(place, gt, cols, late, keep, send):
    weight_blocks(place, gt, cols, keep, send)


def weight_one_kernel(place, g0, g1, g2, g3, cols, late, keep, send, gt):
    for turn, grad in enumerate((g0, g1, g2, g3)):
        gt[:, turn * S : (turn + 1) * S] = jnp.transpose(grad[...].astype(F32)).astype(BF)
    weight_blocks(place, gt, cols, keep, send)


def merge_kernel(place, k1, s1, k2, s2, rk, rs, *outs):
    first = place[0] % 2 == 0
    line = place[0] // 16
    for turn, out in enumerate(outs):
        rows = pl.ds(pl.multiple_of(32 * (line ^ turn), 32), 32)
        for at, (keep, come) in ((0, (k1, s1)), (32, (k2, s2))):
            total = keep[rows, :].astype(F32) + come[rows, :].astype(F32)
            out[at : at + 32, 0 : 7 * C] = total.astype(BF)
        mine, other = rk[rows, :], rs[rows, :]
        out[0:32, 7 * C : 8 * C] = jnp.where(first, mine, other)
        out[32:64, 7 * C : 8 * C] = jnp.where(first, other, mine)


def line_kernel(place, a0, a1, a2, a3, out):
    line = place[0] // 16
    to, at = iota((64, 64), 0), iota((64, 64), 1)
    order = onehot(at == 32 * ((to % 8) // 4) + 4 * (to // 8) + to % 4)
    parts = (a0, a1, a2, a3)
    for n in range(7):
        lanes = slice(n * C, (n + 1) * C)
        total = a0[:, lanes].astype(F32)
        for part in parts[1:]:
            total = total + part[:, lanes].astype(F32)
        out[:, lanes] = mm(order, total.astype(BF)).astype(BF)
    for turn, part in enumerate(parts):
        to = pl.multiple_of(7 * C + (line ^ turn) * C, C)
        out[:, pl.ds(to, C)] = mm(order, part[:, 7 * C : 8 * C]).astype(BF)


def final_kernel(scale, arrived, rows, one, two):
    total = jnp.sum(arrived[:, :, 0 : 7 * C].astype(F32), axis=0) * scale
    one[...] = total[0:4, 0:QW]
    two[...] = total[4:8, 0:QW]
    to, at = iota((48, 64), 0), iota((48, 64), 1)
    spot = onehot((at // 8 == to // 6) & (at % 8 == 4 * ((to % 6) // 3) + to % 3))
    for line in range(4):
        piece = arrived[:, :, (7 + line) * C : (8 + line) * C].reshape(64, C)
        rows[48 * line : 48 * line + 48, :] = mm(spot, piece).astype(BF)


def sds(shape, dtype):
    return jax.ShapeDtypeStruct(shape, dtype)


SMEM = pl.BlockSpec(memory_space=pltpu.SMEM)
VM = pl.BlockSpec(memory_space=pltpu.VMEM)
HBM = pl.BlockSpec(memory_space=pltpu.HBM)
ANY = pl.BlockSpec(memory_space=pl.ANY)


def call(kernel, outs, *args, scratch=(), specs=None, late=0, flops=10**5):
    if specs is None:
        specs = [SMEM] + [VM] * (len(args) - 1 - late) + [ANY] * late
    return pl.pallas_call(
        kernel,
        out_shape=outs,
        in_specs=specs,
        out_specs=jax.tree.map(lambda _: VM, outs),
        scratch_shapes=list(scratch),
        compiler_params=pltpu.CompilerParams(vmem_limit_bytes=40 * 2**20),
        cost_estimate=pl.CostEstimate(flops=flops, bytes_accessed=10**4, transcendentals=0),
    )(*args)


def spread(place, nbt, grad, weight, *picks):
    edge = sds((96 + (picks[0].shape[0] if picks else 0), C), BF)
    return call(
        spread_with_kernel if picks else spread_kernel,
        (sds((S, C), F32), edge, edge, sds((64, C), BF)),
        place,
        nbt,
        grad,
        weight,
        *picks,
        scratch=[pltpu.VMEM((EXT, C), F32)],
    )


def swap(value, axis, turn):
    size = lax.axis_size(axis)
    step = 1 if turn == 1 else -1
    pairs = [(n, (n + (step if n % 2 == 0 else -step)) % size) for n in range(size)]
    return lax.ppermute(value, axis, pairs)


def cross(value, axis, mask):
    return lax.ppermute(value, axis, [(n, n ^ mask) for n in range(lax.axis_size(axis))])


def give_back(place, loc, m1, m2):
    m1, m2 = swap(m1, "gx", 1), swap(m2, "gx", 2)
    n1, n2 = call(pass_kernel, (sds((96, C), BF), sds((96, C), BF)), place, loc, m1, m2)
    return (m1, m2, swap(n1, "gy", 1), swap(n2, "gy", 2)), n1


def body(features, pre_act, grad_out, weight_one, weight_two, neighbours, halo_list, send_list):
    gx = lax.axis_size("gx")
    scale = 1.0 / math.sqrt(S * gx * lax.axis_size("gy"))
    place = jnp.stack([lax.axis_index("gx"), lax.axis_index("gy")]).astype(jnp.int32)
    tile = sds((S, C), BF)
    pay, nbt, hrow, srow, pre, grad = call(
        pack_kernel,
        (
            sds((S + 32, 3 * C), BF),
            sds((32, C), F32),
            sds((8, C), jnp.int32),
            sds((8, C), jnp.int32),
            tile,
            tile,
        ),
        place,
        *[
            pltpu.with_memory_space_constraint(value, pltpu.HBM)
            for value in (
                features,
                pre_act,
                grad_out,
                neighbours.T,
                halo_list,
                jnp.transpose(send_list, (2, 0, 1)),
            )
        ],
        specs=[SMEM] + [HBM] * 6,
        flops=4 * 10**9,
        scratch=[
            pltpu.VMEM((K, S), jnp.int32),
            pltpu.VMEM((1, 8, 24), jnp.int32),
            pltpu.VMEM((3, 1, 64), jnp.int32),
            pltpu.SemaphoreType.DMA((6,)),
        ],
    )
    pays = [pay] + [cross(pay, "gy", d) for d in (1, 2, 3)]
    own, m1, m2, loc = spread(place, nbt, grad, weight_two)
    back = pltpu.VMEM((8, HB, C), BF)
    arrived, passed = give_back(place, loc, m1, m2)
    picks = sds((768, C), BF)
    o1, o2, near = call(
        pick_kernel,
        (picks, picks, sds((4, 64, 2 * C), BF)),
        place,
        *pays,
        passed,
        scratch=[pltpu.VMEM((4, 8 * HB, 2 * C), BF)],
        late=1,
    )
    grad_pre, ordered = call(
        gate_kernel,
        (tile, tile),
        place,
        own,
        *arrived,
        hrow,
        pre,
        near,
        scratch=[back],
        late=1,
    )
    grads = [ordered] + [cross(ordered, "gy", d) for d in (1, 2, 3)]
    own, m1, m2, loc = spread(place, nbt, grad_pre, weight_one, o1, o2)
    arrived, passed = give_back(place, loc, m1, m2)
    wide = 7 * C
    half = sds((128, wide), BF)
    stack = sds((4 * S, wide), BF)
    turned, cols_one, cols_two = call(
        columns_kernel,
        (sds((C, 4 * S), BF), stack, stack),
        place,
        *pays,
        arrived[0],
        arrived[1],
        near,
        passed,
        scratch=[
            pltpu.VMEM((EXT, 2 * C), BF),
            pltpu.VMEM((32, C), F32),
            pltpu.VMEM((128, C), F32),
        ],
        late=1,
    )
    some = sds((128, C), BF)
    rows_keep, rows_send = call(
        rows_kernel,
        (some, some),
        place,
        own,
        *arrived,
        hrow,
        grad,
        srow,
        turned,
        *grads[1:],
        scratch=[back],
        late=4,
    )
    rows_come = cross(rows_send, "gx", 1)
    full = sds((128, wide), F32)
    keep_two, send_two = call(
        weight_two_kernel, (full, full), place, turned, cols_two, rows_keep, late=1
    )
    come_two = cross(send_two, "gx", 1)
    keep_one, send_one = call(
        weight_one_kernel,
        (half, half),
        place,
        *grads,
        cols_one,
        keep_two,
        scratch=[pltpu.VMEM((C, 4 * S), BF)],
        late=1,
    )
    come_one = cross(send_one, "gx", 1)
    chunk = sds((64, 8 * C), BF)
    chunks = call(
        merge_kernel,
        (chunk,) * 4,
        place,
        keep_one,
        come_one,
        keep_two,
        come_two,
        rows_keep,
        rows_come,
    )
    chunks = [chunks[0]] + [cross(chunks[d], "gx", 16 * d) for d in (1, 2, 3)]
    summed = call(line_kernel, sds((64, 11 * C), BF), place, *chunks)
    groups = [[16 * y + 2 * z + e for z in range(8)] for y in range(4) for e in range(2)]
    collected = lax.all_to_all(
        summed.reshape(8, 8, 11 * C),
        "gx",
        split_axis=0,
        concat_axis=0,
        tiled=True,
        axis_index_groups=groups,
    )
    out = sds((4, QW), F32)
    return call(
        lambda *refs: final_kernel(scale, *refs), (tile, out, out), collected, specs=[VM]
    )


def solution(mesh):
    in_specs = (
        P(("gx", "gy"), None),
        P(("gx", "gy"), None),
        P(("gx", "gy"), None),
        P(),
        P(),
        P(("gx", "gy"), None),
        P(("gx", "gy"), None, None),
        P(("gx", "gy"), None, None),
    )
    out_specs = (P(("gx", "gy"), None), P("gx", "gy"), P("gx", "gy"))
    return jax.shard_map(body, mesh=mesh, in_specs=in_specs, out_specs=out_specs, check_vma=False)
```

```python
import math

import jax
import jax.numpy as jnp
from jax import lax
from jax.experimental import pallas as pl
from jax.experimental.pallas import tpu as pltpu
from jax.sharding import PartitionSpec as P

C = 256
K = 27
S = 192
HB = 32
EXT = S + 8 * HB
QW = 1728
BF = jnp.bfloat16
F32 = jnp.float32


def iota(shape, dim):
    return lax.broadcasted_iota(jnp.int32, shape, dim)


def onehot(mask):
    return jnp.where(mask, 1.0, 0.0).astype(BF)


def mm(a, b):
    return lax.dot_general(a, b, (((1,), (0,)), ((), ())), preferred_element_type=F32)


def mm_t(a, b):
    return lax.dot_general(a, b, (((0,), (0,)), ((), ())), preferred_element_type=F32)


def direction(a, b):
    grid = 3 * (a + 1) + (b + 1)
    return grid - jnp.where(grid > 4, 1, 0)


def channel_order():
    out = iota((C, C), 1)
    parity, rest = out // 128, out % 128
    source = 8 * (rest // 4) + 4 * parity + rest % 4
    return onehot(iota((C, C), 0) == source)


def halo_matrix(halo_row):
    return onehot(iota((S, 8 * HB), 0) == halo_row)


def pack_kernel(
    place, feat, pre, grad, nbr, halo, send, pay, nbt, hrow, srow, pre_out, grad_out,
    ids, halo_ids, send_ids, sems
):
    copies = [
        pltpu.make_async_copy(source, target, sems.at[n])
        for n, (source, target) in enumerate(
            (
                (nbr, ids),
                (halo, halo_ids),
                (send, send_ids),
                (feat, pay.at[0:S, 0:C]),
                (grad, grad_out),
                (pre, pre_out),
            )
        )
    ]
    for copy in copies:
        copy.start()
    for copy in copies:
        copy.wait()
    table = ids[...].astype(F32)
    heading = jnp.floor((table - S + 0.5) * (1.0 / 24.0))
    table = jnp.where(table >= S, table + 8.0 * heading, table)
    nbt[...] = jnp.full(nbt.shape, -1.0, F32)
    nbt[0:K, 0:S] = table
    shifted_up = table + 1.0
    high = jnp.floor(shifted_up * (1.0 / 16.0))
    pay[S : S + 32, :] = jnp.zeros((32, 3 * C), BF)
    pay[S : S + K, 0:S] = high.astype(BF)
    pay[S : S + K, C : C + S] = (shifted_up - 16.0 * high).astype(BF)
    z = pre_out[...].astype(F32)
    pay[0:S, C : 2 * C] = (z * (1.0 / (1.0 + jnp.exp(-z)))).astype(BF)
    pay[0:S, 2 * C : 3 * C] = mm(grad_out[...], channel_order()).astype(BF)
    halo_up = (halo_ids[0] + 1).astype(F32).astype(BF)
    spread = mm(halo_up, onehot(iota((24, 8 * HB), 1) % HB == iota((24, 8 * HB), 0)))
    row = jnp.sum(
        jnp.where(iota((8, 8 * HB), 1) // HB == iota((8, 8 * HB), 0), spread, 0.0),
        axis=0,
        keepdims=True,
    )
    hrow[...] = jnp.broadcast_to(row.astype(jnp.int32) - 1, hrow.shape)
    pay[S : S + 32, 2 * C : 3 * C] = jnp.broadcast_to(row, (32, C)).astype(BF)
    lane, peer = iota((64, C), 1), iota((64, C), 0)
    parity = jnp.where(lane < 128, place[0] % 2, 1 - place[0] % 2)
    pick = onehot(peer == 2 * ((lane % 128) // 4) + parity)
    spot = iota((1, C), 1) % 4
    total = jnp.zeros((1, C), F32)
    for c in range(3):
        up = jnp.broadcast_to((send_ids[c] + 1).astype(F32), (8, 64)).astype(BF)
        total = jnp.where(spot == c, mm(up, pick)[0:1, :], total)
    srow[...] = jnp.broadcast_to(total.astype(jnp.int32) - 1, srow.shape)


def spread_kernel(place, nbt, grad, weight, own, m1, m2, loc, acc):
    rows = iota((EXT, C), 0)
    table = nbt[...].astype(jnp.int32)
    gradient = grad[...]
    none = jnp.zeros((C - S, C), BF)
    masks, terms = [], []
    for k in range(K):
        masks.append(onehot(rows == table[k : k + 1, :]))
        terms += [mm(gradient, weight[:, k * C : (k + 1) * C]).astype(BF), none]
    acc[...] = mm(jnp.concatenate(masks, axis=1), jnp.concatenate(terms, axis=0))
    even = place[0] % 2 == 0
    own[...] = acc[0:S, :]
    first, last = jnp.where(even, S, S + 160), jnp.where(even, S + 160, S)
    m1[...] = acc[pl.ds(pl.multiple_of(first, 32), 96), :].astype(BF)
    m2[...] = acc[pl.ds(pl.multiple_of(last, 32), 96), :].astype(BF)
    loc[...] = acc[S + 96 : S + 160, :].astype(BF)


def inner(position, count):
    return (position > 0) & (position < count - 1)


def masked(keep, rows):
    return jnp.where(keep, rows, jnp.zeros_like(rows))


def pass_kernel(place, loc, m2, m1, n2, n1):
    even = place[1] % 2 == 0
    first = jnp.where(even, 0, 1)
    far = inner(place[0], 64)
    for out, side in ((n1, first), (n2, 1 - first)):
        out[0:32, :] = loc[pl.ds(pl.multiple_of(side * 32, 32), 32), :]
        out[32:64, :] = m1[pl.ds(pl.multiple_of(side * 64, 32), 32), :]
        out[64:96, :] = masked(far, m2[pl.ds(pl.multiple_of(side * 64, 32), 32), :])


def settled(place, own, m1, m2, n1, n2, hrow, back):
    da = jnp.where(place[0] % 2 == 0, 1, -1)
    db = jnp.where(place[1] % 2 == 0, 1, -1)
    back[direction(da, 0)] = m1[32:64, :]
    back[direction(-da, 0)] = masked(inner(place[0], 64), m2[32:64, :])
    beside = inner(place[1], 4)
    for ref, side, keep in ((n1, db, True), (n2, -db, beside)):
        rows = ref[...] if keep is True else masked(keep, ref[...])
        back[direction(0, side)] = rows[0:32, :]
        back[direction(da, side)] = rows[32:64, :]
        back[direction(-da, side)] = rows[64:96, :]
    rows = back[...].reshape(8 * HB, C)
    return own[...] + mm(halo_matrix(hrow[0:1, :]), rows)


def gate_kernel(place, own, m1, m2, n1, n2, hrow, pre, out, ordered, back):
    hidden_grad = settled(place, own, m1, m2, n1, n2, hrow, back)
    z = pre[...].astype(F32)
    g = 1.0 / (1.0 + jnp.exp(-z))
    value = (hidden_grad * g * (1.0 + z * (1.0 - g))).astype(BF)
    out[...] = value
    ordered[...] = mm(value, channel_order()).astype(BF)


def rows_kernel(place, own, m1, m2, n1, n2, hrow, grad, srow, t, g2, g1, g3, keep, send, back):
    total = settled(place, own, m1, m2, n1, n2, hrow, back)
    value = (grad[...].astype(F32) + total).astype(BF)
    chosen = mm_t(onehot(iota((S, C), 0) == srow[0:1, :]), value).astype(BF)
    keep[...] = chosen[0:128, :]
    send[...] = chosen[128:256, :]


def pick_kernel(place, p0, p2, p1, p3, m1, m2, o1, o2, loc, picked):
    column = place[1]
    o1[0:96, :] = m1[...]
    o2[0:96, :] = m2[...]
    for turn, pay in enumerate((p0, p1, p2, p3)):
        halo_row = pay[S : S + 16, 2 * C : 3 * C].astype(F32)[0:1, :].astype(jnp.int32) - 1
        rows = mm_t(halo_matrix(halo_row), pay[0:S, 0 : 2 * C])
        picked[column ^ turn] = rows.astype(BF)
    even = place[0] % 2 == 0
    up = pl.multiple_of(jnp.where(even, 160, 0), 32)
    down = pl.multiple_of(jnp.where(even, 0, 160), 32)
    none = jnp.zeros((HB, 2 * C), BF)
    for tile in range(4):
        for b in (-1, 0, 1):
            source = tile - b
            at = HB * (b + 1)
            for out, side in ((o1, up), (o2, down)):
                rows = picked[source, pl.ds(side + at, HB), :] if 0 <= source < 4 else none
                to = 96 + 96 * tile + at
                out[to : to + HB, :] = rows[:, 0:C]
                out[to + 384 : to + 384 + HB, :] = rows[:, C : 2 * C]
            if b:
                to = 0 if b < 0 else HB
                rows = picked[source, 96 + to : 96 + to + HB, :] if 0 <= source < 4 else none
                loc[tile, to : to + HB, :] = rows


def columns_kernel(
    place, p0, p2, p1, p3, r2, r1, loc, late, gt, cols_one, cols_two, ext, ids, sel
):
    column = place[1]
    start = column * QW
    first_k = start // C
    offset = start % C
    even = place[0] % 2 == 0
    far = inner(place[0], 64)
    shift = onehot(iota((C, C), 0) == (iota((C, C), 1) + offset) % C)
    lane = iota((S, 2 * C), 1) % C
    early = lane < C - offset
    for turn, pay in enumerate((p0, p1, p2, p3)):
        tile = column ^ turn
        for half in range(2):
            lanes = slice(half * C, (half + 1) * C)
            at = pl.multiple_of(96 + 384 * half + 96 * tile, 32)
            above, below = r1[pl.ds(at, 96), :], masked(far, r2[pl.ds(at, 96), :])
            for to, piece in (
                (0, pay[0:S, lanes]),
                (S, jnp.where(even, above, below)),
                (S + 96, loc[tile, :, lanes]),
                (S + 160, jnp.where(even, below, above)),
            ):
                ext[to : to + piece.shape[0], lanes] = mm(piece, shift).astype(BF)
        gt[:, turn * S : (turn + 1) * S] = jnp.transpose(
            pay[0:S, 2 * C : 3 * C].astype(F32)
        ).astype(BF)
        high = pay[S : S + 32, 0:C].astype(F32)
        low = pay[S : S + 32, C : 2 * C].astype(F32)
        ids[0:32, :] = 16.0 * high + low - 1.0
        for part in range(8):
            sel[part : part + 1, :] = ids[pl.ds(first_k + part, 1), :]
        table = jnp.transpose(sel[...])[:, 0:8].astype(jnp.int32)
        extended = ext[...]
        previous = None
        for part in range(8):
            match = onehot(iota((S, EXT), 1) == table[0:S, part : part + 1])
            block = mm(match, extended).astype(BF)
            if part:
                merged = jnp.where(early, previous, block)
                at = (part - 1) * C
                cols_one[turn * S : (turn + 1) * S, at : at + C] = merged[:, 0:C]
                cols_two[turn * S : (turn + 1) * S, at : at + C] = merged[:, C : 2 * C]
            previous = block


def weight_blocks(place, gt, cols, keep, send):
    mine = pl.multiple_of((place[0] % 2) * 128, 128)
    other = pl.multiple_of(128 - mine, 128)
    for out, at in ((keep, mine), (send, other)):
        left = gt[pl.ds(at, 128), :]
        for part in range(7):
            out[:, part * C : (part + 1) * C] = mm(
                left, cols[:, part * C : (part + 1) * C]
            ).astype(out.dtype)


def weight_two_kernel(place, gt, cols, late, keep, send):
    weight_blocks(place, gt, cols, keep, send)


def weight_one_kernel(place, g0, g2, g1, g3, cols, late, keep, send, gt):
    for turn, grad in enumerate((g0, g1, g2, g3)):
        gt[:, turn * S : (turn + 1) * S] = jnp.transpose(grad[...].astype(F32)).astype(BF)
    weight_blocks(place, gt, cols, keep, send)


def merge_kernel(place, k1, s1, k2, s2, rk, rs, *outs):
    first = place[0] % 2 == 0
    line = place[0] // 16
    for turn, out in enumerate(outs):
        rows = pl.ds(pl.multiple_of(32 * (line ^ turn), 32), 32)
        for at, (keep, come) in ((0, (k1, s1)), (32, (k2, s2))):
            total = keep[rows, :].astype(F32) + come[rows, :].astype(F32)
            out[at : at + 32, 0 : 7 * C] = total.astype(BF)
        mine, other = rk[rows, :], rs[rows, :]
        out[0:32, 7 * C : 8 * C] = jnp.where(first, mine, other)
        out[32:64, 7 * C : 8 * C] = jnp.where(first, other, mine)


def line_kernel(place, a0, a2, a1, a3, out):
    line = place[0] // 16
    to, at = iota((64, 64), 0), iota((64, 64), 1)
    order = onehot(at == 32 * ((to % 8) // 4) + 4 * (to // 8) + to % 4)
    parts = (a0, a1, a2, a3)
    for n in range(7):
        lanes = slice(n * C, (n + 1) * C)
        total = a0[:, lanes].astype(F32)
        for part in parts[1:]:
            total = total + part[:, lanes].astype(F32)
        out[:, lanes] = mm(order, total.astype(BF)).astype(BF)
    for turn, part in enumerate(parts):
        to = pl.multiple_of(7 * C + (line ^ turn) * C, C)
        out[:, pl.ds(to, C)] = mm(order, part[:, 7 * C : 8 * C]).astype(BF)


def final_kernel(scale, arrived, rows, one, two):
    total = jnp.sum(arrived[:, :, 0 : 7 * C].astype(F32), axis=0) * scale
    one[...] = total[0:4, 0:QW]
    two[...] = total[4:8, 0:QW]
    to, at = iota((48, 64), 0), iota((48, 64), 1)
    spot = onehot((at // 8 == to // 6) & (at % 8 == 4 * ((to % 6) // 3) + to % 3))
    for line in range(4):
        piece = arrived[:, :, (7 + line) * C : (8 + line) * C].reshape(64, C)
        rows[48 * line : 48 * line + 48, :] = mm(spot, piece).astype(BF)


def sds(shape, dtype):
    return jax.ShapeDtypeStruct(shape, dtype)


SMEM = pl.BlockSpec(memory_space=pltpu.SMEM)
VM = pl.BlockSpec(memory_space=pltpu.VMEM)
HBM = pl.BlockSpec(memory_space=pltpu.HBM)
ANY = pl.BlockSpec(memory_space=pl.ANY)


def call(kernel, outs, *args, scratch=(), specs=None, late=0, flops=10**5):
    if specs is None:
        specs = [SMEM] + [VM] * (len(args) - 1 - late) + [ANY] * late
    return pl.pallas_call(
        kernel,
        out_shape=outs,
        in_specs=specs,
        out_specs=jax.tree.map(lambda _: VM, outs),
        scratch_shapes=list(scratch),
        compiler_params=pltpu.CompilerParams(vmem_limit_bytes=40 * 2**20),
        cost_estimate=pl.CostEstimate(flops=flops, bytes_accessed=10**4, transcendentals=0),
    )(*args)


def spread(place, nbt, grad, weight):
    edge = sds((96, C), BF)
    return call(
        spread_kernel,
        (sds((S, C), F32), edge, edge, sds((64, C), BF)),
        place,
        nbt,
        grad,
        weight,
        scratch=[pltpu.VMEM((EXT, C), F32)],
    )


def swap(value, axis, turn):
    gx, gy = lax.axis_size("gx"), lax.axis_size("gy")
    pairs = []
    for i in range(gx):
        for j in range(gy):
            n, size = (i, gx) if axis == "gx" else (j, gy)
            q = n ^ 1 if turn == 1 else ((n + 1) ^ 1) - 1
            if axis == "gx":
                to = (q, j) if 0 <= q < size else (i, j ^ 1)
            else:
                to = (i, q) if 0 <= q < size else (i ^ 1, j)
            pairs.append((i * gy + j, to[0] * gy + to[1]))
    return lax.ppermute(value, ("gx", "gy"), pairs)


def cross(value, axis, mask):
    return lax.ppermute(value, axis, [(n, n ^ mask) for n in range(lax.axis_size(axis))])


def gathered(value, axis, base=1):
    return [value] + [cross(value, axis, base * d) for d in (2, 1, 3)]


def give_back(place, loc, m1, m2):
    m2, m1 = swap(m2, "gx", 2), swap(m1, "gx", 1)
    n2, n1 = call(pass_kernel, (sds((96, C), BF), sds((96, C), BF)), place, loc, m2, m1)
    return (m1, m2, swap(n1, "gy", 1), swap(n2, "gy", 2)), n1


def body(features, pre_act, grad_out, weight_one, weight_two, neighbours, halo_list, send_list):
    gx = lax.axis_size("gx")
    scale = 1.0 / math.sqrt(S * gx * lax.axis_size("gy"))
    place = jnp.stack([lax.axis_index("gx"), lax.axis_index("gy")]).astype(jnp.int32)
    tile = sds((S, C), BF)
    pay, nbt, hrow, srow, pre, grad = call(
        pack_kernel,
        (
            sds((S + 32, 3 * C), BF),
            sds((32, C), F32),
            sds((8, C), jnp.int32),
            sds((8, C), jnp.int32),
            tile,
            tile,
        ),
        place,
        *[
            pltpu.with_memory_space_constraint(value, pltpu.HBM)
            for value in (
                features,
                pre_act,
                grad_out,
                neighbours.T,
                halo_list,
                jnp.transpose(send_list, (2, 0, 1)),
            )
        ],
        specs=[SMEM] + [HBM] * 6,
        flops=4 * 10**9,
        scratch=[
            pltpu.VMEM((K, S), jnp.int32),
            pltpu.VMEM((1, 8, 24), jnp.int32),
            pltpu.VMEM((3, 1, 64), jnp.int32),
            pltpu.SemaphoreType.DMA((6,)),
        ],
    )
    pays = gathered(pay, "gy")
    own, m1, m2, loc = spread(place, nbt, grad, weight_two)
    back = pltpu.VMEM((8, HB, C), BF)
    arrived, _ = give_back(place, loc, m1, m2)
    grad_pre, ordered = call(
        gate_kernel, (tile, tile), place, own, *arrived, hrow, pre, scratch=[back]
    )
    grads = gathered(ordered, "gy")
    own, m1, m2, loc = spread(place, nbt, grad_pre, weight_one)
    picks = sds((96 + 768, C), BF)
    m1, m2, near = call(
        pick_kernel,
        (picks, picks, sds((4, 64, 2 * C), BF)),
        place,
        *pays,
        m1,
        m2,
        scratch=[pltpu.VMEM((4, 8 * HB, 2 * C), BF)],
    )
    arrived, passed = give_back(place, loc, m1, m2)
    wide = 7 * C
    half = sds((128, wide), BF)
    stack = sds((4 * S, wide), BF)
    turned, cols_one, cols_two = call(
        columns_kernel,
        (sds((C, 4 * S), BF), stack, stack),
        place,
        *pays,
        arrived[1],
        arrived[0],
        near,
        passed,
        scratch=[
            pltpu.VMEM((EXT, 2 * C), BF),
            pltpu.VMEM((32, C), F32),
            pltpu.VMEM((128, C), F32),
        ],
        late=1,
    )
    some = sds((128, C), BF)
    rows_keep, rows_send = call(
        rows_kernel,
        (some, some),
        place,
        own,
        *arrived,
        hrow,
        grad,
        srow,
        turned,
        *grads[1:],
        scratch=[back],
        late=4,
    )
    rows_come = cross(rows_send, "gx", 1)
    full = sds((128, wide), F32)
    keep_two, send_two = call(
        weight_two_kernel, (full, full), place, turned, cols_two, rows_keep, late=1
    )
    come_two = cross(send_two, "gx", 1)
    keep_one, send_one = call(
        weight_one_kernel,
        (half, half),
        place,
        *grads,
        cols_one,
        keep_two,
        scratch=[pltpu.VMEM((C, 4 * S), BF)],
        late=1,
    )
    come_one = cross(send_one, "gx", 1)
    chunk = sds((64, 8 * C), BF)
    chunks = call(
        merge_kernel,
        (chunk,) * 4,
        place,
        keep_one,
        come_one,
        keep_two,
        come_two,
        rows_keep,
        rows_come,
    )
    chunks = [chunks[0]] + [cross(chunks[d], "gx", 16 * d) for d in (2, 1, 3)]
    summed = call(line_kernel, sds((64, 11 * C), BF), place, *chunks)
    groups = [[16 * y + 2 * z + e for z in range(8)] for y in range(4) for e in range(2)]
    collected = lax.all_to_all(
        summed.reshape(8, 8, 11 * C),
        "gx",
        split_axis=0,
        concat_axis=0,
        tiled=True,
        axis_index_groups=groups,
    )
    out = sds((4, QW), F32)
    return call(
        lambda *refs: final_kernel(scale, *refs), (tile, out, out), collected, specs=[VM]
    )


def solution(mesh):
    in_specs = (
        P(("gx", "gy"), None),
        P(("gx", "gy"), None),
        P(("gx", "gy"), None),
        P(),
        P(),
        P(("gx", "gy"), None),
        P(("gx", "gy"), None, None),
        P(("gx", "gy"), None, None),
    )
    out_specs = (P(("gx", "gy"), None), P("gx", "gy"), P("gx", "gy"))
    return jax.shard_map(body, mesh=mesh, in_specs=in_specs, out_specs=out_specs, check_vma=False)
```

```python
import functools
import math

import jax
import jax.numpy as jnp
from jax import lax
from jax.experimental import pallas as pl
from jax.experimental.pallas import tpu as pltpu
from jax.sharding import PartitionSpec as P

C = 256
K = 27
S = 192
HB = 32
EXT = S + 8 * HB
QW = 1728
BF = jnp.bfloat16
F32 = jnp.float32


def iota(shape, dim):
    return lax.broadcasted_iota(jnp.int32, shape, dim)


def onehot(mask):
    return jnp.where(mask, 1.0, 0.0).astype(BF)


def mm(a, b):
    return lax.dot_general(a, b, (((1,), (0,)), ((), ())), preferred_element_type=F32)


def mm_t(a, b):
    return lax.dot_general(a, b, (((0,), (0,)), ((), ())), preferred_element_type=F32)


def direction(a, b):
    grid = 3 * (a + 1) + (b + 1)
    return grid - jnp.where(grid > 4, 1, 0)


def channel_order():
    out = iota((C, C), 1)
    parity, rest = out // 128, out % 128
    source = 8 * (rest // 4) + 4 * parity + rest % 4
    return onehot(iota((C, C), 0) == source)


def halo_matrix(halo_row):
    return onehot(iota((S, 8 * HB), 0) == halo_row)


def pack_kernel(
    place, feat, pre, grad, nbr, halo, send, pay, nbt, hrow, srow, pre_out, grad_out,
    ids, halo_ids, send_ids, sems
):
    copies = [
        pltpu.make_async_copy(source, target, sems.at[n])
        for n, (source, target) in enumerate(
            (
                (nbr, ids),
                (halo, halo_ids),
                (send, send_ids),
                (feat, pay.at[0:S, 0:C]),
                (grad, grad_out),
                (pre, pre_out),
            )
        )
    ]
    for copy in copies:
        copy.start()
    for copy in copies:
        copy.wait()
    table = ids[...].astype(F32)
    heading = jnp.floor((table - S + 0.5) * (1.0 / 24.0))
    table = jnp.where(table >= S, table + 8.0 * heading, table)
    nbt[...] = jnp.full(nbt.shape, -1.0, F32)
    nbt[0:K, 0:S] = table
    shifted_up = table + 1.0
    high = jnp.floor(shifted_up * (1.0 / 16.0))
    pay[S : S + 32, :] = jnp.zeros((32, 2 * C), BF)
    pay[S : S + K, 0:S] = high.astype(BF)
    pay[S : S + K, C : C + S] = (shifted_up - 16.0 * high).astype(BF)
    z = pre_out[...].astype(F32)
    pay[0:S, C : 2 * C] = (z * (1.0 / (1.0 + jnp.exp(-z)))).astype(BF)
    halo_up = (halo_ids[0] + 1).astype(F32).astype(BF)
    spread = mm(halo_up, onehot(iota((24, 8 * HB), 1) % HB == iota((24, 8 * HB), 0)))
    row = jnp.sum(
        jnp.where(iota((8, 8 * HB), 1) // HB == iota((8, 8 * HB), 0), spread, 0.0),
        axis=0,
        keepdims=True,
    )
    hrow[...] = jnp.broadcast_to(row.astype(jnp.int32) - 1, hrow.shape)
    tail = pay[S + 16 : S + 32, 0:C].astype(F32)
    pay[S + 16 : S + 32, 0:C] = jnp.where(iota((16, C), 0) == 15, row, tail).astype(BF)
    lane, peer = iota((64, C), 1), iota((64, C), 0)
    parity = jnp.where(lane < 128, place[0] % 2, 1 - place[0] % 2)
    pick = onehot(peer == 2 * ((lane % 128) // 4) + parity)
    spot = iota((1, C), 1) % 4
    total = jnp.zeros((1, C), F32)
    for c in range(3):
        up = jnp.broadcast_to((send_ids[c] + 1).astype(F32), (8, 64)).astype(BF)
        total = jnp.where(spot == c, mm(up, pick)[0:1, :], total)
    srow[...] = jnp.broadcast_to(total.astype(jnp.int32) - 1, srow.shape)


def spread_kernel(place, nbt, grad, weight, own, m1, m2, loc, acc):
    rows = iota((EXT, C), 0)
    table = nbt[...].astype(jnp.int32)
    gradient = grad[...]
    none = jnp.zeros((C - S, C), BF)
    masks, terms = [], []
    for k in range(K):
        masks.append(onehot(rows == table[k : k + 1, :]))
        terms += [mm(gradient, weight[:, k * C : (k + 1) * C]).astype(BF), none]
    acc[...] = mm(jnp.concatenate(masks, axis=1), jnp.concatenate(terms, axis=0))
    even = place[0] % 2 == 0
    own[...] = acc[0:S, :]
    first, last = jnp.where(even, S, S + 160), jnp.where(even, S + 160, S)
    m1[...] = acc[pl.ds(pl.multiple_of(first, 32), 96), :].astype(BF)
    m2[...] = acc[pl.ds(pl.multiple_of(last, 32), 96), :].astype(BF)
    loc[...] = acc[S + 96 : S + 160, :].astype(BF)


def inner(position, count):
    return (position > 0) & (position < count - 1)


def masked(keep, rows):
    return jnp.where(keep, rows, jnp.zeros_like(rows))


def pass_kernel(place, loc, m2, m1, late, n2, n1):
    even = place[1] % 2 == 0
    first = jnp.where(even, 0, 1)
    far = inner(place[0], 64)
    for out, side in ((n1, first), (n2, 1 - first)):
        out[0:32, :] = loc[pl.ds(pl.multiple_of(side * 32, 32), 32), :]
        out[32:64, :] = m1[pl.ds(pl.multiple_of(side * 64, 32), 32), :]
        out[64:96, :] = masked(far, m2[pl.ds(pl.multiple_of(side * 64, 32), 32), :])


def settled(place, own, m1, m2, n1, n2, hrow, back):
    da = jnp.where(place[0] % 2 == 0, 1, -1)
    db = jnp.where(place[1] % 2 == 0, 1, -1)
    back[direction(da, 0)] = m1[32:64, :]
    back[direction(-da, 0)] = masked(inner(place[0], 64), m2[32:64, :])
    beside = inner(place[1], 4)
    for ref, side, keep in ((n1, db, True), (n2, -db, beside)):
        rows = ref[...] if keep is True else masked(keep, ref[...])
        back[direction(0, side)] = rows[0:32, :]
        back[direction(da, side)] = rows[32:64, :]
        back[direction(-da, side)] = rows[64:96, :]
    rows = back[...].reshape(8 * HB, C)
    return own[...] + mm(halo_matrix(hrow[0:1, :]), rows)


def gate_kernel(place, own, m2, m1, n2, n1, hrow, pre, grad, late, out, ordered, back):
    hidden_grad = settled(place, own, m1, m2, n1, n2, hrow, back)
    z = pre[...].astype(F32)
    g = 1.0 / (1.0 + jnp.exp(-z))
    value = (hidden_grad * g * (1.0 + z * (1.0 - g))).astype(BF)
    out[...] = value
    order = channel_order()
    ordered[:, 0:C] = mm(grad[...], order).astype(BF)
    ordered[:, C : 2 * C] = mm(value, order).astype(BF)


def rows_kernel(place, own, m2, m1, n2, n1, hrow, grad, srow, late, keep, send, back):
    total = settled(place, own, m1, m2, n1, n2, hrow, back)
    value = (grad[...].astype(F32) + total).astype(BF)
    chosen = mm_t(onehot(iota((S, C), 0) == srow[0:1, :]), value).astype(BF)
    keep[...] = chosen[0:128, :]
    send[...] = chosen[128:256, :]


def pick_kernel(place, p0, p2, p1, p3, late, o2, o1, loc, picked):
    column = place[1]
    for turn, pay in enumerate((p0, p1, p2, p3)):
        halo_row = pay[S + 16 : S + 32, 0:C].astype(F32)[15:16, :].astype(jnp.int32) - 1
        rows = mm_t(halo_matrix(halo_row), pay[0:S, 0 : 2 * C])
        picked[column ^ turn] = rows.astype(BF)
    even = place[0] % 2 == 0
    up = pl.multiple_of(jnp.where(even, 160, 0), 32)
    down = pl.multiple_of(jnp.where(even, 0, 160), 32)
    none = jnp.zeros((HB, 2 * C), BF)
    for tile in range(4):
        for b in (-1, 0, 1):
            source = tile - b
            at = HB * (b + 1)
            for out, side in ((o1, up), (o2, down)):
                rows = picked[source, pl.ds(side + at, HB), :] if 0 <= source < 4 else none
                to = 96 * tile + at
                out[to : to + HB, :] = rows[:, 0:C]
                out[to + 384 : to + 384 + HB, :] = rows[:, C : 2 * C]
            if b:
                to = 0 if b < 0 else HB
                rows = picked[source, 96 + to : 96 + to + HB, :] if 0 <= source < 4 else none
                loc[tile, to : to + HB, :] = rows


def columns_kernel(
    place, p0, p2, p1, p3, r2, r1, loc, late, cols_one, cols_two, ext, ids, sel
):
    column = place[1]
    start = column * QW
    first_k = start // C
    offset = start % C
    even = place[0] % 2 == 0
    far = inner(place[0], 64)
    shift = onehot(iota((C, C), 0) == (iota((C, C), 1) + offset) % C)
    lane = iota((S, 2 * C), 1) % C
    early = lane < C - offset
    for turn, pay in enumerate((p0, p1, p2, p3)):
        tile = column ^ turn
        for half in range(2):
            lanes = slice(half * C, (half + 1) * C)
            at = pl.multiple_of(384 * half + 96 * tile, 32)
            above, below = r1[pl.ds(at, 96), :], masked(far, r2[pl.ds(at, 96), :])
            for to, piece in (
                (0, pay[0:S, lanes]),
                (S, jnp.where(even, above, below)),
                (S + 96, loc[tile, :, lanes]),
                (S + 160, jnp.where(even, below, above)),
            ):
                ext[to : to + piece.shape[0], lanes] = mm(piece, shift).astype(BF)
        high = pay[S : S + 32, 0:C].astype(F32)
        low = pay[S : S + 32, C : 2 * C].astype(F32)
        ids[0:32, :] = 16.0 * high + low - 1.0
        for part in range(8):
            sel[part : part + 1, :] = ids[pl.ds(first_k + part, 1), :]
        table = jnp.transpose(sel[...])[:, 0:8].astype(jnp.int32)
        extended = ext[...]
        previous = None
        for part in range(8):
            match = onehot(iota((S, EXT), 1) == table[0:S, part : part + 1])
            block = mm(match, extended).astype(BF)
            if part:
                merged = jnp.where(early, previous, block)
                at = (part - 1) * C
                cols_one[turn * S : (turn + 1) * S, at : at + C] = merged[:, 0:C]
                cols_two[turn * S : (turn + 1) * S, at : at + C] = merged[:, C : 2 * C]
            previous = block


def weight_kernel(lanes, place, g0, g2, g1, g3, cols, late, keep, send, gt):
    for turn, grad in enumerate((g0, g1, g2, g3)):
        gt[:, turn * S : (turn + 1) * S] = jnp.transpose(grad[:, lanes].astype(F32)).astype(BF)
    mine = pl.multiple_of((place[0] % 2) * 128, 128)
    other = pl.multiple_of(128 - mine, 128)
    for out, at in ((keep, mine), (send, other)):
        left = gt[pl.ds(at, 128), :]
        for part in range(7):
            lanes = slice(part * C, (part + 1) * C)
            out[:, lanes] = mm(left, cols[:, lanes]).astype(out.dtype)


def merge_kernel(place, k1, s1, k2, s2, rk, rs, *outs):
    first = place[0] % 2 == 0
    line = place[0] // 16
    for turn, out in enumerate(outs):
        rows = pl.ds(pl.multiple_of(32 * (line ^ turn), 32), 32)
        for at, (keep, come) in ((0, (k1, s1)), (32, (k2, s2))):
            total = keep[rows, :].astype(F32) + come[rows, :].astype(F32)
            out[at : at + 32, 0 : 7 * C] = total.astype(BF)
        mine, other = rk[rows, :], rs[rows, :]
        out[0:32, 7 * C : 8 * C] = jnp.where(first, mine, other)
        out[32:64, 7 * C : 8 * C] = jnp.where(first, other, mine)


def line_kernel(place, a0, a2, a1, a3, out):
    line = place[0] // 16
    to, at = iota((64, 64), 0), iota((64, 64), 1)
    order = onehot(at == 32 * ((to % 8) // 4) + 4 * (to // 8) + to % 4)
    parts = (a0, a1, a2, a3)
    for n in range(7):
        lanes = slice(n * C, (n + 1) * C)
        total = a0[:, lanes].astype(F32)
        for part in parts[1:]:
            total = total + part[:, lanes].astype(F32)
        out[:, lanes] = mm(order, total.astype(BF)).astype(BF)
    for turn, part in enumerate(parts):
        to = pl.multiple_of(7 * C + (line ^ turn) * C, C)
        out[:, pl.ds(to, C)] = mm(order, part[:, 7 * C : 8 * C]).astype(BF)


def final_kernel(scale, arrived, rows, one, two):
    total = jnp.sum(arrived[:, :, 0 : 7 * C].astype(F32), axis=0) * scale
    one[...] = total[0:4, 0:QW]
    two[...] = total[4:8, 0:QW]
    to, at = iota((48, 64), 0), iota((48, 64), 1)
    spot = onehot((at // 8 == to // 6) & (at % 8 == 4 * ((to % 6) // 3) + to % 3))
    for line in range(4):
        piece = arrived[:, :, (7 + line) * C : (8 + line) * C].reshape(64, C)
        rows[48 * line : 48 * line + 48, :] = mm(spot, piece).astype(BF)


def sds(shape, dtype):
    return jax.ShapeDtypeStruct(shape, dtype)


SMEM = pl.BlockSpec(memory_space=pltpu.SMEM)
VM = pl.BlockSpec(memory_space=pltpu.VMEM)
HBM = pl.BlockSpec(memory_space=pltpu.HBM)
ANY = pl.BlockSpec(memory_space=pl.ANY)


def call(kernel, outs, *args, scratch=(), specs=None, late=0, flops=10**5):
    if specs is None:
        specs = [SMEM] + [VM] * (len(args) - 1 - late) + [ANY] * late
    return pl.pallas_call(
        kernel,
        out_shape=outs,
        in_specs=specs,
        out_specs=jax.tree.map(lambda _: VM, outs),
        scratch_shapes=list(scratch),
        compiler_params=pltpu.CompilerParams(vmem_limit_bytes=40 * 2**20),
        cost_estimate=pl.CostEstimate(flops=flops, bytes_accessed=10**4, transcendentals=0),
    )(*args)


def spread(place, nbt, grad, weight, flops):
    edge = sds((96, C), BF)
    return call(
        spread_kernel,
        (sds((S, C), F32), edge, edge, sds((64, C), BF)),
        place,
        nbt,
        grad,
        weight,
        scratch=[pltpu.VMEM((EXT, C), F32)],
        flops=flops,
    )


def swap(value, axis, turn):
    gx, gy = lax.axis_size("gx"), lax.axis_size("gy")
    pairs = []
    for i in range(gx):
        for j in range(gy):
            n, size = (i, gx) if axis == "gx" else (j, gy)
            q = n ^ 1 if turn == 1 else ((n + 1) ^ 1) - 1
            if axis == "gx":
                to = (q, j) if 0 <= q < size else (i, j ^ 1)
            else:
                to = (i, q) if 0 <= q < size else (i ^ 1, j)
            pairs.append((i * gy + j, to[0] * gy + to[1]))
    return lax.ppermute(value, ("gx", "gy"), pairs)


def cross(value, axis, mask):
    return lax.ppermute(value, axis, [(n, n ^ mask) for n in range(lax.axis_size(axis))])


def gathered(value, axis, base=1):
    return [value] + [cross(value, axis, base * d) for d in (2, 1, 3)]


def halo_lines(m2, m1):
    return swap(m2, "gx", 2), swap(m1, "gx", 1)


def halo_columns(place, loc, m2, m1, late):
    edge = sds((96, C), BF)
    n2, n1 = call(pass_kernel, (edge, edge), place, loc, m2, m1, late, late=1)
    return n1, swap(n2, "gy", 2), swap(n1, "gy", 1)


def body(features, pre_act, grad_out, weight_one, weight_two, neighbours, halo_list, send_list):
    gx = lax.axis_size("gx")
    scale = 1.0 / math.sqrt(S * gx * lax.axis_size("gy"))
    place = jnp.stack([lax.axis_index("gx"), lax.axis_index("gy")]).astype(jnp.int32)
    tile = sds((S, C), BF)
    pay, nbt, hrow, srow, pre, grad = call(
        pack_kernel,
        (
            sds((S + 32, 2 * C), BF),
            sds((32, C), F32),
            sds((8, C), jnp.int32),
            sds((8, C), jnp.int32),
            tile,
            tile,
        ),
        place,
        *[
            pltpu.with_memory_space_constraint(value, pltpu.HBM)
            for value in (
                features,
                pre_act,
                grad_out,
                neighbours.T,
                halo_list,
                jnp.transpose(send_list, (2, 0, 1)),
            )
        ],
        specs=[SMEM] + [HBM] * 6,
        flops=4 * 10**9,
        scratch=[
            pltpu.VMEM((K, S), jnp.int32),
            pltpu.VMEM((1, 8, 24), jnp.int32),
            pltpu.VMEM((3, 1, 64), jnp.int32),
            pltpu.SemaphoreType.DMA((6,)),
        ],
    )
    pays = gathered(pay, "gy")
    back = pltpu.VMEM((8, HB, C), BF)
    own, m1, m2, loc = spread(place, nbt, grad, weight_two, 10**5)
    m2, m1 = halo_lines(m2, m1)
    passed, n2, n1 = halo_columns(place, loc, m2, m1, own)
    picks = sds((768, C), BF)
    o2, o1, near = call(
        pick_kernel,
        (picks, picks, sds((4, 64, 2 * C), BF)),
        place,
        *pays,
        passed,
        scratch=[pltpu.VMEM((4, 8 * HB, 2 * C), BF)],
        late=1,
    )
    r2, r1 = halo_lines(o2, o1)
    grad_pre, ordered = call(
        gate_kernel,
        (tile, sds((S, 2 * C), BF)),
        place,
        own,
        m2,
        m1,
        n2,
        n1,
        hrow,
        pre,
        grad,
        near,
        scratch=[back],
        late=1,
    )
    grads = gathered(ordered, "gy")
    own, m1, m2, loc = spread(place, nbt, grad_pre, weight_one, 4 * 10**9)
    m2, m1 = halo_lines(m2, m1)
    wide = 7 * C
    stack = sds((4 * S, wide), BF)
    cols_one, cols_two = call(
        columns_kernel,
        (stack, stack),
        place,
        *pays,
        r2,
        r1,
        near,
        own,
        scratch=[
            pltpu.VMEM((EXT, 2 * C), BF),
            pltpu.VMEM((32, C), F32),
            pltpu.VMEM((128, C), F32),
        ],
        late=1,
        flops=4 * 10**9,
    )
    passed, n2, n1 = halo_columns(place, loc, m2, m1, cols_two)

    def halves(which, cols, kind, late, flops):
        lanes = slice(which * C, (which + 1) * C)
        half = sds((128, wide), kind)
        return call(
            functools.partial(weight_kernel, lanes),
            (half, half),
            place,
            *grads,
            cols,
            late,
            scratch=[pltpu.VMEM((C, 4 * S), BF)],
            late=1,
            flops=flops,
        )

    keep_two, send_two = halves(0, cols_two, F32, passed, 4 * 10**9)
    come_two = cross(send_two, "gx", 1)
    keep_one, send_one = halves(1, cols_one, BF, keep_two, 10**5)
    some = sds((128, C), BF)
    rows_keep, rows_send = call(
        rows_kernel,
        (some, some),
        place,
        own,
        m2,
        m1,
        n2,
        n1,
        hrow,
        grad,
        srow,
        keep_one,
        scratch=[back],
        late=1,
        flops=2 * 10**10,
    )
    rows_come = cross(rows_send, "gx", 1)
    come_one = cross(send_one, "gx", 1)
    chunk = sds((64, 8 * C), BF)
    chunks = call(
        merge_kernel,
        (chunk,) * 4,
        place,
        keep_one,
        come_one,
        keep_two,
        come_two,
        rows_keep,
        rows_come,
    )
    chunks = [chunks[0]] + [cross(chunks[d], "gx", 16 * d) for d in (2, 1, 3)]
    summed = call(line_kernel, sds((64, 11 * C), BF), place, *chunks)
    groups = [[16 * y + 2 * z + e for z in range(8)] for y in range(4) for e in range(2)]
    collected = lax.all_to_all(
        summed.reshape(8, 8, 11 * C),
        "gx",
        split_axis=0,
        concat_axis=0,
        tiled=True,
        axis_index_groups=groups,
    )
    out = sds((4, QW), F32)
    return call(
        lambda *refs: final_kernel(scale, *refs), (tile, out, out), collected, specs=[VM]
    )


def solution(mesh):
    in_specs = (
        P(("gx", "gy"), None),
        P(("gx", "gy"), None),
        P(("gx", "gy"), None),
        P(),
        P(),
        P(("gx", "gy"), None),
        P(("gx", "gy"), None, None),
        P(("gx", "gy"), None, None),
    )
    out_specs = (P(("gx", "gy"), None), P("gx", "gy"), P("gx", "gy"))
    return jax.shard_map(body, mesh=mesh, in_specs=in_specs, out_specs=out_specs, check_vma=False)
```

```python
import functools
import math

import jax
import jax.numpy as jnp
from jax import lax
from jax.experimental import pallas as pl
from jax.experimental.pallas import tpu as pltpu
from jax.sharding import PartitionSpec as P

C = 256
K = 27
S = 192
HB = 32
EXT = S + 8 * HB
QW = 1728
BF = jnp.bfloat16
F32 = jnp.float32


def iota(shape, dim):
    return lax.broadcasted_iota(jnp.int32, shape, dim)


def onehot(mask):
    return jnp.where(mask, 1.0, 0.0).astype(BF)


def mm(a, b):
    return lax.dot_general(a, b, (((1,), (0,)), ((), ())), preferred_element_type=F32)


def mm_t(a, b):
    return lax.dot_general(a, b, (((0,), (0,)), ((), ())), preferred_element_type=F32)


def direction(a, b):
    grid = 3 * (a + 1) + (b + 1)
    return grid - jnp.where(grid > 4, 1, 0)


def channel_order():
    out = iota((C, C), 1)
    parity, rest = out // 128, out % 128
    source = 8 * (rest // 4) + 4 * parity + rest % 4
    return onehot(iota((C, C), 0) == source)


def halo_matrix(halo_row):
    return onehot(iota((S, 8 * HB), 0) == halo_row)


def pack_kernel(
    place, feat, pre, grad, nbr, halo, send, pay, nbt, hrow, srow, pre_out, grad_out,
    ids, halo_ids, send_ids, sems
):
    copies = [
        pltpu.make_async_copy(source, target, sems.at[n])
        for n, (source, target) in enumerate(
            (
                (nbr, ids),
                (halo, halo_ids),
                (send, send_ids),
                (feat, pay.at[0:S, 0:C]),
                (grad, grad_out),
                (pre, pre_out),
            )
        )
    ]
    for copy in copies:
        copy.start()
    for copy in copies:
        copy.wait()
    table = ids[...].astype(F32)
    heading = jnp.floor((table - S + 0.5) * (1.0 / 24.0))
    table = jnp.where(table >= S, table + 8.0 * heading, table)
    nbt[...] = jnp.full(nbt.shape, -1.0, F32)
    nbt[0:K, 0:S] = table
    shifted_up = table + 1.0
    high = jnp.floor(shifted_up * (1.0 / 16.0))
    pay[S : S + 32, :] = jnp.zeros((32, 2 * C), BF)
    pay[S : S + K, 0:S] = high.astype(BF)
    pay[S : S + K, C : C + S] = (shifted_up - 16.0 * high).astype(BF)
    z = pre_out[...].astype(F32)
    pay[0:S, C : 2 * C] = (z * (1.0 / (1.0 + jnp.exp(-z)))).astype(BF)
    halo_up = (halo_ids[0] + 1).astype(F32).astype(BF)
    spread = mm(halo_up, onehot(iota((24, 8 * HB), 1) % HB == iota((24, 8 * HB), 0)))
    row = jnp.sum(
        jnp.where(iota((8, 8 * HB), 1) // HB == iota((8, 8 * HB), 0), spread, 0.0),
        axis=0,
        keepdims=True,
    )
    hrow[...] = jnp.broadcast_to(row.astype(jnp.int32) - 1, hrow.shape)
    tail = pay[S + 16 : S + 32, 0:C].astype(F32)
    pay[S + 16 : S + 32, 0:C] = jnp.where(iota((16, C), 0) == 15, row, tail).astype(BF)
    lane, peer = iota((64, C), 1), iota((64, C), 0)
    parity = jnp.where(lane < 128, place[0] % 2, 1 - place[0] % 2)
    pick = onehot(peer == 2 * ((lane % 128) // 4) + parity)
    spot = iota((1, C), 1) % 4
    total = jnp.zeros((1, C), F32)
    for c in range(3):
        up = jnp.broadcast_to((send_ids[c] + 1).astype(F32), (8, 64)).astype(BF)
        total = jnp.where(spot == c, mm(up, pick)[0:1, :], total)
    srow[...] = jnp.broadcast_to(total.astype(jnp.int32) - 1, srow.shape)


def spread_kernel(place, nbt, grad, weight, own, m1, m2, loc, acc):
    rows = iota((EXT, C), 0)
    table = nbt[...].astype(jnp.int32)
    gradient = grad[...]
    none = jnp.zeros((C - S, C), BF)
    masks, terms = [], []
    for k in range(K):
        masks.append(onehot(rows == table[k : k + 1, :]))
        terms += [mm(gradient, weight[:, k * C : (k + 1) * C]).astype(BF), none]
    acc[...] = mm(jnp.concatenate(masks, axis=1), jnp.concatenate(terms, axis=0))
    even = place[0] % 2 == 0
    own[...] = acc[0:S, :]
    first, last = jnp.where(even, S, S + 160), jnp.where(even, S + 160, S)
    m1[...] = acc[pl.ds(pl.multiple_of(first, 32), 96), :].astype(BF)
    m2[...] = acc[pl.ds(pl.multiple_of(last, 32), 96), :].astype(BF)
    loc[...] = acc[S + 96 : S + 160, :].astype(BF)


def inner(position, count):
    return (position > 0) & (position < count - 1)


def masked(keep, rows):
    return jnp.where(keep, rows, jnp.zeros_like(rows))


def pass_kernel(place, loc, m2, m1, late, n2, n1):
    even = place[1] % 2 == 0
    first = jnp.where(even, 0, 1)
    far = inner(place[0], 64)
    for out, side in ((n1, first), (n2, 1 - first)):
        out[0:32, :] = loc[pl.ds(pl.multiple_of(side * 32, 32), 32), :]
        out[32:64, :] = m1[pl.ds(pl.multiple_of(side * 64, 32), 32), :]
        out[64:96, :] = masked(far, m2[pl.ds(pl.multiple_of(side * 64, 32), 32), :])


def settled(place, own, m1, m2, n1, n2, hrow, back):
    da = jnp.where(place[0] % 2 == 0, 1, -1)
    db = jnp.where(place[1] % 2 == 0, 1, -1)
    back[direction(da, 0)] = m1[32:64, :]
    back[direction(-da, 0)] = masked(inner(place[0], 64), m2[32:64, :])
    beside = inner(place[1], 4)
    for ref, side, keep in ((n1, db, True), (n2, -db, beside)):
        rows = ref[...] if keep is True else masked(keep, ref[...])
        back[direction(0, side)] = rows[0:32, :]
        back[direction(da, side)] = rows[32:64, :]
        back[direction(-da, side)] = rows[64:96, :]
    rows = back[...].reshape(8 * HB, C)
    return own[...] + mm(halo_matrix(hrow[0:1, :]), rows)


def gate_kernel(place, own, m2, m1, n2, n1, hrow, pre, grad, late, out, ordered, back):
    hidden_grad = settled(place, own, m1, m2, n1, n2, hrow, back)
    z = pre[...].astype(F32)
    g = 1.0 / (1.0 + jnp.exp(-z))
    value = (hidden_grad * g * (1.0 + z * (1.0 - g))).astype(BF)
    out[...] = value
    order = channel_order()
    ordered[:, 0:C] = mm(grad[...], order).astype(BF)
    ordered[:, C : 2 * C] = mm(value, order).astype(BF)


def rows_kernel(place, own, m2, m1, n2, n1, hrow, grad, srow, late, keep, send, back):
    total = settled(place, own, m1, m2, n1, n2, hrow, back)
    value = (grad[...].astype(F32) + total).astype(BF)
    chosen = mm_t(onehot(iota((S, C), 0) == srow[0:1, :]), value).astype(BF)
    keep[...] = chosen[0:128, :]
    send[...] = chosen[128:256, :]


def pick_kernel(place, p0, p2, p1, p3, late, o2, o1, loc, picked):
    column = place[1]
    for turn, pay in enumerate((p0, p1, p2, p3)):
        halo_row = pay[S + 16 : S + 32, 0:C].astype(F32)[15:16, :].astype(jnp.int32) - 1
        rows = mm_t(halo_matrix(halo_row), pay[0:S, 0 : 2 * C])
        picked[column ^ turn] = rows.astype(BF)
    even = place[0] % 2 == 0
    up = pl.multiple_of(jnp.where(even, 160, 0), 32)
    down = pl.multiple_of(jnp.where(even, 0, 160), 32)
    none = jnp.zeros((HB, 2 * C), BF)
    for tile in range(4):
        for b in (-1, 0, 1):
            source = tile - b
            at = HB * (b + 1)
            for out, side in ((o1, up), (o2, down)):
                rows = picked[source, pl.ds(side + at, HB), :] if 0 <= source < 4 else none
                to = 96 * tile + at
                out[to : to + HB, :] = rows[:, 0:C]
                out[to + 384 : to + 384 + HB, :] = rows[:, C : 2 * C]
            if b:
                to = 0 if b < 0 else HB
                rows = picked[source, 96 + to : 96 + to + HB, :] if 0 <= source < 4 else none
                loc[tile, to : to + HB, :] = rows


def columns_kernel(
    place, p0, p2, p1, p3, r2, r1, loc, late, cols_one, cols_two, ext, ids, sel
):
    column = place[1]
    start = column * QW
    first_k = start // C
    offset = start % C
    even = place[0] % 2 == 0
    far = inner(place[0], 64)
    shift = onehot(iota((C, C), 0) == (iota((C, C), 1) + offset) % C)
    lane = iota((S, 2 * C), 1) % C
    early = lane < C - offset
    for turn, pay in enumerate((p0, p1, p2, p3)):
        tile = column ^ turn
        for half in range(2):
            lanes = slice(half * C, (half + 1) * C)
            at = pl.multiple_of(384 * half + 96 * tile, 32)
            above, below = r1[pl.ds(at, 96), :], masked(far, r2[pl.ds(at, 96), :])
            for to, piece in (
                (0, pay[0:S, lanes]),
                (S, jnp.where(even, above, below)),
                (S + 96, loc[tile, :, lanes]),
                (S + 160, jnp.where(even, below, above)),
            ):
                ext[to : to + piece.shape[0], lanes] = mm(piece, shift).astype(BF)
        high = pay[S : S + 32, 0:C].astype(F32)
        low = pay[S : S + 32, C : 2 * C].astype(F32)
        ids[0:32, :] = 16.0 * high + low - 1.0
        for part in range(8):
            sel[part : part + 1, :] = ids[pl.ds(first_k + part, 1), :]
        table = jnp.transpose(sel[...])[:, 0:8].astype(jnp.int32)
        extended = ext[...]
        match = [
            onehot(iota((S, EXT), 1) == table[0:S, part : part + 1]) for part in range(8)
        ]
        found = mm(jnp.concatenate(match, axis=0), extended).astype(BF)
        for part in range(7):
            merged = jnp.where(
                early, found[part * S : (part + 1) * S], found[(part + 1) * S : (part + 2) * S]
            )
            lanes = slice(part * C, (part + 1) * C)
            cols_one[turn * S : (turn + 1) * S, lanes] = merged[:, 0:C]
            cols_two[turn * S : (turn + 1) * S, lanes] = merged[:, C : 2 * C]


def weight_kernel(lanes, place, g0, g2, g1, g3, cols, t2, t1, keep, send, gt):
    for turn, grad in enumerate((g0, g1, g2, g3)):
        gt[:, turn * S : (turn + 1) * S] = jnp.transpose(grad[:, lanes].astype(F32)).astype(BF)
    mine = pl.multiple_of((place[0] % 2) * 128, 128)
    other = pl.multiple_of(128 - mine, 128)
    left = jnp.concatenate([gt[pl.ds(mine, 128), :], gt[pl.ds(other, 128), :]], axis=0)
    for part in range(7):
        lanes = slice(part * C, (part + 1) * C)
        block = mm(left, cols[:, lanes])
        keep[:, lanes] = block[0:128].astype(keep.dtype)
        send[:, lanes] = block[128:256].astype(send.dtype)


def merge_kernel(place, k1, s1, k2, s2, *outs):
    line = place[0] // 16
    for turn, out in enumerate(outs):
        rows = pl.ds(pl.multiple_of(32 * (line ^ turn), 32), 32)
        for at, (keep, come) in ((0, (k1, s1)), (32, (k2, s2))):
            total = keep[rows, :].astype(F32) + come[rows, :].astype(F32)
            out[at : at + 32, :] = total.astype(BF)


def sort_kernel(place, rk, rs, *outs):
    first = place[0] % 2 == 0
    line = place[0] // 16
    for turn, out in enumerate(outs):
        rows = pl.ds(pl.multiple_of(32 * (line ^ turn), 32), 32)
        mine, other = rk[rows, :], rs[rows, :]
        out[0:32, :] = jnp.where(first, mine, other)
        out[32:64, :] = jnp.where(first, other, mine)


def line_kernel(place, a0, a2, a1, a3, b0, b2, b1, b3, out):
    line = place[0] // 16
    to, at = iota((64, 64), 0), iota((64, 64), 1)
    order = onehot(at == 32 * ((to % 8) // 4) + 4 * (to // 8) + to % 4)
    for n in range(7):
        lanes = slice(n * C, (n + 1) * C)
        total = a0[:, lanes].astype(F32)
        for part in (a1, a2, a3):
            total = total + part[:, lanes].astype(F32)
        out[:, lanes] = mm(order, total.astype(BF)).astype(BF)
    for n in range(3):
        index = 8 * n + to % 8
        total = jnp.zeros((64, C), F32)
        for turn, part in enumerate((b0, b1, b2, b3)):
            row = 32 * ((index % 6) // 3) + 4 * (to // 8) + index % 3
            total = total + mm(onehot((index // 6 == (line ^ turn)) & (at == row)), part[...])
        out[:, (7 + n) * C : (8 + n) * C] = total.astype(BF)


def final_kernel(scale, arrived, rows, one, two):
    total = jnp.sum(arrived[:, :, 0 : 7 * C].astype(F32), axis=0) * scale
    one[...] = total[0:4, 0:QW]
    two[...] = total[4:8, 0:QW]
    to, at = iota((S, 64), 0), iota((S, 64), 1)
    value = jnp.zeros((S, C), F32)
    for n in range(3):
        spot = (at // 8 == (to // 6) % 8) & (8 * n + at % 8 == 6 * (to // 48) + to % 6)
        piece = arrived[:, :, (7 + n) * C : (8 + n) * C].reshape(64, C)
        value = value + mm(onehot(spot), piece)
    rows[...] = value.astype(BF)


def sds(shape, dtype):
    return jax.ShapeDtypeStruct(shape, dtype)


SMEM = pl.BlockSpec(memory_space=pltpu.SMEM)
VM = pl.BlockSpec(memory_space=pltpu.VMEM)
HBM = pl.BlockSpec(memory_space=pltpu.HBM)
ANY = pl.BlockSpec(memory_space=pl.ANY)


def call(kernel, outs, *args, scratch=(), specs=None, late=0, flops=10**5):
    if specs is None:
        specs = [SMEM] + [VM] * (len(args) - 1 - late) + [ANY] * late
    return pl.pallas_call(
        kernel,
        out_shape=outs,
        in_specs=specs,
        out_specs=jax.tree.map(lambda _: VM, outs),
        scratch_shapes=list(scratch),
        compiler_params=pltpu.CompilerParams(vmem_limit_bytes=40 * 2**20),
        cost_estimate=pl.CostEstimate(flops=flops, bytes_accessed=10**4, transcendentals=0),
    )(*args)


def spread(place, nbt, grad, weight, flops):
    edge = sds((96, C), BF)
    return call(
        spread_kernel,
        (sds((S, C), F32), edge, edge, sds((64, C), BF)),
        place,
        nbt,
        grad,
        weight,
        scratch=[pltpu.VMEM((EXT, C), F32)],
        flops=flops,
    )


def swap(value, axis, turn):
    gx, gy = lax.axis_size("gx"), lax.axis_size("gy")
    pairs = []
    for i in range(gx):
        for j in range(gy):
            n, size = (i, gx) if axis == "gx" else (j, gy)
            q = n ^ 1 if turn == 1 else ((n + 1) ^ 1) - 1
            if axis == "gx":
                to = (q, j) if 0 <= q < size else (i, j ^ 1)
            else:
                to = (i, q) if 0 <= q < size else (i ^ 1, j)
            pairs.append((i * gy + j, to[0] * gy + to[1]))
    return lax.ppermute(value, ("gx", "gy"), pairs)


def cross(value, axis, mask):
    return lax.ppermute(value, axis, [(n, n ^ mask) for n in range(lax.axis_size(axis))])


def gathered(value, axis, base=1):
    return [value] + [cross(value, axis, base * d) for d in (2, 1, 3)]


def halo_lines(m2, m1):
    return swap(m2, "gx", 2), swap(m1, "gx", 1)


def halo_columns(place, loc, m2, m1, late, flops=10**5):
    edge = sds((96, C), BF)
    n2, n1 = call(pass_kernel, (edge, edge), place, loc, m2, m1, late, late=1, flops=flops)
    return n1, swap(n2, "gy", 2), swap(n1, "gy", 1)


def body(features, pre_act, grad_out, weight_one, weight_two, neighbours, halo_list, send_list):
    gx = lax.axis_size("gx")
    scale = 1.0 / math.sqrt(S * gx * lax.axis_size("gy"))
    place = jnp.stack([lax.axis_index("gx"), lax.axis_index("gy")]).astype(jnp.int32)
    tile = sds((S, C), BF)
    pay, nbt, hrow, srow, pre, grad = call(
        pack_kernel,
        (
            sds((S + 32, 2 * C), BF),
            sds((32, C), F32),
            sds((8, C), jnp.int32),
            sds((8, C), jnp.int32),
            tile,
            tile,
        ),
        place,
        *[
            pltpu.with_memory_space_constraint(value, pltpu.HBM)
            for value in (
                features,
                pre_act,
                grad_out,
                neighbours.T,
                halo_list,
                jnp.transpose(send_list, (2, 0, 1)),
            )
        ],
        specs=[SMEM] + [HBM] * 6,
        flops=4 * 10**9,
        scratch=[
            pltpu.VMEM((K, S), jnp.int32),
            pltpu.VMEM((1, 8, 24), jnp.int32),
            pltpu.VMEM((3, 1, 64), jnp.int32),
            pltpu.SemaphoreType.DMA((6,)),
        ],
    )
    pays = gathered(pay, "gy")
    back = pltpu.VMEM((8, HB, C), BF)
    own, m1, m2, loc = spread(place, nbt, grad, weight_two, 10**5)
    m2, m1 = halo_lines(m2, m1)
    passed, n2, n1 = halo_columns(place, loc, m2, m1, own)
    picks = sds((768, C), BF)
    o2, o1, near = call(
        pick_kernel,
        (picks, picks, sds((4, 64, 2 * C), BF)),
        place,
        *pays,
        passed,
        scratch=[pltpu.VMEM((4, 8 * HB, 2 * C), BF)],
        late=1,
    )
    r2, r1 = halo_lines(o2, o1)
    grad_pre, ordered = call(
        gate_kernel,
        (tile, sds((S, 2 * C), BF)),
        place,
        own,
        m2,
        m1,
        n2,
        n1,
        hrow,
        pre,
        grad,
        near,
        scratch=[back],
        late=1,
    )
    grads = gathered(ordered, "gy")
    own, m1, m2, loc = spread(place, nbt, grad_pre, weight_one, 4 * 10**9)
    m2, m1 = halo_lines(m2, m1)
    wide = 7 * C
    stack = sds((4 * S, wide), BF)
    cols_one, cols_two = call(
        columns_kernel,
        (stack, stack),
        place,
        *pays,
        r2,
        r1,
        near,
        own,
        scratch=[
            pltpu.VMEM((EXT, 2 * C), BF),
            pltpu.VMEM((32, C), F32),
            pltpu.VMEM((128, C), F32),
        ],
        late=1,
        flops=4 * 10**9,
    )

    def halves(which, cols, kind, flops, *late):
        lanes = slice(which * C, (which + 1) * C)
        half = sds((128, wide), kind)
        return call(
            functools.partial(weight_kernel, lanes),
            (half, half),
            place,
            *grads,
            cols,
            *late,
            scratch=[pltpu.VMEM((C, 4 * S), BF)],
            late=2,
            flops=flops,
        )

    keep_two, send_two = halves(0, cols_two, F32, 4 * 10**9, m2, m1)
    come_two = cross(send_two, "gx", 1)
    keep_one, send_one = halves(1, cols_one, BF, 10**5, keep_two, keep_two)
    come_one = cross(send_one, "gx", 1)
    chunks = call(
        merge_kernel, (sds((64, wide), BF),) * 4, place, keep_one, come_one, keep_two, come_two
    )
    sums = [chunks[0]] + [cross(chunks[d], "gx", 16 * d) for d in (2, 1, 3)]
    n2, n1 = halo_columns(place, loc, m2, m1, chunks[0], 2 * 10**10)[1:]
    some = sds((128, C), BF)
    rows_keep, rows_send = call(
        rows_kernel,
        (some, some),
        place,
        own,
        m2,
        m1,
        n2,
        n1,
        hrow,
        grad,
        srow,
        n1,
        scratch=[back],
        late=1,
    )
    rows_come = cross(rows_send, "gx", 1)
    sorts = call(sort_kernel, (sds((64, C), BF),) * 4, place, rows_keep, rows_come)
    rows = [sorts[0]] + [cross(sorts[d], "gx", 16 * d) for d in (2, 1, 3)]
    summed = call(line_kernel, sds((64, 10 * C), BF), place, *sums, *rows)
    groups = [[16 * y + 2 * z + e for z in range(8)] for y in range(4) for e in range(2)]
    collected = lax.all_to_all(
        summed.reshape(8, 8, 10 * C),
        "gx",
        split_axis=0,
        concat_axis=0,
        tiled=True,
        axis_index_groups=groups,
    )
    out = sds((4, QW), F32)
    return call(
        lambda *refs: final_kernel(scale, *refs), (tile, out, out), collected, specs=[VM]
    )


def solution(mesh):
    in_specs = (
        P(("gx", "gy"), None),
        P(("gx", "gy"), None),
        P(("gx", "gy"), None),
        P(),
        P(),
        P(("gx", "gy"), None),
        P(("gx", "gy"), None, None),
        P(("gx", "gy"), None, None),
    )
    out_specs = (P(("gx", "gy"), None), P("gx", "gy"), P("gx", "gy"))
    return jax.shard_map(body, mesh=mesh, in_specs=in_specs, out_specs=out_specs, check_vma=False)
```

```python
import functools
import math

import jax
import jax.numpy as jnp
from jax import lax
from jax.experimental import pallas as pl
from jax.experimental.pallas import tpu as pltpu
from jax.sharding import PartitionSpec as P

C = 256
K = 27
S = 192
HB = 32
EXT = S + 8 * HB
QW = 1728
BF = jnp.bfloat16
F32 = jnp.float32


def iota(shape, dim):
    return lax.broadcasted_iota(jnp.int32, shape, dim)


def onehot(mask):
    return jnp.where(mask, 1.0, 0.0).astype(BF)


def mm(a, b):
    return lax.dot_general(a, b, (((1,), (0,)), ((), ())), preferred_element_type=F32)


def mm_t(a, b):
    return lax.dot_general(a, b, (((0,), (0,)), ((), ())), preferred_element_type=F32)


def direction(a, b):
    grid = 3 * (a + 1) + (b + 1)
    return grid - jnp.where(grid > 4, 1, 0)


def channel_order():
    out = iota((C, C), 1)
    parity, rest = out // 128, out % 128
    source = 8 * (rest // 4) + 4 * parity + rest % 4
    return onehot(iota((C, C), 0) == source)


def halo_matrix(halo_row):
    return onehot(iota((S, 8 * HB), 0) == halo_row)


def pack_kernel(
    place, feat, pre, grad, nbr, halo, send, pay, nbt, hrow, srow, pre_out, grad_out,
    ids, halo_ids, send_ids, sems
):
    copies = [
        pltpu.make_async_copy(source, target, sems.at[n])
        for n, (source, target) in enumerate(
            (
                (nbr, ids),
                (halo, halo_ids),
                (send, send_ids),
                (feat, pay.at[0:S, 0:C]),
                (grad, grad_out),
                (pre, pre_out),
            )
        )
    ]
    for copy in copies:
        copy.start()
    for copy in copies:
        copy.wait()
    table = ids[...].astype(F32)
    heading = jnp.floor((table - S + 0.5) * (1.0 / 24.0))
    table = jnp.where(table >= S, table + 8.0 * heading, table)
    nbt[...] = jnp.full(nbt.shape, -1.0, F32)
    nbt[0:K, 0:S] = table
    shifted_up = table + 1.0
    high = jnp.floor(shifted_up * (1.0 / 16.0))
    pay[S : S + 32, :] = jnp.zeros((32, 2 * C), BF)
    pay[S : S + K, 0:S] = high.astype(BF)
    pay[S : S + K, C : C + S] = (shifted_up - 16.0 * high).astype(BF)
    z = pre_out[...].astype(F32)
    pay[0:S, C : 2 * C] = (z * (1.0 / (1.0 + jnp.exp(-z)))).astype(BF)
    halo_up = (halo_ids[0] + 1).astype(F32).astype(BF)
    spread = mm(halo_up, onehot(iota((24, 8 * HB), 1) % HB == iota((24, 8 * HB), 0)))
    row = jnp.sum(
        jnp.where(iota((8, 8 * HB), 1) // HB == iota((8, 8 * HB), 0), spread, 0.0),
        axis=0,
        keepdims=True,
    )
    hrow[...] = jnp.broadcast_to(row.astype(jnp.int32) - 1, hrow.shape)
    tail = pay[S + 16 : S + 32, 0:C].astype(F32)
    pay[S + 16 : S + 32, 0:C] = jnp.where(iota((16, C), 0) == 15, row, tail).astype(BF)
    lane, peer = iota((64, C), 1), iota((64, C), 0)
    parity = jnp.where(lane < 128, place[0] % 2, 1 - place[0] % 2)
    pick = onehot(peer == 2 * ((lane % 128) // 4) + parity)
    spot = iota((1, C), 1) % 4
    total = jnp.zeros((1, C), F32)
    for c in range(3):
        up = jnp.broadcast_to((send_ids[c] + 1).astype(F32), (8, 64)).astype(BF)
        total = jnp.where(spot == c, mm(up, pick)[0:1, :], total)
    srow[...] = jnp.broadcast_to(total.astype(jnp.int32) - 1, srow.shape)


def spread_kernel(place, nbt, grad, weight, own, m1, m2, loc, acc):
    rows = iota((EXT, C), 0)
    table = nbt[...].astype(jnp.int32)
    gradient = grad[...]
    none = jnp.zeros((C - S, C), BF)
    masks, terms = [], []
    for k in range(K):
        masks.append(onehot(rows == table[k : k + 1, :]))
        terms += [mm(gradient, weight[:, k * C : (k + 1) * C]).astype(BF), none]
    acc[...] = mm(jnp.concatenate(masks, axis=1), jnp.concatenate(terms, axis=0))
    even = place[0] % 2 == 0
    own[...] = acc[0:S, :]
    first, last = jnp.where(even, S, S + 160), jnp.where(even, S + 160, S)
    m1[...] = acc[pl.ds(pl.multiple_of(first, 32), 96), :].astype(BF)
    m2[...] = acc[pl.ds(pl.multiple_of(last, 32), 96), :].astype(BF)
    loc[...] = acc[S + 96 : S + 160, :].astype(BF)


def inner(position, count):
    return (position > 0) & (position < count - 1)


def masked(keep, rows):
    return jnp.where(keep, rows, jnp.zeros_like(rows))


def pass_kernel(place, loc, m2, m1, late, n2, n1):
    even = place[1] % 2 == 0
    first = jnp.where(even, 0, 1)
    far = inner(place[0], 64)
    for out, side in ((n1, first), (n2, 1 - first)):
        out[0:32, :] = loc[pl.ds(pl.multiple_of(side * 32, 32), 32), :]
        out[32:64, :] = m1[pl.ds(pl.multiple_of(side * 64, 32), 32), :]
        out[64:96, :] = masked(far, m2[pl.ds(pl.multiple_of(side * 64, 32), 32), :])


def settled(place, own, m1, m2, n1, n2, hrow, back):
    da = jnp.where(place[0] % 2 == 0, 1, -1)
    db = jnp.where(place[1] % 2 == 0, 1, -1)
    back[direction(da, 0)] = m1[32:64, :]
    back[direction(-da, 0)] = masked(inner(place[0], 64), m2[32:64, :])
    beside = inner(place[1], 4)
    for ref, side, keep in ((n1, db, True), (n2, -db, beside)):
        rows = ref[...] if keep is True else masked(keep, ref[...])
        back[direction(0, side)] = rows[0:32, :]
        back[direction(da, side)] = rows[32:64, :]
        back[direction(-da, side)] = rows[64:96, :]
    rows = back[...].reshape(8 * HB, C)
    return own[...] + mm(halo_matrix(hrow[0:1, :]), rows)


def gate_kernel(place, own, m2, m1, n2, n1, hrow, pre, grad, late, out, ordered, back):
    hidden_grad = settled(place, own, m1, m2, n1, n2, hrow, back)
    z = pre[...].astype(F32)
    g = 1.0 / (1.0 + jnp.exp(-z))
    value = (hidden_grad * g * (1.0 + z * (1.0 - g))).astype(BF)
    out[...] = value
    order = channel_order()
    ordered[:, 0:C] = mm(grad[...], order).astype(BF)
    ordered[:, C : 2 * C] = mm(value, order).astype(BF)


def rows_kernel(place, own, m2, m1, n2, n1, hrow, grad, srow, late, keep, send, back):
    total = settled(place, own, m1, m2, n1, n2, hrow, back)
    value = (grad[...].astype(F32) + total).astype(BF)
    chosen = mm_t(onehot(iota((S, C), 0) == srow[0:1, :]), value).astype(BF)
    keep[...] = chosen[0:128, :]
    send[...] = chosen[128:256, :]


def pick_kernel(place, p0, p2, p1, p3, late, o2, o1, loc, picked):
    column = place[1]
    for turn, pay in enumerate((p0, p1, p2, p3)):
        halo_row = pay[S + 16 : S + 32, 0:C].astype(F32)[15:16, :].astype(jnp.int32) - 1
        rows = mm_t(halo_matrix(halo_row), pay[0:S, 0 : 2 * C])
        picked[column ^ turn] = rows.astype(BF)
    even = place[0] % 2 == 0
    up = pl.multiple_of(jnp.where(even, 160, 0), 32)
    down = pl.multiple_of(jnp.where(even, 0, 160), 32)
    none = jnp.zeros((HB, 2 * C), BF)
    for tile in range(4):
        for b in (-1, 0, 1):
            source = tile - b
            at = HB * (b + 1)
            for out, side in ((o1, up), (o2, down)):
                rows = picked[source, pl.ds(side + at, HB), :] if 0 <= source < 4 else none
                to = 96 * tile + at
                out[to : to + HB, :] = rows[:, 0:C]
                out[to + 384 : to + 384 + HB, :] = rows[:, C : 2 * C]
            if b:
                to = 0 if b < 0 else HB
                rows = picked[source, 96 + to : 96 + to + HB, :] if 0 <= source < 4 else none
                loc[tile, to : to + HB, :] = rows


def columns_kernel(
    place, p0, p2, p1, p3, r2, r1, loc, late, cols_one, cols_two, ext, ids, sel
):
    column = place[1]
    start = column * QW
    first_k = start // C
    offset = start % C
    even = place[0] % 2 == 0
    far = inner(place[0], 64)
    shift = onehot(iota((C, C), 0) == (iota((C, C), 1) + offset) % C)
    lane = iota((S, 2 * C), 1) % C
    early = lane < C - offset
    for turn, pay in enumerate((p0, p1, p2, p3)):
        tile = column ^ turn
        for half in range(2):
            lanes = slice(half * C, (half + 1) * C)
            at = pl.multiple_of(384 * half + 96 * tile, 32)
            above, below = r1[pl.ds(at, 96), :], masked(far, r2[pl.ds(at, 96), :])
            for to, piece in (
                (0, pay[0:S, lanes]),
                (S, jnp.where(even, above, below)),
                (S + 96, loc[tile, :, lanes]),
                (S + 160, jnp.where(even, below, above)),
            ):
                ext[to : to + piece.shape[0], lanes] = mm(piece, shift).astype(BF)
        high = pay[S : S + 32, 0:C].astype(F32)
        low = pay[S : S + 32, C : 2 * C].astype(F32)
        ids[0:32, :] = 16.0 * high + low - 1.0
        for part in range(8):
            sel[part : part + 1, :] = ids[pl.ds(first_k + part, 1), :]
        table = jnp.transpose(sel[...])[:, 0:8].astype(jnp.int32)
        extended = ext[...]
        match = [
            onehot(iota((S, EXT), 1) == table[0:S, part : part + 1]) for part in range(8)
        ]
        found = mm(jnp.concatenate(match, axis=0), extended).astype(BF)
        for part in range(7):
            merged = jnp.where(
                early, found[part * S : (part + 1) * S], found[(part + 1) * S : (part + 2) * S]
            )
            lanes = slice(part * C, (part + 1) * C)
            cols_one[turn * S : (turn + 1) * S, lanes] = merged[:, 0:C]
            cols_two[turn * S : (turn + 1) * S, lanes] = merged[:, C : 2 * C]


def weight_kernel(lanes, place, g0, g2, g1, g3, cols, late, keep, send, gt):
    for turn, grad in enumerate((g0, g1, g2, g3)):
        gt[:, turn * S : (turn + 1) * S] = jnp.transpose(grad[:, lanes].astype(F32)).astype(BF)
    mine = pl.multiple_of((place[0] % 2) * 128, 128)
    other = pl.multiple_of(128 - mine, 128)
    left = jnp.concatenate([gt[pl.ds(mine, 128), :], gt[pl.ds(other, 128), :]], axis=0)
    for part in range(7):
        lanes = slice(part * C, (part + 1) * C)
        block = mm(left, cols[:, lanes])
        keep[:, lanes] = block[0:128].astype(keep.dtype)
        send[:, lanes] = block[128:256].astype(send.dtype)


def merge_two_kernel(place, keep, come, late, *outs):
    line = place[0] // 16
    for turn, out in enumerate(outs):
        rows = pl.ds(pl.multiple_of(32 * (line ^ turn), 32), 32)
        out[...] = (keep[rows, :] + come[rows, :]).astype(BF)


def merge_one_kernel(place, keep, come, rk, rs, late, *outs):
    first = place[0] % 2 == 0
    line = place[0] // 16
    for turn, out in enumerate(outs):
        rows = pl.ds(pl.multiple_of(32 * (line ^ turn), 32), 32)
        total = keep[rows, :].astype(F32) + come[rows, :].astype(F32)
        out[:, 0 : 7 * C] = total.astype(BF)
        mine, other = rk[rows, :], rs[rows, :]
        out[:, 7 * C : 8 * C] = jnp.where(first, mine, other)
        out[:, 8 * C : 9 * C] = jnp.where(first, other, mine)


def line_two_kernel(place, a0, a2, a1, a3, out):
    total = a0[...].astype(F32)
    for part in (a1, a2, a3):
        total = total + part[...].astype(F32)
    out[...] = total.astype(BF)


def line_one_kernel(place, two, b0, b2, b1, b3, out):
    line = place[0] // 16
    to, at = iota((64, 32), 0), iota((64, 32), 1)
    for n in range(7):
        lanes = slice(n * C, (n + 1) * C)
        total = b0[:, lanes].astype(F32)
        for part in (b1, b2, b3):
            total = total + part[:, lanes].astype(F32)
        block = jnp.zeros((64, C), F32)
        for which, value in ((0, total.astype(BF)), (1, two[:, lanes])):
            spot = ((to % 8) // 4 == which) & (at == 4 * (to // 8) + to % 4)
            block = block + mm(onehot(spot), value)
        out[:, lanes] = block.astype(BF)
    for n in range(3):
        index = 8 * n + to % 8
        total = jnp.zeros((64, C), F32)
        for turn, part in enumerate((b0, b1, b2, b3)):
            from_line = (index // 6 == (line ^ turn)) & (at == 4 * (to // 8) + index % 3)
            for core in range(2):
                spot = onehot(from_line & ((index % 6) // 3 == core))
                total = total + mm(spot, part[:, (7 + core) * C : (8 + core) * C])
        out[:, (7 + n) * C : (8 + n) * C] = total.astype(BF)


def final_kernel(scale, arrived, rows, one, two):
    total = jnp.sum(arrived[:, :, 0 : 7 * C].astype(F32), axis=0) * scale
    one[...] = total[0:4, 0:QW]
    two[...] = total[4:8, 0:QW]
    to, at = iota((S, 64), 0), iota((S, 64), 1)
    value = jnp.zeros((S, C), F32)
    for n in range(3):
        spot = (at // 8 == (to // 6) % 8) & (8 * n + at % 8 == 6 * (to // 48) + to % 6)
        piece = arrived[:, :, (7 + n) * C : (8 + n) * C].reshape(64, C)
        value = value + mm(onehot(spot), piece)
    rows[...] = value.astype(BF)


def sds(shape, dtype):
    return jax.ShapeDtypeStruct(shape, dtype)


SMEM = pl.BlockSpec(memory_space=pltpu.SMEM)
VM = pl.BlockSpec(memory_space=pltpu.VMEM)
HBM = pl.BlockSpec(memory_space=pltpu.HBM)
ANY = pl.BlockSpec(memory_space=pl.ANY)


def call(kernel, outs, *args, scratch=(), specs=None, late=0, flops=10**5):
    if specs is None:
        specs = [SMEM] + [VM] * (len(args) - 1 - late) + [ANY] * late
    return pl.pallas_call(
        kernel,
        out_shape=outs,
        in_specs=specs,
        out_specs=jax.tree.map(lambda _: VM, outs),
        scratch_shapes=list(scratch),
        compiler_params=pltpu.CompilerParams(vmem_limit_bytes=40 * 2**20),
        cost_estimate=pl.CostEstimate(flops=flops, bytes_accessed=10**4, transcendentals=0),
    )(*args)


def spread(place, nbt, grad, weight, flops):
    edge = sds((96, C), BF)
    return call(
        spread_kernel,
        (sds((S, C), F32), edge, edge, sds((64, C), BF)),
        place,
        nbt,
        grad,
        weight,
        scratch=[pltpu.VMEM((EXT, C), F32)],
        flops=flops,
    )


def swap(value, axis, turn):
    gx, gy = lax.axis_size("gx"), lax.axis_size("gy")
    pairs = []
    for i in range(gx):
        for j in range(gy):
            n, size = (i, gx) if axis == "gx" else (j, gy)
            q = n ^ 1 if turn == 1 else ((n + 1) ^ 1) - 1
            if axis == "gx":
                to = (q, j) if 0 <= q < size else (i, j ^ 1)
            else:
                to = (i, q) if 0 <= q < size else (i ^ 1, j)
            pairs.append((i * gy + j, to[0] * gy + to[1]))
    return lax.ppermute(value, ("gx", "gy"), pairs)


def cross(value, axis, mask):
    return lax.ppermute(value, axis, [(n, n ^ mask) for n in range(lax.axis_size(axis))])


def gathered(value, axis, base=1):
    return [value] + [cross(value, axis, base * d) for d in (2, 1, 3)]


def halo_lines(m2, m1):
    return swap(m2, "gx", 2), swap(m1, "gx", 1)


def halo_columns(place, loc, m2, m1, late, flops=10**5):
    edge = sds((96, C), BF)
    n2, n1 = call(pass_kernel, (edge, edge), place, loc, m2, m1, late, late=1, flops=flops)
    return n1, swap(n2, "gy", 2), swap(n1, "gy", 1)


def body(features, pre_act, grad_out, weight_one, weight_two, neighbours, halo_list, send_list):
    gx = lax.axis_size("gx")
    scale = 1.0 / math.sqrt(S * gx * lax.axis_size("gy"))
    place = jnp.stack([lax.axis_index("gx"), lax.axis_index("gy")]).astype(jnp.int32)
    tile = sds((S, C), BF)
    pay, nbt, hrow, srow, pre, grad = call(
        pack_kernel,
        (
            sds((S + 32, 2 * C), BF),
            sds((32, C), F32),
            sds((8, C), jnp.int32),
            sds((8, C), jnp.int32),
            tile,
            tile,
        ),
        place,
        *[
            pltpu.with_memory_space_constraint(value, pltpu.HBM)
            for value in (
                features,
                pre_act,
                grad_out,
                neighbours.T,
                halo_list,
                jnp.transpose(send_list, (2, 0, 1)),
            )
        ],
        specs=[SMEM] + [HBM] * 6,
        flops=4 * 10**9,
        scratch=[
            pltpu.VMEM((K, S), jnp.int32),
            pltpu.VMEM((1, 8, 24), jnp.int32),
            pltpu.VMEM((3, 1, 64), jnp.int32),
            pltpu.SemaphoreType.DMA((6,)),
        ],
    )
    pays = gathered(pay, "gy")
    back = pltpu.VMEM((8, HB, C), BF)
    own, m1, m2, loc = spread(place, nbt, grad, weight_two, 10**5)
    m2, m1 = halo_lines(m2, m1)
    passed, n2, n1 = halo_columns(place, loc, m2, m1, own)
    picks = sds((768, C), BF)
    o2, o1, near = call(
        pick_kernel,
        (picks, picks, sds((4, 64, 2 * C), BF)),
        place,
        *pays,
        passed,
        scratch=[pltpu.VMEM((4, 8 * HB, 2 * C), BF)],
        late=1,
    )
    r2, r1 = halo_lines(o2, o1)
    grad_pre, ordered = call(
        gate_kernel,
        (tile, sds((S, 2 * C), BF)),
        place,
        own,
        m2,
        m1,
        n2,
        n1,
        hrow,
        pre,
        grad,
        near,
        scratch=[back],
        late=1,
    )
    grads = gathered(ordered, "gy")
    own, m1, m2, loc = spread(place, nbt, grad_pre, weight_one, 4 * 10**9)
    m2, m1 = halo_lines(m2, m1)
    wide = 7 * C
    stack = sds((4 * S, wide), BF)
    cols_one, cols_two = call(
        columns_kernel,
        (stack, stack),
        place,
        *pays,
        r2,
        r1,
        near,
        own,
        scratch=[
            pltpu.VMEM((EXT, 2 * C), BF),
            pltpu.VMEM((32, C), F32),
            pltpu.VMEM((128, C), F32),
        ],
        late=1,
        flops=4 * 10**9,
    )
    passed, n2, n1 = halo_columns(place, loc, m2, m1, cols_two)

    def halves(which, cols, kind, flops, late):
        lanes = slice(which * C, (which + 1) * C)
        half = sds((128, wide), kind)
        return call(
            functools.partial(weight_kernel, lanes),
            (half, half),
            place,
            *grads,
            cols,
            late,
            scratch=[pltpu.VMEM((C, 4 * S), BF)],
            late=1,
            flops=flops,
        )

    keep_two, send_two = halves(0, cols_two, F32, 4 * 10**9, passed)
    come_two = cross(send_two, "gx", 1)
    keep_one, send_one = halves(1, cols_one, BF, 10**5, keep_two)
    come_one = cross(send_one, "gx", 1)
    some = sds((128, C), BF)
    rows_keep, rows_send = call(
        rows_kernel,
        (some, some),
        place,
        own,
        m2,
        m1,
        n2,
        n1,
        hrow,
        grad,
        srow,
        keep_one,
        scratch=[back],
        late=1,
        flops=2 * 10**10,
    )
    rows_come = cross(rows_send, "gx", 1)

    def lines(chunks):
        return [chunks[0]] + [cross(chunks[d], "gx", 16 * d) for d in (2, 1, 3)]

    two = call(
        merge_two_kernel,
        (sds((32, wide), BF),) * 4,
        place,
        keep_two,
        come_two,
        rows_keep,
        late=1,
    )
    one = call(
        merge_one_kernel,
        (sds((32, 9 * C), BF),) * 4,
        place,
        keep_one,
        come_one,
        rows_keep,
        rows_come,
        two[0],
        late=1,
        flops=2 * 10**10,
    )
    sum_two = call(
        line_two_kernel, sds((32, wide), BF), place, *lines(two), flops=2 * 10**10
    )
    summed = call(line_one_kernel, sds((64, 10 * C), BF), place, sum_two, *lines(one))
    groups = [[16 * y + 2 * z + e for z in range(8)] for y in range(4) for e in range(2)]
    collected = lax.all_to_all(
        summed.reshape(8, 8, 10 * C),
        "gx",
        split_axis=0,
        concat_axis=0,
        tiled=True,
        axis_index_groups=groups,
    )
    out = sds((4, QW), F32)
    return call(
        lambda *refs: final_kernel(scale, *refs), (tile, out, out), collected, specs=[VM]
    )


def solution(mesh):
    in_specs = (
        P(("gx", "gy"), None),
        P(("gx", "gy"), None),
        P(("gx", "gy"), None),
        P(),
        P(),
        P(("gx", "gy"), None),
        P(("gx", "gy"), None, None),
        P(("gx", "gy"), None, None),
    )
    out_specs = (P(("gx", "gy"), None), P("gx", "gy"), P("gx", "gy"))
    return jax.shard_map(body, mesh=mesh, in_specs=in_specs, out_specs=out_specs, check_vma=False)
```

```python
import functools
import math

import jax
import jax.numpy as jnp
from jax import lax
from jax.experimental import pallas as pl
from jax.experimental.pallas import tpu as pltpu
from jax.sharding import PartitionSpec as P

C = 256
K = 27
S = 192
HB = 32
EXT = S + 8 * HB
QW = 1728
BF = jnp.bfloat16
F32 = jnp.float32


def iota(shape, dim):
    return lax.broadcasted_iota(jnp.int32, shape, dim)


def onehot(mask):
    return jnp.where(mask, 1.0, 0.0).astype(BF)


def mm(a, b):
    return lax.dot_general(a, b, (((1,), (0,)), ((), ())), preferred_element_type=F32)


def mm_t(a, b):
    return lax.dot_general(a, b, (((0,), (0,)), ((), ())), preferred_element_type=F32)


def direction(a, b):
    grid = 3 * (a + 1) + (b + 1)
    return grid - jnp.where(grid > 4, 1, 0)


def channel_order():
    out = iota((C, C), 1)
    parity, rest = out // 128, out % 128
    source = 8 * (rest // 4) + 4 * parity + rest % 4
    return onehot(iota((C, C), 0) == source)


def halo_matrix(halo_row):
    return onehot(iota((S, 8 * HB), 0) == halo_row)


def pack_kernel(
    place, feat, pre, grad, nbr, halo, send, pay, nbt, hrow, srow, pre_out, grad_out,
    ids, halo_ids, send_ids, sems
):
    copies = [
        pltpu.make_async_copy(source, target, sems.at[n])
        for n, (source, target) in enumerate(
            (
                (nbr, ids),
                (halo, halo_ids),
                (send, send_ids),
                (feat, pay.at[0:S, 0:C]),
                (grad, grad_out),
                (pre, pre_out),
            )
        )
    ]
    for copy in copies:
        copy.start()
    for copy in copies:
        copy.wait()
    table = ids[...].astype(F32)
    heading = jnp.floor((table - S + 0.5) * (1.0 / 24.0))
    table = jnp.where(table >= S, table + 8.0 * heading, table)
    nbt[...] = jnp.full(nbt.shape, -1.0, F32)
    nbt[0:K, 0:S] = table
    shifted_up = table + 1.0
    high = jnp.floor(shifted_up * (1.0 / 16.0))
    pay[S : S + 32, :] = jnp.zeros((32, 2 * C), BF)
    pay[S : S + K, 0:S] = high.astype(BF)
    pay[S : S + K, C : C + S] = (shifted_up - 16.0 * high).astype(BF)
    z = pre_out[...].astype(F32)
    pay[0:S, C : 2 * C] = (z * (1.0 / (1.0 + jnp.exp(-z)))).astype(BF)
    halo_up = (halo_ids[0] + 1).astype(F32).astype(BF)
    spread = mm(halo_up, onehot(iota((24, 8 * HB), 1) % HB == iota((24, 8 * HB), 0)))
    row = jnp.sum(
        jnp.where(iota((8, 8 * HB), 1) // HB == iota((8, 8 * HB), 0), spread, 0.0),
        axis=0,
        keepdims=True,
    )
    hrow[...] = jnp.broadcast_to(row.astype(jnp.int32) - 1, hrow.shape)
    tail = pay[S + 16 : S + 32, 0:C].astype(F32)
    pay[S + 16 : S + 32, 0:C] = jnp.where(iota((16, C), 0) == 15, row, tail).astype(BF)
    lane, peer = iota((64, C), 1), iota((64, C), 0)
    parity = jnp.where(lane < 128, place[0] % 2, 1 - place[0] % 2)
    pick = onehot(peer == 2 * ((lane % 128) // 4) + parity)
    spot = iota((1, C), 1) % 4
    total = jnp.zeros((1, C), F32)
    for c in range(3):
        up = jnp.broadcast_to((send_ids[c] + 1).astype(F32), (8, 64)).astype(BF)
        total = jnp.where(spot == c, mm(up, pick)[0:1, :], total)
    srow[...] = jnp.broadcast_to(total.astype(jnp.int32) - 1, srow.shape)


def spread_kernel(place, nbt, grad, weight, own, m1, m2, loc, acc):
    rows = iota((EXT, C), 0)
    table = nbt[...].astype(jnp.int32)
    gradient = grad[...]
    none = jnp.zeros((C - S, C), BF)
    masks, terms = [], []
    for k in range(K):
        masks.append(onehot(rows == table[k : k + 1, :]))
        terms += [mm(gradient, weight[:, k * C : (k + 1) * C]).astype(BF), none]
    acc[...] = mm(jnp.concatenate(masks, axis=1), jnp.concatenate(terms, axis=0))
    even = place[0] % 2 == 0
    own[...] = acc[0:S, :]
    first, last = jnp.where(even, S, S + 160), jnp.where(even, S + 160, S)
    m1[...] = acc[pl.ds(pl.multiple_of(first, 32), 96), :].astype(BF)
    m2[...] = acc[pl.ds(pl.multiple_of(last, 32), 96), :].astype(BF)
    loc[...] = acc[S + 96 : S + 160, :].astype(BF)


def inner(position, count):
    return (position > 0) & (position < count - 1)


def masked(keep, rows):
    return jnp.where(keep, rows, jnp.zeros_like(rows))


def pass_kernel(place, loc, m2, m1, late, n2, n1):
    even = place[1] % 2 == 0
    first = jnp.where(even, 0, 1)
    far = inner(place[0], 64)
    for out, side in ((n1, first), (n2, 1 - first)):
        out[0:32, :] = loc[pl.ds(pl.multiple_of(side * 32, 32), 32), :]
        out[32:64, :] = m1[pl.ds(pl.multiple_of(side * 64, 32), 32), :]
        out[64:96, :] = masked(far, m2[pl.ds(pl.multiple_of(side * 64, 32), 32), :])


def settled(place, own, m1, m2, n1, n2, hrow, back):
    da = jnp.where(place[0] % 2 == 0, 1, -1)
    db = jnp.where(place[1] % 2 == 0, 1, -1)
    back[direction(da, 0)] = m1[32:64, :]
    back[direction(-da, 0)] = masked(inner(place[0], 64), m2[32:64, :])
    beside = inner(place[1], 4)
    for ref, side, keep in ((n1, db, True), (n2, -db, beside)):
        rows = ref[...] if keep is True else masked(keep, ref[...])
        back[direction(0, side)] = rows[0:32, :]
        back[direction(da, side)] = rows[32:64, :]
        back[direction(-da, side)] = rows[64:96, :]
    rows = back[...].reshape(8 * HB, C)
    return own[...] + mm(halo_matrix(hrow[0:1, :]), rows)


def gate_kernel(place, own, m2, m1, n2, n1, hrow, pre, grad, late, out, ordered, back):
    hidden_grad = settled(place, own, m1, m2, n1, n2, hrow, back)
    z = pre[...].astype(F32)
    g = 1.0 / (1.0 + jnp.exp(-z))
    value = (hidden_grad * g * (1.0 + z * (1.0 - g))).astype(BF)
    out[...] = value
    order = channel_order()
    ordered[:, 0:C] = mm(grad[...], order).astype(BF)
    ordered[:, C : 2 * C] = mm(value, order).astype(BF)


def rows_kernel(place, own, m2, m1, n2, n1, hrow, grad, srow, late, keep, send, back):
    total = settled(place, own, m1, m2, n1, n2, hrow, back)
    value = (grad[...].astype(F32) + total).astype(BF)
    chosen = mm_t(onehot(iota((S, C), 0) == srow[0:1, :]), value).astype(BF)
    keep[...] = chosen[0:128, :]
    send[...] = chosen[128:256, :]


def pick_kernel(place, p0, p2, p1, p3, late, o2, o1, loc, picked):
    column = place[1]
    for turn, pay in enumerate((p0, p1, p2, p3)):
        halo_row = pay[S + 16 : S + 32, 0:C].astype(F32)[15:16, :].astype(jnp.int32) - 1
        rows = mm_t(halo_matrix(halo_row), pay[0:S, 0 : 2 * C])
        picked[column ^ turn] = rows.astype(BF)
    even = place[0] % 2 == 0
    up = pl.multiple_of(jnp.where(even, 160, 0), 32)
    down = pl.multiple_of(jnp.where(even, 0, 160), 32)
    none = jnp.zeros((HB, 2 * C), BF)
    for tile in range(4):
        for b in (-1, 0, 1):
            source = tile - b
            at = HB * (b + 1)
            for out, side in ((o1, up), (o2, down)):
                rows = picked[source, pl.ds(side + at, HB), :] if 0 <= source < 4 else none
                to = 96 * tile + at
                out[to : to + HB, :] = rows[:, 0:C]
                out[to + 384 : to + 384 + HB, :] = rows[:, C : 2 * C]
            if b:
                to = 0 if b < 0 else HB
                rows = picked[source, 96 + to : 96 + to + HB, :] if 0 <= source < 4 else none
                loc[tile, to : to + HB, :] = rows


def columns_kernel(
    place, p0, p2, p1, p3, r2, r1, loc, late, cols_one, cols_two, ext, ids, sel
):
    column = place[1]
    start = column * QW
    first_k = start // C
    offset = start % C
    even = place[0] % 2 == 0
    far = inner(place[0], 64)
    shift = onehot(iota((C, C), 0) == (iota((C, C), 1) + offset) % C)
    lane = iota((S, 2 * C), 1) % C
    early = lane < C - offset
    for turn, pay in enumerate((p0, p1, p2, p3)):
        tile = column ^ turn
        for half in range(2):
            lanes = slice(half * C, (half + 1) * C)
            at = pl.multiple_of(384 * half + 96 * tile, 32)
            above, below = r1[pl.ds(at, 96), :], masked(far, r2[pl.ds(at, 96), :])
            for to, piece in (
                (0, pay[0:S, lanes]),
                (S, jnp.where(even, above, below)),
                (S + 96, loc[tile, :, lanes]),
                (S + 160, jnp.where(even, below, above)),
            ):
                ext[to : to + piece.shape[0], lanes] = mm(piece, shift).astype(BF)
        high = pay[S : S + 32, 0:C].astype(F32)
        low = pay[S : S + 32, C : 2 * C].astype(F32)
        ids[0:32, :] = 16.0 * high + low - 1.0
        for part in range(8):
            sel[part : part + 1, :] = ids[pl.ds(first_k + part, 1), :]
        table = jnp.transpose(sel[...])[:, 0:8].astype(jnp.int32)
        extended = ext[...]
        match = [
            onehot(iota((S, EXT), 1) == table[0:S, part : part + 1]) for part in range(8)
        ]
        found = mm(jnp.concatenate(match, axis=0), extended).astype(BF)
        for part in range(7):
            merged = jnp.where(
                early, found[part * S : (part + 1) * S], found[(part + 1) * S : (part + 2) * S]
            )
            lanes = slice(part * C, (part + 1) * C)
            cols_one[turn * S : (turn + 1) * S, lanes] = merged[:, 0:C]
            cols_two[turn * S : (turn + 1) * S, lanes] = merged[:, C : 2 * C]


def weight_kernel(lanes, place, g0, g2, g1, g3, cols, late, keep, send, gt):
    for turn, grad in enumerate((g0, g1, g2, g3)):
        gt[:, turn * S : (turn + 1) * S] = jnp.transpose(grad[:, lanes].astype(F32)).astype(BF)
    mine = pl.multiple_of((place[0] % 2) * 128, 128)
    other = pl.multiple_of(128 - mine, 128)
    left = jnp.concatenate([gt[pl.ds(mine, 128), :], gt[pl.ds(other, 128), :]], axis=0)
    for part in range(7):
        lanes = slice(part * C, (part + 1) * C)
        block = mm(left, cols[:, lanes])
        keep[:, lanes] = block[0:128].astype(keep.dtype)
        send[:, lanes] = block[128:256].astype(send.dtype)


def merge_two_kernel(place, keep, come, late, *outs):
    line = place[0] // 16
    for turn, out in enumerate(outs):
        rows = pl.ds(pl.multiple_of(32 * (line ^ turn), 32), 32)
        out[...] = (keep[rows, :] + come[rows, :]).astype(BF)


def merge_one_kernel(place, keep, come, rk, rs, late, *outs):
    first = place[0] % 2 == 0
    line = place[0] // 16
    for turn, out in enumerate(outs):
        rows = pl.ds(pl.multiple_of(32 * (line ^ turn), 32), 32)
        total = keep[rows, :].astype(F32) + come[rows, :].astype(F32)
        out[:, 0 : 7 * C] = total.astype(BF)
        mine, other = rk[rows, :], rs[rows, :]
        out[:, 7 * C : 8 * C] = jnp.where(first, mine, other)
        out[:, 8 * C : 9 * C] = jnp.where(first, other, mine)


def line_two_kernel(place, a0, a2, a1, a3, out):
    total = a0[...].astype(F32)
    for part in (a1, a2, a3):
        total = total + part[...].astype(F32)
    out[...] = total.astype(BF)


def line_one_kernel(place, two, b0, b2, b1, b3, *outs_and_whole):
    outs, whole = outs_and_whole[:-1], outs_and_whole[-1]
    line = place[0] // 16
    to, at = iota((64, 32), 0), iota((64, 32), 1)
    for n in range(7):
        lanes = slice(n * C, (n + 1) * C)
        total = b0[:, lanes].astype(F32)
        for part in (b1, b2, b3):
            total = total + part[:, lanes].astype(F32)
        block = jnp.zeros((64, C), F32)
        for which, value in ((0, total.astype(BF)), (1, two[:, lanes])):
            spot = ((to % 8) // 4 == which) & (at == 4 * (to // 8) + to % 4)
            block = block + mm(onehot(spot), value)
        whole[:, lanes] = block
    for n in range(3):
        index = 8 * n + to % 8
        total = jnp.zeros((64, C), F32)
        for turn, part in enumerate((b0, b1, b2, b3)):
            from_line = (index // 6 == (line ^ turn)) & (at == 4 * (to // 8) + index % 3)
            for core in range(2):
                spot = onehot(from_line & ((index % 6) // 3 == core))
                total = total + mm(spot, part[:, (7 + core) * C : (8 + core) * C])
        whole[:, (7 + n) * C : (8 + n) * C] = total
    chip = (place[0] // 2) % 8
    for turn, out in enumerate(outs):
        part = whole[pl.ds(pl.multiple_of(8 * (chip ^ turn), 8), 8), :]
        out[...] = jnp.concatenate([part[:, 0 : 5 * C], part[:, 5 * C : 10 * C]], axis=0).astype(BF)


def final_kernel(scale, place, *refs):
    arrived, (rows, one, two, spread) = refs[:-4], refs[-4:]
    chip = (place[0] // 2) % 8
    total = jnp.zeros((16, 5 * C), F32)
    for (turn, _), ref in zip(TURNS, arrived):
        part = ref[...].astype(F32)
        total = total + part
        spread[pl.ds(pl.multiple_of(8 * (chip ^ turn), 8), 8), :] = part[8:16, 2 * C : 5 * C]
    total = total * scale
    for out, at in ((one, 0), (two, 4)):
        out[:, 0 : 5 * C] = total[at : at + 4, :]
        out[:, 5 * C : QW] = total[8 + at : 12 + at, 0 : QW - 5 * C]
    to, at = iota((S, 64), 0), iota((S, 64), 1)
    value = jnp.zeros((S, C), F32)
    for n in range(3):
        spot = (at // 8 == (to // 6) % 8) & (8 * n + at % 8 == 6 * (to // 48) + to % 6)
        value = value + mm(onehot(spot), spread[:, n * C : (n + 1) * C].astype(BF))
    rows[...] = value.astype(BF)


TURNS = ((0, 0), (4, 8), (3, 6), (5, 10), (2, 4), (6, 12), (1, 2), (7, 14))


def sds(shape, dtype):
    return jax.ShapeDtypeStruct(shape, dtype)


SMEM = pl.BlockSpec(memory_space=pltpu.SMEM)
VM = pl.BlockSpec(memory_space=pltpu.VMEM)
HBM = pl.BlockSpec(memory_space=pltpu.HBM)
ANY = pl.BlockSpec(memory_space=pl.ANY)


def call(kernel, outs, *args, scratch=(), specs=None, late=0, flops=10**5):
    if specs is None:
        specs = [SMEM] + [VM] * (len(args) - 1 - late) + [ANY] * late
    return pl.pallas_call(
        kernel,
        out_shape=outs,
        in_specs=specs,
        out_specs=jax.tree.map(lambda _: VM, outs),
        scratch_shapes=list(scratch),
        compiler_params=pltpu.CompilerParams(vmem_limit_bytes=40 * 2**20),
        cost_estimate=pl.CostEstimate(flops=flops, bytes_accessed=10**4, transcendentals=0),
    )(*args)


def spread(place, nbt, grad, weight, flops):
    edge = sds((96, C), BF)
    return call(
        spread_kernel,
        (sds((S, C), F32), edge, edge, sds((64, C), BF)),
        place,
        nbt,
        grad,
        weight,
        scratch=[pltpu.VMEM((EXT, C), F32)],
        flops=flops,
    )


def swap(value, axis, turn):
    gx, gy = lax.axis_size("gx"), lax.axis_size("gy")
    pairs = []
    for i in range(gx):
        for j in range(gy):
            n, size = (i, gx) if axis == "gx" else (j, gy)
            q = n ^ 1 if turn == 1 else ((n + 1) ^ 1) - 1
            if axis == "gx":
                to = (q, j) if 0 <= q < size else (i, j ^ 1)
            else:
                to = (i, q) if 0 <= q < size else (i ^ 1, j)
            pairs.append((i * gy + j, to[0] * gy + to[1]))
    return lax.ppermute(value, ("gx", "gy"), pairs)


def cross(value, axis, mask):
    return lax.ppermute(value, axis, [(n, n ^ mask) for n in range(lax.axis_size(axis))])


def gathered(value, axis, base=1):
    return [value] + [cross(value, axis, base * d) for d in (2, 1, 3)]


def halo_lines(m2, m1):
    return swap(m2, "gx", 2), swap(m1, "gx", 1)


def halo_columns(place, loc, m2, m1, late, flops=10**5):
    edge = sds((96, C), BF)
    n2, n1 = call(pass_kernel, (edge, edge), place, loc, m2, m1, late, late=1, flops=flops)
    return n1, swap(n2, "gy", 2), swap(n1, "gy", 1)


def body(features, pre_act, grad_out, weight_one, weight_two, neighbours, halo_list, send_list):
    scale = 1.0 / math.sqrt(S * lax.axis_size("gx") * lax.axis_size("gy"))
    place = jnp.stack([lax.axis_index("gx"), lax.axis_index("gy")]).astype(jnp.int32)
    tile = sds((S, C), BF)
    pay, nbt, hrow, srow, pre, grad = call(
        pack_kernel,
        (
            sds((S + 32, 2 * C), BF),
            sds((32, C), F32),
            sds((8, C), jnp.int32),
            sds((8, C), jnp.int32),
            tile,
            tile,
        ),
        place,
        *[
            pltpu.with_memory_space_constraint(value, pltpu.HBM)
            for value in (
                features,
                pre_act,
                grad_out,
                neighbours.T,
                halo_list,
                jnp.transpose(send_list, (2, 0, 1)),
            )
        ],
        specs=[SMEM] + [HBM] * 6,
        flops=4 * 10**9,
        scratch=[
            pltpu.VMEM((K, S), jnp.int32),
            pltpu.VMEM((1, 8, 24), jnp.int32),
            pltpu.VMEM((3, 1, 64), jnp.int32),
            pltpu.SemaphoreType.DMA((6,)),
        ],
    )
    pays = gathered(pay, "gy")
    back = pltpu.VMEM((8, HB, C), BF)
    own, m1, m2, loc = spread(place, nbt, grad, weight_two, 10**5)
    m2, m1 = halo_lines(m2, m1)
    passed, n2, n1 = halo_columns(place, loc, m2, m1, own)
    picks = sds((768, C), BF)
    o2, o1, near = call(
        pick_kernel,
        (picks, picks, sds((4, 64, 2 * C), BF)),
        place,
        *pays,
        passed,
        scratch=[pltpu.VMEM((4, 8 * HB, 2 * C), BF)],
        late=1,
    )
    r2, r1 = halo_lines(o2, o1)
    grad_pre, ordered = call(
        gate_kernel,
        (tile, sds((S, 2 * C), BF)),
        place,
        own,
        m2,
        m1,
        n2,
        n1,
        hrow,
        pre,
        grad,
        near,
        scratch=[back],
        late=1,
    )
    grads = gathered(ordered, "gy")
    own, m1, m2, loc = spread(place, nbt, grad_pre, weight_one, 4 * 10**9)
    m2, m1 = halo_lines(m2, m1)
    wide = 7 * C
    stack = sds((4 * S, wide), BF)
    cols_one, cols_two = call(
        columns_kernel,
        (stack, stack),
        place,
        *pays,
        r2,
        r1,
        near,
        own,
        scratch=[
            pltpu.VMEM((EXT, 2 * C), BF),
            pltpu.VMEM((32, C), F32),
            pltpu.VMEM((128, C), F32),
        ],
        late=1,
        flops=4 * 10**9,
    )
    passed, n2, n1 = halo_columns(place, loc, m2, m1, cols_two)

    def halves(which, cols, kind, flops, late):
        lanes = slice(which * C, (which + 1) * C)
        half = sds((128, wide), kind)
        return call(
            functools.partial(weight_kernel, lanes),
            (half, half),
            place,
            *grads,
            cols,
            late,
            scratch=[pltpu.VMEM((C, 4 * S), BF)],
            late=1,
            flops=flops,
        )

    keep_two, send_two = halves(0, cols_two, F32, 4 * 10**9, passed)
    come_two = cross(send_two, "gx", 1)
    keep_one, send_one = halves(1, cols_one, BF, 10**5, keep_two)
    come_one = cross(send_one, "gx", 1)
    some = sds((128, C), BF)
    rows_keep, rows_send = call(
        rows_kernel,
        (some, some),
        place,
        own,
        m2,
        m1,
        n2,
        n1,
        hrow,
        grad,
        srow,
        keep_one,
        scratch=[back],
        late=1,
        flops=2 * 10**10,
    )
    rows_come = cross(rows_send, "gx", 1)

    def lines(chunks):
        return [chunks[0]] + [cross(chunks[d], "gx", 16 * d) for d in (2, 1, 3)]

    two = call(
        merge_two_kernel,
        (sds((32, wide), BF),) * 4,
        place,
        keep_two,
        come_two,
        rows_keep,
        late=1,
    )
    one = call(
        merge_one_kernel,
        (sds((32, 9 * C), BF),) * 4,
        place,
        keep_one,
        come_one,
        rows_keep,
        rows_come,
        two[0],
        late=1,
        flops=2 * 10**10,
    )
    sum_two = call(
        line_two_kernel, sds((32, wide), BF), place, *lines(two), flops=2 * 10**10
    )
    pieces = call(
        line_one_kernel,
        (sds((16, 5 * C), BF),) * 8,
        place,
        sum_two,
        *lines(one),
        scratch=[pltpu.VMEM((64, 10 * C), F32)],
    )
    collected = [cross(pieces[turn], "gx", mask) if mask else pieces[0] for turn, mask in TURNS]
    out = sds((4, QW), F32)
    return call(
        functools.partial(final_kernel, scale),
        (tile, out, out),
        place,
        *collected,
        scratch=[pltpu.VMEM((64, 3 * C), F32)],
    )


def solution(mesh):
    in_specs = (
        P(("gx", "gy"), None),
        P(("gx", "gy"), None),
        P(("gx", "gy"), None),
        P(),
        P(),
        P(("gx", "gy"), None),
        P(("gx", "gy"), None, None),
        P(("gx", "gy"), None, None),
    )
    out_specs = (P(("gx", "gy"), None), P("gx", "gy"), P("gx", "gy"))
    return jax.shard_map(body, mesh=mesh, in_specs=in_specs, out_specs=out_specs, check_vma=False)
```

```python
import functools
import math

import jax
import jax.numpy as jnp
from jax import lax
from jax.experimental import pallas as pl
from jax.experimental.pallas import tpu as pltpu
from jax.sharding import PartitionSpec as P

C = 256
K = 27
S = 192
HB = 32
EXT = S + 8 * HB
QW = 1728
BF = jnp.bfloat16
F32 = jnp.float32


def iota(shape, dim):
    return lax.broadcasted_iota(jnp.int32, shape, dim)


def onehot(mask):
    return jnp.where(mask, 1.0, 0.0).astype(BF)


def mm(a, b):
    return lax.dot_general(a, b, (((1,), (0,)), ((), ())), preferred_element_type=F32)


def mm_t(a, b):
    return lax.dot_general(a, b, (((0,), (0,)), ((), ())), preferred_element_type=F32)


def direction(a, b):
    grid = 3 * (a + 1) + (b + 1)
    return grid - jnp.where(grid > 4, 1, 0)


def channel_order():
    out = iota((C, C), 1)
    parity, rest = out // 128, out % 128
    source = 8 * (rest // 4) + 4 * parity + rest % 4
    return onehot(iota((C, C), 0) == source)


def halo_matrix(halo_row):
    return onehot(iota((S, 8 * HB), 0) == halo_row)


def pack_kernel(
    place, feat, pre, grad, nbr, halo, send, pay, p2, p1, p3, nbt, hrow, srow, pre_out,
    grad_out, ids, halo_ids, send_ids, feat_in, sems
):
    copies = [
        pltpu.make_async_copy(source, target, sems.at[n])
        for n, (source, target) in enumerate(
            (
                (nbr, ids),
                (halo, halo_ids),
                (send, send_ids),
                (feat, feat_in),
                (grad, grad_out),
                (pre, pre_out),
            )
        )
    ]
    for copy in copies:
        copy.start()
    for copy in copies:
        copy.wait()
    table = ids[...].astype(F32)
    heading = jnp.floor((table - S + 0.5) * (1.0 / 24.0))
    table = jnp.where(table >= S, table + 8.0 * heading, table)
    nbt[...] = jnp.full(nbt.shape, -1.0, F32)
    nbt[0:K, 0:S] = table
    shifted_up = table + 1.0
    high = jnp.floor(shifted_up * (1.0 / 16.0))
    tail = jnp.zeros((32, 2 * C), F32)
    z = pre_out[...].astype(F32)
    hidden = (z * (1.0 / (1.0 + jnp.exp(-z)))).astype(BF)
    halo_up = (halo_ids[0] + 1).astype(F32).astype(BF)
    spread = mm(halo_up, onehot(iota((24, 8 * HB), 1) % HB == iota((24, 8 * HB), 0)))
    row = jnp.sum(
        jnp.where(iota((8, 8 * HB), 1) // HB == iota((8, 8 * HB), 0), spread, 0.0),
        axis=0,
        keepdims=True,
    )
    hrow[...] = jnp.broadcast_to(row.astype(jnp.int32) - 1, hrow.shape)
    pay[S : S + 32, :] = tail.astype(BF)
    pay[S : S + K, 0:S] = high.astype(BF)
    pay[S : S + K, C : C + S] = (shifted_up - 16.0 * high).astype(BF)
    last = pay[S + 16 : S + 32, 0:C].astype(F32)
    pay[S + 16 : S + 32, 0:C] = jnp.where(iota((16, C), 0) == 15, row, last).astype(BF)
    both = jnp.concatenate([feat_in[...], hidden], axis=0)
    for turn, out in ((0, pay), (1, p1), (2, p2), (3, p3)):
        offset = ((place[1] ^ turn) * QW) % C
        turned = mm(both, onehot(iota((C, C), 0) == (iota((C, C), 1) + offset) % C)).astype(BF)
        out[0:S, 0:C] = turned[0:S]
        out[0:S, C : 2 * C] = turned[S : 2 * S]
        if turn:
            out[S : S + 32, :] = pay[S : S + 32, :]
    lane, peer = iota((64, C), 1), iota((64, C), 0)
    parity = jnp.where(lane < 128, place[0] % 2, 1 - place[0] % 2)
    pick = onehot(peer == 2 * ((lane % 128) // 4) + parity)
    spot = iota((1, C), 1) % 4
    total = jnp.zeros((1, C), F32)
    for c in range(3):
        up = jnp.broadcast_to((send_ids[c] + 1).astype(F32), (8, 64)).astype(BF)
        total = jnp.where(spot == c, mm(up, pick)[0:1, :], total)
    srow[...] = jnp.broadcast_to(total.astype(jnp.int32) - 1, srow.shape)


def spread_kernel(place, nbt, grad, weight, own, m1, m2, loc, acc):
    rows = iota((EXT, C), 0)
    table = nbt[...].astype(jnp.int32)
    gradient = grad[...]
    none = jnp.zeros((C - S, C), BF)
    masks, terms = [], []
    for k in range(K):
        masks.append(onehot(rows == table[k : k + 1, :]))
        terms += [mm(gradient, weight[:, k * C : (k + 1) * C]).astype(BF), none]
    acc[...] = mm(jnp.concatenate(masks, axis=1), jnp.concatenate(terms, axis=0))
    even = place[0] % 2 == 0
    own[...] = acc[0:S, :]
    first, last = jnp.where(even, S, S + 160), jnp.where(even, S + 160, S)
    m1[...] = acc[pl.ds(pl.multiple_of(first, 32), 96), :].astype(BF)
    m2[...] = acc[pl.ds(pl.multiple_of(last, 32), 96), :].astype(BF)
    loc[...] = acc[S + 96 : S + 160, :].astype(BF)


def inner(position, count):
    return (position > 0) & (position < count - 1)


def masked(keep, rows):
    return jnp.where(keep, rows, jnp.zeros_like(rows))


def pass_kernel(place, loc, m2, m1, late, n2, n1):
    even = place[1] % 2 == 0
    first = jnp.where(even, 0, 1)
    far = inner(place[0], 64)
    for out, side in ((n1, first), (n2, 1 - first)):
        out[0:32, :] = loc[pl.ds(pl.multiple_of(side * 32, 32), 32), :]
        out[32:64, :] = m1[pl.ds(pl.multiple_of(side * 64, 32), 32), :]
        out[64:96, :] = masked(far, m2[pl.ds(pl.multiple_of(side * 64, 32), 32), :])


def settled(place, own, m1, m2, n1, n2, hrow, back):
    da = jnp.where(place[0] % 2 == 0, 1, -1)
    db = jnp.where(place[1] % 2 == 0, 1, -1)
    back[direction(da, 0)] = m1[32:64, :]
    back[direction(-da, 0)] = masked(inner(place[0], 64), m2[32:64, :])
    beside = inner(place[1], 4)
    for ref, side, keep in ((n1, db, True), (n2, -db, beside)):
        rows = ref[...] if keep is True else masked(keep, ref[...])
        back[direction(0, side)] = rows[0:32, :]
        back[direction(da, side)] = rows[32:64, :]
        back[direction(-da, side)] = rows[64:96, :]
    rows = back[...].reshape(8 * HB, C)
    return own[...] + mm(halo_matrix(hrow[0:1, :]), rows)


def gate_kernel(place, own, m2, m1, n2, n1, hrow, pre, grad, late, out, ordered, back):
    hidden_grad = settled(place, own, m1, m2, n1, n2, hrow, back)
    z = pre[...].astype(F32)
    g = 1.0 / (1.0 + jnp.exp(-z))
    value = (hidden_grad * g * (1.0 + z * (1.0 - g))).astype(BF)
    out[...] = value
    order = channel_order()
    ordered[:, 0:C] = mm(grad[...], order).astype(BF)
    ordered[:, C : 2 * C] = mm(value, order).astype(BF)


def rows_kernel(place, own, m2, m1, n2, n1, hrow, grad, srow, late, keep, send, back):
    total = settled(place, own, m1, m2, n1, n2, hrow, back)
    value = (grad[...].astype(F32) + total).astype(BF)
    chosen = mm_t(onehot(iota((S, C), 0) == srow[0:1, :]), value).astype(BF)
    keep[...] = chosen[0:128, :]
    send[...] = chosen[128:256, :]


def pick_kernel(place, p0, p2, p1, p3, late, o2, o1, loc, picked):
    column = place[1]
    for turn, pay in enumerate((p0, p1, p2, p3)):
        halo_row = pay[S + 16 : S + 32, 0:C].astype(F32)[15:16, :].astype(jnp.int32) - 1
        rows = mm_t(halo_matrix(halo_row), pay[0:S, 0 : 2 * C])
        picked[column ^ turn] = rows.astype(BF)
    even = place[0] % 2 == 0
    up = pl.multiple_of(jnp.where(even, 160, 0), 32)
    down = pl.multiple_of(jnp.where(even, 0, 160), 32)
    none = jnp.zeros((HB, 2 * C), BF)
    for tile in range(4):
        for b in (-1, 0, 1):
            source = tile - b
            at = HB * (b + 1)
            for out, side in ((o1, up), (o2, down)):
                rows = picked[source, pl.ds(side + at, HB), :] if 0 <= source < 4 else none
                to = 96 * tile + at
                out[to : to + HB, :] = rows[:, 0:C]
                out[to + 384 : to + 384 + HB, :] = rows[:, C : 2 * C]
            if b:
                to = 0 if b < 0 else HB
                rows = picked[source, 96 + to : 96 + to + HB, :] if 0 <= source < 4 else none
                loc[tile, to : to + HB, :] = rows


def columns_kernel(
    place, p0, p2, p1, p3, r2, r1, loc, late, cols_one, cols_two, ext, ids, sel
):
    column = place[1]
    start = column * QW
    first_k = start // C
    offset = start % C
    even = place[0] % 2 == 0
    far = inner(place[0], 64)
    lane = iota((S, 2 * C), 1) % C
    early = lane < C - offset
    for turn, pay in enumerate((p0, p1, p2, p3)):
        tile = column ^ turn
        for half in range(2):
            lanes = slice(half * C, (half + 1) * C)
            at = pl.multiple_of(384 * half + 96 * tile, 32)
            above, below = r1[pl.ds(at, 96), :], masked(far, r2[pl.ds(at, 96), :])
            for to, piece in (
                (0, pay[0:S, lanes]),
                (S, jnp.where(even, above, below)),
                (S + 96, loc[tile, :, lanes]),
                (S + 160, jnp.where(even, below, above)),
            ):
                ext[to : to + piece.shape[0], lanes] = piece
        high = pay[S : S + 32, 0:C].astype(F32)
        low = pay[S : S + 32, C : 2 * C].astype(F32)
        ids[0:32, :] = 16.0 * high + low - 1.0
        for part in range(8):
            sel[part : part + 1, :] = ids[pl.ds(first_k + part, 1), :]
        table = jnp.transpose(sel[...])[:, 0:8].astype(jnp.int32)
        extended = ext[...]
        match = [
            onehot(iota((S, EXT), 1) == table[0:S, part : part + 1]) for part in range(8)
        ]
        found = mm(jnp.concatenate(match, axis=0), extended).astype(BF)
        for part in range(7):
            merged = jnp.where(
                early, found[part * S : (part + 1) * S], found[(part + 1) * S : (part + 2) * S]
            )
            lanes = slice(part * C, (part + 1) * C)
            cols_one[turn * S : (turn + 1) * S, lanes] = merged[:, 0:C]
            cols_two[turn * S : (turn + 1) * S, lanes] = merged[:, C : 2 * C]


def weight_kernel(lanes, place, g0, g2, g1, g3, cols, late, keep, send, gt):
    for turn, grad in enumerate((g0, g1, g2, g3)):
        gt[:, turn * S : (turn + 1) * S] = jnp.transpose(grad[:, lanes].astype(F32)).astype(BF)
    mine = pl.multiple_of((place[0] % 2) * 128, 128)
    other = pl.multiple_of(128 - mine, 128)
    left = jnp.concatenate([gt[pl.ds(mine, 128), :], gt[pl.ds(other, 128), :]], axis=0)
    for part in range(7):
        lanes = slice(part * C, (part + 1) * C)
        block = mm(left, cols[:, lanes])
        keep[:, lanes] = block[0:128].astype(keep.dtype)
        send[:, lanes] = block[128:256].astype(send.dtype)


def merge_two_kernel(place, keep, come, late, *outs):
    line = place[0] // 16
    for turn, out in enumerate(outs):
        rows = pl.ds(pl.multiple_of(32 * (line ^ turn), 32), 32)
        out[...] = (keep[rows, :] + come[rows, :]).astype(BF)


def merge_one_kernel(place, keep, come, rk, rs, late, *outs):
    first = place[0] % 2 == 0
    line = place[0] // 16
    for turn, out in enumerate(outs):
        rows = pl.ds(pl.multiple_of(32 * (line ^ turn), 32), 32)
        total = keep[rows, :].astype(F32) + come[rows, :].astype(F32)
        out[:, 0 : 7 * C] = total.astype(BF)
        mine, other = rk[rows, :], rs[rows, :]
        out[:, 7 * C : 8 * C] = jnp.where(first, mine, other)
        out[:, 8 * C : 9 * C] = jnp.where(first, other, mine)


def line_two_kernel(place, a0, a2, a1, a3, out):
    total = a0[...].astype(F32)
    for part in (a1, a2, a3):
        total = total + part[...].astype(F32)
    out[...] = total.astype(BF)


def line_one_kernel(place, two, b0, b2, b1, b3, out):
    line = place[0] // 16
    to, at = iota((64, 32), 0), iota((64, 32), 1)
    for n in range(7):
        lanes = slice(n * C, (n + 1) * C)
        total = b0[:, lanes].astype(F32)
        for part in (b1, b2, b3):
            total = total + part[:, lanes].astype(F32)
        block = jnp.zeros((64, C), F32)
        for which, value in ((0, total.astype(BF)), (1, two[:, lanes])):
            spot = ((to % 8) // 4 == which) & (at == 4 * (to // 8) + to % 4)
            block = block + mm(onehot(spot), value)
        out[:, lanes] = block.astype(BF)
    for n in range(3):
        index = 8 * n + to % 8
        total = jnp.zeros((64, C), F32)
        for turn, part in enumerate((b0, b1, b2, b3)):
            from_line = (index // 6 == (line ^ turn)) & (at == 4 * (to // 8) + index % 3)
            for core in range(2):
                spot = onehot(from_line & ((index % 6) // 3 == core))
                total = total + mm(spot, part[:, (7 + core) * C : (8 + core) * C])
        out[:, (7 + n) * C : (8 + n) * C] = total.astype(BF)


def final_kernel(scale, arrived, rows, one, two):
    total = jnp.sum(arrived[:, :, 0 : 7 * C].astype(F32), axis=0) * scale
    one[...] = total[0:4, 0:QW]
    two[...] = total[4:8, 0:QW]
    to, at = iota((S, 64), 0), iota((S, 64), 1)
    value = jnp.zeros((S, C), F32)
    for n in range(3):
        spot = (at // 8 == (to // 6) % 8) & (8 * n + at % 8 == 6 * (to // 48) + to % 6)
        piece = arrived[:, :, (7 + n) * C : (8 + n) * C].reshape(64, C)
        value = value + mm(onehot(spot), piece)
    rows[...] = value.astype(BF)


def sds(shape, dtype):
    return jax.ShapeDtypeStruct(shape, dtype)


SMEM = pl.BlockSpec(memory_space=pltpu.SMEM)
VM = pl.BlockSpec(memory_space=pltpu.VMEM)
HBM = pl.BlockSpec(memory_space=pltpu.HBM)
ANY = pl.BlockSpec(memory_space=pl.ANY)


def call(kernel, outs, *args, scratch=(), specs=None, late=0, flops=10**5):
    if specs is None:
        specs = [SMEM] + [VM] * (len(args) - 1 - late) + [ANY] * late
    return pl.pallas_call(
        kernel,
        out_shape=outs,
        in_specs=specs,
        out_specs=jax.tree.map(lambda _: VM, outs),
        scratch_shapes=list(scratch),
        compiler_params=pltpu.CompilerParams(vmem_limit_bytes=40 * 2**20),
        cost_estimate=pl.CostEstimate(flops=flops, bytes_accessed=10**4, transcendentals=0),
    )(*args)


def spread(place, nbt, grad, weight, flops):
    edge = sds((96, C), BF)
    return call(
        spread_kernel,
        (sds((S, C), F32), edge, edge, sds((64, C), BF)),
        place,
        nbt,
        grad,
        weight,
        scratch=[pltpu.VMEM((EXT, C), F32)],
        flops=flops,
    )


def swap(value, axis, turn):
    gx, gy = lax.axis_size("gx"), lax.axis_size("gy")
    pairs = []
    for i in range(gx):
        for j in range(gy):
            n, size = (i, gx) if axis == "gx" else (j, gy)
            q = n ^ 1 if turn == 1 else ((n + 1) ^ 1) - 1
            if axis == "gx":
                to = (q, j) if 0 <= q < size else (i, j ^ 1)
            else:
                to = (i, q) if 0 <= q < size else (i ^ 1, j)
            pairs.append((i * gy + j, to[0] * gy + to[1]))
    return lax.ppermute(value, ("gx", "gy"), pairs)


def cross(value, axis, mask):
    return lax.ppermute(value, axis, [(n, n ^ mask) for n in range(lax.axis_size(axis))])


def gathered(value, axis, base=1):
    return [value] + [cross(value, axis, base * d) for d in (2, 1, 3)]


def halo_lines(m2, m1):
    return swap(m2, "gx", 2), swap(m1, "gx", 1)


def halo_columns(place, loc, m2, m1, late, flops=10**5):
    edge = sds((96, C), BF)
    n2, n1 = call(pass_kernel, (edge, edge), place, loc, m2, m1, late, late=1, flops=flops)
    return n1, swap(n2, "gy", 2), swap(n1, "gy", 1)


def body(features, pre_act, grad_out, weight_one, weight_two, neighbours, halo_list, send_list):
    gx = lax.axis_size("gx")
    scale = 1.0 / math.sqrt(S * gx * lax.axis_size("gy"))
    place = jnp.stack([lax.axis_index("gx"), lax.axis_index("gy")]).astype(jnp.int32)
    tile = sds((S, C), BF)
    pay, p2, p1, p3, nbt, hrow, srow, pre, grad = call(
        pack_kernel,
        (
            *[sds((S + 32, 2 * C), BF)] * 4,
            sds((32, C), F32),
            sds((8, C), jnp.int32),
            sds((8, C), jnp.int32),
            tile,
            tile,
        ),
        place,
        *[
            pltpu.with_memory_space_constraint(value, pltpu.HBM)
            for value in (
                features,
                pre_act,
                grad_out,
                neighbours.T,
                halo_list,
                jnp.transpose(send_list, (2, 0, 1)),
            )
        ],
        specs=[SMEM] + [HBM] * 6,
        flops=4 * 10**9,
        scratch=[
            pltpu.VMEM((K, S), jnp.int32),
            pltpu.VMEM((1, 8, 24), jnp.int32),
            pltpu.VMEM((3, 1, 64), jnp.int32),
            pltpu.VMEM((S, C), BF),
            pltpu.SemaphoreType.DMA((6,)),
        ],
    )
    pays = [pay] + [cross(value, "gy", d) for d, value in ((2, p2), (1, p1), (3, p3))]
    back = pltpu.VMEM((8, HB, C), BF)
    own, m1, m2, loc = spread(place, nbt, grad, weight_two, 10**5)
    m2, m1 = halo_lines(m2, m1)
    passed, n2, n1 = halo_columns(place, loc, m2, m1, own)
    picks = sds((768, C), BF)
    o2, o1, near = call(
        pick_kernel,
        (picks, picks, sds((4, 64, 2 * C), BF)),
        place,
        *pays,
        passed,
        scratch=[pltpu.VMEM((4, 8 * HB, 2 * C), BF)],
        late=1,
    )
    r2, r1 = halo_lines(o2, o1)
    grad_pre, ordered = call(
        gate_kernel,
        (tile, sds((S, 2 * C), BF)),
        place,
        own,
        m2,
        m1,
        n2,
        n1,
        hrow,
        pre,
        grad,
        near,
        scratch=[back],
        late=1,
    )
    grads = gathered(ordered, "gy")
    own, m1, m2, loc = spread(place, nbt, grad_pre, weight_one, 4 * 10**9)
    m2, m1 = halo_lines(m2, m1)
    wide = 7 * C
    stack = sds((4 * S, wide), BF)
    cols_one, cols_two = call(
        columns_kernel,
        (stack, stack),
        place,
        *pays,
        r2,
        r1,
        near,
        own,
        scratch=[
            pltpu.VMEM((EXT, 2 * C), BF),
            pltpu.VMEM((32, C), F32),
            pltpu.VMEM((128, C), F32),
        ],
        late=1,
        flops=4 * 10**9,
    )
    passed, n2, n1 = halo_columns(place, loc, m2, m1, cols_two)

    def halves(which, cols, kind, flops, late):
        lanes = slice(which * C, (which + 1) * C)
        half = sds((128, wide), kind)
        return call(
            functools.partial(weight_kernel, lanes),
            (half, half),
            place,
            *grads,
            cols,
            late,
            scratch=[pltpu.VMEM((C, 4 * S), BF)],
            late=1,
            flops=flops,
        )

    keep_two, send_two = halves(0, cols_two, F32, 4 * 10**9, passed)
    come_two = cross(send_two, "gx", 1)
    keep_one, send_one = halves(1, cols_one, BF, 10**5, keep_two)
    come_one = cross(send_one, "gx", 1)
    some = sds((128, C), BF)
    rows_keep, rows_send = call(
        rows_kernel,
        (some, some),
        place,
        own,
        m2,
        m1,
        n2,
        n1,
        hrow,
        grad,
        srow,
        keep_one,
        scratch=[back],
        late=1,
        flops=2 * 10**10,
    )
    rows_come = cross(rows_send, "gx", 1)

    def lines(chunks):
        return [chunks[0]] + [cross(chunks[d], "gx", 16 * d) for d in (2, 1, 3)]

    two = call(
        merge_two_kernel,
        (sds((32, wide), BF),) * 4,
        place,
        keep_two,
        come_two,
        rows_keep,
        late=1,
    )
    one = call(
        merge_one_kernel,
        (sds((32, 9 * C), BF),) * 4,
        place,
        keep_one,
        come_one,
        rows_keep,
        rows_come,
        two[0],
        late=1,
        flops=2 * 10**10,
    )
    sum_two = call(
        line_two_kernel, sds((32, wide), BF), place, *lines(two), flops=2 * 10**10
    )
    summed = call(line_one_kernel, sds((64, 10 * C), BF), place, sum_two, *lines(one))
    groups = [[16 * y + 2 * z + e for z in range(8)] for y in range(4) for e in range(2)]
    collected = lax.all_to_all(
        summed.reshape(8, 8, 10 * C),
        "gx",
        split_axis=0,
        concat_axis=0,
        tiled=True,
        axis_index_groups=groups,
    )
    out = sds((4, QW), F32)
    return call(
        lambda *refs: final_kernel(scale, *refs), (tile, out, out), collected, specs=[VM]
    )


def solution(mesh):
    in_specs = (
        P(("gx", "gy"), None),
        P(("gx", "gy"), None),
        P(("gx", "gy"), None),
        P(),
        P(),
        P(("gx", "gy"), None),
        P(("gx", "gy"), None, None),
        P(("gx", "gy"), None, None),
    )
    out_specs = (P(("gx", "gy"), None), P("gx", "gy"), P("gx", "gy"))
    return jax.shard_map(body, mesh=mesh, in_specs=in_specs, out_specs=out_specs, check_vma=False)
```

```python
import functools
import math

import jax
import jax.numpy as jnp
from jax import lax
from jax.experimental import pallas as pl
from jax.experimental.pallas import tpu as pltpu
from jax.sharding import PartitionSpec as P

C = 256
K = 27
S = 192
HB = 32
EXT = S + 8 * HB
QW = 1728
HALF = 896
BF = jnp.bfloat16
F32 = jnp.float32


def iota(shape, dim):
    return lax.broadcasted_iota(jnp.int32, shape, dim)


def onehot(mask):
    return jnp.where(mask, 1.0, 0.0).astype(BF)


def mm(a, b):
    return lax.dot_general(a, b, (((1,), (0,)), ((), ())), preferred_element_type=F32)


def mm_t(a, b):
    return lax.dot_general(a, b, (((0,), (0,)), ((), ())), preferred_element_type=F32)


def direction(a, b):
    grid = 3 * (a + 1) + (b + 1)
    return grid - jnp.where(grid > 4, 1, 0)


def channel_order():
    out = iota((C, C), 1)
    parity, rest = out // 128, out % 128
    source = 8 * (rest // 4) + 4 * parity + rest % 4
    return onehot(iota((C, C), 0) == source)


def halo_matrix(halo_row):
    return onehot(iota((S, 8 * HB), 0) == halo_row)


def pack_kernel(
    place, feat, pre, grad, nbr, halo, send, pay, p2, p1, p3, nbt, hrow, srow, pre_out,
    grad_out, ids, halo_ids, send_ids, feat_in, sems
):
    copies = [
        pltpu.make_async_copy(source, target, sems.at[n])
        for n, (source, target) in enumerate(
            (
                (nbr, ids),
                (halo, halo_ids),
                (send, send_ids),
                (feat, feat_in),
                (grad, grad_out),
                (pre, pre_out),
            )
        )
    ]
    for copy in copies:
        copy.start()
    for copy in copies:
        copy.wait()
    table = ids[...].astype(F32)
    heading = jnp.floor((table - S + 0.5) * (1.0 / 24.0))
    table = jnp.where(table >= S, table + 8.0 * heading, table)
    nbt[...] = jnp.full(nbt.shape, -1.0, F32)
    nbt[0:K, 0:S] = table
    shifted_up = table + 1.0
    high = jnp.floor(shifted_up * (1.0 / 16.0))
    tail = jnp.zeros((32, 2 * C), F32)
    z = pre_out[...].astype(F32)
    hidden = (z * (1.0 / (1.0 + jnp.exp(-z)))).astype(BF)
    halo_up = (halo_ids[0] + 1).astype(F32).astype(BF)
    spread = mm(halo_up, onehot(iota((24, 8 * HB), 1) % HB == iota((24, 8 * HB), 0)))
    row = jnp.sum(
        jnp.where(iota((8, 8 * HB), 1) // HB == iota((8, 8 * HB), 0), spread, 0.0),
        axis=0,
        keepdims=True,
    )
    hrow[...] = jnp.broadcast_to(row.astype(jnp.int32) - 1, hrow.shape)
    pay[S : S + 32, :] = tail.astype(BF)
    pay[S : S + K, 0:S] = high.astype(BF)
    pay[S : S + K, C : C + S] = (shifted_up - 16.0 * high).astype(BF)
    last = pay[S + 16 : S + 32, 0:C].astype(F32)
    pay[S + 16 : S + 32, 0:C] = jnp.where(iota((16, C), 0) == 15, row, last).astype(BF)
    both = jnp.concatenate([feat_in[...], hidden], axis=0)
    for turn, out in ((0, pay), (1, p1), (2, p2), (3, p3)):
        offset = ((place[1] ^ turn) * QW) % C
        turned = mm(both, onehot(iota((C, C), 0) == (iota((C, C), 1) + offset) % C)).astype(BF)
        out[0:S, 0:C] = turned[0:S]
        out[0:S, C : 2 * C] = turned[S : 2 * S]
        if turn:
            out[S : S + 32, :] = pay[S : S + 32, :]
    lane, peer = iota((64, C), 1), iota((64, C), 0)
    parity = jnp.where(lane < 128, place[0] % 2, 1 - place[0] % 2)
    pick = onehot(peer == 2 * ((lane % 128) // 4) + parity)
    spot = iota((1, C), 1) % 4
    total = jnp.zeros((1, C), F32)
    for c in range(3):
        up = jnp.broadcast_to((send_ids[c] + 1).astype(F32), (8, 64)).astype(BF)
        total = jnp.where(spot == c, mm(up, pick)[0:1, :], total)
    srow[...] = jnp.broadcast_to(total.astype(jnp.int32) - 1, srow.shape)


def spread_kernel(place, nbt, grad, weight, own, m1, m2, loc, acc):
    rows = iota((EXT, C), 0)
    table = nbt[...].astype(jnp.int32)
    gradient = grad[...]
    none = jnp.zeros((C - S, C), BF)
    masks, terms = [], []
    for k in range(K):
        masks.append(onehot(rows == table[k : k + 1, :]))
        terms += [mm(gradient, weight[:, k * C : (k + 1) * C]).astype(BF), none]
    acc[...] = mm(jnp.concatenate(masks, axis=1), jnp.concatenate(terms, axis=0))
    even = place[0] % 2 == 0
    own[...] = acc[0:S, :]
    first, last = jnp.where(even, S, S + 160), jnp.where(even, S + 160, S)
    m1[...] = acc[pl.ds(pl.multiple_of(first, 32), 96), :].astype(BF)
    m2[...] = acc[pl.ds(pl.multiple_of(last, 32), 96), :].astype(BF)
    loc[...] = acc[S + 96 : S + 160, :].astype(BF)


def inner(position, count):
    return (position > 0) & (position < count - 1)


def masked(keep, rows):
    return jnp.where(keep, rows, jnp.zeros_like(rows))


def pass_kernel(place, loc, m2, m1, late, n2, n1):
    even = place[1] % 2 == 0
    first = jnp.where(even, 0, 1)
    far = inner(place[0], 64)
    for out, side in ((n1, first), (n2, 1 - first)):
        out[0:32, :] = loc[pl.ds(pl.multiple_of(side * 32, 32), 32), :]
        out[32:64, :] = m1[pl.ds(pl.multiple_of(side * 64, 32), 32), :]
        out[64:96, :] = masked(far, m2[pl.ds(pl.multiple_of(side * 64, 32), 32), :])


def settled(place, own, m1, m2, n1, n2, hrow, back):
    da = jnp.where(place[0] % 2 == 0, 1, -1)
    db = jnp.where(place[1] % 2 == 0, 1, -1)
    back[direction(da, 0)] = m1[32:64, :]
    back[direction(-da, 0)] = masked(inner(place[0], 64), m2[32:64, :])
    beside = inner(place[1], 4)
    for ref, side, keep in ((n1, db, True), (n2, -db, beside)):
        rows = ref[...] if keep is True else masked(keep, ref[...])
        back[direction(0, side)] = rows[0:32, :]
        back[direction(da, side)] = rows[32:64, :]
        back[direction(-da, side)] = rows[64:96, :]
    rows = back[...].reshape(8 * HB, C)
    return own[...] + mm(halo_matrix(hrow[0:1, :]), rows)


def gate_kernel(place, own, m2, m1, n2, n1, hrow, pre, grad, late, out, ordered, back):
    hidden_grad = settled(place, own, m1, m2, n1, n2, hrow, back)
    z = pre[...].astype(F32)
    g = 1.0 / (1.0 + jnp.exp(-z))
    value = (hidden_grad * g * (1.0 + z * (1.0 - g))).astype(BF)
    out[...] = value
    order = channel_order()
    ordered[:, 0:C] = mm(grad[...], order).astype(BF)
    ordered[:, C : 2 * C] = mm(value, order).astype(BF)


def rows_kernel(place, own, m2, m1, n2, n1, hrow, grad, srow, late, keep, send, back):
    total = settled(place, own, m1, m2, n1, n2, hrow, back)
    value = (grad[...].astype(F32) + total).astype(BF)
    chosen = mm_t(onehot(iota((S, C), 0) == srow[0:1, :]), value).astype(BF)
    keep[...] = chosen[0:128, :]
    send[...] = chosen[128:256, :]


def pick_kernel(place, p0, p2, p1, p3, late, o2, o1, loc, picked):
    column = place[1]
    for turn, pay in enumerate((p0, p1, p2, p3)):
        halo_row = pay[S + 16 : S + 32, 0:C].astype(F32)[15:16, :].astype(jnp.int32) - 1
        rows = mm_t(halo_matrix(halo_row), pay[0:S, 0 : 2 * C])
        picked[column ^ turn] = rows.astype(BF)
    even = place[0] % 2 == 0
    up = pl.multiple_of(jnp.where(even, 160, 0), 32)
    down = pl.multiple_of(jnp.where(even, 0, 160), 32)
    none = jnp.zeros((HB, 2 * C), BF)
    for tile in range(4):
        for b in (-1, 0, 1):
            source = tile - b
            at = HB * (b + 1)
            for out, side in ((o1, up), (o2, down)):
                rows = picked[source, pl.ds(side + at, HB), :] if 0 <= source < 4 else none
                to = 96 * tile + at
                out[to : to + HB, :] = rows[:, 0:C]
                out[to + 384 : to + 384 + HB, :] = rows[:, C : 2 * C]
            if b:
                to = 0 if b < 0 else HB
                rows = picked[source, 96 + to : 96 + to + HB, :] if 0 <= source < 4 else none
                loc[tile, to : to + HB, :] = rows


def columns_kernel(
    place, p0, p2, p1, p3, r2, r1, loc, late, cols_one, cols_two, ext, ids, sel
):
    column = place[1]
    start = column * QW
    first_k = start // C
    offset = start % C
    even = place[0] % 2 == 0
    far = inner(place[0], 64)
    lane = iota((S, 2 * C), 1) % C
    early = lane < C - offset
    for turn, pay in enumerate((p0, p1, p2, p3)):
        tile = column ^ turn
        for half in range(2):
            lanes = slice(half * C, (half + 1) * C)
            at = pl.multiple_of(384 * half + 96 * tile, 32)
            above, below = r1[pl.ds(at, 96), :], masked(far, r2[pl.ds(at, 96), :])
            for to, piece in (
                (0, pay[0:S, lanes]),
                (S, jnp.where(even, above, below)),
                (S + 96, loc[tile, :, lanes]),
                (S + 160, jnp.where(even, below, above)),
            ):
                ext[to : to + piece.shape[0], lanes] = piece
        high = pay[S : S + 32, 0:C].astype(F32)
        low = pay[S : S + 32, C : 2 * C].astype(F32)
        ids[0:32, :] = 16.0 * high + low - 1.0
        for part in range(8):
            sel[part : part + 1, :] = ids[pl.ds(first_k + part, 1), :]
        table = jnp.transpose(sel[...])[:, 0:8].astype(jnp.int32)
        extended = ext[...]
        match = [
            onehot(iota((S, EXT), 1) == table[0:S, part : part + 1]) for part in range(8)
        ]
        found = mm(jnp.concatenate(match, axis=0), extended).astype(BF)
        for part in range(7):
            merged = jnp.where(
                early, found[part * S : (part + 1) * S], found[(part + 1) * S : (part + 2) * S]
            )
            lanes = slice(part * C, (part + 1) * C)
            cols_one[turn * S : (turn + 1) * S, lanes] = merged[:, 0:C]
            cols_two[turn * S : (turn + 1) * S, lanes] = merged[:, C : 2 * C]


def weight_kernel(lanes, place, g0, g2, g1, g3, cols, late, keep, send, gt):
    for turn, grad in enumerate((g0, g1, g2, g3)):
        gt[:, turn * S : (turn + 1) * S] = jnp.transpose(grad[:, lanes].astype(F32)).astype(BF)
    mine = pl.multiple_of((place[0] % 2) * 128, 128)
    other = pl.multiple_of(128 - mine, 128)
    left = jnp.concatenate([gt[pl.ds(mine, 128), :], gt[pl.ds(other, 128), :]], axis=0)
    for part in range(7):
        lanes = slice(part * C, (part + 1) * C)
        block = mm(left, cols[:, lanes])
        keep[:, lanes] = block[0:128].astype(keep.dtype)
        send[:, lanes] = block[128:256].astype(send.dtype)


def chunk(place, turn):
    return pl.ds(pl.multiple_of(32 * ((place[0] // 16) ^ turn), 32), 32)


def merge_two_kernel(place, keep, come, late, to1, to3, own, across):
    part = [keep[chunk(place, t), :] + come[chunk(place, t), :] for t in range(4)]
    to1[0:32, :] = part[1][:, 0:HALF].astype(BF)
    to1[32:64, :] = part[2][:, 0:HALF].astype(BF)
    to3[0:32, :] = part[3][:, HALF:].astype(BF)
    to3[32:64, :] = part[2][:, HALF:].astype(BF)
    own[...] = part[0]
    across[:, 0:HALF] = part[3][:, 0:HALF]
    across[:, HALF:] = part[1][:, HALF:]


def merge_one_kernel(place, keep, come, rk, rs, late, to1, to3, own, across, mine):
    part = [
        keep[chunk(place, t), :].astype(F32) + come[chunk(place, t), :].astype(F32)
        for t in range(4)
    ]
    first = place[0] % 2 == 0
    rows = []
    for t in range(4):
        here, other = rk[chunk(place, t), :], rs[chunk(place, t), :]
        rows.append((jnp.where(first, here, other), jnp.where(first, other, here)))
    for out, t, lanes, core in ((to1, 1, slice(0, HALF), 0), (to3, 3, slice(HALF, 7 * C), 1)):
        out[0:32, 0:HALF] = part[t][:, lanes].astype(BF)
        out[32:64, 0:HALF] = part[2][:, lanes].astype(BF)
        out[0:32, HALF : HALF + C] = rows[t][0]
        out[32:64, HALF : HALF + C] = rows[t][1]
        out[0:32, HALF + C : HALF + C + 128] = rows[2][core][:, 0:128]
        out[32:64, HALF + C : HALF + C + 128] = rows[2][core][:, 128:256]
    own[...] = part[0]
    across[:, 0:HALF] = part[3][:, 0:HALF]
    across[:, HALF:] = part[1][:, HALF:]
    mine[:, 0:C] = rows[0][0]
    mine[:, C : 2 * C] = rows[0][1]


def half_two_kernel(place, own, across, a1, a3, to3, to1, total):
    to3[...] = (across[:, 0:HALF] + a1[32:64, :].astype(F32)).astype(BF)
    to1[...] = (across[:, HALF:] + a3[32:64, :].astype(F32)).astype(BF)
    total[:, 0:HALF] = own[:, 0:HALF] + a1[0:32, :].astype(F32)
    total[:, HALF:] = own[:, HALF:] + a3[0:32, :].astype(F32)


def half_one_kernel(place, own, across, a1, a3, to3, to1, total):
    for out, ref, lanes in ((to3, a1, slice(0, HALF)), (to1, a3, slice(HALF, 7 * C))):
        out[:, 0:HALF] = (across[:, lanes] + ref[32:64, 0:HALF].astype(F32)).astype(BF)
        out[:, HALF : HALF + 128] = ref[0:32, HALF + C : HALF + C + 128]
        out[:, HALF + 128 : HALF + C] = ref[32:64, HALF + C : HALF + C + 128]
        total[:, lanes] = own[:, lanes] + ref[0:32, 0:HALF].astype(F32)


def line_two_kernel(place, total, b3, b1, out):
    out[:, 0:HALF] = (total[:, 0:HALF] + b3[...].astype(F32)).astype(BF)
    out[:, HALF:] = (total[:, HALF:] + b1[...].astype(F32)).astype(BF)


def line_one_kernel(place, two, total, mine, a1, a3, b3, b1, out, one):
    line = place[0] // 16
    one[:, 0:HALF] = (total[:, 0:HALF] + b3[:, 0:HALF].astype(F32)).astype(BF)
    one[:, HALF:] = (total[:, HALF:] + b1[:, 0:HALF].astype(F32)).astype(BF)
    to, at = iota((64, 32), 0), iota((64, 32), 1)
    spots = [onehot(((to % 8) // 4 == n) & (at == 4 * (to // 8) + to % 4)) for n in range(2)]
    for n in range(7):
        lanes = slice(n * C, (n + 1) * C)
        block = mm(spots[0], one[:, lanes]) + mm(spots[1], two[:, lanes])
        out[:, lanes] = block.astype(BF)
    direct = slice(HALF, HALF + C)
    sources = (
        (0, (mine[:, 0:C], mine[:, C : 2 * C])),
        (1, (a1[0:32, direct], a1[32:64, direct])),
        (2, (b3[:, direct], b1[:, direct])),
        (3, (a3[0:32, direct], a3[32:64, direct])),
    )
    for n in range(3):
        index = 8 * n + to % 8
        found = jnp.zeros((64, C), F32)
        for turn, cores in sources:
            from_line = (index // 6 == (line ^ turn)) & (at == 4 * (to // 8) + index % 3)
            for core in range(2):
                spot = onehot(from_line & ((index % 6) // 3 == core))
                found = found + mm(spot, cores[core])
        out[:, (7 + n) * C : (8 + n) * C] = found.astype(BF)


def final_kernel(scale, arrived, rows, one, two):
    total = jnp.sum(arrived[:, :, 0 : 7 * C].astype(F32), axis=0) * scale
    one[...] = total[0:4, 0:QW]
    two[...] = total[4:8, 0:QW]
    to, at = iota((S, 64), 0), iota((S, 64), 1)
    value = jnp.zeros((S, C), F32)
    for n in range(3):
        spot = (at // 8 == (to // 6) % 8) & (8 * n + at % 8 == 6 * (to // 48) + to % 6)
        piece = arrived[:, :, (7 + n) * C : (8 + n) * C].reshape(64, C)
        value = value + mm(onehot(spot), piece)
    rows[...] = value.astype(BF)


def sds(shape, dtype):
    return jax.ShapeDtypeStruct(shape, dtype)


SMEM = pl.BlockSpec(memory_space=pltpu.SMEM)
VM = pl.BlockSpec(memory_space=pltpu.VMEM)
HBM = pl.BlockSpec(memory_space=pltpu.HBM)
ANY = pl.BlockSpec(memory_space=pl.ANY)


def call(kernel, outs, *args, scratch=(), specs=None, late=0, flops=10**5):
    if specs is None:
        specs = [SMEM] + [VM] * (len(args) - 1 - late) + [ANY] * late
    return pl.pallas_call(
        kernel,
        out_shape=outs,
        in_specs=specs,
        out_specs=jax.tree.map(lambda _: VM, outs),
        scratch_shapes=list(scratch),
        compiler_params=pltpu.CompilerParams(vmem_limit_bytes=40 * 2**20),
        cost_estimate=pl.CostEstimate(flops=flops, bytes_accessed=10**4, transcendentals=0),
    )(*args)


def spread(place, nbt, grad, weight, flops):
    edge = sds((96, C), BF)
    return call(
        spread_kernel,
        (sds((S, C), F32), edge, edge, sds((64, C), BF)),
        place,
        nbt,
        grad,
        weight,
        scratch=[pltpu.VMEM((EXT, C), F32)],
        flops=flops,
    )


def swap(value, axis, turn):
    gx, gy = lax.axis_size("gx"), lax.axis_size("gy")
    pairs = []
    for i in range(gx):
        for j in range(gy):
            n, size = (i, gx) if axis == "gx" else (j, gy)
            q = n ^ 1 if turn == 1 else ((n + 1) ^ 1) - 1
            if axis == "gx":
                to = (q, j) if 0 <= q < size else (i, j ^ 1)
            else:
                to = (i, q) if 0 <= q < size else (i ^ 1, j)
            pairs.append((i * gy + j, to[0] * gy + to[1]))
    return lax.ppermute(value, ("gx", "gy"), pairs)


def cross(value, axis, mask):
    return lax.ppermute(value, axis, [(n, n ^ mask) for n in range(lax.axis_size(axis))])


def gathered(value, axis, base=1):
    return [value] + [cross(value, axis, base * d) for d in (2, 1, 3)]


def halo_lines(m2, m1):
    return swap(m2, "gx", 2), swap(m1, "gx", 1)


def halo_columns(place, loc, m2, m1, late, flops=10**5):
    edge = sds((96, C), BF)
    n2, n1 = call(pass_kernel, (edge, edge), place, loc, m2, m1, late, late=1, flops=flops)
    return n1, swap(n2, "gy", 2), swap(n1, "gy", 1)


def body(features, pre_act, grad_out, weight_one, weight_two, neighbours, halo_list, send_list):
    gx = lax.axis_size("gx")
    scale = 1.0 / math.sqrt(S * gx * lax.axis_size("gy"))
    place = jnp.stack([lax.axis_index("gx"), lax.axis_index("gy")]).astype(jnp.int32)
    tile = sds((S, C), BF)
    pay, p2, p1, p3, nbt, hrow, srow, pre, grad = call(
        pack_kernel,
        (
            *[sds((S + 32, 2 * C), BF)] * 4,
            sds((32, C), F32),
            sds((8, C), jnp.int32),
            sds((8, C), jnp.int32),
            tile,
            tile,
        ),
        place,
        *[
            pltpu.with_memory_space_constraint(value, pltpu.HBM)
            for value in (
                features,
                pre_act,
                grad_out,
                neighbours.T,
                halo_list,
                jnp.transpose(send_list, (2, 0, 1)),
            )
        ],
        specs=[SMEM] + [HBM] * 6,
        flops=4 * 10**9,
        scratch=[
            pltpu.VMEM((K, S), jnp.int32),
            pltpu.VMEM((1, 8, 24), jnp.int32),
            pltpu.VMEM((3, 1, 64), jnp.int32),
            pltpu.VMEM((S, C), BF),
            pltpu.SemaphoreType.DMA((6,)),
        ],
    )
    pays = [pay] + [cross(value, "gy", d) for d, value in ((2, p2), (1, p1), (3, p3))]
    back = pltpu.VMEM((8, HB, C), BF)
    own, m1, m2, loc = spread(place, nbt, grad, weight_two, 10**5)
    m2, m1 = halo_lines(m2, m1)
    passed, n2, n1 = halo_columns(place, loc, m2, m1, own)
    picks = sds((768, C), BF)
    o2, o1, near = call(
        pick_kernel,
        (picks, picks, sds((4, 64, 2 * C), BF)),
        place,
        *pays,
        passed,
        scratch=[pltpu.VMEM((4, 8 * HB, 2 * C), BF)],
        late=1,
    )
    r2, r1 = halo_lines(o2, o1)
    grad_pre, ordered = call(
        gate_kernel,
        (tile, sds((S, 2 * C), BF)),
        place,
        own,
        m2,
        m1,
        n2,
        n1,
        hrow,
        pre,
        grad,
        near,
        scratch=[back],
        late=1,
    )
    grads = gathered(ordered, "gy")
    own, m1, m2, loc = spread(place, nbt, grad_pre, weight_one, 4 * 10**9)
    m2, m1 = halo_lines(m2, m1)
    wide = 7 * C
    stack = sds((4 * S, wide), BF)
    cols_one, cols_two = call(
        columns_kernel,
        (stack, stack),
        place,
        *pays,
        r2,
        r1,
        near,
        own,
        scratch=[
            pltpu.VMEM((EXT, 2 * C), BF),
            pltpu.VMEM((32, C), F32),
            pltpu.VMEM((128, C), F32),
        ],
        late=1,
        flops=4 * 10**9,
    )
    passed, n2, n1 = halo_columns(place, loc, m2, m1, cols_two)

    def halves(which, cols, kind, flops, late):
        lanes = slice(which * C, (which + 1) * C)
        half = sds((128, wide), kind)
        return call(
            functools.partial(weight_kernel, lanes),
            (half, half),
            place,
            *grads,
            cols,
            late,
            scratch=[pltpu.VMEM((C, 4 * S), BF)],
            late=1,
            flops=flops,
        )

    keep_two, send_two = halves(0, cols_two, F32, 4 * 10**9, passed)
    come_two = cross(send_two, "gx", 1)
    keep_one, send_one = halves(1, cols_one, BF, 10**5, keep_two)
    come_one = cross(send_one, "gx", 1)
    some = sds((128, C), BF)
    rows_keep, rows_send = call(
        rows_kernel,
        (some, some),
        place,
        own,
        m2,
        m1,
        n2,
        n1,
        hrow,
        grad,
        srow,
        keep_one,
        scratch=[back],
        late=1,
        flops=2 * 10**10,
    )
    rows_come = cross(rows_send, "gx", 1)

    both = lambda a, b: (cross(a, "gx", 16), cross(b, "gx", 48))
    full = sds((32, wide), F32)
    first = sds((64, HALF), BF)
    *sent, own_two, across = call(
        merge_two_kernel,
        (first, first, full, full),
        place,
        keep_two,
        come_two,
        rows_keep,
        late=1,
    )
    a1, a3 = both(*sent)
    second = sds((32, HALF), BF)
    to3, to1, sum_two = call(
        half_two_kernel, (second, second, full), place, own_two, across, a1, a3, flops=4 * 10**9
    )
    b1, b3 = both(to1, to3)
    sum_two = call(
        line_two_kernel, sds((32, wide), BF), place, sum_two, b3, b1, flops=2 * 10**9
    )
    first = sds((64, HALF + C + 128), BF)
    *sent, own_one, across, mine = call(
        merge_one_kernel,
        (first, first, full, full, sds((32, 2 * C), BF)),
        place,
        keep_one,
        come_one,
        rows_keep,
        rows_come,
        own_two,
        late=1,
        flops=2 * 10**10,
    )
    a1, a3 = both(*sent)
    second = sds((32, HALF + C), BF)
    to3, to1, sum_one = call(
        half_one_kernel, (second, second, full), place, own_one, across, a1, a3
    )
    b1, b3 = both(to1, to3)
    summed = call(
        line_one_kernel,
        sds((64, 10 * C), BF),
        place,
        sum_two,
        sum_one,
        mine,
        a1,
        a3,
        b3,
        b1,
        scratch=[pltpu.VMEM((32, wide), BF)],
    )
    groups = [[16 * y + 2 * z + e for z in range(8)] for y in range(4) for e in range(2)]
    collected = lax.all_to_all(
        summed.reshape(8, 8, 10 * C),
        "gx",
        split_axis=0,
        concat_axis=0,
        tiled=True,
        axis_index_groups=groups,
    )
    out = sds((4, QW), F32)
    return call(
        lambda *refs: final_kernel(scale, *refs), (tile, out, out), collected, specs=[VM]
    )


def solution(mesh):
    in_specs = (
        P(("gx", "gy"), None),
        P(("gx", "gy"), None),
        P(("gx", "gy"), None),
        P(),
        P(),
        P(("gx", "gy"), None),
        P(("gx", "gy"), None, None),
        P(("gx", "gy"), None, None),
    )
    out_specs = (P(("gx", "gy"), None), P("gx", "gy"), P("gx", "gy"))
    return jax.shard_map(body, mesh=mesh, in_specs=in_specs, out_specs=out_specs, check_vma=False)
```

```python
import functools
import math

import jax
import jax.numpy as jnp
from jax import lax
from jax.experimental import pallas as pl
from jax.experimental.pallas import tpu as pltpu
from jax.sharding import PartitionSpec as P

C = 256
K = 27
S = 192
HB = 32
EXT = S + 8 * HB
QW = 1728
HALF = 896
BF = jnp.bfloat16
F32 = jnp.float32


def iota(shape, dim):
    return lax.broadcasted_iota(jnp.int32, shape, dim)


def onehot(mask):
    return jnp.where(mask, 1.0, 0.0).astype(BF)


def mm(a, b):
    return lax.dot_general(a, b, (((1,), (0,)), ((), ())), preferred_element_type=F32)


def mm_t(a, b):
    return lax.dot_general(a, b, (((0,), (0,)), ((), ())), preferred_element_type=F32)


def direction(a, b):
    grid = 3 * (a + 1) + (b + 1)
    return grid - jnp.where(grid > 4, 1, 0)


def channel_order():
    out = iota((C, C), 1)
    parity, rest = out // 128, out % 128
    source = 8 * (rest // 4) + 4 * parity + rest % 4
    return onehot(iota((C, C), 0) == source)


def halo_matrix(halo_row):
    return onehot(iota((S, 8 * HB), 0) == halo_row)


def pack_kernel(
    place, feat, pre, grad, nbr, halo, send, pay, p2, p1, p3, nbt, hrow, srow, pre_out,
    grad_out, ids, halo_ids, send_ids, feat_in, sems
):
    copies = [
        pltpu.make_async_copy(source, target, sems.at[n])
        for n, (source, target) in enumerate(
            (
                (nbr, ids),
                (halo, halo_ids),
                (send, send_ids),
                (feat, feat_in),
                (grad, grad_out),
                (pre, pre_out),
            )
        )
    ]
    for copy in copies:
        copy.start()
    for copy in copies:
        copy.wait()
    table = ids[...].astype(F32)
    heading = jnp.floor((table - S + 0.5) * (1.0 / 24.0))
    table = jnp.where(table >= S, table + 8.0 * heading, table)
    nbt[...] = jnp.full(nbt.shape, -1.0, F32)
    nbt[0:K, 0:S] = table
    shifted_up = table + 1.0
    high = jnp.floor(shifted_up * (1.0 / 16.0))
    tail = jnp.zeros((32, 2 * C), F32)
    z = pre_out[...].astype(F32)
    hidden = (z * (1.0 / (1.0 + jnp.exp(-z)))).astype(BF)
    halo_up = (halo_ids[0] + 1).astype(F32).astype(BF)
    spread = mm(halo_up, onehot(iota((24, 8 * HB), 1) % HB == iota((24, 8 * HB), 0)))
    row = jnp.sum(
        jnp.where(iota((8, 8 * HB), 1) // HB == iota((8, 8 * HB), 0), spread, 0.0),
        axis=0,
        keepdims=True,
    )
    hrow[...] = jnp.broadcast_to(row.astype(jnp.int32) - 1, hrow.shape)
    pay[S : S + 32, :] = tail.astype(BF)
    pay[S : S + K, 0:S] = high.astype(BF)
    pay[S : S + K, C : C + S] = (shifted_up - 16.0 * high).astype(BF)
    last = pay[S + 16 : S + 32, 0:C].astype(F32)
    pay[S + 16 : S + 32, 0:C] = jnp.where(iota((16, C), 0) == 15, row, last).astype(BF)
    both = jnp.concatenate([feat_in[...], hidden], axis=0)
    for turn, out in ((0, pay), (1, p1), (2, p2), (3, p3)):
        offset = ((place[1] ^ turn) * QW) % C
        turned = mm(both, onehot(iota((C, C), 0) == (iota((C, C), 1) + offset) % C)).astype(BF)
        out[0:S, 0:C] = turned[0:S]
        out[0:S, C : 2 * C] = turned[S : 2 * S]
        if turn:
            out[S : S + 32, :] = pay[S : S + 32, :]
    lane, peer = iota((64, C), 1), iota((64, C), 0)
    parity = jnp.where(lane < 128, place[0] % 2, 1 - place[0] % 2)
    pick = onehot(peer == 2 * ((lane % 128) // 4) + parity)
    spot = iota((1, C), 1) % 4
    total = jnp.zeros((1, C), F32)
    for c in range(3):
        up = jnp.broadcast_to((send_ids[c] + 1).astype(F32), (8, 64)).astype(BF)
        total = jnp.where(spot == c, mm(up, pick)[0:1, :], total)
    srow[...] = jnp.broadcast_to(total.astype(jnp.int32) - 1, srow.shape)


def spread_kernel(place, nbt, grad, weight, own, m1, m2, loc, acc):
    rows = iota((EXT, C), 0)
    table = nbt[...].astype(jnp.int32)
    gradient = grad[...]
    none = jnp.zeros((C - S, C), BF)
    masks, terms = [], []
    for k in range(K):
        masks.append(onehot(rows == table[k : k + 1, :]))
        terms += [mm(gradient, weight[:, k * C : (k + 1) * C]).astype(BF), none]
    acc[...] = mm(jnp.concatenate(masks, axis=1), jnp.concatenate(terms, axis=0))
    even = place[0] % 2 == 0
    own[...] = acc[0:S, :]
    first, last = jnp.where(even, S, S + 160), jnp.where(even, S + 160, S)
    m1[...] = acc[pl.ds(pl.multiple_of(first, 32), 96), :].astype(BF)
    m2[...] = acc[pl.ds(pl.multiple_of(last, 32), 96), :].astype(BF)
    loc[...] = acc[S + 96 : S + 160, :].astype(BF)


def inner(position, count):
    return (position > 0) & (position < count - 1)


def masked(keep, rows):
    return jnp.where(keep, rows, jnp.zeros_like(rows))


def pass_kernel(place, loc, m2, m1, late, n2, n1):
    even = place[1] % 2 == 0
    first = jnp.where(even, 0, 1)
    far = inner(place[0], 64)
    for out, side in ((n1, first), (n2, 1 - first)):
        out[0:32, :] = loc[pl.ds(pl.multiple_of(side * 32, 32), 32), :]
        out[32:64, :] = m1[pl.ds(pl.multiple_of(side * 64, 32), 32), :]
        out[64:96, :] = masked(far, m2[pl.ds(pl.multiple_of(side * 64, 32), 32), :])


def settled(place, own, m1, m2, n1, n2, hrow, back):
    da = jnp.where(place[0] % 2 == 0, 1, -1)
    db = jnp.where(place[1] % 2 == 0, 1, -1)
    back[direction(da, 0)] = m1[32:64, :]
    back[direction(-da, 0)] = masked(inner(place[0], 64), m2[32:64, :])
    beside = inner(place[1], 4)
    for ref, side, keep in ((n1, db, True), (n2, -db, beside)):
        rows = ref[...] if keep is True else masked(keep, ref[...])
        back[direction(0, side)] = rows[0:32, :]
        back[direction(da, side)] = rows[32:64, :]
        back[direction(-da, side)] = rows[64:96, :]
    rows = back[...].reshape(8 * HB, C)
    return own[...] + mm(halo_matrix(hrow[0:1, :]), rows)


def gate_kernel(place, own, m2, m1, n2, n1, hrow, pre, grad, late, out, ordered, back):
    hidden_grad = settled(place, own, m1, m2, n1, n2, hrow, back)
    z = pre[...].astype(F32)
    g = 1.0 / (1.0 + jnp.exp(-z))
    value = (hidden_grad * g * (1.0 + z * (1.0 - g))).astype(BF)
    out[...] = value
    order = channel_order()
    ordered[:, 0:C] = mm(grad[...], order).astype(BF)
    ordered[:, C : 2 * C] = mm(value, order).astype(BF)


def rows_kernel(place, own, m2, m1, n2, n1, hrow, grad, srow, late, keep, send, back):
    total = settled(place, own, m1, m2, n1, n2, hrow, back)
    value = (grad[...].astype(F32) + total).astype(BF)
    chosen = mm_t(onehot(iota((S, C), 0) == srow[0:1, :]), value).astype(BF)
    keep[...] = chosen[0:128, :]
    send[...] = chosen[128:256, :]


def pick_kernel(place, p0, p2, p1, p3, late, o2, o1, loc, picked):
    column = place[1]
    for turn, pay in enumerate((p0, p1, p2, p3)):
        halo_row = pay[S + 16 : S + 32, 0:C].astype(F32)[15:16, :].astype(jnp.int32) - 1
        rows = mm_t(halo_matrix(halo_row), pay[0:S, 0 : 2 * C])
        picked[column ^ turn] = rows.astype(BF)
    even = place[0] % 2 == 0
    up = pl.multiple_of(jnp.where(even, 160, 0), 32)
    down = pl.multiple_of(jnp.where(even, 0, 160), 32)
    none = jnp.zeros((HB, 2 * C), BF)
    for tile in range(4):
        for b in (-1, 0, 1):
            source = tile - b
            at = HB * (b + 1)
            for out, side in ((o1, up), (o2, down)):
                rows = picked[source, pl.ds(side + at, HB), :] if 0 <= source < 4 else none
                to = 96 * tile + at
                out[to : to + HB, :] = rows[:, 0:C]
                out[to + 384 : to + 384 + HB, :] = rows[:, C : 2 * C]
            if b:
                to = 0 if b < 0 else HB
                rows = picked[source, 96 + to : 96 + to + HB, :] if 0 <= source < 4 else none
                loc[tile, to : to + HB, :] = rows


def columns_kernel(
    place, p0, p2, p1, p3, r2, r1, loc, late, cols_one, cols_two, ext, ids, sel
):
    column = place[1]
    start = column * QW
    first_k = start // C
    offset = start % C
    even = place[0] % 2 == 0
    far = inner(place[0], 64)
    lane = iota((S, 2 * C), 1) % C
    early = lane < C - offset
    for turn, pay in enumerate((p0, p1, p2, p3)):
        tile = column ^ turn
        for half in range(2):
            lanes = slice(half * C, (half + 1) * C)
            at = pl.multiple_of(384 * half + 96 * tile, 32)
            above, below = r1[pl.ds(at, 96), :], masked(far, r2[pl.ds(at, 96), :])
            for to, piece in (
                (0, pay[0:S, lanes]),
                (S, jnp.where(even, above, below)),
                (S + 96, loc[tile, :, lanes]),
                (S + 160, jnp.where(even, below, above)),
            ):
                ext[to : to + piece.shape[0], lanes] = piece
        high = pay[S : S + 32, 0:C].astype(F32)
        low = pay[S : S + 32, C : 2 * C].astype(F32)
        ids[0:32, :] = 16.0 * high + low - 1.0
        for part in range(8):
            sel[part : part + 1, :] = ids[pl.ds(first_k + part, 1), :]
        table = jnp.transpose(sel[...])[:, 0:8].astype(jnp.int32)
        extended = ext[...]
        match = [
            onehot(iota((S, EXT), 1) == table[0:S, part : part + 1]) for part in range(8)
        ]
        found = mm(jnp.concatenate(match, axis=0), extended).astype(BF)
        for part in range(7):
            merged = jnp.where(
                early, found[part * S : (part + 1) * S], found[(part + 1) * S : (part + 2) * S]
            )
            lanes = slice(part * C, (part + 1) * C)
            cols_one[turn * S : (turn + 1) * S, lanes] = merged[:, 0:C]
            cols_two[turn * S : (turn + 1) * S, lanes] = merged[:, C : 2 * C]


def weight_kernel(lanes, place, g0, g2, g1, g3, cols, late, keep, send, gt):
    for turn, grad in enumerate((g0, g1, g2, g3)):
        gt[:, turn * S : (turn + 1) * S] = jnp.transpose(grad[:, lanes].astype(F32)).astype(BF)
    mine = pl.multiple_of((place[0] % 2) * 128, 128)
    other = pl.multiple_of(128 - mine, 128)
    left = jnp.concatenate([gt[pl.ds(mine, 128), :], gt[pl.ds(other, 128), :]], axis=0)
    for part in range(7):
        lanes = slice(part * C, (part + 1) * C)
        block = mm(left, cols[:, lanes])
        keep[:, lanes] = block[0:128].astype(keep.dtype)
        send[:, lanes] = block[128:256].astype(send.dtype)


def chunk(place, turn):
    return pl.ds(pl.multiple_of(32 * ((place[0] // 16) ^ turn), 32), 32)


def merge_kernel(place, k2, s2, k1, s1, rk, rs, to1, to3, own, across, mine):
    first = place[0] % 2 == 0
    rows = []
    for t in range(4):
        here, other = rk[chunk(place, t), :], rs[chunk(place, t), :]
        rows.append((jnp.where(first, here, other), jnp.where(first, other, here)))
    for at, keep, come in ((0, k2, s2), (1, k1, s1)):
        part = [
            keep[chunk(place, t), :].astype(F32) + come[chunk(place, t), :].astype(F32)
            for t in range(4)
        ]
        lanes = slice(at * HALF, (at + 1) * HALF)
        low, high = slice(0, HALF), slice(HALF, 2 * HALF)
        for out, t, side in ((to1, 1, low), (to3, 3, high)):
            out[0:32, lanes] = part[t][:, side].astype(BF)
            out[32:64, lanes] = part[2][:, side].astype(BF)
        own[at] = part[0]
        across[at, :, low] = part[3][:, low]
        across[at, :, high] = part[1][:, high]
    for out, t, core in ((to1, 1, 0), (to3, 3, 1)):
        out[0:32, 7 * C : 8 * C] = rows[t][0]
        out[32:64, 7 * C : 8 * C] = rows[t][1]
        out[0:32, 8 * C : 8 * C + 128] = rows[2][core][:, 0:128]
        out[32:64, 8 * C : 8 * C + 128] = rows[2][core][:, 128:256]
    mine[:, 0:C] = rows[0][0]
    mine[:, C : 2 * C] = rows[0][1]


def half_kernel(place, own, across, a1, a3, to3, to1, total):
    for out, ref, side in ((to3, a1, slice(0, HALF)), (to1, a3, slice(HALF, 2 * HALF))):
        for at in range(2):
            lanes = slice(at * HALF, (at + 1) * HALF)
            out[:, lanes] = (across[at, :, side] + ref[32:64, lanes].astype(F32)).astype(BF)
            total[at, :, side] = own[at, :, side] + ref[0:32, lanes].astype(F32)
        out[:, 7 * C : 7 * C + 128] = ref[0:32, 8 * C : 8 * C + 128]
        out[:, 7 * C + 128 : 8 * C] = ref[32:64, 8 * C : 8 * C + 128]


def line_kernel(place, total, mine, a1, a3, b3, b1, out, both):
    line = place[0] // 16
    for ref, side in ((b3, slice(0, HALF)), (b1, slice(HALF, 2 * HALF))):
        for at in range(2):
            lanes = slice(at * HALF, (at + 1) * HALF)
            value = total[at, :, side] + ref[:, lanes].astype(F32)
            both[32 * (1 - at) : 32 * (2 - at), side] = value.astype(BF)
    to, at = iota((64, 64), 0), iota((64, 64), 1)
    order = onehot(at == 32 * ((to % 8) // 4) + 4 * (to // 8) + to % 4)
    for n in range(7):
        lanes = slice(n * C, (n + 1) * C)
        out[:, lanes] = mm(order, both[:, lanes]).astype(BF)
    direct = slice(7 * C, 8 * C)
    sources = (
        (0, (mine[:, 0:C], mine[:, C : 2 * C])),
        (1, (a1[0:32, direct], a1[32:64, direct])),
        (2, (b3[:, direct], b1[:, direct])),
        (3, (a3[0:32, direct], a3[32:64, direct])),
    )
    to, at = iota((64, 32), 0), iota((64, 32), 1)
    for n in range(3):
        index = 8 * n + to % 8
        found = jnp.zeros((64, C), F32)
        for turn, cores in sources:
            from_line = (index // 6 == (line ^ turn)) & (at == 4 * (to // 8) + index % 3)
            for core in range(2):
                spot = onehot(from_line & ((index % 6) // 3 == core))
                found = found + mm(spot, cores[core])
        out[:, (7 + n) * C : (8 + n) * C] = found.astype(BF)


def final_kernel(scale, arrived, rows, one, two):
    total = jnp.sum(arrived[:, :, 0 : 7 * C].astype(F32), axis=0) * scale
    one[...] = total[0:4, 0:QW]
    two[...] = total[4:8, 0:QW]
    to, at = iota((S, 64), 0), iota((S, 64), 1)
    value = jnp.zeros((S, C), F32)
    for n in range(3):
        spot = (at // 8 == (to // 6) % 8) & (8 * n + at % 8 == 6 * (to // 48) + to % 6)
        piece = arrived[:, :, (7 + n) * C : (8 + n) * C].reshape(64, C)
        value = value + mm(onehot(spot), piece)
    rows[...] = value.astype(BF)


def sds(shape, dtype):
    return jax.ShapeDtypeStruct(shape, dtype)


SMEM = pl.BlockSpec(memory_space=pltpu.SMEM)
VM = pl.BlockSpec(memory_space=pltpu.VMEM)
HBM = pl.BlockSpec(memory_space=pltpu.HBM)
ANY = pl.BlockSpec(memory_space=pl.ANY)


def call(kernel, outs, *args, scratch=(), specs=None, late=0, flops=10**5):
    if specs is None:
        specs = [SMEM] + [VM] * (len(args) - 1 - late) + [ANY] * late
    return pl.pallas_call(
        kernel,
        out_shape=outs,
        in_specs=specs,
        out_specs=jax.tree.map(lambda _: VM, outs),
        scratch_shapes=list(scratch),
        compiler_params=pltpu.CompilerParams(vmem_limit_bytes=40 * 2**20),
        cost_estimate=pl.CostEstimate(flops=flops, bytes_accessed=10**4, transcendentals=0),
    )(*args)


def spread(place, nbt, grad, weight, flops):
    edge = sds((96, C), BF)
    return call(
        spread_kernel,
        (sds((S, C), F32), edge, edge, sds((64, C), BF)),
        place,
        nbt,
        grad,
        weight,
        scratch=[pltpu.VMEM((EXT, C), F32)],
        flops=flops,
    )


def swap(value, axis, turn):
    gx, gy = lax.axis_size("gx"), lax.axis_size("gy")
    pairs = []
    for i in range(gx):
        for j in range(gy):
            n, size = (i, gx) if axis == "gx" else (j, gy)
            q = n ^ 1 if turn == 1 else ((n + 1) ^ 1) - 1
            if axis == "gx":
                to = (q, j) if 0 <= q < size else (i, j ^ 1)
            else:
                to = (i, q) if 0 <= q < size else (i ^ 1, j)
            pairs.append((i * gy + j, to[0] * gy + to[1]))
    return lax.ppermute(value, ("gx", "gy"), pairs)


def cross(value, axis, mask):
    return lax.ppermute(value, axis, [(n, n ^ mask) for n in range(lax.axis_size(axis))])


def gathered(value, axis, base=1):
    return [value] + [cross(value, axis, base * d) for d in (2, 1, 3)]


def halo_lines(m2, m1):
    return swap(m2, "gx", 2), swap(m1, "gx", 1)


def halo_columns(place, loc, m2, m1, late, flops=10**5):
    edge = sds((96, C), BF)
    n2, n1 = call(pass_kernel, (edge, edge), place, loc, m2, m1, late, late=1, flops=flops)
    return n1, swap(n2, "gy", 2), swap(n1, "gy", 1)


def body(features, pre_act, grad_out, weight_one, weight_two, neighbours, halo_list, send_list):
    gx = lax.axis_size("gx")
    scale = 1.0 / math.sqrt(S * gx * lax.axis_size("gy"))
    place = jnp.stack([lax.axis_index("gx"), lax.axis_index("gy")]).astype(jnp.int32)
    tile = sds((S, C), BF)
    pay, p2, p1, p3, nbt, hrow, srow, pre, grad = call(
        pack_kernel,
        (
            *[sds((S + 32, 2 * C), BF)] * 4,
            sds((32, C), F32),
            sds((8, C), jnp.int32),
            sds((8, C), jnp.int32),
            tile,
            tile,
        ),
        place,
        *[
            pltpu.with_memory_space_constraint(value, pltpu.HBM)
            for value in (
                features,
                pre_act,
                grad_out,
                neighbours.T,
                halo_list,
                jnp.transpose(send_list, (2, 0, 1)),
            )
        ],
        specs=[SMEM] + [HBM] * 6,
        flops=4 * 10**9,
        scratch=[
            pltpu.VMEM((K, S), jnp.int32),
            pltpu.VMEM((1, 8, 24), jnp.int32),
            pltpu.VMEM((3, 1, 64), jnp.int32),
            pltpu.VMEM((S, C), BF),
            pltpu.SemaphoreType.DMA((6,)),
        ],
    )
    pays = [pay] + [cross(value, "gy", d) for d, value in ((2, p2), (1, p1), (3, p3))]
    back = pltpu.VMEM((8, HB, C), BF)
    own, m1, m2, loc = spread(place, nbt, grad, weight_two, 10**5)
    m2, m1 = halo_lines(m2, m1)
    passed, n2, n1 = halo_columns(place, loc, m2, m1, own)
    picks = sds((768, C), BF)
    o2, o1, near = call(
        pick_kernel,
        (picks, picks, sds((4, 64, 2 * C), BF)),
        place,
        *pays,
        passed,
        scratch=[pltpu.VMEM((4, 8 * HB, 2 * C), BF)],
        late=1,
    )
    r2, r1 = halo_lines(o2, o1)
    grad_pre, ordered = call(
        gate_kernel,
        (tile, sds((S, 2 * C), BF)),
        place,
        own,
        m2,
        m1,
        n2,
        n1,
        hrow,
        pre,
        grad,
        near,
        scratch=[back],
        late=1,
    )
    grads = gathered(ordered, "gy")
    own, m1, m2, loc = spread(place, nbt, grad_pre, weight_one, 4 * 10**9)
    m2, m1 = halo_lines(m2, m1)
    wide = 7 * C
    stack = sds((4 * S, wide), BF)
    cols_one, cols_two = call(
        columns_kernel,
        (stack, stack),
        place,
        *pays,
        r2,
        r1,
        near,
        own,
        scratch=[
            pltpu.VMEM((EXT, 2 * C), BF),
            pltpu.VMEM((32, C), F32),
            pltpu.VMEM((128, C), F32),
        ],
        late=1,
        flops=4 * 10**9,
    )
    passed, n2, n1 = halo_columns(place, loc, m2, m1, cols_two)

    def halves(which, cols, kind, flops, late):
        lanes = slice(which * C, (which + 1) * C)
        half = sds((128, wide), kind)
        return call(
            functools.partial(weight_kernel, lanes),
            (half, half),
            place,
            *grads,
            cols,
            late,
            scratch=[pltpu.VMEM((C, 4 * S), BF)],
            late=1,
            flops=flops,
        )

    keep_two, send_two = halves(0, cols_two, F32, 4 * 10**9, passed)
    come_two = cross(send_two, "gx", 1)
    keep_one, send_one = halves(1, cols_one, BF, 10**5, keep_two)
    come_one = cross(send_one, "gx", 1)
    some = sds((128, C), BF)
    rows_keep, rows_send = call(
        rows_kernel,
        (some, some),
        place,
        own,
        m2,
        m1,
        n2,
        n1,
        hrow,
        grad,
        srow,
        keep_one,
        scratch=[back],
        late=1,
        flops=2 * 10**10,
    )
    rows_come = cross(rows_send, "gx", 1)

    both = lambda a, b: (cross(a, "gx", 16), cross(b, "gx", 48))
    step = sds((64, 8 * C + 128), BF)
    full = sds((2, 32, wide), F32)
    to1, to3, own_sum, across, mine = call(
        merge_kernel,
        (step, step, full, full, sds((32, 2 * C), BF)),
        place,
        keep_two,
        come_two,
        keep_one,
        come_one,
        rows_keep,
        rows_come,
    )
    a1, a3 = both(to1, to3)
    step = sds((32, 8 * C), BF)
    to3, to1, total = call(
        half_kernel, (step, step, full), place, own_sum, across, a1, a3
    )
    b1, b3 = both(to1, to3)
    summed = call(
        line_kernel,
        sds((64, 10 * C), BF),
        place,
        total,
        mine,
        a1,
        a3,
        b3,
        b1,
        scratch=[pltpu.VMEM((64, wide), BF)],
    )
    groups = [[16 * y + 2 * z + e for z in range(8)] for y in range(4) for e in range(2)]
    collected = lax.all_to_all(
        summed.reshape(8, 8, 10 * C),
        "gx",
        split_axis=0,
        concat_axis=0,
        tiled=True,
        axis_index_groups=groups,
    )
    out = sds((4, QW), F32)
    return call(
        lambda *refs: final_kernel(scale, *refs), (tile, out, out), collected, specs=[VM]
    )


def solution(mesh):
    in_specs = (
        P(("gx", "gy"), None),
        P(("gx", "gy"), None),
        P(("gx", "gy"), None),
        P(),
        P(),
        P(("gx", "gy"), None),
        P(("gx", "gy"), None, None),
        P(("gx", "gy"), None, None),
    )
    out_specs = (P(("gx", "gy"), None), P("gx", "gy"), P("gx", "gy"))
    return jax.shard_map(body, mesh=mesh, in_specs=in_specs, out_specs=out_specs, check_vma=False)
```

```python
import functools
import math

import jax
import jax.numpy as jnp
from jax import lax
from jax.experimental import pallas as pl
from jax.experimental.pallas import tpu as pltpu
from jax.sharding import PartitionSpec as P

C = 256
K = 27
S = 192
HB = 32
EXT = S + 8 * HB
QW = 1728
HALF = 896
BF = jnp.bfloat16
F32 = jnp.float32


def iota(shape, dim):
    return lax.broadcasted_iota(jnp.int32, shape, dim)


def onehot(mask):
    return jnp.where(mask, 1.0, 0.0).astype(BF)


def mm(a, b):
    return lax.dot_general(a, b, (((1,), (0,)), ((), ())), preferred_element_type=F32)


def mm_t(a, b):
    return lax.dot_general(a, b, (((0,), (0,)), ((), ())), preferred_element_type=F32)


def direction(a, b):
    grid = 3 * (a + 1) + (b + 1)
    return grid - jnp.where(grid > 4, 1, 0)


def channel_order():
    out = iota((C, C), 1)
    parity, rest = out // 128, out % 128
    source = 8 * (rest // 4) + 4 * parity + rest % 4
    return onehot(iota((C, C), 0) == source)


def halo_matrix(halo_row):
    return onehot(iota((S, 8 * HB), 0) == halo_row)


def pack_kernel(
    place, feat, pre, grad, nbr, halo, send, pay, p2, p1, p3, nbt, hrow, srow, pre_out,
    grad_out, ids, halo_ids, send_ids, feat_in, sems
):
    copies = [
        pltpu.make_async_copy(source, target, sems.at[n])
        for n, (source, target) in enumerate(
            (
                (nbr, ids),
                (halo, halo_ids),
                (send, send_ids),
                (feat, feat_in),
                (grad, grad_out),
                (pre, pre_out),
            )
        )
    ]
    for copy in copies:
        copy.start()
    for copy in copies:
        copy.wait()
    table = ids[...].astype(F32)
    heading = jnp.floor((table - S + 0.5) * (1.0 / 24.0))
    table = jnp.where(table >= S, table + 8.0 * heading, table)
    nbt[...] = jnp.full(nbt.shape, -1.0, F32)
    nbt[0:K, 0:S] = table
    shifted_up = table + 1.0
    high = jnp.floor(shifted_up * (1.0 / 16.0))
    tail = jnp.zeros((32, 2 * C), F32)
    z = pre_out[...].astype(F32)
    hidden = (z * (1.0 / (1.0 + jnp.exp(-z)))).astype(BF)
    halo_up = (halo_ids[0] + 1).astype(F32).astype(BF)
    spread = mm(halo_up, onehot(iota((24, 8 * HB), 1) % HB == iota((24, 8 * HB), 0)))
    row = jnp.sum(
        jnp.where(iota((8, 8 * HB), 1) // HB == iota((8, 8 * HB), 0), spread, 0.0),
        axis=0,
        keepdims=True,
    )
    hrow[...] = jnp.broadcast_to(row.astype(jnp.int32) - 1, hrow.shape)
    pay[S : S + 32, :] = tail.astype(BF)
    pay[S : S + K, 0:S] = high.astype(BF)
    pay[S : S + K, C : C + S] = (shifted_up - 16.0 * high).astype(BF)
    last = pay[S + 16 : S + 32, 0:C].astype(F32)
    pay[S + 16 : S + 32, 0:C] = jnp.where(iota((16, C), 0) == 15, row, last).astype(BF)
    both = jnp.concatenate([feat_in[...], hidden], axis=0)
    for turn, out in ((0, pay), (1, p1), (2, p2), (3, p3)):
        offset = ((place[1] ^ turn) * QW) % C
        turned = mm(both, onehot(iota((C, C), 0) == (iota((C, C), 1) + offset) % C)).astype(BF)
        out[0:S, 0:C] = turned[0:S]
        out[0:S, C : 2 * C] = turned[S : 2 * S]
        if turn:
            out[S : S + 32, :] = pay[S : S + 32, :]
    lane, peer = iota((64, C), 1), iota((64, C), 0)
    parity = jnp.where(lane < 128, place[0] % 2, 1 - place[0] % 2)
    pick = onehot(peer == 2 * ((lane % 128) // 4) + parity)
    spot = iota((1, C), 1) % 4
    total = jnp.zeros((1, C), F32)
    for c in range(3):
        up = jnp.broadcast_to((send_ids[c] + 1).astype(F32), (8, 64)).astype(BF)
        total = jnp.where(spot == c, mm(up, pick)[0:1, :], total)
    srow[...] = jnp.broadcast_to(total.astype(jnp.int32) - 1, srow.shape)


def spread_kernel(place, nbt, grad, weight, own, m1, m2, loc, acc):
    rows = iota((EXT, C), 0)
    table = nbt[...].astype(jnp.int32)
    gradient = grad[...]
    none = jnp.zeros((C - S, C), BF)
    masks, terms = [], []
    for k in range(K):
        masks.append(onehot(rows == table[k : k + 1, :]))
        terms += [mm(gradient, weight[:, k * C : (k + 1) * C]).astype(BF), none]
    acc[...] = mm(jnp.concatenate(masks, axis=1), jnp.concatenate(terms, axis=0))
    even = place[0] % 2 == 0
    own[...] = acc[0:S, :]
    first, last = jnp.where(even, S, S + 160), jnp.where(even, S + 160, S)
    m1[...] = acc[pl.ds(pl.multiple_of(first, 32), 96), :].astype(BF)
    m2[...] = acc[pl.ds(pl.multiple_of(last, 32), 96), :].astype(BF)
    loc[...] = acc[S + 96 : S + 160, :].astype(BF)


def inner(position, count):
    return (position > 0) & (position < count - 1)


def masked(keep, rows):
    return jnp.where(keep, rows, jnp.zeros_like(rows))


def pass_kernel(place, loc, m2, m1, late, n2, n1):
    even = place[1] % 2 == 0
    first = jnp.where(even, 0, 1)
    far = inner(place[0], 64)
    for out, side in ((n1, first), (n2, 1 - first)):
        out[0:32, :] = loc[pl.ds(pl.multiple_of(side * 32, 32), 32), :]
        out[32:64, :] = m1[pl.ds(pl.multiple_of(side * 64, 32), 32), :]
        out[64:96, :] = masked(far, m2[pl.ds(pl.multiple_of(side * 64, 32), 32), :])


def settled(place, own, m1, m2, n1, n2, hrow, back):
    da = jnp.where(place[0] % 2 == 0, 1, -1)
    db = jnp.where(place[1] % 2 == 0, 1, -1)
    back[direction(da, 0)] = m1[32:64, :]
    back[direction(-da, 0)] = masked(inner(place[0], 64), m2[32:64, :])
    beside = inner(place[1], 4)
    for ref, side, keep in ((n1, db, True), (n2, -db, beside)):
        rows = ref[...] if keep is True else masked(keep, ref[...])
        back[direction(0, side)] = rows[0:32, :]
        back[direction(da, side)] = rows[32:64, :]
        back[direction(-da, side)] = rows[64:96, :]
    rows = back[...].reshape(8 * HB, C)
    return own[...] + mm(halo_matrix(hrow[0:1, :]), rows)


def gate_kernel(place, own, m2, m1, n2, n1, hrow, pre, grad, late, out, ordered, back):
    hidden_grad = settled(place, own, m1, m2, n1, n2, hrow, back)
    z = pre[...].astype(F32)
    g = 1.0 / (1.0 + jnp.exp(-z))
    value = (hidden_grad * g * (1.0 + z * (1.0 - g))).astype(BF)
    out[...] = value
    order = channel_order()
    ordered[:, 0:C] = mm(grad[...], order).astype(BF)
    ordered[:, C : 2 * C] = mm(value, order).astype(BF)


def rows_kernel(place, own, m2, m1, n2, n1, hrow, grad, srow, late, keep, send, back):
    total = settled(place, own, m1, m2, n1, n2, hrow, back)
    value = (grad[...].astype(F32) + total).astype(BF)
    chosen = mm_t(onehot(iota((S, C), 0) == srow[0:1, :]), value).astype(BF)
    keep[...] = chosen[0:128, :]
    send[...] = chosen[128:256, :]


def pick_kernel(place, p0, p2, p1, p3, late, o2, o1, loc, picked):
    column = place[1]
    for turn, pay in enumerate((p0, p1, p2, p3)):
        halo_row = pay[S + 16 : S + 32, 0:C].astype(F32)[15:16, :].astype(jnp.int32) - 1
        rows = mm_t(halo_matrix(halo_row), pay[0:S, 0 : 2 * C])
        picked[column ^ turn] = rows.astype(BF)
    even = place[0] % 2 == 0
    up = pl.multiple_of(jnp.where(even, 160, 0), 32)
    down = pl.multiple_of(jnp.where(even, 0, 160), 32)
    none = jnp.zeros((HB, 2 * C), BF)
    for tile in range(4):
        for b in (-1, 0, 1):
            source = tile - b
            at = HB * (b + 1)
            for out, side in ((o1, up), (o2, down)):
                rows = picked[source, pl.ds(side + at, HB), :] if 0 <= source < 4 else none
                to = 96 * tile + at
                out[to : to + HB, :] = rows[:, 0:C]
                out[to + 384 : to + 384 + HB, :] = rows[:, C : 2 * C]
            if b:
                to = 0 if b < 0 else HB
                rows = picked[source, 96 + to : 96 + to + HB, :] if 0 <= source < 4 else none
                loc[tile, to : to + HB, :] = rows


def columns_kernel(
    place, p0, p2, p1, p3, r2, r1, loc, late, cols_one, cols_two, ext, ids, sel
):
    column = place[1]
    start = column * QW
    first_k = start // C
    offset = start % C
    even = place[0] % 2 == 0
    far = inner(place[0], 64)
    lane = iota((S, 2 * C), 1) % C
    early = lane < C - offset
    for turn, pay in enumerate((p0, p1, p2, p3)):
        tile = column ^ turn
        for half in range(2):
            lanes = slice(half * C, (half + 1) * C)
            at = pl.multiple_of(384 * half + 96 * tile, 32)
            above, below = r1[pl.ds(at, 96), :], masked(far, r2[pl.ds(at, 96), :])
            for to, piece in (
                (0, pay[0:S, lanes]),
                (S, jnp.where(even, above, below)),
                (S + 96, loc[tile, :, lanes]),
                (S + 160, jnp.where(even, below, above)),
            ):
                ext[to : to + piece.shape[0], lanes] = piece
        high = pay[S : S + 32, 0:C].astype(F32)
        low = pay[S : S + 32, C : 2 * C].astype(F32)
        ids[0:32, :] = 16.0 * high + low - 1.0
        for part in range(8):
            sel[part : part + 1, :] = ids[pl.ds(first_k + part, 1), :]
        table = jnp.transpose(sel[...])[:, 0:8].astype(jnp.int32)
        extended = ext[...]
        match = [
            onehot(iota((S, EXT), 1) == table[0:S, part : part + 1]) for part in range(8)
        ]
        found = mm(jnp.concatenate(match, axis=0), extended).astype(BF)
        for part in range(7):
            merged = jnp.where(
                early, found[part * S : (part + 1) * S], found[(part + 1) * S : (part + 2) * S]
            )
            lanes = slice(part * C, (part + 1) * C)
            cols_one[turn * S : (turn + 1) * S, lanes] = merged[:, 0:C]
            cols_two[turn * S : (turn + 1) * S, lanes] = merged[:, C : 2 * C]


def weight_kernel(lanes, place, g0, g2, g1, g3, cols, late, keep, send, gt):
    for turn, grad in enumerate((g0, g1, g2, g3)):
        gt[:, turn * S : (turn + 1) * S] = jnp.transpose(grad[:, lanes].astype(F32)).astype(BF)
    mine = pl.multiple_of((place[0] % 2) * 128, 128)
    other = pl.multiple_of(128 - mine, 128)
    left = jnp.concatenate([gt[pl.ds(mine, 128), :], gt[pl.ds(other, 128), :]], axis=0)
    for part in range(7):
        lanes = slice(part * C, (part + 1) * C)
        block = mm(left, cols[:, lanes])
        keep[:, lanes] = block[0:128].astype(keep.dtype)
        send[:, lanes] = block[128:256].astype(send.dtype)


def chunk(place, turn):
    return pl.ds(pl.multiple_of(32 * ((place[0] // 16) ^ turn), 32), 32)


def merge_two_kernel(place, keep, come, late, to1, to3, own, across):
    part = [keep[chunk(place, t), :] + come[chunk(place, t), :] for t in range(4)]
    to1[0:32, :] = part[1][:, 0:HALF].astype(BF)
    to1[32:64, :] = part[2][:, 0:HALF].astype(BF)
    to3[0:32, :] = part[3][:, HALF:].astype(BF)
    to3[32:64, :] = part[2][:, HALF:].astype(BF)
    own[...] = part[0]
    across[:, 0:HALF] = part[3][:, 0:HALF]
    across[:, HALF:] = part[1][:, HALF:]


def merge_one_kernel(place, keep, come, rk, rs, late, to1, to3, own, across, mine):
    part = [
        keep[chunk(place, t), :].astype(F32) + come[chunk(place, t), :].astype(F32)
        for t in range(4)
    ]
    first = place[0] % 2 == 0
    rows = []
    for t in range(4):
        here, other = rk[chunk(place, t), :], rs[chunk(place, t), :]
        rows.append((jnp.where(first, here, other), jnp.where(first, other, here)))
    for out, t, lanes, core in ((to1, 1, slice(0, HALF), 0), (to3, 3, slice(HALF, 7 * C), 1)):
        out[0:32, 0:HALF] = part[t][:, lanes].astype(BF)
        out[32:64, 0:HALF] = part[2][:, lanes].astype(BF)
        out[0:32, HALF : HALF + C] = rows[t][0]
        out[32:64, HALF : HALF + C] = rows[t][1]
        out[0:32, HALF + C : HALF + C + 128] = rows[2][core][:, 0:128]
        out[32:64, HALF + C : HALF + C + 128] = rows[2][core][:, 128:256]
    own[...] = part[0]
    across[:, 0:HALF] = part[3][:, 0:HALF]
    across[:, HALF:] = part[1][:, HALF:]
    mine[:, 0:C] = rows[0][0]
    mine[:, C : 2 * C] = rows[0][1]


def half_two_kernel(place, own, across, a1, a3, to3, to1, total):
    to3[...] = (across[:, 0:HALF] + a1[32:64, :].astype(F32)).astype(BF)
    to1[...] = (across[:, HALF:] + a3[32:64, :].astype(F32)).astype(BF)
    total[:, 0:HALF] = own[:, 0:HALF] + a1[0:32, :].astype(F32)
    total[:, HALF:] = own[:, HALF:] + a3[0:32, :].astype(F32)


def half_one_kernel(place, own, across, a1, a3, two3, two1, to3, to1, total):
    for out, ref, two, lanes in (
        (to3, a1, two3, slice(0, HALF)),
        (to1, a3, two1, slice(HALF, 7 * C)),
    ):
        out[:, 0:HALF] = two[...]
        out[:, HALF : 7 * C] = (across[:, lanes] + ref[32:64, 0:HALF].astype(F32)).astype(BF)
        out[:, 7 * C : 7 * C + 128] = ref[0:32, HALF + C : HALF + C + 128]
        out[:, 7 * C + 128 : 8 * C] = ref[32:64, HALF + C : HALF + C + 128]
        total[:, lanes] = own[:, lanes] + ref[0:32, 0:HALF].astype(F32)


def line_kernel(place, sum_two, sum_one, mine, a1, a3, b3, b1, out, two, one):
    line = place[0] // 16
    for at, (total, into) in enumerate(((sum_two, two), (sum_one, one))):
        lanes = slice(at * HALF, (at + 1) * HALF)
        into[:, 0:HALF] = (total[:, 0:HALF] + b3[:, lanes].astype(F32)).astype(BF)
        into[:, HALF:] = (total[:, HALF:] + b1[:, lanes].astype(F32)).astype(BF)
    to, at = iota((64, 32), 0), iota((64, 32), 1)
    spots = [onehot(((to % 8) // 4 == n) & (at == 4 * (to // 8) + to % 4)) for n in range(2)]
    for n in range(7):
        lanes = slice(n * C, (n + 1) * C)
        block = mm(spots[0], one[:, lanes]) + mm(spots[1], two[:, lanes])
        out[:, lanes] = block.astype(BF)
    direct = slice(HALF, HALF + C)
    sources = (
        (0, (mine[:, 0:C], mine[:, C : 2 * C])),
        (1, (a1[0:32, direct], a1[32:64, direct])),
        (2, (b3[:, 7 * C : 8 * C], b1[:, 7 * C : 8 * C])),
        (3, (a3[0:32, direct], a3[32:64, direct])),
    )
    for n in range(3):
        index = 8 * n + to % 8
        found = jnp.zeros((64, C), F32)
        for turn, cores in sources:
            from_line = (index // 6 == (line ^ turn)) & (at == 4 * (to // 8) + index % 3)
            for core in range(2):
                spot = onehot(from_line & ((index % 6) // 3 == core))
                found = found + mm(spot, cores[core])
        out[:, (7 + n) * C : (8 + n) * C] = found.astype(BF)


def final_kernel(scale, arrived, rows, one, two):
    total = jnp.sum(arrived[:, :, 0 : 7 * C].astype(F32), axis=0) * scale
    one[...] = total[0:4, 0:QW]
    two[...] = total[4:8, 0:QW]
    to, at = iota((S, 64), 0), iota((S, 64), 1)
    value = jnp.zeros((S, C), F32)
    for n in range(3):
        spot = (at // 8 == (to // 6) % 8) & (8 * n + at % 8 == 6 * (to // 48) + to % 6)
        piece = arrived[:, :, (7 + n) * C : (8 + n) * C].reshape(64, C)
        value = value + mm(onehot(spot), piece)
    rows[...] = value.astype(BF)


def sds(shape, dtype):
    return jax.ShapeDtypeStruct(shape, dtype)


SMEM = pl.BlockSpec(memory_space=pltpu.SMEM)
VM = pl.BlockSpec(memory_space=pltpu.VMEM)
HBM = pl.BlockSpec(memory_space=pltpu.HBM)
ANY = pl.BlockSpec(memory_space=pl.ANY)


def call(kernel, outs, *args, scratch=(), specs=None, late=0, flops=10**5):
    if specs is None:
        specs = [SMEM] + [VM] * (len(args) - 1 - late) + [ANY] * late
    return pl.pallas_call(
        kernel,
        out_shape=outs,
        in_specs=specs,
        out_specs=jax.tree.map(lambda _: VM, outs),
        scratch_shapes=list(scratch),
        compiler_params=pltpu.CompilerParams(vmem_limit_bytes=40 * 2**20),
        cost_estimate=pl.CostEstimate(flops=flops, bytes_accessed=10**4, transcendentals=0),
    )(*args)


def spread(place, nbt, grad, weight, flops):
    edge = sds((96, C), BF)
    return call(
        spread_kernel,
        (sds((S, C), F32), edge, edge, sds((64, C), BF)),
        place,
        nbt,
        grad,
        weight,
        scratch=[pltpu.VMEM((EXT, C), F32)],
        flops=flops,
    )


def swap(value, axis, turn):
    gx, gy = lax.axis_size("gx"), lax.axis_size("gy")
    pairs = []
    for i in range(gx):
        for j in range(gy):
            n, size = (i, gx) if axis == "gx" else (j, gy)
            q = n ^ 1 if turn == 1 else ((n + 1) ^ 1) - 1
            if axis == "gx":
                to = (q, j) if 0 <= q < size else (i, j ^ 1)
            else:
                to = (i, q) if 0 <= q < size else (i ^ 1, j)
            pairs.append((i * gy + j, to[0] * gy + to[1]))
    return lax.ppermute(value, ("gx", "gy"), pairs)


def cross(value, axis, mask):
    return lax.ppermute(value, axis, [(n, n ^ mask) for n in range(lax.axis_size(axis))])


def gathered(value, axis, base=1):
    return [value] + [cross(value, axis, base * d) for d in (2, 1, 3)]


def halo_lines(m2, m1):
    return swap(m2, "gx", 2), swap(m1, "gx", 1)


def halo_columns(place, loc, m2, m1, late, flops=10**5):
    edge = sds((96, C), BF)
    n2, n1 = call(pass_kernel, (edge, edge), place, loc, m2, m1, late, late=1, flops=flops)
    return n1, swap(n2, "gy", 2), swap(n1, "gy", 1)


def body(features, pre_act, grad_out, weight_one, weight_two, neighbours, halo_list, send_list):
    gx = lax.axis_size("gx")
    scale = 1.0 / math.sqrt(S * gx * lax.axis_size("gy"))
    place = jnp.stack([lax.axis_index("gx"), lax.axis_index("gy")]).astype(jnp.int32)
    tile = sds((S, C), BF)
    pay, p2, p1, p3, nbt, hrow, srow, pre, grad = call(
        pack_kernel,
        (
            *[sds((S + 32, 2 * C), BF)] * 4,
            sds((32, C), F32),
            sds((8, C), jnp.int32),
            sds((8, C), jnp.int32),
            tile,
            tile,
        ),
        place,
        *[
            pltpu.with_memory_space_constraint(value, pltpu.HBM)
            for value in (
                features,
                pre_act,
                grad_out,
                neighbours.T,
                halo_list,
                jnp.transpose(send_list, (2, 0, 1)),
            )
        ],
        specs=[SMEM] + [HBM] * 6,
        flops=4 * 10**9,
        scratch=[
            pltpu.VMEM((K, S), jnp.int32),
            pltpu.VMEM((1, 8, 24), jnp.int32),
            pltpu.VMEM((3, 1, 64), jnp.int32),
            pltpu.VMEM((S, C), BF),
            pltpu.SemaphoreType.DMA((6,)),
        ],
    )
    pays = [pay] + [cross(value, "gy", d) for d, value in ((2, p2), (1, p1), (3, p3))]
    back = pltpu.VMEM((8, HB, C), BF)
    own, m1, m2, loc = spread(place, nbt, grad, weight_two, 10**5)
    m2, m1 = halo_lines(m2, m1)
    passed, n2, n1 = halo_columns(place, loc, m2, m1, own)
    picks = sds((768, C), BF)
    o2, o1, near = call(
        pick_kernel,
        (picks, picks, sds((4, 64, 2 * C), BF)),
        place,
        *pays,
        passed,
        scratch=[pltpu.VMEM((4, 8 * HB, 2 * C), BF)],
        late=1,
    )
    r2, r1 = halo_lines(o2, o1)
    grad_pre, ordered = call(
        gate_kernel,
        (tile, sds((S, 2 * C), BF)),
        place,
        own,
        m2,
        m1,
        n2,
        n1,
        hrow,
        pre,
        grad,
        near,
        scratch=[back],
        late=1,
    )
    grads = gathered(ordered, "gy")
    own, m1, m2, loc = spread(place, nbt, grad_pre, weight_one, 4 * 10**9)
    m2, m1 = halo_lines(m2, m1)
    wide = 7 * C
    stack = sds((4 * S, wide), BF)
    cols_one, cols_two = call(
        columns_kernel,
        (stack, stack),
        place,
        *pays,
        r2,
        r1,
        near,
        own,
        scratch=[
            pltpu.VMEM((EXT, 2 * C), BF),
            pltpu.VMEM((32, C), F32),
            pltpu.VMEM((128, C), F32),
        ],
        late=1,
        flops=4 * 10**9,
    )
    passed, n2, n1 = halo_columns(place, loc, m2, m1, cols_two)

    def halves(which, cols, kind, flops, late):
        lanes = slice(which * C, (which + 1) * C)
        half = sds((128, wide), kind)
        return call(
            functools.partial(weight_kernel, lanes),
            (half, half),
            place,
            *grads,
            cols,
            late,
            scratch=[pltpu.VMEM((C, 4 * S), BF)],
            late=1,
            flops=flops,
        )

    keep_two, send_two = halves(0, cols_two, F32, 4 * 10**9, passed)
    come_two = cross(send_two, "gx", 1)
    keep_one, send_one = halves(1, cols_one, BF, 10**5, keep_two)
    come_one = cross(send_one, "gx", 1)
    some = sds((128, C), BF)
    rows_keep, rows_send = call(
        rows_kernel,
        (some, some),
        place,
        own,
        m2,
        m1,
        n2,
        n1,
        hrow,
        grad,
        srow,
        keep_one,
        scratch=[back],
        late=1,
        flops=2 * 10**10,
    )
    rows_come = cross(rows_send, "gx", 1)

    both = lambda a, b: (cross(a, "gx", 16), cross(b, "gx", 48))
    full = sds((32, wide), F32)
    first = sds((64, HALF), BF)
    *sent, own_two, across = call(
        merge_two_kernel,
        (first, first, full, full),
        place,
        keep_two,
        come_two,
        rows_keep,
        late=1,
    )
    a1, a3 = both(*sent)
    second = sds((32, HALF), BF)
    two3, two1, sum_two = call(
        half_two_kernel, (second, second, full), place, own_two, across, a1, a3, flops=2 * 10**9
    )
    first = sds((64, HALF + C + 128), BF)
    *sent, own_one, across, mine = call(
        merge_one_kernel,
        (first, first, full, full, sds((32, 2 * C), BF)),
        place,
        keep_one,
        come_one,
        rows_keep,
        rows_come,
        own_two,
        late=1,
        flops=2 * 10**10,
    )
    a1, a3 = both(*sent)
    second = sds((32, 8 * C), BF)
    to3, to1, sum_one = call(
        half_one_kernel, (second, second, full), place, own_one, across, a1, a3, two3, two1
    )
    b1, b3 = both(to1, to3)
    summed = call(
        line_kernel,
        sds((64, 10 * C), BF),
        place,
        sum_two,
        sum_one,
        mine,
        a1,
        a3,
        b3,
        b1,
        scratch=[pltpu.VMEM((32, wide), BF)] * 2,
    )
    groups = [[16 * y + 2 * z + e for z in range(8)] for y in range(4) for e in range(2)]
    collected = lax.all_to_all(
        summed.reshape(8, 8, 10 * C),
        "gx",
        split_axis=0,
        concat_axis=0,
        tiled=True,
        axis_index_groups=groups,
    )
    out = sds((4, QW), F32)
    return call(
        lambda *refs: final_kernel(scale, *refs), (tile, out, out), collected, specs=[VM]
    )


def solution(mesh):
    in_specs = (
        P(("gx", "gy"), None),
        P(("gx", "gy"), None),
        P(("gx", "gy"), None),
        P(),
        P(),
        P(("gx", "gy"), None),
        P(("gx", "gy"), None, None),
        P(("gx", "gy"), None, None),
    )
    out_specs = (P(("gx", "gy"), None), P("gx", "gy"), P("gx", "gy"))
    return jax.shard_map(body, mesh=mesh, in_specs=in_specs, out_specs=out_specs, check_vma=False)
```

```python
import functools
import math

import jax
import jax.numpy as jnp
from jax import lax
from jax.experimental import pallas as pl
from jax.experimental.pallas import tpu as pltpu
from jax.sharding import PartitionSpec as P

C = 256
K = 27
S = 192
HB = 32
EXT = S + 8 * HB
QW = 1728
BF = jnp.bfloat16
F32 = jnp.float32


def iota(shape, dim):
    return lax.broadcasted_iota(jnp.int32, shape, dim)


def onehot(mask):
    return jnp.where(mask, 1.0, 0.0).astype(BF)


def mm(a, b):
    return lax.dot_general(a, b, (((1,), (0,)), ((), ())), preferred_element_type=F32)


def mm_t(a, b):
    return lax.dot_general(a, b, (((0,), (0,)), ((), ())), preferred_element_type=F32)


def direction(a, b):
    grid = 3 * (a + 1) + (b + 1)
    return grid - jnp.where(grid > 4, 1, 0)


def channel_order():
    out = iota((C, C), 1)
    parity, rest = out // 128, out % 128
    source = 8 * (rest // 4) + 4 * parity + rest % 4
    return onehot(iota((C, C), 0) == source)


def halo_matrix(halo_row):
    return onehot(iota((S, 8 * HB), 0) == halo_row)


def pack_kernel(
    place, feat, pre, grad, nbr, halo, send, pay, p2, p1, p3, nbt, hrow, srow, pre_out,
    grad_out, ids, halo_ids, send_ids, feat_in, sems
):
    copies = [
        pltpu.make_async_copy(source, target, sems.at[n])
        for n, (source, target) in enumerate(
            (
                (nbr, ids),
                (halo, halo_ids),
                (send, send_ids),
                (feat, feat_in),
                (grad, grad_out),
                (pre, pre_out),
            )
        )
    ]
    for copy in copies:
        copy.start()
    for copy in copies:
        copy.wait()
    table = ids[...].astype(F32)
    heading = jnp.floor((table - S + 0.5) * (1.0 / 24.0))
    table = jnp.where(table >= S, table + 8.0 * heading, table)
    nbt[...] = jnp.full(nbt.shape, -1.0, F32)
    nbt[0:K, 0:S] = table
    shifted_up = table + 1.0
    high = jnp.floor(shifted_up * (1.0 / 16.0))
    tail = jnp.zeros((32, 2 * C), F32)
    z = pre_out[...].astype(F32)
    hidden = (z * (1.0 / (1.0 + jnp.exp(-z)))).astype(BF)
    halo_up = (halo_ids[0] + 1).astype(F32).astype(BF)
    spread = mm(halo_up, onehot(iota((24, 8 * HB), 1) % HB == iota((24, 8 * HB), 0)))
    row = jnp.sum(
        jnp.where(iota((8, 8 * HB), 1) // HB == iota((8, 8 * HB), 0), spread, 0.0),
        axis=0,
        keepdims=True,
    )
    hrow[...] = jnp.broadcast_to(row.astype(jnp.int32) - 1, hrow.shape)
    pay[S : S + 32, :] = tail.astype(BF)
    pay[S : S + K, 0:S] = high.astype(BF)
    pay[S : S + K, C : C + S] = (shifted_up - 16.0 * high).astype(BF)
    last = pay[S + 16 : S + 32, 0:C].astype(F32)
    pay[S + 16 : S + 32, 0:C] = jnp.where(iota((16, C), 0) == 15, row, last).astype(BF)
    both = jnp.concatenate([feat_in[...], hidden], axis=0)
    for turn, out in ((0, pay), (1, p1), (2, p2), (3, p3)):
        offset = ((place[1] ^ turn) * QW) % C
        turned = mm(both, onehot(iota((C, C), 0) == (iota((C, C), 1) + offset) % C)).astype(BF)
        out[0:S, 0:C] = turned[0:S]
        out[0:S, C : 2 * C] = turned[S : 2 * S]
        if turn:
            out[S : S + 32, :] = pay[S : S + 32, :]
    lane, peer = iota((64, C), 1), iota((64, C), 0)
    parity = jnp.where(lane < 128, place[0] % 2, 1 - place[0] % 2)
    pick = onehot(peer == 2 * ((lane % 128) // 4) + parity)
    spot = iota((1, C), 1) % 4
    total = jnp.zeros((1, C), F32)
    for c in range(3):
        up = jnp.broadcast_to((send_ids[c] + 1).astype(F32), (8, 64)).astype(BF)
        total = jnp.where(spot == c, mm(up, pick)[0:1, :], total)
    srow[...] = jnp.broadcast_to(total.astype(jnp.int32) - 1, srow.shape)


def spread_kernel(place, nbt, grad, weight, own, m1, m2, loc, acc):
    rows = iota((EXT, C), 0)
    table = nbt[...].astype(jnp.int32)
    gradient = grad[...]
    none = jnp.zeros((C - S, C), BF)
    masks, terms = [], []
    for k in range(K):
        masks.append(onehot(rows == table[k : k + 1, :]))
        terms += [mm(gradient, weight[:, k * C : (k + 1) * C]).astype(BF), none]
    acc[...] = mm(jnp.concatenate(masks, axis=1), jnp.concatenate(terms, axis=0))
    even = place[0] % 2 == 0
    own[...] = acc[0:S, :]
    first, last = jnp.where(even, S, S + 160), jnp.where(even, S + 160, S)
    m1[...] = acc[pl.ds(pl.multiple_of(first, 32), 96), :].astype(BF)
    m2[...] = acc[pl.ds(pl.multiple_of(last, 32), 96), :].astype(BF)
    loc[...] = acc[S + 96 : S + 160, :].astype(BF)


def inner(position, count):
    return (position > 0) & (position < count - 1)


def masked(keep, rows):
    return jnp.where(keep, rows, jnp.zeros_like(rows))


def pass_kernel(place, loc, m2, m1, late, n2, n1):
    even = place[1] % 2 == 0
    first = jnp.where(even, 0, 1)
    far = inner(place[0], 64)
    for out, side in ((n1, first), (n2, 1 - first)):
        out[0:32, :] = loc[pl.ds(pl.multiple_of(side * 32, 32), 32), :]
        out[32:64, :] = m1[pl.ds(pl.multiple_of(side * 64, 32), 32), :]
        out[64:96, :] = masked(far, m2[pl.ds(pl.multiple_of(side * 64, 32), 32), :])


def settled(place, own, m1, m2, n1, n2, hrow, back):
    da = jnp.where(place[0] % 2 == 0, 1, -1)
    db = jnp.where(place[1] % 2 == 0, 1, -1)
    back[direction(da, 0)] = m1[32:64, :]
    back[direction(-da, 0)] = masked(inner(place[0], 64), m2[32:64, :])
    beside = inner(place[1], 4)
    for ref, side, keep in ((n1, db, True), (n2, -db, beside)):
        rows = ref[...] if keep is True else masked(keep, ref[...])
        back[direction(0, side)] = rows[0:32, :]
        back[direction(da, side)] = rows[32:64, :]
        back[direction(-da, side)] = rows[64:96, :]
    rows = back[...].reshape(8 * HB, C)
    return own[...] + mm(halo_matrix(hrow[0:1, :]), rows)


def gate_kernel(place, own, m2, m1, n2, n1, hrow, pre, grad, late, out, ordered, back):
    hidden_grad = settled(place, own, m1, m2, n1, n2, hrow, back)
    z = pre[...].astype(F32)
    g = 1.0 / (1.0 + jnp.exp(-z))
    value = (hidden_grad * g * (1.0 + z * (1.0 - g))).astype(BF)
    out[...] = value
    order = channel_order()
    ordered[:, 0:C] = mm(grad[...], order).astype(BF)
    ordered[:, C : 2 * C] = mm(value, order).astype(BF)


def rows_kernel(place, own, m2, m1, n2, n1, hrow, grad, srow, late, keep, send, back):
    total = settled(place, own, m1, m2, n1, n2, hrow, back)
    value = (grad[...].astype(F32) + total).astype(BF)
    chosen = mm_t(onehot(iota((S, C), 0) == srow[0:1, :]), value).astype(BF)
    keep[...] = chosen[0:128, :]
    send[...] = chosen[128:256, :]


def pick_kernel(place, p0, p2, p1, p3, late, o2, o1, loc, picked, ids):
    column = place[1]
    pays = (p0, p1, p2, p3)
    for turn, pay in enumerate(pays):
        ids[turn : turn + 1, :] = pay[S + 16 : S + 32, 0:C].astype(F32)[15:16, :] - 1.0
    slots = jnp.transpose(ids[...])[:, 0:8].astype(jnp.int32)
    for turn, pay in enumerate(pays):
        chosen = onehot(iota((8 * HB, S), 1) == slots[:, turn : turn + 1])
        picked[column ^ turn] = mm(chosen, pay[0:S, 0 : 2 * C]).astype(BF)
    even = place[0] % 2 == 0
    up = pl.multiple_of(jnp.where(even, 160, 0), 32)
    down = pl.multiple_of(jnp.where(even, 0, 160), 32)
    none = jnp.zeros((HB, 2 * C), BF)
    for tile in range(4):
        for b in (-1, 0, 1):
            source = tile - b
            at = HB * (b + 1)
            for out, side in ((o1, up), (o2, down)):
                rows = picked[source, pl.ds(side + at, HB), :] if 0 <= source < 4 else none
                to = 96 * tile + at
                out[to : to + HB, :] = rows[:, 0:C]
                out[to + 384 : to + 384 + HB, :] = rows[:, C : 2 * C]
            if b:
                to = 0 if b < 0 else HB
                rows = picked[source, 96 + to : 96 + to + HB, :] if 0 <= source < 4 else none
                loc[tile, to : to + HB, :] = rows


def columns_kernel(
    place, p0, p2, p1, p3, r2, r1, loc, late, cols_one, cols_two, ext, ids, sel
):
    column = place[1]
    start = column * QW
    first_k = start // C
    offset = start % C
    even = place[0] % 2 == 0
    far = inner(place[0], 64)
    lane = iota((S, 2 * C), 1) % C
    early = lane < C - offset
    for turn, pay in enumerate((p0, p1, p2, p3)):
        tile = column ^ turn
        for half in range(2):
            lanes = slice(half * C, (half + 1) * C)
            at = pl.multiple_of(384 * half + 96 * tile, 32)
            above, below = r1[pl.ds(at, 96), :], masked(far, r2[pl.ds(at, 96), :])
            for to, piece in (
                (0, pay[0:S, lanes]),
                (S, jnp.where(even, above, below)),
                (S + 96, loc[tile, :, lanes]),
                (S + 160, jnp.where(even, below, above)),
            ):
                ext[to : to + piece.shape[0], lanes] = piece
        high = pay[S : S + 32, 0:C].astype(F32)
        low = pay[S : S + 32, C : 2 * C].astype(F32)
        ids[0:32, :] = 16.0 * high + low - 1.0
        for part in range(8):
            sel[part : part + 1, :] = ids[pl.ds(first_k + part, 1), :]
        table = jnp.transpose(sel[...])[:, 0:8].astype(jnp.int32)
        extended = ext[...]
        match = [
            onehot(iota((S, EXT), 1) == table[0:S, part : part + 1]) for part in range(8)
        ]
        found = mm(jnp.concatenate(match, axis=0), extended).astype(BF)
        for part in range(7):
            merged = jnp.where(
                early, found[part * S : (part + 1) * S], found[(part + 1) * S : (part + 2) * S]
            )
            lanes = slice(part * C, (part + 1) * C)
            cols_one[turn * S : (turn + 1) * S, lanes] = merged[:, 0:C]
            cols_two[turn * S : (turn + 1) * S, lanes] = merged[:, C : 2 * C]


def weight_kernel(lanes, place, g0, g2, g1, g3, cols, late, keep, send, gt):
    for turn, grad in enumerate((g0, g1, g2, g3)):
        gt[:, turn * S : (turn + 1) * S] = jnp.transpose(grad[:, lanes].astype(F32)).astype(BF)
    mine = pl.multiple_of((place[0] % 2) * 128, 128)
    other = pl.multiple_of(128 - mine, 128)
    left = jnp.concatenate([gt[pl.ds(mine, 128), :], gt[pl.ds(other, 128), :]], axis=0)
    for part in range(7):
        lanes = slice(part * C, (part + 1) * C)
        block = mm(left, cols[:, lanes])
        keep[:, lanes] = block[0:128].astype(keep.dtype)
        send[:, lanes] = block[128:256].astype(send.dtype)


def merge_two_kernel(place, keep, come, late, *outs):
    line = place[0] // 16
    for turn, out in enumerate(outs):
        rows = pl.ds(pl.multiple_of(32 * (line ^ turn), 32), 32)
        out[...] = (keep[rows, :] + come[rows, :]).astype(BF)


def merge_one_kernel(place, keep, come, rk, rs, late, *outs):
    first = place[0] % 2 == 0
    line = place[0] // 16
    for turn, out in enumerate(outs):
        rows = pl.ds(pl.multiple_of(32 * (line ^ turn), 32), 32)
        total = keep[rows, :].astype(F32) + come[rows, :].astype(F32)
        out[:, 0 : 7 * C] = total.astype(BF)
        mine, other = rk[rows, :], rs[rows, :]
        out[:, 7 * C : 8 * C] = jnp.where(first, mine, other)
        out[:, 8 * C : 9 * C] = jnp.where(first, other, mine)


def line_two_kernel(place, a0, a2, a1, a3, out):
    total = a0[...].astype(F32)
    for part in (a1, a2, a3):
        total = total + part[...].astype(F32)
    out[...] = total.astype(BF)


def line_one_kernel(place, two, b0, b2, b1, b3, out):
    line = place[0] // 16
    to, at = iota((64, 64), 0), iota((64, 64), 1)
    order = onehot(at == 32 * ((to % 8) // 4) + 4 * (to // 8) + to % 4)
    for n in range(7):
        lanes = slice(n * C, (n + 1) * C)
        total = b0[:, lanes].astype(F32)
        for part in (b1, b2, b3):
            total = total + part[:, lanes].astype(F32)
        value = jnp.concatenate([total.astype(BF), two[:, lanes]], axis=0)
        out[:, lanes] = mm(order, value).astype(BF)
    sources = [
        part[:, (7 + core) * C : (8 + core) * C] for part in (b0, b1, b2, b3) for core in range(2)
    ]
    stacked = jnp.concatenate(sources, axis=0)
    to, at = iota((64, C), 0), iota((64, C), 1)
    for n in range(3):
        index = 8 * n + to % 8
        spot = (
            (index // 6 == (line ^ (at // 64)))
            & ((index % 6) // 3 == (at // 32) % 2)
            & (at % 32 == 4 * (to // 8) + index % 3)
        )
        out[:, (7 + n) * C : (8 + n) * C] = mm(onehot(spot), stacked).astype(BF)


def final_kernel(scale, arrived, rows, one, two):
    total = jnp.sum(arrived[:, :, 0 : 7 * C].astype(F32), axis=0) * scale
    one[...] = total[0:4, 0:QW]
    two[...] = total[4:8, 0:QW]
    to, at = iota((S, S), 0), iota((S, S), 1)
    spot = ((at % 64) // 8 == (to // 6) % 8) & (
        8 * (at // 64) + at % 8 == 6 * (to // 48) + to % 6
    )
    pieces = [arrived[:, :, (7 + n) * C : (8 + n) * C].reshape(64, C) for n in range(3)]
    rows[...] = mm(onehot(spot), jnp.concatenate(pieces, axis=0)).astype(BF)


def sds(shape, dtype):
    return jax.ShapeDtypeStruct(shape, dtype)


SMEM = pl.BlockSpec(memory_space=pltpu.SMEM)
VM = pl.BlockSpec(memory_space=pltpu.VMEM)
HBM = pl.BlockSpec(memory_space=pltpu.HBM)
ANY = pl.BlockSpec(memory_space=pl.ANY)


def call(kernel, outs, *args, scratch=(), specs=None, late=0, flops=10**5):
    if specs is None:
        specs = [SMEM] + [VM] * (len(args) - 1 - late) + [ANY] * late
    return pl.pallas_call(
        kernel,
        out_shape=outs,
        in_specs=specs,
        out_specs=jax.tree.map(lambda _: VM, outs),
        scratch_shapes=list(scratch),
        compiler_params=pltpu.CompilerParams(vmem_limit_bytes=40 * 2**20),
        cost_estimate=pl.CostEstimate(flops=flops, bytes_accessed=10**4, transcendentals=0),
    )(*args)


def spread(place, nbt, grad, weight, flops):
    edge = sds((96, C), BF)
    return call(
        spread_kernel,
        (sds((S, C), F32), edge, edge, sds((64, C), BF)),
        place,
        nbt,
        grad,
        weight,
        scratch=[pltpu.VMEM((EXT, C), F32)],
        flops=flops,
    )


def swap(value, axis, turn):
    gx, gy = lax.axis_size("gx"), lax.axis_size("gy")
    pairs = []
    for i in range(gx):
        for j in range(gy):
            n, size = (i, gx) if axis == "gx" else (j, gy)
            q = n ^ 1 if turn == 1 else ((n + 1) ^ 1) - 1
            if axis == "gx":
                to = (q, j) if 0 <= q < size else (i, j ^ 1)
            else:
                to = (i, q) if 0 <= q < size else (i ^ 1, j)
            pairs.append((i * gy + j, to[0] * gy + to[1]))
    return lax.ppermute(value, ("gx", "gy"), pairs)


def cross(value, axis, mask):
    return lax.ppermute(value, axis, [(n, n ^ mask) for n in range(lax.axis_size(axis))])


def gathered(value, axis, base=1):
    return [value] + [cross(value, axis, base * d) for d in (2, 1, 3)]


def halo_lines(m2, m1):
    return swap(m2, "gx", 2), swap(m1, "gx", 1)


def halo_columns(place, loc, m2, m1, late, flops=10**5):
    edge = sds((96, C), BF)
    n2, n1 = call(pass_kernel, (edge, edge), place, loc, m2, m1, late, late=1, flops=flops)
    return n1, swap(n2, "gy", 2), swap(n1, "gy", 1)


def body(features, pre_act, grad_out, weight_one, weight_two, neighbours, halo_list, send_list):
    gx = lax.axis_size("gx")
    scale = 1.0 / math.sqrt(S * gx * lax.axis_size("gy"))
    place = jnp.stack([lax.axis_index("gx"), lax.axis_index("gy")]).astype(jnp.int32)
    tile = sds((S, C), BF)
    pay, p2, p1, p3, nbt, hrow, srow, pre, grad = call(
        pack_kernel,
        (
            *[sds((S + 32, 2 * C), BF)] * 4,
            sds((32, C), F32),
            sds((8, C), jnp.int32),
            sds((8, C), jnp.int32),
            tile,
            tile,
        ),
        place,
        *[
            pltpu.with_memory_space_constraint(value, pltpu.HBM)
            for value in (
                features,
                pre_act,
                grad_out,
                neighbours.T,
                halo_list,
                jnp.transpose(send_list, (2, 0, 1)),
            )
        ],
        specs=[SMEM] + [HBM] * 6,
        flops=4 * 10**9,
        scratch=[
            pltpu.VMEM((K, S), jnp.int32),
            pltpu.VMEM((1, 8, 24), jnp.int32),
            pltpu.VMEM((3, 1, 64), jnp.int32),
            pltpu.VMEM((S, C), BF),
            pltpu.SemaphoreType.DMA((6,)),
        ],
    )
    pays = [pay] + [cross(value, "gy", d) for d, value in ((2, p2), (1, p1), (3, p3))]
    back = pltpu.VMEM((8, HB, C), BF)
    own, m1, m2, loc = spread(place, nbt, grad, weight_two, 10**5)
    m2, m1 = halo_lines(m2, m1)
    passed, n2, n1 = halo_columns(place, loc, m2, m1, own)
    picks = sds((768, C), BF)
    o2, o1, near = call(
        pick_kernel,
        (picks, picks, sds((4, 64, 2 * C), BF)),
        place,
        *pays,
        passed,
        scratch=[pltpu.VMEM((4, 8 * HB, 2 * C), BF), pltpu.VMEM((128, C), F32)],
        late=1,
    )
    r2, r1 = halo_lines(o2, o1)
    grad_pre, ordered = call(
        gate_kernel,
        (tile, sds((S, 2 * C), BF)),
        place,
        own,
        m2,
        m1,
        n2,
        n1,
        hrow,
        pre,
        grad,
        near,
        scratch=[back],
        late=1,
    )
    grads = gathered(ordered, "gy")
    own, m1, m2, loc = spread(place, nbt, grad_pre, weight_one, 4 * 10**9)
    m2, m1 = halo_lines(m2, m1)
    wide = 7 * C
    stack = sds((4 * S, wide), BF)
    cols_one, cols_two = call(
        columns_kernel,
        (stack, stack),
        place,
        *pays,
        r2,
        r1,
        near,
        own,
        scratch=[
            pltpu.VMEM((EXT, 2 * C), BF),
            pltpu.VMEM((32, C), F32),
            pltpu.VMEM((128, C), F32),
        ],
        late=1,
        flops=4 * 10**9,
    )
    passed, n2, n1 = halo_columns(place, loc, m2, m1, cols_two)

    def halves(which, cols, kind, flops, late):
        lanes = slice(which * C, (which + 1) * C)
        half = sds((128, wide), kind)
        return call(
            functools.partial(weight_kernel, lanes),
            (half, half),
            place,
            *grads,
            cols,
            late,
            scratch=[pltpu.VMEM((C, 4 * S), BF)],
            late=1,
            flops=flops,
        )

    keep_two, send_two = halves(0, cols_two, F32, 4 * 10**9, passed)
    come_two = cross(send_two, "gx", 1)
    keep_one, send_one = halves(1, cols_one, BF, 10**5, keep_two)
    come_one = cross(send_one, "gx", 1)
    some = sds((128, C), BF)
    rows_keep, rows_send = call(
        rows_kernel,
        (some, some),
        place,
        own,
        m2,
        m1,
        n2,
        n1,
        hrow,
        grad,
        srow,
        keep_one,
        scratch=[back],
        late=1,
        flops=2 * 10**10,
    )
    rows_come = cross(rows_send, "gx", 1)

    def lines(chunks):
        return [chunks[0]] + [cross(chunks[d], "gx", 16 * d) for d in (2, 1, 3)]

    two = call(
        merge_two_kernel,
        (sds((32, wide), BF),) * 4,
        place,
        keep_two,
        come_two,
        rows_keep,
        late=1,
    )
    one = call(
        merge_one_kernel,
        (sds((32, 9 * C), BF),) * 4,
        place,
        keep_one,
        come_one,
        rows_keep,
        rows_come,
        two[0],
        late=1,
        flops=2 * 10**10,
    )
    sum_two = call(
        line_two_kernel, sds((32, wide), BF), place, *lines(two), flops=2 * 10**10
    )
    summed = call(line_one_kernel, sds((64, 10 * C), BF), place, sum_two, *lines(one))
    groups = [[16 * y + 2 * z + e for z in range(8)] for y in range(4) for e in range(2)]
    collected = lax.all_to_all(
        summed.reshape(8, 8, 10 * C),
        "gx",
        split_axis=0,
        concat_axis=0,
        tiled=True,
        axis_index_groups=groups,
    )
    out = sds((4, QW), F32)
    return call(
        lambda *refs: final_kernel(scale, *refs), (tile, out, out), collected, specs=[VM]
    )


def solution(mesh):
    in_specs = (
        P(("gx", "gy"), None),
        P(("gx", "gy"), None),
        P(("gx", "gy"), None),
        P(),
        P(),
        P(("gx", "gy"), None),
        P(("gx", "gy"), None, None),
        P(("gx", "gy"), None, None),
    )
    out_specs = (P(("gx", "gy"), None), P("gx", "gy"), P("gx", "gy"))
    return jax.shard_map(body, mesh=mesh, in_specs=in_specs, out_specs=out_specs, check_vma=False)
```

```python
import functools
import math

import jax
import jax.numpy as jnp
from jax import lax
from jax.experimental import pallas as pl
from jax.experimental.pallas import tpu as pltpu
from jax.sharding import PartitionSpec as P

C = 256
K = 27
S = 192
HB = 32
EXT = S + 8 * HB
QW = 1728
BF = jnp.bfloat16
F32 = jnp.float32


def iota(shape, dim):
    return lax.broadcasted_iota(jnp.int32, shape, dim)


def onehot(mask):
    return jnp.where(mask, 1.0, 0.0).astype(BF)


def mm(a, b):
    return lax.dot_general(a, b, (((1,), (0,)), ((), ())), preferred_element_type=F32)


def mm_t(a, b):
    return lax.dot_general(a, b, (((0,), (0,)), ((), ())), preferred_element_type=F32)


def direction(a, b):
    grid = 3 * (a + 1) + (b + 1)
    return grid - jnp.where(grid > 4, 1, 0)


def channel_order():
    out = iota((C, C), 1)
    parity, rest = out // 128, out % 128
    source = 8 * (rest // 4) + 4 * parity + rest % 4
    return onehot(iota((C, C), 0) == source)


def halo_matrix(halo_row):
    return onehot(iota((S, 8 * HB), 0) == halo_row)


def turn_channels(column, both):
    offset = (column * QW) % C
    return mm(both[...], onehot(iota((C, C), 0) == (iota((C, C), 1) + offset) % C)).astype(BF)


def peers_kernel(place, pay, both, p2, p1, p3):
    for turn, out in ((2, p2), (1, p1), (3, p3)):
        turned = turn_channels(place[1] ^ turn, both)
        out[0:S, 0:C] = turned[0:S]
        out[0:S, C : 2 * C] = turned[S : 2 * S]
        out[S : S + 32, :] = pay[S : S + 32, :]


def pack_kernel(
    place, feat, pre, grad, nbr, halo, send, pay, both, nbt, hrow, srow, pre_out, grad_out,
    ids, halo_ids, send_ids, feat_in, sems
):
    copies = [
        pltpu.make_async_copy(source, target, sems.at[n])
        for n, (source, target) in enumerate(
            (
                (nbr, ids),
                (halo, halo_ids),
                (send, send_ids),
                (feat, feat_in),
                (grad, grad_out),
                (pre, pre_out),
            )
        )
    ]
    for copy in copies:
        copy.start()
    for copy in copies:
        copy.wait()
    table = ids[...].astype(F32)
    heading = jnp.floor((table - S + 0.5) * (1.0 / 24.0))
    table = jnp.where(table >= S, table + 8.0 * heading, table)
    nbt[...] = jnp.full(nbt.shape, -1.0, F32)
    nbt[0:K, 0:S] = table
    shifted_up = table + 1.0
    high = jnp.floor(shifted_up * (1.0 / 16.0))
    tail = jnp.zeros((32, 2 * C), F32)
    z = pre_out[...].astype(F32)
    hidden = (z * (1.0 / (1.0 + jnp.exp(-z)))).astype(BF)
    halo_up = (halo_ids[0] + 1).astype(F32).astype(BF)
    spread = mm(halo_up, onehot(iota((24, 8 * HB), 1) % HB == iota((24, 8 * HB), 0)))
    row = jnp.sum(
        jnp.where(iota((8, 8 * HB), 1) // HB == iota((8, 8 * HB), 0), spread, 0.0),
        axis=0,
        keepdims=True,
    )
    hrow[...] = jnp.broadcast_to(row.astype(jnp.int32) - 1, hrow.shape)
    pay[S : S + 32, :] = tail.astype(BF)
    pay[S : S + K, 0:S] = high.astype(BF)
    pay[S : S + K, C : C + S] = (shifted_up - 16.0 * high).astype(BF)
    last = pay[S + 16 : S + 32, 0:C].astype(F32)
    pay[S + 16 : S + 32, 0:C] = jnp.where(iota((16, C), 0) == 15, row, last).astype(BF)
    both[0:S, :] = feat_in[...]
    both[S : 2 * S, :] = hidden
    turned = turn_channels(place[1], both)
    pay[0:S, 0:C] = turned[0:S]
    pay[0:S, C : 2 * C] = turned[S : 2 * S]
    lane, peer = iota((64, C), 1), iota((64, C), 0)
    parity = jnp.where(lane < 128, place[0] % 2, 1 - place[0] % 2)
    pick = onehot(peer == 2 * ((lane % 128) // 4) + parity)
    spot = iota((1, C), 1) % 4
    total = jnp.zeros((1, C), F32)
    for c in range(3):
        up = jnp.broadcast_to((send_ids[c] + 1).astype(F32), (8, 64)).astype(BF)
        total = jnp.where(spot == c, mm(up, pick)[0:1, :], total)
    srow[...] = jnp.broadcast_to(total.astype(jnp.int32) - 1, srow.shape)


def spread_kernel(place, nbt, grad, weight, own, m1, m2, loc, acc):
    rows = iota((EXT, C), 0)
    table = nbt[...].astype(jnp.int32)
    gradient = grad[...]
    none = jnp.zeros((C - S, C), BF)
    masks, terms = [], []
    for k in range(K):
        masks.append(onehot(rows == table[k : k + 1, :]))
        terms += [mm(gradient, weight[:, k * C : (k + 1) * C]).astype(BF), none]
    acc[...] = mm(jnp.concatenate(masks, axis=1), jnp.concatenate(terms, axis=0))
    even = place[0] % 2 == 0
    own[...] = acc[0:S, :]
    first, last = jnp.where(even, S, S + 160), jnp.where(even, S + 160, S)
    m1[...] = acc[pl.ds(pl.multiple_of(first, 32), 96), :].astype(BF)
    m2[...] = acc[pl.ds(pl.multiple_of(last, 32), 96), :].astype(BF)
    loc[...] = acc[S + 96 : S + 160, :].astype(BF)


def inner(position, count):
    return (position > 0) & (position < count - 1)


def masked(keep, rows):
    return jnp.where(keep, rows, jnp.zeros_like(rows))


def pass_kernel(place, loc, m2, m1, late, n2, n1):
    even = place[1] % 2 == 0
    first = jnp.where(even, 0, 1)
    far = inner(place[0], 64)
    for out, side in ((n1, first), (n2, 1 - first)):
        out[0:32, :] = loc[pl.ds(pl.multiple_of(side * 32, 32), 32), :]
        out[32:64, :] = m1[pl.ds(pl.multiple_of(side * 64, 32), 32), :]
        out[64:96, :] = masked(far, m2[pl.ds(pl.multiple_of(side * 64, 32), 32), :])


def settled(place, own, m1, m2, n1, n2, hrow, back):
    da = jnp.where(place[0] % 2 == 0, 1, -1)
    db = jnp.where(place[1] % 2 == 0, 1, -1)
    back[direction(da, 0)] = m1[32:64, :]
    back[direction(-da, 0)] = masked(inner(place[0], 64), m2[32:64, :])
    beside = inner(place[1], 4)
    for ref, side, keep in ((n1, db, True), (n2, -db, beside)):
        rows = ref[...] if keep is True else masked(keep, ref[...])
        back[direction(0, side)] = rows[0:32, :]
        back[direction(da, side)] = rows[32:64, :]
        back[direction(-da, side)] = rows[64:96, :]
    rows = back[...].reshape(8 * HB, C)
    return own[...] + mm(halo_matrix(hrow[0:1, :]), rows)


def gate_kernel(place, own, m2, m1, n2, n1, hrow, pre, grad, late, out, ordered, back):
    hidden_grad = settled(place, own, m1, m2, n1, n2, hrow, back)
    z = pre[...].astype(F32)
    g = 1.0 / (1.0 + jnp.exp(-z))
    value = (hidden_grad * g * (1.0 + z * (1.0 - g))).astype(BF)
    out[...] = value
    order = channel_order()
    ordered[:, 0:C] = mm(grad[...], order).astype(BF)
    ordered[:, C : 2 * C] = mm(value, order).astype(BF)


def rows_kernel(place, own, m2, m1, n2, n1, hrow, grad, srow, late, keep, send, back):
    total = settled(place, own, m1, m2, n1, n2, hrow, back)
    value = (grad[...].astype(F32) + total).astype(BF)
    chosen = mm_t(onehot(iota((S, C), 0) == srow[0:1, :]), value).astype(BF)
    keep[...] = chosen[0:128, :]
    send[...] = chosen[128:256, :]


def pick_kernel(place, p0, p2, p1, p3, late, o2, o1, loc, picked):
    column = place[1]
    for turn, pay in enumerate((p0, p1, p2, p3)):
        halo_row = pay[S + 16 : S + 32, 0:C].astype(F32)[15:16, :].astype(jnp.int32) - 1
        rows = mm_t(halo_matrix(halo_row), pay[0:S, 0 : 2 * C])
        picked[column ^ turn] = rows.astype(BF)
    even = place[0] % 2 == 0
    up = pl.multiple_of(jnp.where(even, 160, 0), 32)
    down = pl.multiple_of(jnp.where(even, 0, 160), 32)
    none = jnp.zeros((HB, 2 * C), BF)
    for tile in range(4):
        for b in (-1, 0, 1):
            source = tile - b
            at = HB * (b + 1)
            for out, side in ((o1, up), (o2, down)):
                rows = picked[source, pl.ds(side + at, HB), :] if 0 <= source < 4 else none
                to = 96 * tile + at
                out[to : to + HB, :] = rows[:, 0:C]
                out[to + 384 : to + 384 + HB, :] = rows[:, C : 2 * C]
            if b:
                to = 0 if b < 0 else HB
                rows = picked[source, 96 + to : 96 + to + HB, :] if 0 <= source < 4 else none
                loc[tile, to : to + HB, :] = rows


def columns_kernel(
    place, p0, p2, p1, p3, r2, r1, loc, late, cols_one, cols_two, ext, ids, sel
):
    column = place[1]
    start = column * QW
    first_k = start // C
    offset = start % C
    even = place[0] % 2 == 0
    far = inner(place[0], 64)
    lane = iota((S, 2 * C), 1) % C
    early = lane < C - offset
    for turn, pay in enumerate((p0, p1, p2, p3)):
        tile = column ^ turn
        for half in range(2):
            lanes = slice(half * C, (half + 1) * C)
            at = pl.multiple_of(384 * half + 96 * tile, 32)
            above, below = r1[pl.ds(at, 96), :], masked(far, r2[pl.ds(at, 96), :])
            for to, piece in (
                (0, pay[0:S, lanes]),
                (S, jnp.where(even, above, below)),
                (S + 96, loc[tile, :, lanes]),
                (S + 160, jnp.where(even, below, above)),
            ):
                ext[to : to + piece.shape[0], lanes] = piece
        high = pay[S : S + 32, 0:C].astype(F32)
        low = pay[S : S + 32, C : 2 * C].astype(F32)
        ids[0:32, :] = 16.0 * high + low - 1.0
        for part in range(8):
            sel[part : part + 1, :] = ids[pl.ds(first_k + part, 1), :]
        table = jnp.transpose(sel[...])[:, 0:8].astype(jnp.int32)
        extended = ext[...]
        match = [
            onehot(iota((S, EXT), 1) == table[0:S, part : part + 1]) for part in range(8)
        ]
        found = mm(jnp.concatenate(match, axis=0), extended).astype(BF)
        for part in range(7):
            merged = jnp.where(
                early, found[part * S : (part + 1) * S], found[(part + 1) * S : (part + 2) * S]
            )
            lanes = slice(part * C, (part + 1) * C)
            cols_one[turn * S : (turn + 1) * S, lanes] = merged[:, 0:C]
            cols_two[turn * S : (turn + 1) * S, lanes] = merged[:, C : 2 * C]


def weight_kernel(lanes, place, g0, g2, g1, g3, cols, late, keep, send, gt):
    for turn, grad in enumerate((g0, g1, g2, g3)):
        gt[:, turn * S : (turn + 1) * S] = jnp.transpose(grad[:, lanes].astype(F32)).astype(BF)
    mine = pl.multiple_of((place[0] % 2) * 128, 128)
    other = pl.multiple_of(128 - mine, 128)
    left = jnp.concatenate([gt[pl.ds(mine, 128), :], gt[pl.ds(other, 128), :]], axis=0)
    for part in range(7):
        lanes = slice(part * C, (part + 1) * C)
        block = mm(left, cols[:, lanes])
        keep[:, lanes] = block[0:128].astype(keep.dtype)
        send[:, lanes] = block[128:256].astype(send.dtype)


def merge_two_kernel(place, keep, come, late, *outs):
    line = place[0] // 16
    for turn, out in enumerate(outs):
        rows = pl.ds(pl.multiple_of(32 * (line ^ turn), 32), 32)
        out[...] = (keep[rows, :] + come[rows, :]).astype(BF)


def merge_one_kernel(place, keep, come, rk, rs, late, *outs):
    first = place[0] % 2 == 0
    line = place[0] // 16
    for turn, out in enumerate(outs):
        rows = pl.ds(pl.multiple_of(32 * (line ^ turn), 32), 32)
        total = keep[rows, :].astype(F32) + come[rows, :].astype(F32)
        out[:, 0 : 7 * C] = total.astype(BF)
        mine, other = rk[rows, :], rs[rows, :]
        out[:, 7 * C : 8 * C] = jnp.where(first, mine, other)
        out[:, 8 * C : 9 * C] = jnp.where(first, other, mine)


def line_two_kernel(place, a0, a2, a1, a3, out):
    total = a0[...].astype(F32)
    for part in (a1, a2, a3):
        total = total + part[...].astype(F32)
    out[...] = total.astype(BF)


def line_one_kernel(place, two, b0, b2, b1, b3, out):
    line = place[0] // 16
    to, at = iota((64, 64), 0), iota((64, 64), 1)
    order = onehot(at == 32 * ((to % 8) // 4) + 4 * (to // 8) + to % 4)
    for n in range(7):
        lanes = slice(n * C, (n + 1) * C)
        total = b0[:, lanes].astype(F32)
        for part in (b1, b2, b3):
            total = total + part[:, lanes].astype(F32)
        value = jnp.concatenate([total.astype(BF), two[:, lanes]], axis=0)
        out[:, lanes] = mm(order, value).astype(BF)
    sources = [
        part[:, (7 + core) * C : (8 + core) * C] for part in (b0, b1, b2, b3) for core in range(2)
    ]
    stacked = jnp.concatenate(sources, axis=0)
    to, at = iota((64, C), 0), iota((64, C), 1)
    for n in range(3):
        index = 8 * n + to % 8
        spot = (
            (index // 6 == (line ^ (at // 64)))
            & ((index % 6) // 3 == (at // 32) % 2)
            & (at % 32 == 4 * (to // 8) + index % 3)
        )
        out[:, (7 + n) * C : (8 + n) * C] = mm(onehot(spot), stacked).astype(BF)


def final_kernel(scale, arrived, rows, one, two):
    total = jnp.sum(arrived[:, :, 0 : 7 * C].astype(F32), axis=0) * scale
    one[...] = total[0:4, 0:QW]
    two[...] = total[4:8, 0:QW]
    to, at = iota((S, S), 0), iota((S, S), 1)
    spot = ((at % 64) // 8 == (to // 6) % 8) & (
        8 * (at // 64) + at % 8 == 6 * (to // 48) + to % 6
    )
    pieces = [arrived[:, :, (7 + n) * C : (8 + n) * C].reshape(64, C) for n in range(3)]
    rows[...] = mm(onehot(spot), jnp.concatenate(pieces, axis=0)).astype(BF)


def sds(shape, dtype):
    return jax.ShapeDtypeStruct(shape, dtype)


SMEM = pl.BlockSpec(memory_space=pltpu.SMEM)
VM = pl.BlockSpec(memory_space=pltpu.VMEM)
HBM = pl.BlockSpec(memory_space=pltpu.HBM)
ANY = pl.BlockSpec(memory_space=pl.ANY)


def call(kernel, outs, *args, scratch=(), specs=None, late=0, flops=10**5):
    if specs is None:
        specs = [SMEM] + [VM] * (len(args) - 1 - late) + [ANY] * late
    return pl.pallas_call(
        kernel,
        out_shape=outs,
        in_specs=specs,
        out_specs=jax.tree.map(lambda _: VM, outs),
        scratch_shapes=list(scratch),
        compiler_params=pltpu.CompilerParams(vmem_limit_bytes=40 * 2**20),
        cost_estimate=pl.CostEstimate(flops=flops, bytes_accessed=10**4, transcendentals=0),
    )(*args)


def spread(place, nbt, grad, weight, flops):
    edge = sds((96, C), BF)
    return call(
        spread_kernel,
        (sds((S, C), F32), edge, edge, sds((64, C), BF)),
        place,
        nbt,
        grad,
        weight,
        scratch=[pltpu.VMEM((EXT, C), F32)],
        flops=flops,
    )


def swap(value, axis, turn):
    gx, gy = lax.axis_size("gx"), lax.axis_size("gy")
    pairs = []
    for i in range(gx):
        for j in range(gy):
            n, size = (i, gx) if axis == "gx" else (j, gy)
            q = n ^ 1 if turn == 1 else ((n + 1) ^ 1) - 1
            if axis == "gx":
                to = (q, j) if 0 <= q < size else (i, j ^ 1)
            else:
                to = (i, q) if 0 <= q < size else (i ^ 1, j)
            pairs.append((i * gy + j, to[0] * gy + to[1]))
    return lax.ppermute(value, ("gx", "gy"), pairs)


def cross(value, axis, mask):
    return lax.ppermute(value, axis, [(n, n ^ mask) for n in range(lax.axis_size(axis))])


def gathered(value, axis, base=1):
    return [value] + [cross(value, axis, base * d) for d in (2, 1, 3)]


def halo_lines(m2, m1):
    return swap(m2, "gx", 2), swap(m1, "gx", 1)


def halo_columns(place, loc, m2, m1, late, flops=10**5):
    edge = sds((96, C), BF)
    n2, n1 = call(pass_kernel, (edge, edge), place, loc, m2, m1, late, late=1, flops=flops)
    return n1, swap(n2, "gy", 2), swap(n1, "gy", 1)


def body(features, pre_act, grad_out, weight_one, weight_two, neighbours, halo_list, send_list):
    gx = lax.axis_size("gx")
    scale = 1.0 / math.sqrt(S * gx * lax.axis_size("gy"))
    place = jnp.stack([lax.axis_index("gx"), lax.axis_index("gy")]).astype(jnp.int32)
    tile = sds((S, C), BF)
    pay, both, nbt, hrow, srow, pre, grad = call(
        pack_kernel,
        (
            sds((S + 32, 2 * C), BF),
            sds((2 * S, C), BF),
            sds((32, C), F32),
            sds((8, C), jnp.int32),
            sds((8, C), jnp.int32),
            tile,
            tile,
        ),
        place,
        *[
            pltpu.with_memory_space_constraint(value, pltpu.HBM)
            for value in (
                features,
                pre_act,
                grad_out,
                neighbours.T,
                halo_list,
                jnp.transpose(send_list, (2, 0, 1)),
            )
        ],
        specs=[SMEM] + [HBM] * 6,
        scratch=[
            pltpu.VMEM((K, S), jnp.int32),
            pltpu.VMEM((1, 8, 24), jnp.int32),
            pltpu.VMEM((3, 1, 64), jnp.int32),
            pltpu.VMEM((S, C), BF),
            pltpu.SemaphoreType.DMA((6,)),
        ],
    )
    peer = sds((S + 32, 2 * C), BF)
    p2, p1, p3 = call(peers_kernel, (peer,) * 3, place, pay, both, flops=4 * 10**9)
    pays = [pay] + [cross(value, "gy", d) for d, value in ((2, p2), (1, p1), (3, p3))]
    back = pltpu.VMEM((8, HB, C), BF)
    own, m1, m2, loc = spread(place, nbt, grad, weight_two, 10**5)
    m2, m1 = halo_lines(m2, m1)
    passed, n2, n1 = halo_columns(place, loc, m2, m1, own)
    picks = sds((768, C), BF)
    o2, o1, near = call(
        pick_kernel,
        (picks, picks, sds((4, 64, 2 * C), BF)),
        place,
        *pays,
        passed,
        scratch=[pltpu.VMEM((4, 8 * HB, 2 * C), BF)],
        late=1,
    )
    r2, r1 = halo_lines(o2, o1)
    grad_pre, ordered = call(
        gate_kernel,
        (tile, sds((S, 2 * C), BF)),
        place,
        own,
        m2,
        m1,
        n2,
        n1,
        hrow,
        pre,
        grad,
        near,
        scratch=[back],
        late=1,
    )
    grads = gathered(ordered, "gy")
    own, m1, m2, loc = spread(place, nbt, grad_pre, weight_one, 4 * 10**9)
    m2, m1 = halo_lines(m2, m1)
    wide = 7 * C
    stack = sds((4 * S, wide), BF)
    cols_one, cols_two = call(
        columns_kernel,
        (stack, stack),
        place,
        *pays,
        r2,
        r1,
        near,
        own,
        scratch=[
            pltpu.VMEM((EXT, 2 * C), BF),
            pltpu.VMEM((32, C), F32),
            pltpu.VMEM((128, C), F32),
        ],
        late=1,
        flops=4 * 10**9,
    )
    passed, n2, n1 = halo_columns(place, loc, m2, m1, cols_two)

    def halves(which, cols, kind, flops, late):
        lanes = slice(which * C, (which + 1) * C)
        half = sds((128, wide), kind)
        return call(
            functools.partial(weight_kernel, lanes),
            (half, half),
            place,
            *grads,
            cols,
            late,
            scratch=[pltpu.VMEM((C, 4 * S), BF)],
            late=1,
            flops=flops,
        )

    keep_two, send_two = halves(0, cols_two, F32, 4 * 10**9, passed)
    come_two = cross(send_two, "gx", 1)
    keep_one, send_one = halves(1, cols_one, BF, 10**5, keep_two)
    come_one = cross(send_one, "gx", 1)
    some = sds((128, C), BF)
    rows_keep, rows_send = call(
        rows_kernel,
        (some, some),
        place,
        own,
        m2,
        m1,
        n2,
        n1,
        hrow,
        grad,
        srow,
        keep_one,
        scratch=[back],
        late=1,
        flops=2 * 10**10,
    )
    rows_come = cross(rows_send, "gx", 1)

    def lines(chunks):
        return [chunks[0]] + [cross(chunks[d], "gx", 16 * d) for d in (2, 1, 3)]

    two = call(
        merge_two_kernel,
        (sds((32, wide), BF),) * 4,
        place,
        keep_two,
        come_two,
        rows_keep,
        late=1,
    )
    one = call(
        merge_one_kernel,
        (sds((32, 9 * C), BF),) * 4,
        place,
        keep_one,
        come_one,
        rows_keep,
        rows_come,
        two[0],
        late=1,
        flops=2 * 10**10,
    )
    sum_two = call(
        line_two_kernel, sds((32, wide), BF), place, *lines(two), flops=2 * 10**10
    )
    summed = call(line_one_kernel, sds((64, 10 * C), BF), place, sum_two, *lines(one))
    groups = [[16 * y + 2 * z + e for z in range(8)] for y in range(4) for e in range(2)]
    collected = lax.all_to_all(
        summed.reshape(8, 8, 10 * C),
        "gx",
        split_axis=0,
        concat_axis=0,
        tiled=True,
        axis_index_groups=groups,
    )
    out = sds((4, QW), F32)
    return call(
        lambda *refs: final_kernel(scale, *refs), (tile, out, out), collected, specs=[VM]
    )


def solution(mesh):
    in_specs = (
        P(("gx", "gy"), None),
        P(("gx", "gy"), None),
        P(("gx", "gy"), None),
        P(),
        P(),
        P(("gx", "gy"), None),
        P(("gx", "gy"), None, None),
        P(("gx", "gy"), None, None),
    )
    out_specs = (P(("gx", "gy"), None), P("gx", "gy"), P("gx", "gy"))
    return jax.shard_map(body, mesh=mesh, in_specs=in_specs, out_specs=out_specs, check_vma=False)
```

```python
import functools
import math

import jax
import jax.numpy as jnp
from jax import lax
from jax.experimental import pallas as pl
from jax.experimental.pallas import tpu as pltpu
from jax.sharding import PartitionSpec as P

C = 256
K = 27
S = 192
HB = 32
EXT = S + 8 * HB
QW = 1728
BF = jnp.bfloat16
F32 = jnp.float32


def iota(shape, dim):
    return lax.broadcasted_iota(jnp.int32, shape, dim)


def onehot(mask):
    return jnp.where(mask, 1.0, 0.0).astype(BF)


def mm(a, b):
    return lax.dot_general(a, b, (((1,), (0,)), ((), ())), preferred_element_type=F32)


def mm_t(a, b):
    return lax.dot_general(a, b, (((0,), (0,)), ((), ())), preferred_element_type=F32)


def direction(a, b):
    grid = 3 * (a + 1) + (b + 1)
    return grid - jnp.where(grid > 4, 1, 0)


def channel_order():
    out = iota((C, C), 1)
    parity, rest = out // 128, out % 128
    source = 8 * (rest // 4) + 4 * parity + rest % 4
    return onehot(iota((C, C), 0) == source)


def halo_matrix(halo_row):
    return onehot(iota((S, 8 * HB), 0) == halo_row)


def pack_kernel(
    place, feat, pre, grad, nbr, halo, send, pay, p2, p1, p3, nbt, hrow, srow, pre_out,
    grad_out, ids, halo_ids, send_ids, feat_in, sems
):
    copies = [
        pltpu.make_async_copy(source, target, sems.at[n])
        for n, (source, target) in enumerate(
            (
                (nbr, ids),
                (halo, halo_ids),
                (send, send_ids),
                (feat, feat_in),
                (grad, grad_out),
                (pre, pre_out),
            )
        )
    ]
    for copy in copies:
        copy.start()
    for copy in copies:
        copy.wait()
    table = ids[...].astype(F32)
    heading = jnp.floor((table - S + 0.5) * (1.0 / 24.0))
    table = jnp.where(table >= S, table + 8.0 * heading, table)
    nbt[...] = jnp.full(nbt.shape, -1.0, F32)
    nbt[0:K, 0:S] = table
    shifted_up = table + 1.0
    high = jnp.floor(shifted_up * (1.0 / 16.0))
    tail = jnp.zeros((32, 2 * C), F32)
    z = pre_out[...].astype(F32)
    hidden = (z * (1.0 / (1.0 + jnp.exp(-z)))).astype(BF)
    halo_up = (halo_ids[0] + 1).astype(F32).astype(BF)
    spread = mm(halo_up, onehot(iota((24, 8 * HB), 1) % HB == iota((24, 8 * HB), 0)))
    row = jnp.sum(
        jnp.where(iota((8, 8 * HB), 1) // HB == iota((8, 8 * HB), 0), spread, 0.0),
        axis=0,
        keepdims=True,
    )
    hrow[...] = jnp.broadcast_to(row.astype(jnp.int32) - 1, hrow.shape)
    pay[S : S + 32, :] = tail.astype(BF)
    pay[S : S + K, 0:S] = high.astype(BF)
    pay[S : S + K, C : C + S] = (shifted_up - 16.0 * high).astype(BF)
    last = pay[S + 16 : S + 32, 0:C].astype(F32)
    pay[S + 16 : S + 32, 0:C] = jnp.where(iota((16, C), 0) == 15, row, last).astype(BF)
    both = jnp.concatenate([feat_in[...], hidden], axis=0)
    for turn, out in ((0, pay), (1, p1), (2, p2), (3, p3)):
        offset = ((place[1] ^ turn) * QW) % C
        turned = mm(both, onehot(iota((C, C), 0) == (iota((C, C), 1) + offset) % C)).astype(BF)
        out[0:S, 0:C] = turned[0:S]
        out[0:S, C : 2 * C] = turned[S : 2 * S]
        if turn:
            out[S : S + 32, :] = pay[S : S + 32, :]
    lane, peer = iota((64, C), 1), iota((64, C), 0)
    parity = jnp.where(lane < 128, place[0] % 2, 1 - place[0] % 2)
    pick = onehot(peer == 2 * ((lane % 128) // 4) + parity)
    spot = iota((1, C), 1) % 4
    total = jnp.zeros((1, C), F32)
    for c in range(3):
        up = jnp.broadcast_to((send_ids[c] + 1).astype(F32), (8, 64)).astype(BF)
        total = jnp.where(spot == c, mm(up, pick)[0:1, :], total)
    srow[...] = jnp.broadcast_to(total.astype(jnp.int32) - 1, srow.shape)


def spread_kernel(place, nbt, grad, weight, own, m1, m2, loc, acc):
    rows = iota((EXT, C), 0)
    table = nbt[...].astype(jnp.int32)
    gradient = grad[...]
    none = jnp.zeros((C - S, C), BF)
    masks, terms = [], []
    for k in range(K):
        masks.append(onehot(rows == table[k : k + 1, :]))
        terms += [mm(gradient, weight[:, k * C : (k + 1) * C]).astype(BF), none]
    acc[...] = mm(jnp.concatenate(masks, axis=1), jnp.concatenate(terms, axis=0))
    even = place[0] % 2 == 0
    own[...] = acc[0:S, :]
    first, last = jnp.where(even, S, S + 160), jnp.where(even, S + 160, S)
    m1[...] = acc[pl.ds(pl.multiple_of(first, 32), 96), :].astype(BF)
    m2[...] = acc[pl.ds(pl.multiple_of(last, 32), 96), :].astype(BF)
    loc[...] = acc[S + 96 : S + 160, :].astype(BF)


def inner(position, count):
    return (position > 0) & (position < count - 1)


def masked(keep, rows):
    return jnp.where(keep, rows, jnp.zeros_like(rows))


def pass_kernel(place, loc, m2, m1, late, n2, n1):
    even = place[1] % 2 == 0
    first = jnp.where(even, 0, 1)
    far = inner(place[0], 64)
    for out, side in ((n1, first), (n2, 1 - first)):
        out[0:32, :] = loc[pl.ds(pl.multiple_of(side * 32, 32), 32), :]
        out[32:64, :] = m1[pl.ds(pl.multiple_of(side * 64, 32), 32), :]
        out[64:96, :] = masked(far, m2[pl.ds(pl.multiple_of(side * 64, 32), 32), :])


def settled(place, own, m1, m2, n1, n2, hrow, back):
    da = jnp.where(place[0] % 2 == 0, 1, -1)
    db = jnp.where(place[1] % 2 == 0, 1, -1)
    back[direction(da, 0)] = m1[32:64, :]
    back[direction(-da, 0)] = masked(inner(place[0], 64), m2[32:64, :])
    beside = inner(place[1], 4)
    for ref, side, keep in ((n1, db, True), (n2, -db, beside)):
        rows = ref[...] if keep is True else masked(keep, ref[...])
        back[direction(0, side)] = rows[0:32, :]
        back[direction(da, side)] = rows[32:64, :]
        back[direction(-da, side)] = rows[64:96, :]
    rows = back[...].reshape(8 * HB, C)
    return own[...] + mm(halo_matrix(hrow[0:1, :]), rows)


def gate_kernel(place, own, m2, m1, n2, n1, hrow, pre, grad, late, out, ordered, back):
    hidden_grad = settled(place, own, m1, m2, n1, n2, hrow, back)
    z = pre[...].astype(F32)
    g = 1.0 / (1.0 + jnp.exp(-z))
    value = (hidden_grad * g * (1.0 + z * (1.0 - g))).astype(BF)
    out[...] = value
    order = channel_order()
    ordered[:, 0:C] = mm(grad[...], order).astype(BF)
    ordered[:, C : 2 * C] = mm(value, order).astype(BF)


def rows_kernel(place, own, m2, m1, n2, n1, hrow, grad, srow, late, keep, send, back):
    total = settled(place, own, m1, m2, n1, n2, hrow, back)
    value = (grad[...].astype(F32) + total).astype(BF)
    chosen = mm_t(onehot(iota((S, C), 0) == srow[0:1, :]), value).astype(BF)
    keep[...] = chosen[0:128, :]
    send[...] = chosen[128:256, :]


def pick_kernel(place, p0, p2, p1, p3, late, o2, o1, loc, picked):
    column = place[1]
    for turn, pay in enumerate((p0, p1, p2, p3)):
        halo_row = pay[S + 16 : S + 32, 0:C].astype(F32)[15:16, :].astype(jnp.int32) - 1
        rows = mm_t(halo_matrix(halo_row), pay[0:S, 0 : 2 * C])
        picked[column ^ turn] = rows.astype(BF)
    even = place[0] % 2 == 0
    up = pl.multiple_of(jnp.where(even, 160, 0), 32)
    down = pl.multiple_of(jnp.where(even, 0, 160), 32)
    none = jnp.zeros((HB, 2 * C), BF)
    for tile in range(4):
        for b in (-1, 0, 1):
            source = tile - b
            at = HB * (b + 1)
            for out, side in ((o1, up), (o2, down)):
                rows = picked[source, pl.ds(side + at, HB), :] if 0 <= source < 4 else none
                to = 96 * tile + at
                out[to : to + HB, :] = rows[:, 0:C]
                out[to + 384 : to + 384 + HB, :] = rows[:, C : 2 * C]
            if b:
                to = 0 if b < 0 else HB
                rows = picked[source, 96 + to : 96 + to + HB, :] if 0 <= source < 4 else none
                loc[tile, to : to + HB, :] = rows


def columns_kernel(
    place, p0, p2, p1, p3, r2, r1, loc, late, cols_one, cols_two, ext, ids, sel
):
    column = place[1]
    start = column * QW
    first_k = start // C
    offset = start % C
    even = place[0] % 2 == 0
    far = inner(place[0], 64)
    lane = iota((S, 2 * C), 1) % C
    early = lane < C - offset
    for turn, pay in enumerate((p0, p1, p2, p3)):
        tile = column ^ turn
        for half in range(2):
            lanes = slice(half * C, (half + 1) * C)
            at = pl.multiple_of(384 * half + 96 * tile, 32)
            above, below = r1[pl.ds(at, 96), :], masked(far, r2[pl.ds(at, 96), :])
            for to, piece in (
                (0, pay[0:S, lanes]),
                (S, jnp.where(even, above, below)),
                (S + 96, loc[tile, :, lanes]),
                (S + 160, jnp.where(even, below, above)),
            ):
                ext[to : to + piece.shape[0], lanes] = piece
        high = pay[S : S + 32, 0:C].astype(F32)
        low = pay[S : S + 32, C : 2 * C].astype(F32)
        ids[0:32, :] = 16.0 * high + low - 1.0
        for part in range(8):
            sel[part : part + 1, :] = ids[pl.ds(first_k + part, 1), :]
        table = jnp.transpose(sel[...])[:, 0:8].astype(jnp.int32)
        extended = ext[...]
        match = [
            onehot(iota((S, EXT), 1) == table[0:S, part : part + 1]) for part in range(8)
        ]
        found = mm(jnp.concatenate(match, axis=0), extended).astype(BF)
        for part in range(7):
            merged = jnp.where(
                early, found[part * S : (part + 1) * S], found[(part + 1) * S : (part + 2) * S]
            )
            lanes = slice(part * C, (part + 1) * C)
            cols_one[turn * S : (turn + 1) * S, lanes] = merged[:, 0:C]
            cols_two[turn * S : (turn + 1) * S, lanes] = merged[:, C : 2 * C]


def weight_kernel(lanes, place, g0, g2, g1, g3, cols, late, keep, send, gt):
    for turn, grad in enumerate((g0, g1, g2, g3)):
        gt[:, turn * S : (turn + 1) * S] = jnp.transpose(grad[:, lanes].astype(F32)).astype(BF)
    mine = pl.multiple_of((place[0] % 2) * 128, 128)
    other = pl.multiple_of(128 - mine, 128)
    left = jnp.concatenate([gt[pl.ds(mine, 128), :], gt[pl.ds(other, 128), :]], axis=0)
    for part in range(7):
        lanes = slice(part * C, (part + 1) * C)
        block = mm(left, cols[:, lanes])
        keep[:, lanes] = block[0:128].astype(keep.dtype)
        send[:, lanes] = block[128:256].astype(send.dtype)


def merge_two_kernel(place, keep, come, late, *outs):
    line = place[0] // 16
    for turn, out in enumerate(outs):
        rows = pl.ds(pl.multiple_of(32 * (line ^ turn), 32), 32)
        out[...] = (keep[rows, :] + come[rows, :]).astype(BF)


def merge_one_kernel(place, keep, come, rk, rs, late, *outs):
    first = place[0] % 2 == 0
    line = place[0] // 16
    for turn, out in enumerate(outs):
        rows = pl.ds(pl.multiple_of(32 * (line ^ turn), 32), 32)
        total = keep[rows, :].astype(F32) + come[rows, :].astype(F32)
        out[:, 0 : 7 * C] = total.astype(BF)
        mine, other = rk[rows, :], rs[rows, :]
        out[:, 7 * C : 8 * C] = jnp.where(first, mine, other)
        out[:, 8 * C : 9 * C] = jnp.where(first, other, mine)


def line_two_kernel(place, a0, a1, a3, a2, out):
    total = a0[...].astype(F32)
    for part in (a1, a2, a3):
        total = total + part[...].astype(F32)
    out[...] = total.astype(BF)


def line_one_kernel(place, two, b0, b1, b3, b2, out):
    line = place[0] // 16
    to, at = iota((64, 64), 0), iota((64, 64), 1)
    order = onehot(at == 32 * ((to % 8) // 4) + 4 * (to // 8) + to % 4)
    for n in range(7):
        lanes = slice(n * C, (n + 1) * C)
        total = b0[:, lanes].astype(F32)
        for part in (b1, b2, b3):
            total = total + part[:, lanes].astype(F32)
        value = jnp.concatenate([total.astype(BF), two[:, lanes]], axis=0)
        out[:, lanes] = mm(order, value).astype(BF)
    sources = [
        part[:, (7 + core) * C : (8 + core) * C] for part in (b0, b1, b2, b3) for core in range(2)
    ]
    stacked = jnp.concatenate(sources, axis=0)
    to, at = iota((64, C), 0), iota((64, C), 1)
    for n in range(3):
        index = 8 * n + to % 8
        spot = (
            (index // 6 == (line ^ (at // 64)))
            & ((index % 6) // 3 == (at // 32) % 2)
            & (at % 32 == 4 * (to // 8) + index % 3)
        )
        out[:, (7 + n) * C : (8 + n) * C] = mm(onehot(spot), stacked).astype(BF)


def final_kernel(scale, arrived, rows, one, two):
    total = jnp.sum(arrived[:, :, 0 : 7 * C].astype(F32), axis=0) * scale
    one[...] = total[0:4, 0:QW]
    two[...] = total[4:8, 0:QW]
    to, at = iota((S, S), 0), iota((S, S), 1)
    spot = ((at % 64) // 8 == (to // 6) % 8) & (
        8 * (at // 64) + at % 8 == 6 * (to // 48) + to % 6
    )
    pieces = [arrived[:, :, (7 + n) * C : (8 + n) * C].reshape(64, C) for n in range(3)]
    rows[...] = mm(onehot(spot), jnp.concatenate(pieces, axis=0)).astype(BF)


def sds(shape, dtype):
    return jax.ShapeDtypeStruct(shape, dtype)


SMEM = pl.BlockSpec(memory_space=pltpu.SMEM)
VM = pl.BlockSpec(memory_space=pltpu.VMEM)
HBM = pl.BlockSpec(memory_space=pltpu.HBM)
ANY = pl.BlockSpec(memory_space=pl.ANY)


def call(kernel, outs, *args, scratch=(), specs=None, late=0, flops=10**5):
    if specs is None:
        specs = [SMEM] + [VM] * (len(args) - 1 - late) + [ANY] * late
    return pl.pallas_call(
        kernel,
        out_shape=outs,
        in_specs=specs,
        out_specs=jax.tree.map(lambda _: VM, outs),
        scratch_shapes=list(scratch),
        compiler_params=pltpu.CompilerParams(vmem_limit_bytes=40 * 2**20),
        cost_estimate=pl.CostEstimate(flops=flops, bytes_accessed=10**4, transcendentals=0),
    )(*args)


def spread(place, nbt, grad, weight, flops):
    edge = sds((96, C), BF)
    return call(
        spread_kernel,
        (sds((S, C), F32), edge, edge, sds((64, C), BF)),
        place,
        nbt,
        grad,
        weight,
        scratch=[pltpu.VMEM((EXT, C), F32)],
        flops=flops,
    )


def swap(value, axis, turn):
    gx, gy = lax.axis_size("gx"), lax.axis_size("gy")
    pairs = []
    for i in range(gx):
        for j in range(gy):
            n, size = (i, gx) if axis == "gx" else (j, gy)
            q = n ^ 1 if turn == 1 else ((n + 1) ^ 1) - 1
            if axis == "gx":
                to = (q, j) if 0 <= q < size else (i, j ^ 1)
            else:
                to = (i, q) if 0 <= q < size else (i ^ 1, j)
            pairs.append((i * gy + j, to[0] * gy + to[1]))
    return lax.ppermute(value, ("gx", "gy"), pairs)


def cross(value, axis, mask):
    return lax.ppermute(value, axis, [(n, n ^ mask) for n in range(lax.axis_size(axis))])


def gathered(value, axis, base=1):
    return [value] + [cross(value, axis, base * d) for d in (2, 1, 3)]


def halo_lines(m2, m1):
    return swap(m2, "gx", 2), swap(m1, "gx", 1)


def halo_columns(place, loc, m2, m1, late, flops=10**5):
    edge = sds((96, C), BF)
    n2, n1 = call(pass_kernel, (edge, edge), place, loc, m2, m1, late, late=1, flops=flops)
    return n1, swap(n2, "gy", 2), swap(n1, "gy", 1)


def body(features, pre_act, grad_out, weight_one, weight_two, neighbours, halo_list, send_list):
    gx = lax.axis_size("gx")
    scale = 1.0 / math.sqrt(S * gx * lax.axis_size("gy"))
    place = jnp.stack([lax.axis_index("gx"), lax.axis_index("gy")]).astype(jnp.int32)
    tile = sds((S, C), BF)
    pay, p2, p1, p3, nbt, hrow, srow, pre, grad = call(
        pack_kernel,
        (
            *[sds((S + 32, 2 * C), BF)] * 4,
            sds((32, C), F32),
            sds((8, C), jnp.int32),
            sds((8, C), jnp.int32),
            tile,
            tile,
        ),
        place,
        *[
            pltpu.with_memory_space_constraint(value, pltpu.HBM)
            for value in (
                features,
                pre_act,
                grad_out,
                neighbours.T,
                halo_list,
                jnp.transpose(send_list, (2, 0, 1)),
            )
        ],
        specs=[SMEM] + [HBM] * 6,
        flops=4 * 10**9,
        scratch=[
            pltpu.VMEM((K, S), jnp.int32),
            pltpu.VMEM((1, 8, 24), jnp.int32),
            pltpu.VMEM((3, 1, 64), jnp.int32),
            pltpu.VMEM((S, C), BF),
            pltpu.SemaphoreType.DMA((6,)),
        ],
    )
    pays = [pay] + [cross(value, "gy", d) for d, value in ((2, p2), (1, p1), (3, p3))]
    back = pltpu.VMEM((8, HB, C), BF)
    own, m1, m2, loc = spread(place, nbt, grad, weight_two, 10**5)
    m2, m1 = halo_lines(m2, m1)
    passed, n2, n1 = halo_columns(place, loc, m2, m1, own)
    picks = sds((768, C), BF)
    o2, o1, near = call(
        pick_kernel,
        (picks, picks, sds((4, 64, 2 * C), BF)),
        place,
        *pays,
        passed,
        scratch=[pltpu.VMEM((4, 8 * HB, 2 * C), BF)],
        late=1,
    )
    r2, r1 = halo_lines(o2, o1)
    grad_pre, ordered = call(
        gate_kernel,
        (tile, sds((S, 2 * C), BF)),
        place,
        own,
        m2,
        m1,
        n2,
        n1,
        hrow,
        pre,
        grad,
        near,
        scratch=[back],
        late=1,
    )
    grads = gathered(ordered, "gy")
    own, m1, m2, loc = spread(place, nbt, grad_pre, weight_one, 4 * 10**9)
    m2, m1 = halo_lines(m2, m1)
    wide = 7 * C
    stack = sds((4 * S, wide), BF)
    cols_one, cols_two = call(
        columns_kernel,
        (stack, stack),
        place,
        *pays,
        r2,
        r1,
        near,
        own,
        scratch=[
            pltpu.VMEM((EXT, 2 * C), BF),
            pltpu.VMEM((32, C), F32),
            pltpu.VMEM((128, C), F32),
        ],
        late=1,
        flops=4 * 10**9,
    )
    passed, n2, n1 = halo_columns(place, loc, m2, m1, cols_two)

    def halves(which, cols, kind, flops, late):
        lanes = slice(which * C, (which + 1) * C)
        half = sds((128, wide), kind)
        return call(
            functools.partial(weight_kernel, lanes),
            (half, half),
            place,
            *grads,
            cols,
            late,
            scratch=[pltpu.VMEM((C, 4 * S), BF)],
            late=1,
            flops=flops,
        )

    keep_two, send_two = halves(0, cols_two, F32, 4 * 10**9, passed)
    come_two = cross(send_two, "gx", 1)
    keep_one, send_one = halves(1, cols_one, BF, 10**5, keep_two)
    come_one = cross(send_one, "gx", 1)
    some = sds((128, C), BF)
    rows_keep, rows_send = call(
        rows_kernel,
        (some, some),
        place,
        own,
        m2,
        m1,
        n2,
        n1,
        hrow,
        grad,
        srow,
        keep_one,
        scratch=[back],
        late=1,
        flops=2 * 10**10,
    )
    rows_come = cross(rows_send, "gx", 1)

    def lines(chunks):
        return [chunks[0]] + [cross(chunks[d], "gx", 16 * d) for d in (1, 3, 2)]

    two = call(
        merge_two_kernel,
        (sds((32, wide), BF),) * 4,
        place,
        keep_two,
        come_two,
        rows_keep,
        late=1,
    )
    one = call(
        merge_one_kernel,
        (sds((32, 9 * C), BF),) * 4,
        place,
        keep_one,
        come_one,
        rows_keep,
        rows_come,
        two[0],
        late=1,
        flops=2 * 10**10,
    )
    sum_two = call(
        line_two_kernel, sds((32, wide), BF), place, *lines(two), flops=2 * 10**10
    )
    summed = call(line_one_kernel, sds((64, 10 * C), BF), place, sum_two, *lines(one))
    groups = [[16 * y + 2 * z + e for z in range(8)] for y in range(4) for e in range(2)]
    collected = lax.all_to_all(
        summed.reshape(8, 8, 10 * C),
        "gx",
        split_axis=0,
        concat_axis=0,
        tiled=True,
        axis_index_groups=groups,
    )
    out = sds((4, QW), F32)
    return call(
        lambda *refs: final_kernel(scale, *refs), (tile, out, out), collected, specs=[VM]
    )


def solution(mesh):
    in_specs = (
        P(("gx", "gy"), None),
        P(("gx", "gy"), None),
        P(("gx", "gy"), None),
        P(),
        P(),
        P(("gx", "gy"), None),
        P(("gx", "gy"), None, None),
        P(("gx", "gy"), None, None),
    )
    out_specs = (P(("gx", "gy"), None), P("gx", "gy"), P("gx", "gy"))
    return jax.shard_map(body, mesh=mesh, in_specs=in_specs, out_specs=out_specs, check_vma=False)
```

```python
import functools
import math

import jax
import jax.numpy as jnp
from jax import lax
from jax.experimental import pallas as pl
from jax.experimental.pallas import tpu as pltpu
from jax.sharding import PartitionSpec as P

C = 256
K = 27
S = 192
HB = 32
EXT = S + 8 * HB
QW = 1728
BF = jnp.bfloat16
F32 = jnp.float32


def iota(shape, dim):
    return lax.broadcasted_iota(jnp.int32, shape, dim)


def onehot(mask):
    return jnp.where(mask, 1.0, 0.0).astype(BF)


def mm(a, b):
    return lax.dot_general(a, b, (((1,), (0,)), ((), ())), preferred_element_type=F32)


def mm_t(a, b):
    return lax.dot_general(a, b, (((0,), (0,)), ((), ())), preferred_element_type=F32)


def direction(a, b):
    grid = 3 * (a + 1) + (b + 1)
    return grid - jnp.where(grid > 4, 1, 0)


def channel_order():
    out = iota((C, C), 1)
    parity, rest = out // 128, out % 128
    source = 8 * (rest // 4) + 4 * parity + rest % 4
    return onehot(iota((C, C), 0) == source)


def halo_matrix(halo_row):
    return onehot(iota((S, 8 * HB), 0) == halo_row)


def pack_kernel(
    place, feat, pre, grad, nbr, halo, send, pay, p2, p1, p3, nbt, hrow, srow, pre_out,
    grad_out, ids, halo_ids, send_ids, feat_in, sems
):
    copies = [
        pltpu.make_async_copy(source, target, sems.at[n])
        for n, (source, target) in enumerate(
            (
                (nbr, ids),
                (halo, halo_ids),
                (send, send_ids),
                (feat, feat_in),
                (grad, grad_out),
                (pre, pre_out),
            )
        )
    ]
    for copy in copies:
        copy.start()
    for copy in copies:
        copy.wait()
    table = ids[...].astype(F32)
    heading = jnp.floor((table - S + 0.5) * (1.0 / 24.0))
    table = jnp.where(table >= S, table + 8.0 * heading, table)
    nbt[...] = jnp.full(nbt.shape, -1.0, F32)
    nbt[0:K, 0:S] = table
    z = pre_out[...].astype(F32)
    hidden = (z * (1.0 / (1.0 + jnp.exp(-z)))).astype(BF)
    halo_up = (halo_ids[0] + 1).astype(F32).astype(BF)
    spread = mm(halo_up, onehot(iota((24, 8 * HB), 1) % HB == iota((24, 8 * HB), 0)))
    row = jnp.sum(
        jnp.where(iota((8, 8 * HB), 1) // HB == iota((8, 8 * HB), 0), spread, 0.0),
        axis=0,
        keepdims=True,
    )
    hrow[...] = jnp.broadcast_to(row.astype(jnp.int32) - 1, hrow.shape)
    shifted_up = nbt[...] + 1.0
    high = jnp.floor(shifted_up * (1.0 / 16.0))
    low = shifted_up - 16.0 * high
    pay[S : S + 32, 0:C] = jnp.where(iota((32, C), 0) == 31, row, high).astype(BF)
    pay[S : S + 32, C : 2 * C] = low.astype(BF)
    both = jnp.concatenate([feat_in[...], hidden], axis=0)
    for turn, out in ((0, pay), (1, p1), (2, p2), (3, p3)):
        offset = ((place[1] ^ turn) * QW) % C
        turned = mm(both, onehot(iota((C, C), 0) == (iota((C, C), 1) + offset) % C)).astype(BF)
        out[0:S, 0:C] = turned[0:S]
        out[0:S, C : 2 * C] = turned[S : 2 * S]
        if turn:
            out[S : S + 32, :] = pay[S : S + 32, :]
    lane, peer = iota((64, C), 1), iota((64, C), 0)
    parity = jnp.where(lane < 128, place[0] % 2, 1 - place[0] % 2)
    pick = onehot(peer == 2 * ((lane % 128) // 4) + parity)
    spot = iota((1, C), 1) % 4
    total = jnp.zeros((1, C), F32)
    for c in range(3):
        up = jnp.broadcast_to((send_ids[c] + 1).astype(F32), (8, 64)).astype(BF)
        total = jnp.where(spot == c, mm(up, pick)[0:1, :], total)
    srow[...] = jnp.broadcast_to(total.astype(jnp.int32) - 1, srow.shape)


def spread_kernel(place, nbt, grad, weight, own, m1, m2, loc, acc):
    rows = iota((EXT, C), 0)
    table = nbt[...].astype(jnp.int32)
    gradient = grad[...]
    none = jnp.zeros((C - S, C), BF)
    masks, terms = [], []
    for k in range(K):
        masks.append(onehot(rows == table[k : k + 1, :]))
        terms += [mm(gradient, weight[:, k * C : (k + 1) * C]).astype(BF), none]
    acc[...] = mm(jnp.concatenate(masks, axis=1), jnp.concatenate(terms, axis=0))
    even = place[0] % 2 == 0
    own[...] = acc[0:S, :]
    first, last = jnp.where(even, S, S + 160), jnp.where(even, S + 160, S)
    m1[...] = acc[pl.ds(pl.multiple_of(first, 32), 96), :].astype(BF)
    m2[...] = acc[pl.ds(pl.multiple_of(last, 32), 96), :].astype(BF)
    loc[...] = acc[S + 96 : S + 160, :].astype(BF)


def inner(position, count):
    return (position > 0) & (position < count - 1)


def masked(keep, rows):
    return jnp.where(keep, rows, jnp.zeros_like(rows))


def pass_kernel(place, loc, m2, m1, late, n2, n1):
    even = place[1] % 2 == 0
    first = jnp.where(even, 0, 1)
    far = inner(place[0], 64)
    for out, side in ((n1, first), (n2, 1 - first)):
        out[0:32, :] = loc[pl.ds(pl.multiple_of(side * 32, 32), 32), :]
        out[32:64, :] = m1[pl.ds(pl.multiple_of(side * 64, 32), 32), :]
        out[64:96, :] = masked(far, m2[pl.ds(pl.multiple_of(side * 64, 32), 32), :])


def settled(place, own, m1, m2, n1, n2, hrow, back):
    da = jnp.where(place[0] % 2 == 0, 1, -1)
    db = jnp.where(place[1] % 2 == 0, 1, -1)
    back[direction(da, 0)] = m1[32:64, :]
    back[direction(-da, 0)] = masked(inner(place[0], 64), m2[32:64, :])
    beside = inner(place[1], 4)
    for ref, side, keep in ((n1, db, True), (n2, -db, beside)):
        rows = ref[...] if keep is True else masked(keep, ref[...])
        back[direction(0, side)] = rows[0:32, :]
        back[direction(da, side)] = rows[32:64, :]
        back[direction(-da, side)] = rows[64:96, :]
    rows = back[...].reshape(8 * HB, C)
    return own[...] + mm(halo_matrix(hrow[0:1, :]), rows)


def gate_kernel(place, own, m2, m1, n2, n1, hrow, pre, grad, late, out, ordered, back):
    hidden_grad = settled(place, own, m1, m2, n1, n2, hrow, back)
    z = pre[...].astype(F32)
    g = 1.0 / (1.0 + jnp.exp(-z))
    value = (hidden_grad * g * (1.0 + z * (1.0 - g))).astype(BF)
    out[...] = value
    order = channel_order()
    ordered[:, 0:C] = mm(grad[...], order).astype(BF)
    ordered[:, C : 2 * C] = mm(value, order).astype(BF)


def rows_kernel(place, own, m2, m1, n2, n1, hrow, grad, srow, late, keep, send, back):
    total = settled(place, own, m1, m2, n1, n2, hrow, back)
    value = (grad[...].astype(F32) + total).astype(BF)
    chosen = mm_t(onehot(iota((S, C), 0) == srow[0:1, :]), value).astype(BF)
    keep[...] = chosen[0:128, :]
    send[...] = chosen[128:256, :]


def pick_kernel(place, p0, p2, p1, p3, late, o2, o1, loc, picked):
    column = place[1]
    for turn, pay in enumerate((p0, p1, p2, p3)):
        halo_row = pay[S + 16 : S + 32, 0:C].astype(F32)[15:16, :].astype(jnp.int32) - 1
        rows = mm_t(halo_matrix(halo_row), pay[0:S, 0 : 2 * C])
        picked[column ^ turn] = rows.astype(BF)
    even = place[0] % 2 == 0
    up = pl.multiple_of(jnp.where(even, 160, 0), 32)
    down = pl.multiple_of(jnp.where(even, 0, 160), 32)
    none = jnp.zeros((HB, 2 * C), BF)
    for tile in range(4):
        for b in (-1, 0, 1):
            source = tile - b
            at = HB * (b + 1)
            for out, side in ((o1, up), (o2, down)):
                rows = picked[source, pl.ds(side + at, HB), :] if 0 <= source < 4 else none
                to = 96 * tile + at
                out[to : to + HB, :] = rows[:, 0:C]
                out[to + 384 : to + 384 + HB, :] = rows[:, C : 2 * C]
            if b:
                to = 0 if b < 0 else HB
                rows = picked[source, 96 + to : 96 + to + HB, :] if 0 <= source < 4 else none
                loc[tile, to : to + HB, :] = rows


def columns_kernel(
    place, p0, p2, p1, p3, r2, r1, loc, late, cols_one, cols_two, ext, ids, sel
):
    column = place[1]
    start = column * QW
    first_k = start // C
    offset = start % C
    even = place[0] % 2 == 0
    far = inner(place[0], 64)
    lane = iota((S, 2 * C), 1) % C
    early = lane < C - offset
    for turn, pay in enumerate((p0, p1, p2, p3)):
        tile = column ^ turn
        for half in range(2):
            lanes = slice(half * C, (half + 1) * C)
            at = pl.multiple_of(384 * half + 96 * tile, 32)
            above, below = r1[pl.ds(at, 96), :], masked(far, r2[pl.ds(at, 96), :])
            for to, piece in (
                (0, pay[0:S, lanes]),
                (S, jnp.where(even, above, below)),
                (S + 96, loc[tile, :, lanes]),
                (S + 160, jnp.where(even, below, above)),
            ):
                ext[to : to + piece.shape[0], lanes] = piece
        high = pay[S : S + 32, 0:C].astype(F32)
        low = pay[S : S + 32, C : 2 * C].astype(F32)
        ids[0:32, :] = 16.0 * high + low - 1.0
        for part in range(8):
            sel[part : part + 1, :] = ids[pl.ds(first_k + part, 1), :]
        table = jnp.transpose(sel[...])[:, 0:8].astype(jnp.int32)
        extended = ext[...]
        match = [
            onehot(iota((S, EXT), 1) == table[0:S, part : part + 1]) for part in range(8)
        ]
        found = mm(jnp.concatenate(match, axis=0), extended).astype(BF)
        for part in range(7):
            merged = jnp.where(
                early, found[part * S : (part + 1) * S], found[(part + 1) * S : (part + 2) * S]
            )
            lanes = slice(part * C, (part + 1) * C)
            cols_one[turn * S : (turn + 1) * S, lanes] = merged[:, 0:C]
            cols_two[turn * S : (turn + 1) * S, lanes] = merged[:, C : 2 * C]


def weight_kernel(lanes, place, g0, g2, g1, g3, cols, late, keep, send, gt):
    for turn, grad in enumerate((g0, g1, g2, g3)):
        gt[:, turn * S : (turn + 1) * S] = jnp.transpose(grad[:, lanes].astype(F32)).astype(BF)
    mine = pl.multiple_of((place[0] % 2) * 128, 128)
    other = pl.multiple_of(128 - mine, 128)
    left = jnp.concatenate([gt[pl.ds(mine, 128), :], gt[pl.ds(other, 128), :]], axis=0)
    for part in range(7):
        lanes = slice(part * C, (part + 1) * C)
        block = mm(left, cols[:, lanes])
        keep[:, lanes] = block[0:128].astype(keep.dtype)
        send[:, lanes] = block[128:256].astype(send.dtype)


def merge_two_kernel(place, keep, come, late, *outs):
    line = place[0] // 16
    for turn, out in enumerate(outs):
        rows = pl.ds(pl.multiple_of(32 * (line ^ turn), 32), 32)
        out[...] = (keep[rows, :] + come[rows, :]).astype(BF)


def merge_one_kernel(place, keep, come, rk, rs, late, *outs):
    first = place[0] % 2 == 0
    line = place[0] // 16
    for turn, out in enumerate(outs):
        rows = pl.ds(pl.multiple_of(32 * (line ^ turn), 32), 32)
        total = keep[rows, :].astype(F32) + come[rows, :].astype(F32)
        out[:, 0 : 7 * C] = total.astype(BF)
        mine, other = rk[rows, :], rs[rows, :]
        out[:, 7 * C : 8 * C] = jnp.where(first, mine, other)
        out[:, 8 * C : 9 * C] = jnp.where(first, other, mine)


def line_two_kernel(place, a0, a1, a3, a2, out):
    total = a0[...].astype(F32)
    for part in (a1, a2, a3):
        total = total + part[...].astype(F32)
    out[...] = total.astype(BF)


def line_one_kernel(place, two, b0, b1, b3, b2, out):
    line = place[0] // 16
    to, at = iota((64, 64), 0), iota((64, 64), 1)
    order = onehot(at == 32 * ((to % 8) // 4) + 4 * (to // 8) + to % 4)
    for n in range(7):
        lanes = slice(n * C, (n + 1) * C)
        total = b0[:, lanes].astype(F32)
        for part in (b1, b2, b3):
            total = total + part[:, lanes].astype(F32)
        value = jnp.concatenate([total.astype(BF), two[:, lanes]], axis=0)
        out[:, lanes] = mm(order, value).astype(BF)
    sources = [
        part[:, (7 + core) * C : (8 + core) * C] for part in (b0, b1, b2, b3) for core in range(2)
    ]
    stacked = jnp.concatenate(sources, axis=0)
    to, at = iota((64, C), 0), iota((64, C), 1)
    for n in range(3):
        index = 8 * n + to % 8
        spot = (
            (index // 6 == (line ^ (at // 64)))
            & ((index % 6) // 3 == (at // 32) % 2)
            & (at % 32 == 4 * (to // 8) + index % 3)
        )
        out[:, (7 + n) * C : (8 + n) * C] = mm(onehot(spot), stacked).astype(BF)


def final_kernel(scale, arrived, rows, one, two):
    total = jnp.sum(arrived[:, :, 0 : 7 * C].astype(F32), axis=0) * scale
    one[...] = total[0:4, 0:QW]
    two[...] = total[4:8, 0:QW]
    to, at = iota((S, S), 0), iota((S, S), 1)
    spot = ((at % 64) // 8 == (to // 6) % 8) & (
        8 * (at // 64) + at % 8 == 6 * (to // 48) + to % 6
    )
    found = arrived[:, :, 7 * C : 10 * C].astype(F32)
    pieces = [found[:, :, n * C : (n + 1) * C].reshape(64, C).astype(BF) for n in range(3)]
    rows[...] = mm(onehot(spot), jnp.concatenate(pieces, axis=0)).astype(BF)


def sds(shape, dtype):
    return jax.ShapeDtypeStruct(shape, dtype)


SMEM = pl.BlockSpec(memory_space=pltpu.SMEM)
VM = pl.BlockSpec(memory_space=pltpu.VMEM)
HBM = pl.BlockSpec(memory_space=pltpu.HBM)
ANY = pl.BlockSpec(memory_space=pl.ANY)


def call(kernel, outs, *args, scratch=(), specs=None, late=0, flops=10**5):
    if specs is None:
        specs = [SMEM] + [VM] * (len(args) - 1 - late) + [ANY] * late
    return pl.pallas_call(
        kernel,
        out_shape=outs,
        in_specs=specs,
        out_specs=jax.tree.map(lambda _: VM, outs),
        scratch_shapes=list(scratch),
        compiler_params=pltpu.CompilerParams(vmem_limit_bytes=40 * 2**20),
        cost_estimate=pl.CostEstimate(flops=flops, bytes_accessed=10**4, transcendentals=0),
    )(*args)


def spread(place, nbt, grad, weight, flops):
    edge = sds((96, C), BF)
    return call(
        spread_kernel,
        (sds((S, C), F32), edge, edge, sds((64, C), BF)),
        place,
        nbt,
        grad,
        weight,
        scratch=[pltpu.VMEM((EXT, C), F32)],
        flops=flops,
    )


def swap(value, axis, turn):
    gx, gy = lax.axis_size("gx"), lax.axis_size("gy")
    pairs = []
    for i in range(gx):
        for j in range(gy):
            n, size = (i, gx) if axis == "gx" else (j, gy)
            q = n ^ 1 if turn == 1 else ((n + 1) ^ 1) - 1
            if axis == "gx":
                to = (q, j) if 0 <= q < size else (i, j ^ 1)
            else:
                to = (i, q) if 0 <= q < size else (i ^ 1, j)
            pairs.append((i * gy + j, to[0] * gy + to[1]))
    return lax.ppermute(value, ("gx", "gy"), pairs)


def cross(value, axis, mask):
    return lax.ppermute(value, axis, [(n, n ^ mask) for n in range(lax.axis_size(axis))])


def gathered(value, axis, base=1):
    return [value] + [cross(value, axis, base * d) for d in (2, 1, 3)]


def halo_lines(m2, m1):
    return swap(m2, "gx", 2), swap(m1, "gx", 1)


def halo_columns(place, loc, m2, m1, late, flops=10**5):
    edge = sds((96, C), BF)
    n2, n1 = call(pass_kernel, (edge, edge), place, loc, m2, m1, late, late=1, flops=flops)
    return n1, swap(n2, "gy", 2), swap(n1, "gy", 1)


def body(features, pre_act, grad_out, weight_one, weight_two, neighbours, halo_list, send_list):
    gx = lax.axis_size("gx")
    scale = 1.0 / math.sqrt(S * gx * lax.axis_size("gy"))
    place = jnp.stack([lax.axis_index("gx"), lax.axis_index("gy")]).astype(jnp.int32)
    tile = sds((S, C), BF)
    pay, p2, p1, p3, nbt, hrow, srow, pre, grad = call(
        pack_kernel,
        (
            *[sds((S + 32, 2 * C), BF)] * 4,
            sds((32, C), F32),
            sds((8, C), jnp.int32),
            sds((8, C), jnp.int32),
            tile,
            tile,
        ),
        place,
        *[
            pltpu.with_memory_space_constraint(value, pltpu.HBM)
            for value in (
                features,
                pre_act,
                grad_out,
                neighbours.T,
                halo_list,
                jnp.transpose(send_list, (2, 0, 1)),
            )
        ],
        specs=[SMEM] + [HBM] * 6,
        flops=4 * 10**9,
        scratch=[
            pltpu.VMEM((K, S), jnp.int32),
            pltpu.VMEM((1, 8, 24), jnp.int32),
            pltpu.VMEM((3, 1, 64), jnp.int32),
            pltpu.VMEM((S, C), BF),
            pltpu.SemaphoreType.DMA((6,)),
        ],
    )
    pays = [pay] + [cross(value, "gy", d) for d, value in ((2, p2), (1, p1), (3, p3))]
    back = pltpu.VMEM((8, HB, C), BF)
    own, m1, m2, loc = spread(place, nbt, grad, weight_two, 10**5)
    m2, m1 = halo_lines(m2, m1)
    passed, n2, n1 = halo_columns(place, loc, m2, m1, own)
    picks = sds((768, C), BF)
    o2, o1, near = call(
        pick_kernel,
        (picks, picks, sds((4, 64, 2 * C), BF)),
        place,
        *pays,
        passed,
        scratch=[pltpu.VMEM((4, 8 * HB, 2 * C), BF)],
        late=1,
    )
    r2, r1 = halo_lines(o2, o1)
    grad_pre, ordered = call(
        gate_kernel,
        (tile, sds((S, 2 * C), BF)),
        place,
        own,
        m2,
        m1,
        n2,
        n1,
        hrow,
        pre,
        grad,
        near,
        scratch=[back],
        late=1,
    )
    grads = gathered(ordered, "gy")
    own, m1, m2, loc = spread(place, nbt, grad_pre, weight_one, 4 * 10**9)
    m2, m1 = halo_lines(m2, m1)
    wide = 7 * C
    stack = sds((4 * S, wide), BF)
    cols_one, cols_two = call(
        columns_kernel,
        (stack, stack),
        place,
        *pays,
        r2,
        r1,
        near,
        own,
        scratch=[
            pltpu.VMEM((EXT, 2 * C), BF),
            pltpu.VMEM((32, C), F32),
            pltpu.VMEM((128, C), F32),
        ],
        late=1,
        flops=4 * 10**9,
    )
    passed, n2, n1 = halo_columns(place, loc, m2, m1, cols_two)

    def halves(which, cols, kind, flops, late):
        lanes = slice(which * C, (which + 1) * C)
        half = sds((128, wide), kind)
        return call(
            functools.partial(weight_kernel, lanes),
            (half, half),
            place,
            *grads,
            cols,
            late,
            scratch=[pltpu.VMEM((C, 4 * S), BF)],
            late=1,
            flops=flops,
        )

    keep_two, send_two = halves(0, cols_two, F32, 4 * 10**9, passed)
    come_two = cross(send_two, "gx", 1)
    keep_one, send_one = halves(1, cols_one, BF, 10**5, keep_two)
    come_one = cross(send_one, "gx", 1)
    some = sds((128, C), BF)
    rows_keep, rows_send = call(
        rows_kernel,
        (some, some),
        place,
        own,
        m2,
        m1,
        n2,
        n1,
        hrow,
        grad,
        srow,
        keep_one,
        scratch=[back],
        late=1,
        flops=2 * 10**10,
    )
    rows_come = cross(rows_send, "gx", 1)

    def lines(chunks):
        return [chunks[0]] + [cross(chunks[d], "gx", 16 * d) for d in (1, 3, 2)]

    two = call(
        merge_two_kernel,
        (sds((32, wide), BF),) * 4,
        place,
        keep_two,
        come_two,
        rows_keep,
        late=1,
    )
    one = call(
        merge_one_kernel,
        (sds((32, 9 * C), BF),) * 4,
        place,
        keep_one,
        come_one,
        rows_keep,
        rows_come,
        two[0],
        late=1,
        flops=2 * 10**10,
    )
    sum_two = call(
        line_two_kernel, sds((32, wide), BF), place, *lines(two), flops=2 * 10**10
    )
    summed = call(line_one_kernel, sds((64, 10 * C), BF), place, sum_two, *lines(one))
    groups = [[16 * y + 2 * z + e for z in range(8)] for y in range(4) for e in range(2)]
    collected = lax.all_to_all(
        summed.reshape(8, 8, 10 * C),
        "gx",
        split_axis=0,
        concat_axis=0,
        tiled=True,
        axis_index_groups=groups,
    )
    out = sds((4, QW), F32)
    return call(
        lambda *refs: final_kernel(scale, *refs), (tile, out, out), collected, specs=[VM]
    )


def solution(mesh):
    in_specs = (
        P(("gx", "gy"), None),
        P(("gx", "gy"), None),
        P(("gx", "gy"), None),
        P(),
        P(),
        P(("gx", "gy"), None),
        P(("gx", "gy"), None, None),
        P(("gx", "gy"), None, None),
    )
    out_specs = (P(("gx", "gy"), None), P("gx", "gy"), P("gx", "gy"))
    return jax.shard_map(body, mesh=mesh, in_specs=in_specs, out_specs=out_specs, check_vma=False)
```

```python
import functools
import math

import jax
import jax.numpy as jnp
from jax import lax
from jax.experimental import pallas as pl
from jax.experimental.pallas import tpu as pltpu
from jax.sharding import PartitionSpec as P

C = 256
K = 27
S = 192
HB = 32
EXT = S + 8 * HB
QW = 1728
BF = jnp.bfloat16
F32 = jnp.float32


def iota(shape, dim):
    return lax.broadcasted_iota(jnp.int32, shape, dim)


def onehot(mask):
    return jnp.where(mask, 1.0, 0.0).astype(BF)


def mm(a, b):
    return lax.dot_general(a, b, (((1,), (0,)), ((), ())), preferred_element_type=F32)


def mm_t(a, b):
    return lax.dot_general(a, b, (((0,), (0,)), ((), ())), preferred_element_type=F32)


def direction(a, b):
    grid = 3 * (a + 1) + (b + 1)
    return grid - jnp.where(grid > 4, 1, 0)


def channel_order():
    out = iota((C, C), 1)
    parity, rest = out // 128, out % 128
    source = 8 * (rest // 4) + 4 * parity + rest % 4
    return onehot(iota((C, C), 0) == source)


def halo_matrix(halo_row):
    return onehot(iota((S, 8 * HB), 0) == halo_row)


def pack_kernel(
    place, feat, pre, grad, nbr, halo, send, pay, p2, p1, p3, nbt, hrow, srow, pre_out,
    grad_out, ids, halo_ids, send_ids, feat_in, sems
):
    copies = [
        pltpu.make_async_copy(source, target, sems.at[n])
        for n, (source, target) in enumerate(
            (
                (nbr, ids),
                (halo, halo_ids),
                (send, send_ids),
                (feat, feat_in),
                (grad, grad_out),
                (pre, pre_out),
            )
        )
    ]
    for copy in copies:
        copy.start()
    for copy in copies:
        copy.wait()
    table = ids[...].astype(F32)
    heading = jnp.floor((table - S + 0.5) * (1.0 / 24.0))
    table = jnp.where(table >= S, table + 8.0 * heading, table)
    nbt[...] = jnp.full(nbt.shape, -1.0, F32)
    nbt[0:K, 0:S] = table
    z = pre_out[...].astype(F32)
    hidden = (z * (1.0 / (1.0 + jnp.exp(-z)))).astype(BF)
    halo_up = (halo_ids[0] + 1).astype(F32).astype(BF)
    spread = mm(halo_up, onehot(iota((24, 8 * HB), 1) % HB == iota((24, 8 * HB), 0)))
    row = jnp.sum(
        jnp.where(iota((8, 8 * HB), 1) // HB == iota((8, 8 * HB), 0), spread, 0.0),
        axis=0,
        keepdims=True,
    )
    hrow[...] = jnp.broadcast_to(row.astype(jnp.int32) - 1, hrow.shape)
    shifted_up = nbt[...] + 1.0
    high = jnp.floor(shifted_up * (1.0 / 16.0))
    low = shifted_up - 16.0 * high
    pay[S : S + 32, 0:C] = jnp.where(iota((32, C), 0) == 31, row, high).astype(BF)
    pay[S : S + 32, C : 2 * C] = low.astype(BF)
    both = jnp.concatenate([feat_in[...], hidden], axis=0)
    for turn, out in ((0, pay), (1, p1), (2, p2), (3, p3)):
        offset = ((place[1] ^ turn) * QW) % C
        turned = mm(both, onehot(iota((C, C), 0) == (iota((C, C), 1) + offset) % C)).astype(BF)
        out[0:S, 0:C] = turned[0:S]
        out[0:S, C : 2 * C] = turned[S : 2 * S]
        if turn:
            out[S : S + 32, :] = pay[S : S + 32, :]
    lane, peer = iota((64, C), 1), iota((64, C), 0)
    parity = jnp.where(lane < 128, place[0] % 2, 1 - place[0] % 2)
    pick = onehot(peer == 2 * ((lane % 128) // 4) + parity)
    spot = iota((1, C), 1) % 4
    total = jnp.zeros((1, C), F32)
    for c in range(3):
        up = jnp.broadcast_to((send_ids[c] + 1).astype(F32), (8, 64)).astype(BF)
        total = jnp.where(spot == c, mm(up, pick)[0:1, :], total)
    srow[...] = jnp.broadcast_to(total.astype(jnp.int32) - 1, srow.shape)


def spread_kernel(place, nbt, grad, weight, own, m1, m2, loc, acc):
    rows = iota((EXT, C), 0)
    table = nbt[...].astype(jnp.int32)
    gradient = grad[...]
    none = jnp.zeros((C - S, C), BF)
    masks, terms = [], []
    for k in range(K):
        masks.append(onehot(rows == table[k : k + 1, :]))
        terms += [mm(gradient, weight[:, k * C : (k + 1) * C]).astype(BF), none]
    acc[...] = mm(jnp.concatenate(masks, axis=1), jnp.concatenate(terms, axis=0))
    even = place[0] % 2 == 0
    own[...] = acc[0:S, :]
    first, last = jnp.where(even, S, S + 160), jnp.where(even, S + 160, S)
    m1[...] = acc[pl.ds(pl.multiple_of(first, 32), 96), :].astype(BF)
    m2[...] = acc[pl.ds(pl.multiple_of(last, 32), 96), :].astype(BF)
    loc[...] = acc[S + 96 : S + 160, :].astype(BF)


def inner(position, count):
    return (position > 0) & (position < count - 1)


def masked(keep, rows):
    return jnp.where(keep, rows, jnp.zeros_like(rows))


def pass_kernel(place, loc, m2, m1, late, n2, n1):
    even = place[1] % 2 == 0
    first = jnp.where(even, 0, 1)
    far = inner(place[0], 64)
    for out, side in ((n1, first), (n2, 1 - first)):
        out[0:32, :] = loc[pl.ds(pl.multiple_of(side * 32, 32), 32), :]
        out[32:64, :] = m1[pl.ds(pl.multiple_of(side * 64, 32), 32), :]
        out[64:96, :] = masked(far, m2[pl.ds(pl.multiple_of(side * 64, 32), 32), :])


def settled(place, own, m1, m2, n1, n2, hrow, back):
    da = jnp.where(place[0] % 2 == 0, 1, -1)
    db = jnp.where(place[1] % 2 == 0, 1, -1)
    back[direction(da, 0)] = m1[32:64, :]
    back[direction(-da, 0)] = masked(inner(place[0], 64), m2[32:64, :])
    beside = inner(place[1], 4)
    for ref, side, keep in ((n1, db, True), (n2, -db, beside)):
        rows = ref[...] if keep is True else masked(keep, ref[...])
        back[direction(0, side)] = rows[0:32, :]
        back[direction(da, side)] = rows[32:64, :]
        back[direction(-da, side)] = rows[64:96, :]
    rows = back[...].reshape(8 * HB, C)
    return own[...] + mm(halo_matrix(hrow[0:1, :]), rows)


def gate_kernel(place, own, m2, m1, n2, n1, hrow, pre, grad, late, out, ordered, back):
    hidden_grad = settled(place, own, m1, m2, n1, n2, hrow, back)
    z = pre[...].astype(F32)
    g = 1.0 / (1.0 + jnp.exp(-z))
    value = (hidden_grad * g * (1.0 + z * (1.0 - g))).astype(BF)
    out[...] = value
    order = channel_order()
    ordered[:, 0:C] = mm(grad[...], order).astype(BF)
    ordered[:, C : 2 * C] = mm(value, order).astype(BF)


def rows_kernel(place, own, m2, m1, n2, n1, hrow, grad, srow, late, keep, send, back):
    total = settled(place, own, m1, m2, n1, n2, hrow, back)
    value = (grad[...].astype(F32) + total).astype(BF)
    chosen = mm_t(onehot(iota((S, C), 0) == srow[0:1, :]), value).astype(BF)
    keep[...] = chosen[0:128, :]
    send[...] = chosen[128:256, :]


def pick_kernel(place, p0, p2, p1, p3, late, o2, o1, loc, picked):
    column = place[1]
    for turn, pay in enumerate((p0, p1, p2, p3)):
        halo_row = pay[S + 16 : S + 32, 0:C].astype(F32)[15:16, :].astype(jnp.int32) - 1
        rows = mm_t(halo_matrix(halo_row), pay[0:S, 0 : 2 * C])
        picked[column ^ turn] = rows.astype(BF)
    even = place[0] % 2 == 0
    up = pl.multiple_of(jnp.where(even, 160, 0), 32)
    down = pl.multiple_of(jnp.where(even, 0, 160), 32)
    none = jnp.zeros((HB, 2 * C), BF)
    for tile in range(4):
        for b in (-1, 0, 1):
            source = tile - b
            at = HB * (b + 1)
            for out, side in ((o1, up), (o2, down)):
                rows = picked[source, pl.ds(side + at, HB), :] if 0 <= source < 4 else none
                to = 96 * tile + at
                out[to : to + HB, :] = rows[:, 0:C]
                out[to + 384 : to + 384 + HB, :] = rows[:, C : 2 * C]
            if b:
                to = 0 if b < 0 else HB
                rows = picked[source, 96 + to : 96 + to + HB, :] if 0 <= source < 4 else none
                loc[tile, to : to + HB, :] = rows


def columns_kernel(
    place, p0, p2, p1, p3, r2, r1, loc, late, cols_one, cols_two, ext, ids, sel
):
    column = place[1]
    start = column * QW
    first_k = start // C
    offset = start % C
    even = place[0] % 2 == 0
    far = inner(place[0], 64)
    lane = iota((S, 2 * C), 1) % C
    early = lane < C - offset
    for turn, pay in enumerate((p0, p1, p2, p3)):
        tile = column ^ turn
        for half in range(2):
            lanes = slice(half * C, (half + 1) * C)
            at = pl.multiple_of(384 * half + 96 * tile, 32)
            above, below = r1[pl.ds(at, 96), :], masked(far, r2[pl.ds(at, 96), :])
            for to, piece in (
                (0, pay[0:S, lanes]),
                (S, jnp.where(even, above, below)),
                (S + 96, loc[tile, :, lanes]),
                (S + 160, jnp.where(even, below, above)),
            ):
                ext[to : to + piece.shape[0], lanes] = piece
        high = pay[S : S + 32, 0:C].astype(F32)
        low = pay[S : S + 32, C : 2 * C].astype(F32)
        ids[0:32, :] = 16.0 * high + low - 1.0
        for part in range(8):
            sel[part : part + 1, :] = ids[pl.ds(first_k + part, 1), :]
        table = jnp.transpose(sel[...])[:, 0:8].astype(jnp.int32)
        extended = ext[...]
        match = [
            onehot(iota((S, EXT), 1) == table[0:S, part : part + 1]) for part in range(8)
        ]
        found = mm(jnp.concatenate(match, axis=0), extended).astype(BF)
        for part in range(7):
            merged = jnp.where(
                early, found[part * S : (part + 1) * S], found[(part + 1) * S : (part + 2) * S]
            )
            lanes = slice(part * C, (part + 1) * C)
            cols_one[turn * S : (turn + 1) * S, lanes] = merged[:, 0:C]
            cols_two[turn * S : (turn + 1) * S, lanes] = merged[:, C : 2 * C]


def weight_kernel(lanes, place, g0, g2, g1, g3, cols, late, keep, send, gt):
    for turn, grad in enumerate((g0, g1, g2, g3)):
        gt[:, turn * S : (turn + 1) * S] = jnp.transpose(grad[:, lanes].astype(F32)).astype(BF)
    mine = pl.multiple_of((place[0] % 2) * 128, 128)
    other = pl.multiple_of(128 - mine, 128)
    left = jnp.concatenate([gt[pl.ds(mine, 128), :], gt[pl.ds(other, 128), :]], axis=0)
    for part in range(7):
        lanes = slice(part * C, (part + 1) * C)
        block = mm(left, cols[:, lanes])
        keep[:, lanes] = block[0:128].astype(keep.dtype)
        send[:, lanes] = block[128:256].astype(send.dtype)


def merge_two_kernel(place, keep, come, late, *outs):
    line = place[0] // 16
    for turn, out in enumerate(outs):
        rows = pl.ds(pl.multiple_of(32 * (line ^ turn), 32), 32)
        out[...] = (keep[rows, :] + come[rows, :].astype(F32)).astype(BF)


def merge_one_kernel(place, keep, come, rk, rs, late, *outs):
    first = place[0] % 2 == 0
    line = place[0] // 16
    for turn, out in enumerate(outs):
        rows = pl.ds(pl.multiple_of(32 * (line ^ turn), 32), 32)
        total = keep[rows, :].astype(F32) + come[rows, :].astype(F32)
        out[:, 0 : 7 * C] = total.astype(BF)
        mine, other = rk[rows, :], rs[rows, :]
        out[:, 7 * C : 8 * C] = jnp.where(first, mine, other)
        out[:, 8 * C : 9 * C] = jnp.where(first, other, mine)


def line_two_kernel(place, a0, a1, a3, a2, out):
    total = a0[...].astype(F32)
    for part in (a1, a2, a3):
        total = total + part[...].astype(F32)
    out[...] = total.astype(BF)


def line_one_kernel(place, two, b0, b1, b3, b2, out):
    line = place[0] // 16
    to, at = iota((64, 64), 0), iota((64, 64), 1)
    order = onehot(at == 32 * ((to % 8) // 4) + 4 * (to // 8) + to % 4)
    for n in range(7):
        lanes = slice(n * C, (n + 1) * C)
        total = b0[:, lanes].astype(F32)
        for part in (b1, b2, b3):
            total = total + part[:, lanes].astype(F32)
        value = jnp.concatenate([total.astype(BF), two[:, lanes]], axis=0)
        out[:, lanes] = mm(order, value).astype(BF)
    sources = [
        part[:, (7 + core) * C : (8 + core) * C] for part in (b0, b1, b2, b3) for core in range(2)
    ]
    stacked = jnp.concatenate(sources, axis=0)
    to, at = iota((64, C), 0), iota((64, C), 1)
    for n in range(3):
        index = 8 * n + to % 8
        spot = (
            (index // 6 == (line ^ (at // 64)))
            & ((index % 6) // 3 == (at // 32) % 2)
            & (at % 32 == 4 * (to // 8) + index % 3)
        )
        out[:, (7 + n) * C : (8 + n) * C] = mm(onehot(spot), stacked).astype(BF)


def final_kernel(scale, arrived, rows, one, two):
    total = jnp.sum(arrived[:, :, 0 : 7 * C].astype(F32), axis=0) * scale
    one[...] = total[0:4, 0:QW]
    two[...] = total[4:8, 0:QW]
    to, at = iota((S, S), 0), iota((S, S), 1)
    spot = ((at % 64) // 8 == (to // 6) % 8) & (
        8 * (at // 64) + at % 8 == 6 * (to // 48) + to % 6
    )
    found = arrived[:, :, 7 * C : 10 * C].astype(F32)
    pieces = [found[:, :, n * C : (n + 1) * C].reshape(64, C).astype(BF) for n in range(3)]
    rows[...] = mm(onehot(spot), jnp.concatenate(pieces, axis=0)).astype(BF)


def sds(shape, dtype):
    return jax.ShapeDtypeStruct(shape, dtype)


SMEM = pl.BlockSpec(memory_space=pltpu.SMEM)
VM = pl.BlockSpec(memory_space=pltpu.VMEM)
HBM = pl.BlockSpec(memory_space=pltpu.HBM)
ANY = pl.BlockSpec(memory_space=pl.ANY)


def call(kernel, outs, *args, scratch=(), specs=None, late=0, flops=10**5):
    if specs is None:
        specs = [SMEM] + [VM] * (len(args) - 1 - late) + [ANY] * late
    return pl.pallas_call(
        kernel,
        out_shape=outs,
        in_specs=specs,
        out_specs=jax.tree.map(lambda _: VM, outs),
        scratch_shapes=list(scratch),
        compiler_params=pltpu.CompilerParams(vmem_limit_bytes=40 * 2**20),
        cost_estimate=pl.CostEstimate(flops=flops, bytes_accessed=10**4, transcendentals=0),
    )(*args)


def spread(place, nbt, grad, weight, flops):
    edge = sds((96, C), BF)
    return call(
        spread_kernel,
        (sds((S, C), F32), edge, edge, sds((64, C), BF)),
        place,
        nbt,
        grad,
        weight,
        scratch=[pltpu.VMEM((EXT, C), F32)],
        flops=flops,
    )


def swap(value, axis, turn):
    gx, gy = lax.axis_size("gx"), lax.axis_size("gy")
    pairs = []
    for i in range(gx):
        for j in range(gy):
            n, size = (i, gx) if axis == "gx" else (j, gy)
            q = n ^ 1 if turn == 1 else ((n + 1) ^ 1) - 1
            if axis == "gx":
                to = (q, j) if 0 <= q < size else (i, j ^ 1)
            else:
                to = (i, q) if 0 <= q < size else (i ^ 1, j)
            pairs.append((i * gy + j, to[0] * gy + to[1]))
    return lax.ppermute(value, ("gx", "gy"), pairs)


def cross(value, axis, mask):
    return lax.ppermute(value, axis, [(n, n ^ mask) for n in range(lax.axis_size(axis))])


def gathered(value, axis, base=1):
    return [value] + [cross(value, axis, base * d) for d in (2, 1, 3)]


def halo_lines(m2, m1):
    return swap(m2, "gx", 2), swap(m1, "gx", 1)


def halo_columns(place, loc, m2, m1, late, flops=10**5):
    edge = sds((96, C), BF)
    n2, n1 = call(pass_kernel, (edge, edge), place, loc, m2, m1, late, late=1, flops=flops)
    return n1, swap(n2, "gy", 2), swap(n1, "gy", 1)


def body(features, pre_act, grad_out, weight_one, weight_two, neighbours, halo_list, send_list):
    gx = lax.axis_size("gx")
    scale = 1.0 / math.sqrt(S * gx * lax.axis_size("gy"))
    place = jnp.stack([lax.axis_index("gx"), lax.axis_index("gy")]).astype(jnp.int32)
    tile = sds((S, C), BF)
    pay, p2, p1, p3, nbt, hrow, srow, pre, grad = call(
        pack_kernel,
        (
            *[sds((S + 32, 2 * C), BF)] * 4,
            sds((32, C), F32),
            sds((8, C), jnp.int32),
            sds((8, C), jnp.int32),
            tile,
            tile,
        ),
        place,
        *[
            pltpu.with_memory_space_constraint(value, pltpu.HBM)
            for value in (
                features,
                pre_act,
                grad_out,
                neighbours.T,
                halo_list,
                jnp.transpose(send_list, (2, 0, 1)),
            )
        ],
        specs=[SMEM] + [HBM] * 6,
        flops=4 * 10**9,
        scratch=[
            pltpu.VMEM((K, S), jnp.int32),
            pltpu.VMEM((1, 8, 24), jnp.int32),
            pltpu.VMEM((3, 1, 64), jnp.int32),
            pltpu.VMEM((S, C), BF),
            pltpu.SemaphoreType.DMA((6,)),
        ],
    )
    pays = [pay] + [cross(value, "gy", d) for d, value in ((2, p2), (1, p1), (3, p3))]
    back = pltpu.VMEM((8, HB, C), BF)
    own, m1, m2, loc = spread(place, nbt, grad, weight_two, 10**5)
    m2, m1 = halo_lines(m2, m1)
    passed, n2, n1 = halo_columns(place, loc, m2, m1, own)
    picks = sds((768, C), BF)
    o2, o1, near = call(
        pick_kernel,
        (picks, picks, sds((4, 64, 2 * C), BF)),
        place,
        *pays,
        passed,
        scratch=[pltpu.VMEM((4, 8 * HB, 2 * C), BF)],
        late=1,
    )
    r2, r1 = halo_lines(o2, o1)
    grad_pre, ordered = call(
        gate_kernel,
        (tile, sds((S, 2 * C), BF)),
        place,
        own,
        m2,
        m1,
        n2,
        n1,
        hrow,
        pre,
        grad,
        near,
        scratch=[back],
        late=1,
    )
    grads = gathered(ordered, "gy")
    own, m1, m2, loc = spread(place, nbt, grad_pre, weight_one, 4 * 10**9)
    m2, m1 = halo_lines(m2, m1)
    wide = 7 * C
    stack = sds((4 * S, wide), BF)
    cols_one, cols_two = call(
        columns_kernel,
        (stack, stack),
        place,
        *pays,
        r2,
        r1,
        near,
        own,
        scratch=[
            pltpu.VMEM((EXT, 2 * C), BF),
            pltpu.VMEM((32, C), F32),
            pltpu.VMEM((128, C), F32),
        ],
        late=1,
        flops=4 * 10**9,
    )
    passed, n2, n1 = halo_columns(place, loc, m2, m1, cols_two)

    def halves(which, cols, kind, flops, late):
        lanes = slice(which * C, (which + 1) * C)
        half = sds((128, wide), kind)
        return call(
            functools.partial(weight_kernel, lanes),
            (half, sds((128, wide), BF)),
            place,
            *grads,
            cols,
            late,
            scratch=[pltpu.VMEM((C, 4 * S), BF)],
            late=1,
            flops=flops,
        )

    keep_two, send_two = halves(0, cols_two, F32, 4 * 10**9, passed)
    come_two = cross(send_two, "gx", 1)
    keep_one, send_one = halves(1, cols_one, BF, 10**5, keep_two)
    come_one = cross(send_one, "gx", 1)
    some = sds((128, C), BF)
    rows_keep, rows_send = call(
        rows_kernel,
        (some, some),
        place,
        own,
        m2,
        m1,
        n2,
        n1,
        hrow,
        grad,
        srow,
        keep_one,
        scratch=[back],
        late=1,
        flops=2 * 10**10,
    )
    rows_come = cross(rows_send, "gx", 1)

    def lines(chunks):
        return [chunks[0]] + [cross(chunks[d], "gx", 16 * d) for d in (1, 3, 2)]

    two = call(
        merge_two_kernel,
        (sds((32, wide), BF),) * 4,
        place,
        keep_two,
        come_two,
        rows_keep,
        late=1,
    )
    one = call(
        merge_one_kernel,
        (sds((32, 9 * C), BF),) * 4,
        place,
        keep_one,
        come_one,
        rows_keep,
        rows_come,
        two[0],
        late=1,
        flops=2 * 10**10,
    )
    sum_two = call(
        line_two_kernel, sds((32, wide), BF), place, *lines(two), flops=2 * 10**10
    )
    summed = call(line_one_kernel, sds((64, 10 * C), BF), place, sum_two, *lines(one))
    groups = [[16 * y + 2 * z + e for z in range(8)] for y in range(4) for e in range(2)]
    collected = lax.all_to_all(
        summed.reshape(8, 8, 10 * C),
        "gx",
        split_axis=0,
        concat_axis=0,
        tiled=True,
        axis_index_groups=groups,
    )
    out = sds((4, QW), F32)
    return call(
        lambda *refs: final_kernel(scale, *refs), (tile, out, out), collected, specs=[VM]
    )


def solution(mesh):
    in_specs = (
        P(("gx", "gy"), None),
        P(("gx", "gy"), None),
        P(("gx", "gy"), None),
        P(),
        P(),
        P(("gx", "gy"), None),
        P(("gx", "gy"), None, None),
        P(("gx", "gy"), None, None),
    )
    out_specs = (P(("gx", "gy"), None), P("gx", "gy"), P("gx", "gy"))
    return jax.shard_map(body, mesh=mesh, in_specs=in_specs, out_specs=out_specs, check_vma=False)
```
